128 devices in a mesh: grp: 4 (over x_lo, core), wide: 32 (over y, x_hi, z).
Axes of the slice: x: 4 (x_hi: 2, x_lo: 2; x = x_hi * 2 + x_lo), y: 4, z: 4, core: 2. Of those that a mesh axis runs over, the one named last changes fastest.
Arguments:
- token_ids: int32 [4, 8192], P('grp', 'wide'), may hold values from 0 to 49151
- targets: int32 [4, 8192], P('grp', 'wide'), may hold values from 0 to 49151
- segment_ids: int32 [4, 8192], P('grp', 'wide'), may hold values from 0 to 127, never falling along the last dimension, each value on 1 to 128 neighbouring positions
- row_counts: int32 [4, 32, 3], P('grp', 'wide'), may hold values from 0 to 1, as said below
- embed_table_master: float32 [4, 49152, 576], P('grp', 'wide')
- embed_table_first: float32 [4, 49152, 576], P('grp', 'wide'), may hold values from -2.861023e-06 to 2.861023e-06
- embed_table_second: float32 [4, 49152, 576], P('grp', 'wide'), may hold values from 1.5697491e-15 to 2.5115985e-14
- embed_table_anchor: float32 [49152, 576], P('wide')
- embed_table_momentum: float32 [49152, 576], P('wide'), may hold values from -0.3125 to 0.3125
- attn_in_master: float32 [4, 576, 960], P('grp', None, 'wide')
- attn_in_first: float32 [4, 576, 960], P('grp', None, 'wide'), may hold values from -2.861023e-06 to 2.861023e-06
- attn_in_second: float32 [4, 576, 960], P('grp', None, 'wide'), may hold values from 1.5697491e-15 to 2.5115985e-14
- attn_in_anchor: float32 [576, 960], P(None, 'wide')
- attn_in_momentum: float32 [576, 960], P(None, 'wide'), may hold values from -0.3125 to 0.3125
- ffn_in_master: float32 [4, 576, 3072], P('grp', None, 'wide')
- ffn_in_first: float32 [4, 576, 3072], P('grp', None, 'wide'), may hold values from -2.861023e-06 to 2.861023e-06
- ffn_in_second: float32 [4, 576, 3072], P('grp', None, 'wide'), may hold values from 1.5697491e-15 to 2.5115985e-14
- ffn_in_anchor: float32 [576, 3072], P(None, 'wide')
- ffn_in_momentum: float32 [576, 3072], P(None, 'wide'), may hold values from -0.3125 to 0.3125
- proj_out_master: float32 [4, 2112, 576], P('grp', None, 'wide')
- proj_out_first: float32 [4, 2112, 576], P('grp', None, 'wide'), may hold values from -2.861023e-06 to 2.861023e-06
- proj_out_second: float32 [4, 2112, 576], P('grp', None, 'wide'), may hold values from 1.5697491e-15 to 2.5115985e-14
- proj_out_anchor: float32 [2112, 576], P(None, 'wide')
- proj_out_momentum: float32 [2112, 576], P(None, 'wide'), may hold values from -0.3125 to 0.3125
- norm_gains_master: float32 [4, 3, 576], P('grp')
- norm_gains_first: float32 [4, 3, 576], P('grp'), may hold values from -3.0517578e-05 to 3.0517578e-05
- norm_gains_second: float32 [4, 3, 576], P('grp'), may hold values from 1.5697491e-13 to 2.5115986e-12
- norm_gains_anchor: float32 [3, 576], replicated
- norm_gains_momentum: float32 [3, 576], replicated, may hold values from -0.75 to 0.75
Outputs:
- loss_sum: float32 [4], P('grp')
- weight_total: float32 [4], P('grp')
- grad_norm: float32 [4], P('grp')
- embed_table_diff: float32 [49152, 576], P('wide')
- embed_table_outer: float32 [49152, 576], P('wide')
- embed_table_weight: float32 [49152, 576], P('wide')
- embed_table_first_new: float32 [4, 49152, 576], P('grp', 'wide')
- embed_table_second_new: float32 [4, 49152, 576], P('grp', 'wide')
- attn_in_diff: float32 [576, 960], P(None, 'wide')
- attn_in_outer: float32 [576, 960], P(None, 'wide')
- attn_in_weight: float32 [576, 960], P(None, 'wide')
- attn_in_first_new: float32 [4, 576, 960], P('grp', None, 'wide')
- attn_in_second_new: float32 [4, 576, 960], P('grp', None, 'wide')
- ffn_in_diff: float32 [576, 3072], P(None, 'wide')
- ffn_in_outer: float32 [576, 3072], P(None, 'wide')
- ffn_in_weight: float32 [576, 3072], P(None, 'wide')
- ffn_in_first_new: float32 [4, 576, 3072], P('grp', None, 'wide')
- ffn_in_second_new: float32 [4, 576, 3072], P('grp', None, 'wide')
- proj_out_diff: float32 [2112, 576], P(None, 'wide')
- proj_out_outer: float32 [2112, 576], P(None, 'wide')
- proj_out_weight: float32 [2112, 576], P(None, 'wide')
- proj_out_first_new: float32 [4, 2112, 576], P('grp', None, 'wide')
- proj_out_second_new: float32 [4, 2112, 576], P('grp', None, 'wide')
- norm_gains_diff: float32 [3, 576], replicated
- norm_gains_outer: float32 [3, 576], replicated
- norm_gains_weight: float32 [3, 576], replicated
- norm_gains_first_new: float32 [4, 3, 576], P('grp')
- norm_gains_second_new: float32 [4, 3, 576], P('grp')
The draws below stay inside these ranges and needn't reach their ends.
Inputs may be any that keep to these rules, and one draw needn't show every extreme that they name: `row_counts`: each device's three counts sum to 1 (one row); along wide the source never falls within a group; each group's first device holds a web row and its last a math row.
All inputs are finite; a program needn't handle non-finite values.
Results may differ from the reference program's by a relative error of at most 0.019.
The reference program's roundings to bfloat16 on the way count: a program that leaves them out, or rounds other values in their place, can miss the bound.
Values may be sent and summed in bfloat16 or wider, within the bound.
A program may use at most 192 MiB of HBM per device.

```python
import math
import jax
import jax.numpy as jnp
import numpy as np
from jax import lax

V = 49152
D = 576
H = 9
KVH = 3
HD = 64
FF = 1536
TOK_DEV = 256
STEP = 8
GTOK = 8192
QKV = 960
PARAMS = 31852224
N_GRP = 4
N_WIDE = 32


def paired(key, tag, shape, scale):
    return jax.random.normal(jax.random.fold_in(key, tag), shape, jnp.float32) * scale


def drifted(key, tag, shape, scale):
    base = paired(key, tag, shape, scale)
    drift = jax.random.normal(jax.random.fold_in(key, tag + 1), (N_GRP,) + shape, jnp.float32)
    return base[None] + 0.5 * drift * scale


def vocab_scale(top):
    rising = jnp.arange(V).astype(jnp.float32)[:, None] / V
    return (1.0 + top * rising) / D ** 0.5


def output_scale():
    place = jnp.arange(D + FF)[:, None]
    return jnp.where(place < D, D ** (-0.5), FF ** (-0.5)).astype(jnp.float32)


def gains_base(key):
    rising = 0.5 + jnp.arange(D).astype(jnp.float32) / D
    jitter = jax.random.uniform(jax.random.fold_in(key, 51), (3, D), jnp.float32, 0.8, 1.25)
    return rising[None, :] * jitter


def draw_row_counts(key, part):
    key = jax.random.fold_in(key, 61)
    first_key, second_key = jax.random.split(key, 2)
    first_cut = jax.random.randint(first_key, (N_GRP, 1), 1, N_WIDE // 2 + 1)
    spread = jax.random.randint(second_key, (N_GRP, 1), 0, N_WIDE * 64)
    second_cut = first_cut + 1 + spread % (N_WIDE - 1 - first_cut)
    place = jnp.arange(N_WIDE)[None, :]
    source = (place >= first_cut).astype(jnp.int32) + (place >= second_cut).astype(jnp.int32)
    return (source[:, :, None] == jnp.arange(3)[None, None, :]).astype(jnp.int32)


def draw_embed_table_anchor(key, part):
    top = 2.0
    return paired(key, 11, (V, D), vocab_scale(top))


def draw_embed_table_master(key, part):
    top = 2.0
    return drifted(key, 11, (V, D), vocab_scale(top))


def draw_attn_in_anchor(key, part):
    return paired(key, 21, (D, (H + 2 * KVH) * HD), D ** (-0.5))


def draw_attn_in_master(key, part):
    return drifted(key, 21, (D, (H + 2 * KVH) * HD), D ** (-0.5))


def draw_ffn_in_anchor(key, part):
    return paired(key, 31, (D, 2 * FF), D ** (-0.5))


def draw_ffn_in_master(key, part):
    return drifted(key, 31, (D, 2 * FF), D ** (-0.5))


def draw_proj_out_anchor(key, part):
    return paired(key, 41, (D + FF, D), output_scale())


def draw_proj_out_master(key, part):
    return drifted(key, 41, (D + FF, D), output_scale())


def draw_norm_gains_anchor(key, part):
    return gains_base(key)


def draw_norm_gains_master(key, part):
    drift = jax.random.normal(jax.random.fold_in(key, 52), (N_GRP, 3, D), jnp.float32)
    return gains_base(key)[None] + 0.1 * drift


def touch_ends(drawn, stream_key, low, largest):
    longest = drawn.shape.index(max(drawn.shape))
    spots = []
    for shift in (0, 1):
        where = [jax.random.randint(jax.random.fold_in(stream_key, axis), (), 0, length) for axis, length in enumerate(drawn.shape)]
        where[longest] = (where[longest] + shift) % drawn.shape[longest]
        spots.append(tuple(where))
    return drawn.at[spots[0]].set(low).at[spots[1]].set(largest)


def level_of(stream_key, dims, cuts, low, largest):
    factor_of, own = 1.0, jax.random.fold_in(stream_key, 6)
    for position, shards_of in cuts:
        steps = jnp.exp(jax.random.uniform(jax.random.fold_in(own, position), (shards_of,), jnp.float32, low / len(cuts), largest / len(cuts)))
        factor_of = factor_of * jnp.repeat(steps, dims[position] // shards_of).reshape([-1 if axis == position else 1 for axis in range(len(dims))])
    return factor_of


def cumulative_ranks(amount, slope):
    loads = [(1 << 20) // math.isqrt(standing ** slope) + 1 for standing in range(1, amount + 1)]
    scale = 1 + sum(loads) // (1 << 30)
    return np.cumsum(np.array([max(1, weight // scale) for weight in loads]))


def ranked_ids(own_key, extent, number_of, skew):
    listing = cumulative_ranks(number_of, skew)
    pick = jax.random.randint(jax.random.fold_in(own_key, 1), extent, 0, int(listing[number_of - 1]))
    grade = jnp.searchsorted(jnp.asarray(listing, jnp.int32), pick, side="right")
    return jax.random.permutation(jax.random.fold_in(own_key, 2), number_of)[grade].astype(jnp.int32)


def split_up(number_of, total, limit, skew):
    weights = [(1 << 20) // math.isqrt(rank ** skew) + 1 for rank in range(2, number_of + 1)]
    surplus, holding = total - limit - (number_of - 1), [1] * (number_of - 1)
    while surplus > 0:
        movable = [i for i in range(number_of - 1) if holding[i] < limit]
        mass, budget = sum([weights[i] for i in movable]), surplus
        for i in movable:
            extra = min(limit - holding[i], max(1, budget * weights[i] // mass), surplus)
            holding[i] = holding[i] + extra
            surplus = surplus - extra
    return np.array([limit] + holding)


def ragged(stream_key, amount, total, reach, skew):
    if amount == 2:
        one = jax.random.randint(stream_key, (), max(1, total - reach), min(reach, total - 1) + 1)
        return jnp.stack([one, total - one])
    lengths = jnp.asarray(split_up(amount, total, reach, skew), jnp.int32)
    twos = (amount - 1) // 2
    source_of, receiver = lengths[1:1 + 2 * twos:2], lengths[2:2 + 2 * twos:2]
    room = jnp.minimum(source_of - 1, reach - receiver)
    passed = jax.random.randint(jax.random.fold_in(stream_key, 1), (twos,), 0, 1 << 20) % (room + 1)
    lengths = lengths.at[1:1 + 2 * twos:2].set(source_of - passed).at[2:2 + 2 * twos:2].set(receiver + passed)
    return lengths[jax.random.permutation(jax.random.fold_in(stream_key, 2), amount)]


def normal_values(stream_key, shape, width, most, cuts=(), kind=jnp.bfloat16):
    array = jax.random.normal(stream_key, shape, jnp.float32) * width
    if len(cuts) > 0:
        array = level_of(stream_key, shape, cuts, -0.22, 0.18) * array
    return jnp.clip(array, min=-most, max=most).astype(kind)


def setup_inputs(seed: int = 0) -> dict:
    splits = jax.random.split(jax.random.key(seed), 30)
    return {
        "token_ids": touch_ends(ranked_ids(splits[0], (N_GRP, GTOK), V, 2), jax.random.fold_in(splits[0], 3), 0, V - 1).astype(jnp.int32),
        "targets": touch_ends(ranked_ids(splits[1], (N_GRP, GTOK), V, 2), jax.random.fold_in(splits[1], 3), 0, V - 1).astype(jnp.int32),
        "segment_ids": jax.vmap(lambda own: jnp.searchsorted(jnp.cumsum(ragged(own, 4 * N_WIDE, GTOK, TOK_DEV // 2, 2)), jnp.arange(GTOK), side="right"))(jax.random.split(splits[2], N_GRP)).reshape((N_GRP, GTOK)).astype(jnp.int32),
        "row_counts": draw_row_counts(jax.random.fold_in(splits[29], 71), 0),
        "embed_table_master": draw_embed_table_master(jax.random.fold_in(splits[29], 71), 0),
        "embed_table_first": normal_values(splits[5], (N_GRP, V, D), (0.0011 / PARAMS ** 0.5), 2.86102294921875e-06, ((0, 4), (1, 32)), jnp.float32),
        "embed_table_second": jnp.clip(jnp.exp(math.log(2.5115985476825177e-14) - 2.7725887 * jax.random.uniform(splits[6], (N_GRP, V, D), jnp.float32) ** level_of(splits[6], (N_GRP, V, D), ((0, 4), (1, 32)), -0.2, 0.2)), 1.5697490923015736e-15, 2.5115985476825177e-14),
        "embed_table_anchor": draw_embed_table_anchor(jax.random.fold_in(splits[29], 71), 0),
        "embed_table_momentum": normal_values(splits[8], (V, D), (0.5 / D ** 0.5), 0.3125, ((0, 32),), jnp.float32),
        "attn_in_master": draw_attn_in_master(jax.random.fold_in(splits[29], 71), 0),
        "attn_in_first": normal_values(splits[10], (N_GRP, D, QKV), (0.0011 / PARAMS ** 0.5), 2.86102294921875e-06, ((0, 4), (2, 32)), jnp.float32),
        "attn_in_second": jnp.clip(jnp.exp(math.log(2.5115985476825177e-14) - 2.7725887 * jax.random.uniform(splits[11], (N_GRP, D, QKV), jnp.float32) ** level_of(splits[11], (N_GRP, D, QKV), ((0, 4), (2, 32)), -0.2, 0.2)), 1.5697490923015736e-15, 2.5115985476825177e-14),
        "attn_in_anchor": draw_attn_in_anchor(jax.random.fold_in(splits[29], 71), 0),
        "attn_in_momentum": normal_values(splits[13], (D, QKV), (0.5 / D ** 0.5), 0.3125, ((1, 32),), jnp.float32),
        "ffn_in_master": draw_ffn_in_master(jax.random.fold_in(splits[29], 71), 0),
        "ffn_in_first": normal_values(splits[15], (N_GRP, D, 2 * FF), (0.0011 / PARAMS ** 0.5), 2.86102294921875e-06, ((0, 4), (2, 32)), jnp.float32),
        "ffn_in_second": jnp.clip(jnp.exp(math.log(2.5115985476825177e-14) - 2.7725887 * jax.random.uniform(splits[16], (N_GRP, D, 2 * FF), jnp.float32) ** level_of(splits[16], (N_GRP, D, 2 * FF), ((0, 4), (2, 32)), -0.2, 0.2)), 1.5697490923015736e-15, 2.5115985476825177e-14),
        "ffn_in_anchor": draw_ffn_in_anchor(jax.random.fold_in(splits[29], 71), 0),
        "ffn_in_momentum": normal_values(splits[18], (D, 2 * FF), (0.5 / D ** 0.5), 0.3125, ((1, 32),), jnp.float32),
        "proj_out_master": draw_proj_out_master(jax.random.fold_in(splits[29], 71), 0),
        "proj_out_first": normal_values(splits[20], (N_GRP, D + FF, D), (0.0011 / PARAMS ** 0.5), 2.86102294921875e-06, ((0, 4), (2, 32)), jnp.float32),
        "proj_out_second": jnp.clip(jnp.exp(math.log(2.5115985476825177e-14) - 2.7725887 * jax.random.uniform(splits[21], (N_GRP, D + FF, D), jnp.float32) ** level_of(splits[21], (N_GRP, D + FF, D), ((0, 4), (2, 32)), -0.2, 0.2)), 1.5697490923015736e-15, 2.5115985476825177e-14),
        "proj_out_anchor": draw_proj_out_anchor(jax.random.fold_in(splits[29], 71), 0),
        "proj_out_momentum": normal_values(splits[23], (D + FF, D), (0.5 / D ** 0.5), 0.3125, ((1, 32),), jnp.float32),
        "norm_gains_master": draw_norm_gains_master(jax.random.fold_in(splits[29], 71), 0),
        "norm_gains_first": normal_values(splits[25], (N_GRP, 3, D), (0.011 / PARAMS ** 0.5), 3.0517578125e-05, ((0, 4),), jnp.float32),
        "norm_gains_second": jnp.clip(jnp.exp(math.log(2.5115985680113084e-12) - 2.7725887 * jax.random.uniform(splits[26], (N_GRP, 3, D), jnp.float32) ** level_of(splits[26], (N_GRP, 3, D), ((0, 4),), -0.2, 0.2)), 1.5697491050070678e-13, 2.5115985680113084e-12),
        "norm_gains_anchor": draw_norm_gains_anchor(jax.random.fold_in(splits[29], 71), 0),
        "norm_gains_momentum": normal_values(splits[28], (3, D), 0.05, 0.75, (), jnp.float32),
    }


beta_one = 0.9
beta_two = 0.999
adam_eps = 1e-08
weight_decay = 0.1
inner_rate = 0.02
gain_rate = 0.2
clip_norm = 0.01
penalty_weight = 0.005
outer_rate = 0.7
outer_momentum = 0.9
rope_base = 100000.0
norm_eps = 1e-05
masked_score = -1e+30
highest = lax.Precision.HIGHEST

@jax.custom_vjp
def low(v):
    return lax.optimization_barrier(v.astype(jnp.bfloat16)).astype(jnp.float32)

@jax.custom_vjp
def low_back(v):
    return v

def low_keep(v):
    return (low(v), None)

def low_pass(kept, grad):
    return (grad,)

def back_keep(v):
    return (v, None)

def back_low(kept, grad):
    return (low(grad),)
low.defvjp(low_keep, low_pass)
low_back.defvjp(back_keep, back_low)

def rms_normed(values, gain):
    return values * lax.rsqrt(lax.optimization_barrier(jnp.mean(values * values, -1, keepdims=True)) + norm_eps) * gain

def rotary(length, head_size):
    half = head_size // 2
    freqs = rope_base ** (-(jnp.arange(half, dtype=jnp.float32) * 2.0) / head_size)
    angles = jnp.arange(length, dtype=jnp.float32)[:, None] * freqs[None, :]
    return (jnp.concatenate([jnp.cos(angles)] * 2, -1), jnp.concatenate([jnp.sin(angles)] * 2, -1))

def rotate(values, cosine, sine):
    half = values.shape[-1] // 2
    turned = jnp.concatenate([-values[..., half:], values[..., :half]], -1)
    return values * cosine[:, None, :] + turned * sine[:, None, :]

def group_loss(table, attn_in, ffn_in, proj_out, gains, ids, targets, segments, token_weight, total):
    rows, length = ids.shape
    table_low = low(table)
    attn_low = low(attn_in)
    ffn_low = low(ffn_in)
    proj_low = low(proj_out)
    kv_width = KVH * HD
    hidden = low_back(table_low[ids])
    normed = low(rms_normed(hidden, gains[0]))
    mixed = low_back(jnp.einsum('rsd,de->rse', normed, attn_low, precision=highest))
    cosine, sine = rotary(length, HD)
    queries = low(rotate(mixed[..., :D].reshape(rows, length, H, HD), cosine, sine))
    keys = low(rotate(mixed[..., D:D + kv_width].reshape(rows, length, KVH, HD), cosine, sine))
    values = low(mixed[..., D + kv_width:].reshape(rows, length, KVH, HD))
    queries = queries.reshape(rows, length, KVH, H // KVH, HD)
    scores = low_back(jnp.einsum('rqkgc,rtkc->rkgqt', queries, keys, precision=highest) * HD ** (-0.5))
    place = jnp.arange(length)
    allowed = (place[None, :, None] >= place[None, None, :]) & (segments[:, :, None] == segments[:, None, :])
    scores = jnp.where(allowed[:, None, None], scores, masked_score)
    probs = low(jax.nn.softmax(scores, axis=-1))
    attended = jnp.einsum('rkgqt,rtkc->rqkgc', probs, values, precision=highest).reshape(rows, length, D)
    attended = low(low_back(attended))
    hidden = hidden + low_back(jnp.einsum('rsd,de->rse', attended, proj_low[:D], precision=highest))
    normed = low(rms_normed(hidden, gains[1]))
    gate_up = low_back(jnp.einsum('rsd,de->rse', normed, ffn_low, precision=highest))
    inner = low(jax.nn.silu(gate_up[..., :FF]) * gate_up[..., FF:])
    hidden = hidden + low_back(jnp.einsum('rsf,fd->rsd', inner, proj_low[D:], precision=highest))
    final = low(rms_normed(hidden, gains[2])).reshape(rows * length, D)
    block = math.gcd(rows * length, 1024)

    def head_block(pieces):
        rows_blk, target_blk, weight_blk = pieces
        logits = low_back(jnp.dot(rows_blk, table_low.T, precision=highest))
        normalizer = jax.nn.logsumexp(logits, axis=-1)
        picked = jnp.take_along_axis(logits, target_blk[:, None], -1)[:, 0]
        return jnp.sum(weight_blk * (normalizer - picked + penalty_weight * normalizer * normalizer))
    parts = lax.map(jax.checkpoint(head_block), (final.reshape(-1, block, D), targets.reshape(-1, block), token_weight.reshape(-1, block)))
    loss_total = jnp.sum(parts)
    return (loss_total / total, loss_total)

def reference(token_ids, targets, segment_ids, row_counts, embed_table_master, embed_table_first, embed_table_second, embed_table_anchor, embed_table_momentum, attn_in_master, attn_in_first, attn_in_second, attn_in_anchor, attn_in_momentum, ffn_in_master, ffn_in_first, ffn_in_second, ffn_in_anchor, ffn_in_momentum, proj_out_master, proj_out_first, proj_out_second, proj_out_anchor, proj_out_momentum, norm_gains_master, norm_gains_first, norm_gains_second, norm_gains_anchor, norm_gains_momentum):
    masters = (embed_table_master, attn_in_master, ffn_in_master, proj_out_master, norm_gains_master)
    firsts = (embed_table_first, attn_in_first, ffn_in_first, proj_out_first, norm_gains_first)
    seconds = (embed_table_second, attn_in_second, ffn_in_second, proj_out_second, norm_gains_second)
    anchors = (embed_table_anchor, attn_in_anchor, ffn_in_anchor, proj_out_anchor, norm_gains_anchor)
    momenta = (embed_table_momentum, attn_in_momentum, ffn_in_momentum, proj_out_momentum, norm_gains_momentum)
    rates = (inner_rate, inner_rate, inner_rate, inner_rate, gain_rate)
    decays = (weight_decay, weight_decay, weight_decay, weight_decay, 0.0)
    source_weight = jnp.arange(1, 4).astype(jnp.float32)
    loss_sums, totals, norms = ([], [], [])
    diff_sums = [jnp.zeros_like(anchor) for anchor in anchors]
    new_firsts = [[] for kind in range(5)]
    new_seconds = [[] for kind in range(5)]
    for group in range(N_GRP):
        row_weight = lax.optimization_barrier(jnp.sum(row_counts[group].astype(jnp.float32) * source_weight, -1))
        token_weight = jnp.repeat(row_weight, TOK_DEV)
        total = jnp.sum(token_weight)
        ids = token_ids[group].reshape(N_WIDE, TOK_DEV)
        segments = segment_ids[group].reshape(N_WIDE, TOK_DEV)
        goals = targets[group]
        params = tuple((master[group] for master in masters))

        def scaled(*weights):
            return group_loss(*weights, ids, goals, segments, token_weight, total)
        loss, pull, loss_total = jax.vjp(scaled, *params, has_aux=True)
        grads = pull(jnp.ones_like(loss))
        norm = jnp.sqrt(sum((jnp.sum(grad * grad) for grad in grads)))
        factor = jnp.minimum(1.0, clip_norm / norm)
        for kind in range(5):
            grad = grads[kind] * factor
            first = beta_one * firsts[kind][group] + (1.0 - beta_one) * grad
            second = beta_two * seconds[kind][group] + (1.0 - beta_two) * grad * grad
            ratio = first / (1.0 - beta_one ** STEP) / (jnp.sqrt(second / (1.0 - beta_two ** STEP)) + adam_eps)
            weight = params[kind]
            inner = weight - rates[kind] * (ratio + decays[kind] * weight)
            diff_sums[kind] = diff_sums[kind] + (anchors[kind] - inner)
            new_firsts[kind].append(first)
            new_seconds[kind].append(second)
        loss_sums.append(loss_total)
        totals.append(total)
        norms.append(norm)
    results = [jnp.stack(loss_sums), jnp.stack(totals), jnp.stack(norms)]
    for kind in range(5):
        average = diff_sums[kind] / N_GRP
        outer = outer_momentum * momenta[kind] + average
        weight = anchors[kind] - outer_rate * (average + outer_momentum * outer)
        results += [average, outer, weight, jnp.stack(new_firsts[kind]), jnp.stack(new_seconds[kind])]
    return tuple(results)
```

```python
import functools

import jax
import jax.numpy as jnp
from jax import lax
from jax.experimental import pallas as pl
from jax.experimental.pallas import tpu as pltpu
from jax.sharding import PartitionSpec as P

D = 576
H = 9
KVH = 3
HD = 64
FF = 1536
QKV = 960
STEP = 8
T = 256
SHARD = 1536
NW = 32
NG = 4
CAP = 32
FA_ROWS = 128
WP_ROWS = 320

beta_one = 0.9
beta_two = 0.999
adam_eps = 1e-08
weight_decay = 0.1
inner_rate = 0.02
gain_rate = 0.2
clip_norm = 0.01
penalty_weight = 0.005
outer_rate = 0.7
outer_momentum = 0.9
rope_base = 100000.0
norm_eps = 1e-05
masked_score = -1e30

BF = jnp.bfloat16
F32 = jnp.float32
MESH = pl.DeviceIdType.MESH
VMEM = pl.BlockSpec(memory_space=pltpu.VMEM)
ANY = pl.BlockSpec(memory_space=pl.ANY)
DMA = pltpu.SemaphoreType.DMA
MIB = 1 << 20


def params(collective, mib):
    return pltpu.CompilerParams(
        collective_id=collective, has_side_effects=True, vmem_limit_bytes=mib * MIB
    )


def place():
    me = lax.axis_index("wide")
    return me, me // 8, lax.rem(me // 4, 2), lax.rem(me, 4)


def flat(y, xh, z):
    return y * 8 + xh * 4 + z


def turn4(at, by):
    return lax.rem(at + by, 4)


def remote(src, dst, ssem, rsem, **device):
    return pltpu.make_async_remote_copy(
        src_ref=src,
        dst_ref=dst,
        send_sem=ssem,
        recv_sem=rsem,
        device_id=device,
        device_id_type=MESH,
    )


def greet_wide(me, grp=None):
    barrier = pltpu.get_barrier_semaphore()

    def one(k, carry):
        pl.semaphore_signal(
            barrier, inc=1, device_id={"wide": lax.rem(me + k, NW)}, device_id_type=MESH
        )
        return carry

    lax.fori_loop(1, NW, one, 0)
    count = NW - 1
    if grp is not None:
        for k in range(1, NG):
            pl.semaphore_signal(
                barrier, inc=1, device_id={"grp": lax.rem(grp + k, NG)}, device_id_type=MESH
            )
        count += NG - 1
    pl.semaphore_wait(barrier, count)


class Scatter:
    def __init__(self, src_at, dst_at, ssem, rsem, me):
        self.src_at, self.dst_at, self.ssem, self.rsem, self.me = src_at, dst_at, ssem, rsem, me

    def copy(self, k):
        peer = lax.rem(self.me + k, NW)
        return remote(
            self.src_at(peer), self.dst_at(self.me), self.ssem.at[k], self.rsem.at[self.me], wide=peer
        )

    def start(self):
        def one(k, carry):
            self.copy(k).start()
            return carry

        lax.fori_loop(1, NW, one, 0)

    def wait_recv(self):
        def one(k, carry):
            peer = lax.rem(self.me + k, NW)
            remote(
                self.src_at(peer), self.dst_at(peer), self.ssem.at[k], self.rsem.at[peer], wide=peer
            ).wait_recv()
            return carry

        lax.fori_loop(1, NW, one, 0)

    def wait_send(self):
        def one(k, carry):
            self.copy(k).wait_send()
            return carry

        lax.fori_loop(1, NW, one, 0)


class Gather:
    def __init__(self, x, out, rows, ssem, rsem, lsem):
        self.x, self.out, self.half = x, out, rows // 2
        self.ssem, self.rsem, self.lsem = ssem, rsem, lsem
        self.me, self.y, self.xh, self.z = place()
        self.used = 0
        self.sent = []

    def send(self, src, dst, rsem, peer):
        copy = remote(src, dst, self.ssem.at[self.used], rsem, wide=peer)
        self.used += 1
        copy.start()
        self.sent.append(copy)

    def rows(self, part):
        return pl.ds(part * self.half, self.half)

    def wait(self, block, part=None):
        dst = self.out.at[block] if part is None else self.out.at[block, self.rows(part)]
        remote(
            dst, dst, self.ssem.at[0], self.rsem.at[block, 0 if part is None else part], wide=block
        ).wait_recv()

    def whole(self, src, block):
        y, xh, z = self.y, self.xh, self.z
        for k in (1, 3, 2):
            self.send(src, self.out.at[block], self.rsem.at[block, 0], flat(turn4(y, k), xh, z))
            self.send(src, self.out.at[block], self.rsem.at[block, 0], flat(y, xh, turn4(z, k)))

    def start(self):
        other = flat(self.y, 1 - self.xh, self.z)
        self.send(self.x, self.out.at[self.me], self.rsem.at[self.me, 0], other)
        self.local = pltpu.make_async_copy(self.x, self.out.at[self.me], self.lsem)
        self.local.start()
        self.whole(self.x, self.me)

    def second(self):
        other = flat(self.y, 1 - self.xh, self.z)
        self.wait(other)
        self.whole(self.out.at[other], other)

    def third(self, xh):
        y, z = self.y, self.z
        for k in (1, 3, 2):
            block = flat(turn4(y, k), xh, z)
            self.wait(block)
            for m in (1, 3, 2):
                piece = self.out.at[block, self.rows(0)]
                self.send(piece, piece, self.rsem.at[block, 0], flat(y, self.xh, turn4(z, m)))
            block = flat(y, xh, turn4(z, k))
            self.wait(block)
            for m in (1, 3, 2):
                piece = self.out.at[block, self.rows(1)]
                self.send(piece, piece, self.rsem.at[block, 1], flat(turn4(y, m), self.xh, z))

    def finish(self):
        for xh in (self.xh, 1 - self.xh):
            for k in (1, 2, 3):
                for m in (1, 2, 3):
                    block = flat(turn4(self.y, k), xh, turn4(self.z, m))
                    self.wait(block, 0)
                    self.wait(block, 1)
        for copy in self.sent:
            copy.wait_send()
        self.local.wait()


GATHER_SENDS = 1 + 12 + 36


def look_up(got, table, hot, rows, slot_row):
    asked = got[:, slot_row, :].astype(F32)
    asked = jnp.concatenate([asked, jnp.zeros((128 - NW, 128), F32)], 0).T
    step = 8 * CAP
    for first in range(0, NW, 8):
        for d in range(8):
            column = asked[0:CAP, first + d : first + d + 1]
            lanes = lax.broadcasted_iota(jnp.int32, (CAP, SHARD), 1).astype(F32)
            hot[d * CAP : (d + 1) * CAP, :] = jnp.where(lanes == column, 1.0, 0.0).astype(BF)
        picked = lax.dot_general(
            hot[...], table[...], (((1,), (1,)), ((), ())), preferred_element_type=F32
        )
        rows[first * CAP : first * CAP + step, :] = picked.astype(BF)


def slots(at):
    return pl.ds(pl.multiple_of(at * CAP, CAP), CAP)


def front_kernel(
    msg, table, fa, wp, got, emb, most, table_other, fa_all, wp_all,
    hot, rows, own_most, msg_s, msg_r, emb_s, emb_r, most_s, most_r, swap, fa_s, fa_r, wp_s, wp_r, local,
):
    me, y, xh, z = place()
    grp = lax.axis_index("grp")
    greet_wide(me, grp)
    ask = Scatter(lambda p: msg.at[p], lambda p: got.at[p], msg_s, msg_r, me)
    ask.start()
    got[me] = msg[me]
    gather_fa = Gather(fa, fa_all, FA_ROWS, fa_s, fa_r, local.at[0])
    gather_wp = Gather(wp, wp_all, WP_ROWS, wp_s, wp_r, local.at[1])
    gather_fa.start()
    gather_wp.start()
    trade = remote(table, table_other, swap.at[0], swap.at[1], wide=flat(y, 1 - xh, z))
    trade.start()
    ask.wait_recv()
    look_up(got, table, hot, rows, 0)
    reply = Scatter(lambda p: rows.at[slots(p)], lambda p: emb.at[slots(p)], emb_s, emb_r, me)
    reply.start()
    emb[slots(me), :] = rows[slots(me), :]
    largest = jnp.max(got[:, 4, :], 0, keepdims=True)
    own_most[...] = jnp.broadcast_to(largest, (8, 128))
    most[grp] = own_most[...]
    told = []
    for k in range(1, NG):
        other = lax.rem(grp + k, NG)
        told.append(remote(own_most, most.at[grp], most_s.at[k], most_r.at[grp], grp=other))
        told[-1].start()
    gather_fa.second()
    gather_wp.second()
    for side in (xh, 1 - xh):
        gather_fa.third(side)
        gather_wp.third(side)
    reply.wait_recv()
    for k in range(1, NG):
        other = lax.rem(grp + k, NG)
        remote(own_most, most.at[other], most_s.at[k], most_r.at[other], grp=other).wait_recv()
    ask.wait_send()
    reply.wait_send()
    for copy in told:
        copy.wait_send()
    gather_fa.finish()
    gather_wp.finish()
    trade.wait()


def front(msg, table, fa, wp):
    return pl.pallas_call(
        front_kernel,
        name="front",
        out_shape=(
            jax.ShapeDtypeStruct((NW, 8, 128), jnp.int32),
            jax.ShapeDtypeStruct((NW * CAP, D), BF),
            jax.ShapeDtypeStruct((NG, 8, 128), jnp.int32),
            jax.ShapeDtypeStruct((D, SHARD), BF),
            jax.ShapeDtypeStruct((NW, FA_ROWS, D), BF),
            jax.ShapeDtypeStruct((NW, WP_ROWS, 128), BF),
        ),
        in_specs=[VMEM, VMEM, ANY, ANY],
        out_specs=(VMEM, VMEM, VMEM, ANY, ANY, ANY),
        scratch_shapes=[
            pltpu.VMEM((8 * CAP, SHARD), BF),
            pltpu.VMEM((NW * CAP, D), BF),
            pltpu.VMEM((8, 128), jnp.int32),
            DMA((NW,)),
            DMA((NW,)),
            DMA((NW,)),
            DMA((NW,)),
            DMA((NG,)),
            DMA((NG,)),
            DMA((2,)),
            DMA((GATHER_SENDS,)),
            DMA((NW, 2)),
            DMA((GATHER_SENDS,)),
            DMA((NW, 2)),
            DMA((2,)),
        ],
        compiler_params=params(1, 40),
        cost_estimate=pl.CostEstimate(flops=2 * 10**9, bytes_accessed=3 * 10**7, transcendentals=0),
    )(msg, table, fa, wp)


def more_rows_kernel(msg, table, got, emb, hot, rows, msg_s, msg_r, emb_s, emb_r):
    me = lax.axis_index("wide")
    greet_wide(me)
    ask = Scatter(lambda p: msg.at[p], lambda p: got.at[p], msg_s, msg_r, me)
    ask.start()
    got[me] = msg[me]
    ask.wait_recv()
    look_up(got, table, hot, rows, 0)
    reply = Scatter(lambda p: rows.at[slots(p)], lambda p: emb.at[slots(p)], emb_s, emb_r, me)
    reply.start()
    emb[slots(me), :] = rows[slots(me), :]
    reply.wait_recv()
    ask.wait_send()
    reply.wait_send()


def more_rows(msg, table):
    return pl.pallas_call(
        more_rows_kernel,
        name="more_rows",
        out_shape=(
            jax.ShapeDtypeStruct((NW, 8, 128), jnp.int32),
            jax.ShapeDtypeStruct((NW * CAP, D), BF),
        ),
        in_specs=[VMEM, VMEM],
        out_specs=(VMEM, VMEM),
        scratch_shapes=[pltpu.VMEM((8 * CAP, SHARD), BF), pltpu.VMEM((NW * CAP, D), BF)]
        + [DMA((NW,))] * 4,
        compiler_params=params(2, 40),
    )(msg, table)[1]


def more_grads_kernel(msg, rows, got, out, msg_s, msg_r, row_s, row_r):
    me = lax.axis_index("wide")
    greet_wide(me)
    ask = Scatter(lambda p: msg.at[p], lambda p: got.at[p], msg_s, msg_r, me)
    ask.start()
    give = Scatter(lambda p: rows.at[slots(p)], lambda p: out.at[slots(p)], row_s, row_r, me)
    give.start()
    got[me] = msg[me]
    out[slots(me), :] = rows[slots(me), :]
    ask.wait_recv()
    give.wait_recv()
    ask.wait_send()
    give.wait_send()


def more_grads(msg, rows):
    return pl.pallas_call(
        more_grads_kernel,
        name="more_grads",
        out_shape=(
            jax.ShapeDtypeStruct((NW, 8, 128), jnp.int32),
            jax.ShapeDtypeStruct((NW * CAP, D), BF),
        ),
        in_specs=[VMEM, VMEM],
        out_specs=(VMEM, VMEM),
        scratch_shapes=[DMA((NW,))] * 4,
        compiler_params=params(3, 20),
    )(msg, rows)


VOC = 2 * SHARD
TOK = 16 * T
CH = 512
NCH = VOC // CH
HALF = D // 2


def cols(j):
    return pl.ds(pl.multiple_of(j * T, T), T)


def head_kernel(
    final, rows_t, table, table_other, goal, weights,
    grad_final, head_own, head_other, loss,
    fall, expo, tops, stat, stat_in, coef, coef_in, parts, in_a, in_b, sum_a, sum_b, in_a2, in_b2,
    g_s, g_r, st_s, st_r, co_s, co_r, a_s, a_r, b_s, b_r, a2_s, a2_r, b2_s, b2_r,
):
    me, y, xh, z = place()
    mine = y * 4 + z

    def dev(j):
        return flat(j // 4, xh, lax.rem(j, 4))

    barrier = pltpu.get_barrier_semaphore()

    def greet(k, carry):
        pl.semaphore_signal(
            barrier, inc=1, device_id={"wide": dev(lax.rem(mine + k, 16))}, device_id_type=MESH
        )
        return carry

    lax.fori_loop(1, 16, greet, 0)
    pl.semaphore_wait(barrier, 15)

    upper, lower = pl.ds(0, HALF), pl.ds(HALF, HALF)
    sent = []

    def send(src, dst, ssem, rsem, to):
        copy = remote(src, dst, ssem, rsem, wide=to)
        copy.start()
        sent.append(copy)

    def arrived(dst, rsem):
        remote(dst, dst, g_s.at[0], rsem, wide=dev(mine)).wait_recv()

    fall[:, cols(mine)] = final[...]
    used = 0
    for k in (1, 3, 2):
        for to in (flat(turn4(y, k), xh, z), flat(y, xh, turn4(z, k))):
            send(final, fall.at[:, cols(mine)], g_s.at[used], g_r.at[mine, 0], to)
            used += 1

    def logits(j):
        seen = fall[:, cols(j)]
        goals = goal[j, 0:1, :]
        tip, weight, hit = [], [], jnp.zeros((1, T), F32)
        for c in range(NCH):
            part = jnp.dot(rows_t[c * CH : (c + 1) * CH, :], seen, preferred_element_type=F32)
            top = jnp.max(part, 0, keepdims=True)
            power = jnp.exp(part - top)
            spot = lax.broadcasted_iota(jnp.int32, (CH, T), 0) + c * CH
            hit = hit + jnp.sum(jnp.where(spot == goals, part, 0.0), 0, keepdims=True)
            expo[c * CH : (c + 1) * CH, cols(j)] = power.astype(BF)
            tip.append(top)
            weight.append(jnp.sum(power, 0, keepdims=True))
        top = functools.reduce(jnp.maximum, tip)
        total = sum(w * jnp.exp(t - top) for w, t in zip(weight, tip))
        zero = jnp.zeros((1, T), F32)
        tops[j] = jnp.concatenate(tip + [zero] * (8 - NCH), 0)
        stat[j] = jnp.concatenate([top, total, hit] + [zero] * 5, 0)

    logits(mine)
    for k in (1, 3, 2):
        row, column = turn4(y, k), turn4(z, k)
        block = row * 4 + z
        arrived(fall.at[:, cols(block)], g_r.at[block, 0])
        for m in (1, 3, 2):
            piece = fall.at[upper, cols(block)]
            send(piece, piece, g_s.at[used], g_r.at[block, 0], flat(y, xh, turn4(z, m)))
            used += 1
        block = y * 4 + column
        arrived(fall.at[:, cols(block)], g_r.at[block, 0])
        for m in (1, 3, 2):
            piece = fall.at[lower, cols(block)]
            send(piece, piece, g_s.at[used], g_r.at[block, 1], flat(turn4(y, m), xh, z))
            used += 1

    def tell(j):
        return remote(stat.at[j], stat_in.at[mine], st_s.at[j], st_r.at[mine], wide=dev(j))

    def block_at(k):
        return turn4(y, k // 4) * 4 + turn4(z, lax.rem(k, 4))

    def forward(k, carry):
        j = block_at(k)
        dy, dz = k // 4, lax.rem(k, 4)

        @pl.when((dy > 0) & (dz > 0))
        def _():
            arrived(fall.at[upper, cols(j)], g_r.at[j, 0])
            arrived(fall.at[lower, cols(j)], g_r.at[j, 1])

        logits(j)
        tell(j).start()
        return carry

    stat_in[mine] = stat[mine]
    lax.fori_loop(1, 16, forward, 0)

    def hear(k, carry):
        j = lax.rem(mine + k, 16)
        arrived(stat_in.at[j], st_r.at[j])
        return carry

    lax.fori_loop(1, 16, hear, 0)
    tip, weight, hit = stat_in[:, 0, :], stat_in[:, 1, :], stat_in[:, 2, :]
    top = jnp.max(tip, 0, keepdims=True)
    lse = top + jnp.log(jnp.sum(weight * jnp.exp(tip - top), 0, keepdims=True))
    picked = jnp.sum(hit, 0, keepdims=True)
    share, plain = weights[0:1, :], weights[1:2, :]
    zero = jnp.zeros((1, T), F32)
    coef[...] = jnp.concatenate(
        [lse, share * (1.0 + 2.0 * penalty_weight * lse), share] + [zero] * 5, 0
    )
    loss[...] = jnp.concatenate(
        [plain * (lse - picked + penalty_weight * lse * lse)] + [zero] * 7, 0
    )
    coef_in[mine] = coef[...]

    def spread(k):
        j = lax.rem(mine + k, 16)
        return remote(coef, coef_in.at[mine], co_s.at[k], co_r.at[mine], wide=dev(j))

    def spread_start(k, carry):
        spread(k).start()
        return carry

    lax.fori_loop(1, 16, spread_start, 0)

    def piece_a(dz, row):
        return remote(
            parts.at[row * 4 + turn4(z, dz), upper],
            in_a.at[dz - 1, row],
            a_s.at[dz - 1, row],
            a_r.at[dz - 1, row],
            wide=flat(y, xh, turn4(z, dz)),
        )

    def piece_b(dy, column):
        return remote(
            parts.at[turn4(y, dy) * 4 + column, lower],
            in_b.at[dy - 1, column],
            b_s.at[dy - 1, column],
            b_r.at[dy - 1, column],
            wide=flat(turn4(y, dy), xh, z),
        )

    def backward(k, carry):
        j = block_at(15 - k)
        dy, dz = (15 - k) // 4, lax.rem(15 - k, 4)

        @pl.when(k < 15)
        def _():
            arrived(coef_in.at[j], co_r.at[j])

        lse, soft, pick = coef_in[j, 0:1, :], coef_in[j, 1:2, :], coef_in[j, 2:3, :]
        goals = goal[j, 0:1, :]
        for c in range(NCH):
            scale = soft * jnp.exp(tops[j, c : c + 1, :] - lse)
            power = expo[c * CH : (c + 1) * CH, cols(j)].astype(F32)
            spot = lax.broadcasted_iota(jnp.int32, (CH, T), 0) + c * CH
            grad = power * scale - jnp.where(spot == goals, pick, 0.0)
            expo[c * CH : (c + 1) * CH, cols(j)] = grad.astype(BF)
        product = jnp.dot(table[...], expo[0:SHARD, cols(j)], preferred_element_type=F32)
        product += jnp.dot(table_other[...], expo[SHARD:VOC, cols(j)], preferred_element_type=F32)
        parts[j] = product.astype(BF)

        @pl.when(dz > 0)
        def _():
            piece_a(dz, j // 4).start()

        @pl.when(dy > 0)
        def _():
            piece_b(dy, lax.rem(j, 4)).start()

        return carry

    lax.fori_loop(0, 16, backward, 0)

    def head_chunk(c):
        return lax.dot_general(
            fall[...],
            expo[pl.ds(pl.multiple_of(c * 256, 256), 256), :],
            (((1,), (1,)), ((), ())),
            preferred_element_type=F32,
        )

    def other_chunk(c, carry):
        head_other[:, cols(c)] = head_chunk(c + SHARD // 256).astype(BF)
        return carry

    lax.fori_loop(0, SHARD // 256, other_chunk, 0)

    keep_a = keep_b = None
    for d in (3, 2, 1, 0):
        row = turn4(y, d)
        acc = parts[row * 4 + z, 0:HALF, :].astype(F32)
        for m in (1, 2, 3):
            arrived(in_a.at[m - 1, row], a_r.at[m - 1, row])
            acc = acc + in_a[m - 1, row].astype(F32)
        if d:
            sum_a[d - 1] = acc.astype(BF)
            send(sum_a.at[d - 1], in_a2.at[d - 1], a2_s.at[d - 1], a2_r.at[d - 1], flat(row, xh, z))
        else:
            keep_a = acc
        column = turn4(z, d)
        acc = parts[y * 4 + column, HALF:D, :].astype(F32)
        for m in (1, 2, 3):
            arrived(in_b.at[m - 1, column], b_r.at[m - 1, column])
            acc = acc + in_b[m - 1, column].astype(F32)
        if d:
            sum_b[d - 1] = acc.astype(BF)
            send(sum_b.at[d - 1], in_b2.at[d - 1], b2_s.at[d - 1], b2_r.at[d - 1], flat(y, xh, column))
        else:
            keep_b = acc
    grad_final[0:HALF, :] = keep_a
    grad_final[HALF:D, :] = keep_b

    def own_chunk(c, carry):
        head_own[:, cols(c)] = head_chunk(c)
        return carry

    lax.fori_loop(0, SHARD // 256, own_chunk, 0)
    for d in (1, 2, 3):
        arrived(in_a2.at[d - 1], a2_r.at[d - 1])
        arrived(in_b2.at[d - 1], b2_r.at[d - 1])
    grad_final[0:HALF, :] += sum(in_a2[d].astype(F32) for d in range(3))
    grad_final[HALF:D, :] += sum(in_b2[d].astype(F32) for d in range(3))

    def finish(k, carry):
        tell(block_at(k)).wait_send()
        spread(k).wait_send()
        return carry

    lax.fori_loop(1, 16, finish, 0)
    for copy in sent:
        copy.wait_send()

    def finish_pieces(k, carry):
        piece_a(k // 4 + 1, lax.rem(k, 4)).wait_send()
        piece_b(k // 4 + 1, lax.rem(k, 4)).wait_send()
        return carry

    lax.fori_loop(0, 12, finish_pieces, 0)


def head(final, rows_t, table, table_other, goal, weights):
    return pl.pallas_call(
        head_kernel,
        name="head",
        out_shape=(
            jax.ShapeDtypeStruct((D, T), F32),
            jax.ShapeDtypeStruct((D, SHARD), F32),
            jax.ShapeDtypeStruct((D, SHARD), BF),
            jax.ShapeDtypeStruct((8, T), F32),
        ),
        in_specs=[VMEM] * 6,
        out_specs=(VMEM,) * 4,
        scratch_shapes=[
            pltpu.VMEM((D, TOK), BF),
            pltpu.VMEM((VOC, TOK), BF),
            pltpu.VMEM((16, 8, T), F32),
            pltpu.VMEM((16, 8, T), F32),
            pltpu.VMEM((16, 8, T), F32),
            pltpu.VMEM((8, T), F32),
            pltpu.VMEM((16, 8, T), F32),
            pltpu.VMEM((16, D, T), BF),
            pltpu.VMEM((3, 4, HALF, T), BF),
            pltpu.VMEM((3, 4, HALF, T), BF),
            pltpu.VMEM((3, HALF, T), BF),
            pltpu.VMEM((3, HALF, T), BF),
            pltpu.VMEM((3, HALF, T), BF),
            pltpu.VMEM((3, HALF, T), BF),
            DMA((24,)),
            DMA((16, 2)),
            DMA((16,)),
            DMA((16,)),
            DMA((16,)),
            DMA((16,)),
            DMA((3, 4)),
            DMA((3, 4)),
            DMA((3, 4)),
            DMA((3, 4)),
            DMA((3,)),
            DMA((3,)),
            DMA((3,)),
            DMA((3,)),
        ],
        compiler_params=params(4, 61),
        cost_estimate=pl.CostEstimate(
            flops=6 * VOC * TOK * D, bytes_accessed=2 * 10**7, transcendentals=VOC * TOK
        ),
    )(final, rows_t, table, table_other, goal, weights)


class Reduce:
    def __init__(self, parts, first, first_in, second, second_in, third, third_in, rows, along_z, sems):
        self.parts, self.first, self.first_in = parts, first, first_in
        self.second, self.second_in = second, second_in
        self.third, self.third_in = third, third_in
        self.rows, self.along_z = rows, along_z
        self.s, self.r = sems
        self.me, self.y, self.xh, self.z = place()
        self.sent = []

    def send(self, src, dst, at, to):
        copy = remote(src, dst, self.s.at[at], self.r.at[at], wide=to)
        copy.start()
        self.sent.append(copy)

    def wait(self, dst, at):
        remote(dst, dst, self.s.at[at], self.r.at[at], wide=self.me).wait_recv()

    def one(self, d):
        if self.along_z:
            at = turn4(self.z, d)
            return flat(self.y, self.xh, at), (slice(None), slice(None), at, self.rows)
        at = turn4(self.y, d)
        return flat(at, self.xh, self.z), (at, slice(None), slice(None), self.rows)

    def start(self):
        for d in (2, 1, 3):
            to, index = self.one(d)
            self.send(self.parts.at[index], self.first_in.at[d - 1], d - 1, to)

    def middle(self):
        _, index = self.one(0)
        for d in (1, 2, 3):
            self.wait(self.first_in.at[d - 1], d - 1)
        acc = self.parts[index].astype(F32)
        for d in (1, 2, 3):
            acc = acc + self.first_in[d - 1].astype(F32)
        self.first[...] = acc.astype(BF)
        for d in (2, 1, 3):
            if self.along_z:
                at = turn4(self.y, d)
                src, to = self.first.at[at], flat(at, self.xh, self.z)
            else:
                at = turn4(self.z, d)
                src, to = self.first.at[:, at], flat(self.y, self.xh, at)
            self.send(src, self.second_in.at[d - 1], 2 + d, to)

    def last(self):
        for d in (1, 2, 3):
            self.wait(self.second_in.at[d - 1], 2 + d)
        own = self.first[self.y] if self.along_z else self.first[:, self.z]
        acc = own.astype(F32)
        for d in (1, 2, 3):
            acc = acc + self.second_in[d - 1].astype(F32)
        self.second[...] = acc
        self.third[...] = self.second[1 - self.xh].astype(BF)
        self.send(self.third, self.third_in, 6, flat(self.y, 1 - self.xh, self.z))

    def total(self):
        self.wait(self.third_in, 6)
        return self.second[self.xh] + self.third_in[...].astype(F32)

    def finish(self):
        for copy in self.sent:
            copy.wait_send()


def reduce_scratch(half, lanes):
    shapes = []
    for group in ((4, 2), (2, 4)):
        shapes += [
            pltpu.VMEM(group + (half, lanes), BF),
            pltpu.VMEM((3,) + group + (half, lanes), BF),
            pltpu.VMEM((2, half, lanes), F32),
            pltpu.VMEM((3, 2, half, lanes), BF),
            pltpu.VMEM((half, lanes), BF),
            pltpu.VMEM((half, lanes), BF),
            DMA((7,)),
            DMA((7,)),
        ]
    return shapes


def back_kernel(fa, wp, rows, head_other, extra, fa_sum, wp_sum, rows_in, head_in, extra_sum, *scratch):
    me, y, xh, z = place()
    greet_wide(me)
    streams = []
    for parts, rows_of, at in ((fa, FA_ROWS, 0), (wp, WP_ROWS, 16)):
        for half in range(2):
            base = at + half * 8
            f, f_in, s, s_in, t, t_in, sends, recvs = scratch[base : base + 8]
            streams.append(
                Reduce(
                    parts, f, f_in, s, s_in, t, t_in,
                    pl.ds(half * rows_of // 2, rows_of // 2), half == 0, (sends, recvs),
                )
            )
    extra_in, row_s, row_r, extra_s, extra_r, swap = scratch[32:]
    for stream in streams:
        stream.start()
    give = Scatter(lambda p: rows.at[slots(p)], lambda p: rows_in.at[slots(p)], row_s, row_r, me)
    give.start()
    share = Scatter(lambda p: extra, lambda p: extra_in.at[p], extra_s, extra_r, me)
    share.start()
    trade = remote(head_other, head_in, swap.at[0], swap.at[1], wide=flat(y, 1 - xh, z))
    trade.start()
    rows_in[slots(me), :] = rows[slots(me), :]
    extra_in[me] = extra[...]
    for stream in streams:
        stream.middle()
    for stream in streams:
        stream.last()
    share.wait_recv()
    total = extra_in[0]
    for w in range(1, NW):
        total = total + extra_in[w]
    extra_sum[...] = total
    for out, pair, half in ((fa_sum, streams[:2], FA_ROWS // 2), (wp_sum, streams[2:], WP_ROWS // 2)):
        out[0:half, :] = pair[0].total()
        out[half : 2 * half, :] = pair[1].total()
    give.wait_recv()
    for stream in streams:
        stream.finish()
    give.wait_send()
    share.wait_send()
    trade.wait()


def back(fa, wp, rows, head_other, extra):
    return pl.pallas_call(
        back_kernel,
        name="back",
        out_shape=(
            jax.ShapeDtypeStruct((FA_ROWS, D), F32),
            jax.ShapeDtypeStruct((WP_ROWS, 128), F32),
            jax.ShapeDtypeStruct((NW * CAP, D), BF),
            jax.ShapeDtypeStruct((D, SHARD), BF),
            jax.ShapeDtypeStruct((8, 640), F32),
        ),
        in_specs=[VMEM, VMEM, VMEM, ANY, VMEM],
        out_specs=(VMEM, VMEM, VMEM, ANY, VMEM),
        scratch_shapes=reduce_scratch(FA_ROWS // 2, D)
        + reduce_scratch(WP_ROWS // 2, 128)
        + [pltpu.VMEM((NW, 8, 640), F32)]
        + [DMA((NW,))] * 4
        + [DMA((2,))],
        compiler_params=params(5, 48),
        cost_estimate=pl.CostEstimate(flops=10**8, bytes_accessed=3 * 10**7, transcendentals=0),
    )(fa, wp, rows, head_other, extra)


def norm_kernel(value, out, landing, s, r):
    me = lax.axis_index("wide")
    greet_wide(me)
    share = Scatter(lambda p: value, lambda p: landing.at[p], s, r, me)
    share.start()
    landing[me] = value[...]
    share.wait_recv()
    total = landing[0]
    for w in range(1, NW):
        total = total + landing[w]
    out[...] = total
    share.wait_send()


def norm_sum(value):
    return pl.pallas_call(
        norm_kernel,
        name="norm_sum",
        out_shape=jax.ShapeDtypeStruct((8, 128), F32),
        in_specs=[VMEM],
        out_specs=VMEM,
        scratch_shapes=[pltpu.VMEM((NW, 8, 128), F32), DMA((NW,)), DMA((NW,))],
        compiler_params=params(6, 16),
    )(value)


GRP_PARTS = ((D, SHARD), (FA_ROWS, D), (WP_ROWS, 128))


def group_kernel(*refs):
    values, gains = refs[0:3], refs[3]
    outs, gains_out = refs[4:7], refs[7]
    scratch = refs[8:]
    grp = lax.axis_index("grp")
    core, x = lax.rem(grp, 2), grp // 2
    near, far = x * 2 + 1 - core, (1 - x) * 2 + core
    barrier = pltpu.get_barrier_semaphore()
    for k in range(1, NG):
        pl.semaphore_signal(
            barrier, inc=1, device_id={"grp": lax.rem(grp + k, NG)}, device_id_type=MESH
        )
    pl.semaphore_wait(barrier, NG - 1)
    gains_in, gains_s, gains_r = scratch[15:18]
    told = []
    for k in range(1, NG):
        to = lax.rem(grp + k, NG)
        told.append(remote(gains, gains_in.at[grp], gains_s.at[k], gains_r.at[grp], grp=to))
        told[-1].start()
    gains_in[grp] = gains[...]
    sent = []
    for i, value in enumerate(values):
        half = value.shape[0] // 2
        one, one_in, two, two_in, sems = scratch[5 * i : 5 * i + 5]
        away = pl.ds(pl.multiple_of((1 - core) * half, 16), half)
        one[...] = value[away, :].astype(BF)
        copy = remote(one, one_in, sems.at[0], sems.at[1], grp=near)
        copy.start()
        sent.append(copy)
    for i, value in enumerate(values):
        half = value.shape[0] // 2
        one, one_in, two, two_in, sems = scratch[5 * i : 5 * i + 5]
        kept = pl.ds(pl.multiple_of(core * half, 16), half)
        sent[i].wait_recv()
        two[...] = (value[kept, :] + one_in[...].astype(F32)).astype(BF)
        copy = remote(two, two_in, sems.at[2], sems.at[3], grp=far)
        copy.start()
        sent.append(copy)
    for i, value in enumerate(values):
        half = value.shape[0] // 2
        one, one_in, two, two_in, sems = scratch[5 * i : 5 * i + 5]
        kept = pl.ds(pl.multiple_of(core * half, 16), half)
        sent[3 + i].wait_recv()
        outs[i][kept, :] = two[...].astype(F32) + two_in[...].astype(F32)
        piece = outs[i].at[kept]
        copy = remote(piece, piece, sems.at[4], sems.at[5], grp=near)
        copy.start()
        sent.append(copy)
    for k in range(1, NG):
        other = lax.rem(grp + k, NG)
        remote(gains, gains_in.at[other], gains_s.at[k], gains_r.at[other], grp=other).wait_recv()
    gains_out[...] = (gains_in[0] + gains_in[1]) + (gains_in[2] + gains_in[3])
    for i, value in enumerate(values):
        half = value.shape[0] // 2
        sems = scratch[5 * i + 4]
        away = outs[i].at[pl.ds(pl.multiple_of((1 - core) * half, 16), half)]
        remote(away, away, sems.at[4], sems.at[5], grp=near).wait_recv()
    for copy in sent + told:
        copy.wait_send()


def group_sum(*values):
    scratch = []
    for rows, lanes in GRP_PARTS:
        scratch += [pltpu.VMEM((rows // 2, lanes), BF)] * 4 + [DMA((6,))]
    shapes = GRP_PARTS + ((8, 640),)
    return pl.pallas_call(
        group_kernel,
        name="group_sum",
        out_shape=tuple(jax.ShapeDtypeStruct(shape, F32) for shape in shapes),
        in_specs=[VMEM] * 4,
        out_specs=(VMEM,) * 4,
        scratch_shapes=scratch + [pltpu.VMEM((NG, 8, 640), F32), DMA((NG,)), DMA((NG,))],
        compiler_params=params(7, 40),
        cost_estimate=pl.CostEstimate(flops=10**7, bytes_accessed=2 * 10**7, transcendentals=0),
    )(*values)


def dot(spec, a, b):
    return jnp.einsum(spec, a, b, preferred_element_type=F32)


def rms_normed(values, gain):
    scale = lax.rsqrt(jnp.mean(values * values, 0, keepdims=True) + norm_eps)
    return values * scale * gain[:, None]


def norm_back(values, gain, grad):
    scale = lax.rsqrt(jnp.mean(values * values, 0, keepdims=True) + norm_eps)
    pulled = grad * gain[:, None]
    middle = jnp.mean(values * pulled, 0, keepdims=True)
    return (
        scale * pulled - values * (scale * scale * scale) * middle,
        jnp.sum(grad * values * scale, 1),
    )


def rotary():
    half = HD // 2
    freqs = rope_base ** (-(jnp.arange(half, dtype=F32) * 2.0) / HD)
    angles = freqs[:, None] * jnp.arange(T, dtype=F32)[None, :]
    return (jnp.concatenate([jnp.cos(angles)] * 2, 0), jnp.concatenate([jnp.sin(angles)] * 2, 0))


def rotate(values, cosine, sine):
    half = HD // 2
    turned = jnp.concatenate([-values[..., half:, :], values[..., :half, :]], -2)
    return values * cosine + turned * sine


def unrotate(grad, cosine, sine):
    half = HD // 2
    part = grad * sine
    return grad * cosine + jnp.concatenate([part[..., half:, :], -part[..., :half, :]], -2)


def layer_forward(hidden0, gains, wa, wf, wp, allowed, cosine, sine):
    kv = KVH * HD
    group = H // KVH
    normed1 = rms_normed(hidden0, gains[0]).astype(BF)
    mixed = dot("ed,dt->et", wa, normed1)
    queries = rotate(mixed[:D].reshape(KVH, group, HD, T), cosine, sine).astype(BF)
    keys = rotate(mixed[D : D + kv].reshape(KVH, HD, T), cosine, sine).astype(BF)
    values = mixed[D + kv :].reshape(KVH, HD, T).astype(BF)
    scores = dot("kct,kgcq->kgtq", keys, queries) * HD ** (-0.5)
    scores = jnp.where(allowed, scores, masked_score)
    expo = jnp.exp(scores - jnp.max(scores, -2, keepdims=True))
    soft = expo / jnp.sum(expo, -2, keepdims=True)
    probs = soft.astype(BF)
    attended = dot("kct,kgtq->kgcq", values, probs).reshape(D, T).astype(BF)
    hidden1 = hidden0 + dot("de,et->dt", wp[:, :D], attended)
    normed2 = rms_normed(hidden1, gains[1]).astype(BF)
    gate_up = dot("ed,dt->et", wf, normed2)
    inner = (jax.nn.silu(gate_up[:FF]) * gate_up[FF:]).astype(BF)
    hidden2 = hidden1 + dot("df,ft->dt", wp[:, D:], inner)
    final = rms_normed(hidden2, gains[2]).astype(BF)
    kept = (
        hidden0, normed1, queries, keys, values, soft, probs,
        attended, hidden1, normed2, gate_up, inner, hidden2,
    )
    return final, kept


def layer_backward(grad_final, kept, gains, wa, wf, wp, cosine, sine):
    (
        hidden0, normed1, queries, keys, values, soft, probs,
        attended, hidden1, normed2, gate_up, inner, hidden2,
    ) = kept
    group = H // KVH
    grad_h2, grad_g3 = norm_back(hidden2, gains[2], grad_final)
    branch = grad_h2.astype(BF)
    grad_down = dot("dt,ft->df", branch, inner)
    grad_inner = dot("df,dt->ft", wp[:, D:], branch)
    gate, up = gate_up[:FF], gate_up[FF:]
    sigmoid = jax.nn.sigmoid(gate)
    slope = sigmoid * (1.0 + gate * (1.0 - sigmoid))
    grad_gate_up = jnp.concatenate(
        [grad_inner * up * slope, grad_inner * (gate * sigmoid)], 0
    ).astype(BF)
    grad_ffn = dot("et,dt->ed", grad_gate_up, normed2)
    grad_normed2 = dot("ed,et->dt", wf, grad_gate_up)
    grad_part, grad_g2 = norm_back(hidden1, gains[1], grad_normed2)
    grad_h1 = grad_h2 + grad_part
    branch = grad_h1.astype(BF)
    grad_wo = dot("dt,et->de", branch, attended)
    grad_att = dot("de,dt->et", wp[:, :D], branch).astype(BF).reshape(KVH, group, HD, T)
    grad_probs = dot("kct,kgcq->kgtq", values, grad_att)
    grad_scores = (
        soft * (grad_probs - jnp.sum(soft * grad_probs, -2, keepdims=True))
    ).astype(BF)
    grad_q = dot("kct,kgtq->kgcq", keys, grad_scores) * HD ** (-0.5)
    grad_k = dot("kgcq,kgtq->kct", queries, grad_scores) * HD ** (-0.5)
    grad_v = dot("kgcq,kgtq->kct", grad_att, probs)
    grad_q = unrotate(grad_q, cosine, sine).reshape(D, T)
    grad_k = unrotate(grad_k, cosine, sine).reshape(KVH * HD, T)
    grad_mixed = jnp.concatenate([grad_q, grad_k, grad_v.reshape(KVH * HD, T)], 0).astype(BF)
    grad_attn = dot("et,dt->ed", grad_mixed, normed1)
    grad_normed1 = dot("ed,et->dt", wa, grad_mixed)
    grad_part, grad_g1 = norm_back(hidden0, gains[0], grad_normed1)
    grad_proj = jnp.concatenate([grad_wo, grad_down], 1)
    return (
        (grad_h1 + grad_part).astype(BF),
        grad_attn,
        grad_ffn,
        grad_proj,
        jnp.stack([grad_g1, grad_g2, grad_g3]),
    )


def adam_update(weight, grad, first, second, rate, decay):
    first = beta_one * first + (1.0 - beta_one) * grad
    second = beta_two * second + (1.0 - beta_two) * grad * grad
    ratio = first / (1.0 - beta_one**STEP) / (jnp.sqrt(second / (1.0 - beta_two**STEP)) + adam_eps)
    return (weight - rate * (ratio + decay * weight), first, second)


def pack_fa(attn, ffn):
    pad = [(0, 0)] * (attn.ndim - 2) + [(0, FA_ROWS - 126), (0, 0)]
    return jnp.pad(jnp.concatenate([ffn, attn], -2), pad)


def pack_wp(proj):
    lead = proj.shape[:-2]
    pad = [(0, 0)] * len(lead) + [(0, WP_ROWS - 297), (0, 0)]
    return jnp.pad(proj.reshape(lead + (297, 128)), pad)


def on_device(
    token_ids,
    targets,
    segment_ids,
    row_counts,
    embed_table_master,
    embed_table_first,
    embed_table_second,
    embed_table_anchor,
    embed_table_momentum,
    attn_in_master,
    attn_in_first,
    attn_in_second,
    attn_in_anchor,
    attn_in_momentum,
    ffn_in_master,
    ffn_in_first,
    ffn_in_second,
    ffn_in_anchor,
    ffn_in_momentum,
    proj_out_master,
    proj_out_first,
    proj_out_second,
    proj_out_anchor,
    proj_out_momentum,
    norm_gains_master,
    norm_gains_first,
    norm_gains_second,
    norm_gains_anchor,
    norm_gains_momentum,
):
    me = lax.axis_index("wide")
    xh = lax.rem(me // 4, 2)
    other = flat(me // 8, 1 - xh, lax.rem(me, 4))
    ids = token_ids[0]
    gains = norm_gains_master[0]
    table = embed_table_master[0].T.astype(BF)
    weight = jnp.sum(row_counts[0, 0] * jnp.arange(1, 4))

    owner = ids // SHARD
    local = ids - owner * SHARD
    place_of = jnp.arange(T)
    same = ids[:, None] == ids[None, :]
    first_seen = ~jnp.any(same & (place_of[None, :] < place_of[:, None]), 1)
    rank = jnp.sum(
        (first_seen[None, :] & (owner[None, :] == owner[:, None]) & (ids[None, :] < ids[:, None])),
        1,
        dtype=jnp.int32,
    )
    most = jnp.max(rank) + 1
    slot_place = jnp.arange(NW * CAP)

    def slot_picks(turn):
        at = rank - turn * CAP
        slot = jnp.where((at >= 0) & (at < CAP), owner * CAP + at, -1)
        return slot_place[:, None] == slot[None, :]

    def message(picks):
        asked = jnp.max(jnp.where(picks, local[None, :], -1), 1).reshape(NW, 1, CAP)
        asked = jnp.pad(asked, ((0, 0), (0, 0), (0, 128 - CAP)), constant_values=-1)
        rest = jnp.concatenate(
            [
                targets[0].reshape(2, 128),
                jnp.broadcast_to(weight, (1, 128)),
                jnp.broadcast_to(most, (1, 128)),
                jnp.zeros((3, 128), jnp.int32),
            ],
            0,
        )
        return jnp.concatenate([asked, jnp.broadcast_to(rest[None], (NW, 7, 128))], 1)

    picks = slot_picks(0)
    fa = pack_fa(attn_in_master[0].T, ffn_in_master[0].T).astype(BF)
    wp = pack_wp(proj_out_master[0].T).astype(BF)
    got, rows, most_all, table_other, fa_all, wp_all = front(message(picks), table, fa, wp)
    turns = (jnp.max(most_all) + CAP - 1) // CAP

    def to_tokens(rows, picks):
        return dot("sd,st->dt", rows, picks.astype(BF))

    def more_tokens(carry):
        turn, hidden = carry
        picks = slot_picks(turn)
        return turn + 1, hidden + to_tokens(more_rows(message(picks), table), picks)

    hidden0 = lax.while_loop(
        lambda carry: carry[0] < turns, more_tokens, (jnp.int32(1), to_tokens(rows, picks))
    )[1]

    wf_full = fa_all[:, :96].reshape(2 * FF, D)
    wa_full = fa_all[:, 96:126].reshape(QKV, D)
    wp_full = wp_all[:, :297].reshape(D, D + FF)
    segments = segment_ids[0]
    allowed = (place_of[:, None] <= place_of[None, :]) & (segments[:, None] == segments[None, :])
    cosine, sine = rotary()
    final, kept = layer_forward(hidden0, gains, wa_full, wf_full, wp_full, allowed, cosine, sine)

    total = jnp.sum(got[:, 3, 0]).astype(F32) * T
    goals = got[:, 1:3, :].reshape(4, 2, 4, T)
    goals = jnp.where(xh == 0, goals[:, 0], goals[:, 1]).reshape(16, 1, T)
    near, far = goals - me * SHARD, goals - other * SHARD
    goals = jnp.where(
        (near >= 0) & (near < SHARD), near, jnp.where((far >= 0) & (far < SHARD), far + SHARD, -1)
    )
    goals = jnp.broadcast_to(goals, (16, 8, T))
    plain = weight.astype(F32)
    weights = jnp.concatenate(
        [jnp.full((1, T), plain / total, F32), jnp.full((1, T), plain, F32), jnp.zeros((6, T), F32)], 0
    )
    rows_t = jnp.concatenate([table, table_other], 1).T
    grad_final, head_own, head_other, loss = head(final, rows_t, table, table_other, goals, weights)

    grad_embedded, grad_attn, grad_ffn, grad_proj, grad_gains = layer_backward(
        grad_final, kept, gains, wa_full, wf_full, wp_full, cosine, sine
    )
    fa_parts = pack_fa(
        grad_attn.astype(BF).reshape(NW, 30, D), grad_ffn.astype(BF).reshape(NW, 96, D)
    ).reshape(4, 2, 4, FA_ROWS, D)
    wp_parts = pack_wp(grad_proj.astype(BF).reshape(NW, 18, D + FF)).reshape(4, 2, 4, WP_ROWS, 128)
    extra = jnp.zeros((8, 640), F32).at[:3, :D].set(grad_gains).at[3, 0].set(jnp.sum(loss[0]))

    def to_slots(picks):
        return dot("st,dt->sd", picks.astype(BF), grad_embedded).astype(BF)

    fa_sum, wp_sum, rows_in, head_in, extra_sum = back(
        fa_parts, wp_parts, to_slots(picks), head_other, extra
    )

    def to_table(got, rows):
        asked = got[:, 0, :CAP].reshape(NW * CAP)
        hot = (asked[:, None] == jnp.arange(SHARD)[None, :]).astype(BF)
        return dot("sd,sv->dv", rows, hot)

    def more_table(carry):
        turn, grad = carry
        picks = slot_picks(turn)
        return turn + 1, grad + to_table(*more_grads(message(picks), to_slots(picks)))

    table_grad = lax.while_loop(
        lambda carry: carry[0] < turns,
        more_table,
        (jnp.int32(1), head_own + head_in.astype(F32) + to_table(got, rows_in)),
    )[1]

    sum_gains = extra_sum[:3, :D]
    loss_total = extra_sum[3, 0]
    squares = jnp.sum(table_grad * table_grad) + jnp.sum(fa_sum * fa_sum) + jnp.sum(wp_sum * wp_sum)
    squares = norm_sum(jnp.broadcast_to(squares, (8, 128)))[0, 0]
    norm = jnp.sqrt(squares + jnp.sum(sum_gains * sum_gains))
    factor = jnp.minimum(1.0, clip_norm / norm)

    sum_ffn, sum_attn = fa_sum[:96], fa_sum[96:126]
    sum_proj = wp_sum[:297].reshape(18, D + FF)
    kinds = (
        (
            embed_table_master[0].T,
            table_grad,
            embed_table_first[0].T,
            embed_table_second[0].T,
            embed_table_anchor.T,
            embed_table_momentum.T,
            inner_rate,
            weight_decay,
        ),
        (
            attn_in_master[0].T,
            sum_attn,
            attn_in_first[0].T,
            attn_in_second[0].T,
            attn_in_anchor.T,
            attn_in_momentum.T,
            inner_rate,
            weight_decay,
        ),
        (
            ffn_in_master[0].T,
            sum_ffn,
            ffn_in_first[0].T,
            ffn_in_second[0].T,
            ffn_in_anchor.T,
            ffn_in_momentum.T,
            inner_rate,
            weight_decay,
        ),
        (
            proj_out_master[0].T,
            sum_proj,
            proj_out_first[0].T,
            proj_out_second[0].T,
            proj_out_anchor.T,
            proj_out_momentum.T,
            inner_rate,
            weight_decay,
        ),
        (
            gains,
            sum_gains,
            norm_gains_first[0],
            norm_gains_second[0],
            norm_gains_anchor,
            norm_gains_momentum,
            gain_rate,
            0.0,
        ),
    )
    updated = [
        adam_update(kind[0], kind[1] * factor, kind[2], kind[3], kind[6], kind[7]) for kind in kinds
    ]
    diffs = [kinds[index][4] - updated[index][0] for index in range(5)]
    summed = group_sum(
        diffs[0],
        pack_fa(diffs[1], diffs[2]),
        pack_wp(diffs[3]),
        jnp.zeros((8, 640), F32).at[:3, :D].set(diffs[4]),
    )
    sums = (
        summed[0],
        summed[1][96:126],
        summed[1][:96],
        summed[2][:297].reshape(18, D + FF),
        summed[3][:3, :D],
    )
    results = [loss_total.reshape(1), total.reshape(1), norm.reshape(1)]
    for index in range(5):
        average = sums[index] / NG
        outer = outer_momentum * kinds[index][5] + average
        weight = kinds[index][4] - outer_rate * (average + outer_momentum * outer)
        values = [average, outer, weight, updated[index][1], updated[index][2]]
        if index < 4:
            values = [value.T for value in values]
        results += values[:3] + [values[3][None], values[4][None]]
    return tuple(results)


def solution(mesh):
    in_specs = (
        P("grp", "wide"),
        P("grp", "wide"),
        P("grp", "wide"),
        P("grp", "wide", None),
        P("grp", "wide", None),
        P("grp", "wide", None),
        P("grp", "wide", None),
        P("wide", None),
        P("wide", None),
        P("grp", None, "wide"),
        P("grp", None, "wide"),
        P("grp", None, "wide"),
        P(None, "wide"),
        P(None, "wide"),
        P("grp", None, "wide"),
        P("grp", None, "wide"),
        P("grp", None, "wide"),
        P(None, "wide"),
        P(None, "wide"),
        P("grp", None, "wide"),
        P("grp", None, "wide"),
        P("grp", None, "wide"),
        P(None, "wide"),
        P(None, "wide"),
        P("grp", None, None),
        P("grp", None, None),
        P("grp", None, None),
        P(),
        P(),
    )
    out_specs = (
        P("grp"),
        P("grp"),
        P("grp"),
        P("wide", None),
        P("wide", None),
        P("wide", None),
        P("grp", "wide", None),
        P("grp", "wide", None),
        P(None, "wide"),
        P(None, "wide"),
        P(None, "wide"),
        P("grp", None, "wide"),
        P("grp", None, "wide"),
        P(None, "wide"),
        P(None, "wide"),
        P(None, "wide"),
        P("grp", None, "wide"),
        P("grp", None, "wide"),
        P(None, "wide"),
        P(None, "wide"),
        P(None, "wide"),
        P("grp", None, "wide"),
        P("grp", None, "wide"),
        P(),
        P(),
        P(),
        P("grp", None, None),
        P("grp", None, None),
    )
    return jax.shard_map(
        on_device, mesh=mesh, in_specs=in_specs, out_specs=out_specs, check_vma=False
    )
```

```python
import functools

import jax
import jax.numpy as jnp
from jax import lax
from jax.experimental import pallas as pl
from jax.experimental.pallas import tpu as pltpu
from jax.sharding import PartitionSpec as P

D = 576
H = 9
KVH = 3
HD = 64
FF = 1536
QKV = 960
STEP = 8
T = 256
SHARD = 1536
NW = 32
NG = 4
CAP = 32
FA_ROWS = 128
WP_ROWS = 320

beta_one = 0.9
beta_two = 0.999
adam_eps = 1e-08
weight_decay = 0.1
inner_rate = 0.02
gain_rate = 0.2
clip_norm = 0.01
penalty_weight = 0.005
outer_rate = 0.7
outer_momentum = 0.9
rope_base = 100000.0
norm_eps = 1e-05
masked_score = -1e30

BF = jnp.bfloat16
F32 = jnp.float32
MESH = pl.DeviceIdType.MESH
VMEM = pl.BlockSpec(memory_space=pltpu.VMEM)
ANY = pl.BlockSpec(memory_space=pl.ANY)
DMA = pltpu.SemaphoreType.DMA
MIB = 1 << 20


def params(collective, mib):
    return pltpu.CompilerParams(
        collective_id=collective, has_side_effects=True, vmem_limit_bytes=mib * MIB
    )


def place():
    me = lax.axis_index("wide")
    return me, me // 8, lax.rem(me // 4, 2), lax.rem(me, 4)


def flat(y, xh, z):
    return y * 8 + xh * 4 + z


def turn4(at, by):
    return lax.rem(at + by, 4)


def remote(src, dst, ssem, rsem, **device):
    return pltpu.make_async_remote_copy(
        src_ref=src,
        dst_ref=dst,
        send_sem=ssem,
        recv_sem=rsem,
        device_id=device,
        device_id_type=MESH,
    )


def greet_wide(me, grp=None, sides=False):
    barrier = pltpu.get_barrier_semaphore()

    def one(k, carry):
        pl.semaphore_signal(
            barrier, inc=1, device_id={"wide": lax.rem(me + k, NW)}, device_id_type=MESH
        )
        return carry

    lax.fori_loop(1, NW, one, 0)
    count = NW - 1
    if grp is not None:
        for k in range(1, NG):
            pl.semaphore_signal(
                barrier, inc=1, device_id={"grp": lax.rem(grp + k, NG)}, device_id_type=MESH
            )
        count += NG - 1
    if sides:
        for step in (1, 3):
            pl.semaphore_signal(barrier, inc=1, device_id=beside(step), device_id_type=MESH)
        count += 2
    pl.semaphore_wait(barrier, count)


class Scatter:
    def __init__(self, src_at, dst_at, ssem, rsem, me):
        self.src_at, self.dst_at, self.ssem, self.rsem, self.me = src_at, dst_at, ssem, rsem, me

    def copy(self, k):
        peer = lax.rem(self.me + k, NW)
        return remote(
            self.src_at(peer), self.dst_at(self.me), self.ssem.at[k], self.rsem.at[self.me], wide=peer
        )

    def start(self):
        def one(k, carry):
            self.copy(k).start()
            return carry

        lax.fori_loop(1, NW, one, 0)

    def wait_recv(self):
        def one(k, carry):
            peer = lax.rem(self.me + k, NW)
            remote(
                self.src_at(peer), self.dst_at(peer), self.ssem.at[k], self.rsem.at[peer], wide=peer
            ).wait_recv()
            return carry

        lax.fori_loop(1, NW, one, 0)

    def wait_send(self):
        def one(k, carry):
            self.copy(k).wait_send()
            return carry

        lax.fori_loop(1, NW, one, 0)


class Ring:
    def __init__(self, view, sem, quarter, ssem, at):
        self.view, self.sem, self.q = view, sem, quarter
        self.ssem, self.used, self.sent = ssem, at, []
        self.me, self.y, self.xh, self.z = place()

    def send(self, src, dst, rsem, to):
        copy = remote(src, dst, self.ssem.at[self.used], rsem, wide=flat(to[0], self.xh, to[1]))
        self.used += 1
        copy.start()
        self.sent.append(copy)

    def pass_on(self, y, z, first, count, index, *to):
        piece = self.view(y, z, first * self.q, count * self.q)
        for one in to:
            self.send(piece, piece, self.sem(y, z, index), one)

    def wait(self, y, z, first, count, index):
        piece = self.view(y, z, first * self.q, count * self.q)
        remote(piece, piece, self.ssem.at[0], self.sem(y, z, index), wide=self.me).wait_recv()

    def around(self):
        y, z = self.y, self.z
        return y, z, (turn4(y, 1), z), (turn4(y, 3), z), (y, turn4(z, 1)), (y, turn4(z, 3))

    def own(self, src):
        y, z, y_up, y_down, z_up, z_down = self.around()
        for to in (y_up, y_down, z_up, z_down):
            self.send(src, self.view(y, z, 0, 4 * self.q), self.sem(y, z, 0), to)

    def near(self):
        y, z, y_up, y_down, z_up, z_down = self.around()
        for at, far, turn, half, sides in (
            (y_down, y_up, 0, 0, (z_up, z_down)),
            (y_up, y_down, 1, 0, (z_up, z_down)),
            (z_down, z_up, 0, 2, (y_up, y_down)),
            (z_up, z_down, 1, 2, (y_up, y_down)),
        ):
            self.wait(*at, 0, 4, 0)
            self.pass_on(*at, turn, 1, turn, far)
            self.pass_on(*at, 2 + turn, 1, 2 + turn, far)
            self.pass_on(*at, half, 2, half, *sides)

    def far(self):
        y, z, y_up, y_down, z_up, z_down = self.around()
        for at, half, sides in (
            ((turn4(y, 2), z), 0, (z_up, z_down)),
            ((y, turn4(z, 2)), 2, (y_up, y_down)),
        ):
            for index in range(4):
                self.wait(*at, index, 1, index)
            self.pass_on(*at, half, 2, half, *sides)

    def cross(self):
        y, z, y_up, y_down, z_up, z_down = self.around()
        for k in (1, 3, 2):
            row, column = turn4(y, k), turn4(z, k)
            self.wait(row, z_down[1], 0, 2, 0)
            self.pass_on(row, z_down[1], 0, 1, 0, z_up)
            self.wait(row, z_up[1], 0, 2, 0)
            self.pass_on(row, z_up[1], 1, 1, 1, z_down)
            self.wait(y_down[0], column, 2, 2, 2)
            self.pass_on(y_down[0], column, 2, 1, 2, y_up)
            self.wait(y_up[0], column, 2, 2, 2)
            self.pass_on(y_up[0], column, 3, 1, 3, y_down)

    def last(self):
        y, z = self.y, self.z
        for k in (1, 3, 2):
            row, column = turn4(y, k), turn4(z, k)
            for index in range(2):
                self.wait(row, turn4(z, 2), index, 1, index)
                self.wait(turn4(y, 2), column, 2 + index, 1, 2 + index)

    def finish(self):
        for copy in self.sent:
            copy.wait_send()


RING_SENDS = 36


def beside(step):
    me, y, xh, z = place()
    grp = lax.axis_index("grp")
    low = grp // 2
    side = lax.rem(xh + low + (0 if step == 1 else 1), 2)
    return {"grp": (1 - low) * 2 + lax.rem(grp, 2), "wide": flat(y, side, z)}


class Relay:
    def __init__(self, sources, stops, ends, ssem, rsem):
        self.sources, self.stops, self.ends, self.ssem, self.rsem = sources, stops, ends, ssem, rsem

    def copy(self, src, dst, at, step):
        return remote(src, dst, self.ssem.at[at], self.rsem.at[at], **beside(step))

    def legs(self, hop):
        for i, step in enumerate((1, 3)):
            src = self.sources[i] if hop == 0 else self.stops[i]
            dst = self.stops[i] if hop == 0 else self.ends[i]
            yield self.copy(src, dst, 2 * hop + i, step)

    def start(self):
        for copy in self.legs(0):
            copy.start()

    def forward(self):
        for first, second in zip(self.legs(0), self.legs(1)):
            first.wait_recv()
            second.start()

    def wait(self):
        for copy in self.legs(1):
            copy.wait_recv()

    def finish(self):
        for hop in (0, 1):
            for copy in self.legs(hop):
                copy.wait_send()


def look_up(got, table, hot, rows, slot_row):
    asked = got[:, slot_row, :].astype(F32)
    asked = jnp.concatenate([asked, jnp.zeros((128 - NW, 128), F32)], 0).T
    step = 8 * CAP
    for first in range(0, NW, 8):
        for d in range(8):
            column = asked[0:CAP, first + d : first + d + 1]
            lanes = lax.broadcasted_iota(jnp.int32, (CAP, SHARD), 1).astype(F32)
            hot[d * CAP : (d + 1) * CAP, :] = jnp.where(lanes == column, 1.0, 0.0).astype(BF)
        picked = lax.dot_general(
            hot[...], table[...], (((1,), (1,)), ((), ())), preferred_element_type=F32
        )
        rows[first * CAP : first * CAP + step, :] = picked.astype(BF)


def slots(at):
    return pl.ds(pl.multiple_of(at * CAP, CAP), CAP)


def turn_over(table, rows, first):
    for c in range(0, SHARD, 256):
        rows[first + c : first + c + 256, :] = table[:, c : c + 256].T


def front_kernel(
    msg, table, fa, wp, got, emb, most, table_other, rows_t, fa_all, wp_all,
    hot, rows, own_most, stops, msg_s, msg_r, emb_s, emb_r, most_s, most_r, swap_s, swap_r,
    fa_s, fa_r, wp_s, wp_r, x_s, x_r, local,
):
    me, y, xh, z = place()
    grp = lax.axis_index("grp")
    greet_wide(me, grp, sides=True)
    ask = Scatter(lambda p: msg.at[p], lambda p: got.at[p], msg_s, msg_r, me)
    ask.start()
    got[me] = msg[me]
    other = flat(y, 1 - xh, z)
    over, own, rings = [], [], []
    for i, (x, out, size, ssem, rsem) in enumerate(
        ((fa, fa_all, FA_ROWS, fa_s, fa_r), (wp, wp_all, WP_ROWS, wp_s, wp_r))
    ):
        over.append(remote(x, out.at[me], x_s.at[i], x_r.at[i], wide=other))
        over[-1].start()
        own.append(pltpu.make_async_copy(x, out.at[me], local.at[i]))
        own[-1].start()
        pair = []
        for k, side in enumerate((xh, 1 - xh)):
            pair.append(
                Ring(
                    lambda Y, Z, first, count, out=out, side=side: out.at[
                        flat(Y, side, Z), pl.ds(first, count)
                    ],
                    lambda Y, Z, index, rsem=rsem, side=side: rsem.at[flat(Y, side, Z), index],
                    size // 4,
                    ssem,
                    k * RING_SENDS,
                )
            )
        rings.append(pair)
        pair[0].own(x)
    halves = (pl.ds(0, D // 2), pl.ds(D // 2, D // 2))
    trade = Relay(
        [table.at[half] for half in halves],
        [stops.at[i] for i in range(2)],
        [table_other.at[half] for half in halves],
        swap_s,
        swap_r,
    )
    trade.start()
    ask.wait_recv()
    look_up(got, table, hot, rows, 0)
    reply = Scatter(lambda p: rows.at[slots(p)], lambda p: emb.at[slots(p)], emb_s, emb_r, me)
    reply.start()
    emb[slots(me), :] = rows[slots(me), :]
    largest = jnp.max(got[:, 4, :], 0, keepdims=True)
    own_most[...] = jnp.broadcast_to(largest, (8, 128))
    most[grp] = own_most[...]
    told = []
    for k in range(1, NG):
        to = lax.rem(grp + k, NG)
        told.append(remote(own_most, most.at[grp], most_s.at[k], most_r.at[grp], grp=to))
        told[-1].start()
    for i in range(2):
        rings[i][0].near()
    for i, out in enumerate((fa_all, wp_all)):
        over[i].wait_recv()
        rings[i][1].own(out.at[other])
    for i in range(2):
        rings[i][0].far()
    for i in range(2):
        rings[i][1].near()
    for i in range(2):
        rings[i][0].cross()
    turn_over(table, rows_t, 0)
    trade.forward()
    for i in range(2):
        rings[i][1].far()
    for i in range(2):
        rings[i][1].cross()
    reply.wait_recv()
    for k in range(1, NG):
        to = lax.rem(grp + k, NG)
        remote(own_most, most.at[to], most_s.at[k], most_r.at[to], grp=to).wait_recv()
    trade.wait()
    turn_over(table_other, rows_t, SHARD)
    for pair in rings:
        for ring in pair:
            ring.last()
    ask.wait_send()
    reply.wait_send()
    trade.finish()
    for copy in told + over:
        copy.wait_send()
    for copy in own:
        copy.wait()
    for pair in rings:
        for ring in pair:
            ring.finish()


def front(msg, table, fa, wp):
    return pl.pallas_call(
        front_kernel,
        name="front",
        out_shape=(
            jax.ShapeDtypeStruct((NW, 8, 128), jnp.int32),
            jax.ShapeDtypeStruct((NW * CAP, D), BF),
            jax.ShapeDtypeStruct((NG, 8, 128), jnp.int32),
            jax.ShapeDtypeStruct((D, SHARD), BF),
            jax.ShapeDtypeStruct((2 * SHARD, D), BF),
            jax.ShapeDtypeStruct((NW, FA_ROWS, D), BF),
            jax.ShapeDtypeStruct((NW, WP_ROWS, 128), BF),
        ),
        in_specs=[VMEM, VMEM, ANY, ANY],
        out_specs=(VMEM, VMEM, VMEM, VMEM, VMEM, ANY, ANY),
        scratch_shapes=[
            pltpu.VMEM((8 * CAP, SHARD), BF),
            pltpu.VMEM((NW * CAP, D), BF),
            pltpu.VMEM((8, 128), jnp.int32),
            pltpu.VMEM((2, D // 2, SHARD), BF),
            DMA((NW,)),
            DMA((NW,)),
            DMA((NW,)),
            DMA((NW,)),
            DMA((NG,)),
            DMA((NG,)),
            DMA((4,)),
            DMA((4,)),
            DMA((2 * RING_SENDS,)),
            DMA((NW, 4)),
            DMA((2 * RING_SENDS,)),
            DMA((NW, 4)),
            DMA((2,)),
            DMA((2,)),
            DMA((2,)),
        ],
        compiler_params=params(1, 48),
        cost_estimate=pl.CostEstimate(flops=2 * 10**9, bytes_accessed=3 * 10**7, transcendentals=0),
    )(msg, table, fa, wp)


def more_rows_kernel(msg, table, got, emb, hot, rows, msg_s, msg_r, emb_s, emb_r):
    me = lax.axis_index("wide")
    greet_wide(me)
    ask = Scatter(lambda p: msg.at[p], lambda p: got.at[p], msg_s, msg_r, me)
    ask.start()
    got[me] = msg[me]
    ask.wait_recv()
    look_up(got, table, hot, rows, 0)
    reply = Scatter(lambda p: rows.at[slots(p)], lambda p: emb.at[slots(p)], emb_s, emb_r, me)
    reply.start()
    emb[slots(me), :] = rows[slots(me), :]
    reply.wait_recv()
    ask.wait_send()
    reply.wait_send()


def more_rows(msg, table):
    return pl.pallas_call(
        more_rows_kernel,
        name="more_rows",
        out_shape=(
            jax.ShapeDtypeStruct((NW, 8, 128), jnp.int32),
            jax.ShapeDtypeStruct((NW * CAP, D), BF),
        ),
        in_specs=[VMEM, VMEM],
        out_specs=(VMEM, VMEM),
        scratch_shapes=[pltpu.VMEM((8 * CAP, SHARD), BF), pltpu.VMEM((NW * CAP, D), BF)]
        + [DMA((NW,))] * 4,
        compiler_params=params(2, 40),
    )(msg, table)[1]


def more_grads_kernel(msg, rows, got, out, msg_s, msg_r, row_s, row_r):
    me = lax.axis_index("wide")
    greet_wide(me)
    ask = Scatter(lambda p: msg.at[p], lambda p: got.at[p], msg_s, msg_r, me)
    ask.start()
    give = Scatter(lambda p: rows.at[slots(p)], lambda p: out.at[slots(p)], row_s, row_r, me)
    give.start()
    got[me] = msg[me]
    out[slots(me), :] = rows[slots(me), :]
    ask.wait_recv()
    give.wait_recv()
    ask.wait_send()
    give.wait_send()


def more_grads(msg, rows):
    return pl.pallas_call(
        more_grads_kernel,
        name="more_grads",
        out_shape=(
            jax.ShapeDtypeStruct((NW, 8, 128), jnp.int32),
            jax.ShapeDtypeStruct((NW * CAP, D), BF),
        ),
        in_specs=[VMEM, VMEM],
        out_specs=(VMEM, VMEM),
        scratch_shapes=[DMA((NW,))] * 4,
        compiler_params=params(3, 20),
    )(msg, rows)


VOC = 2 * SHARD
TOK = 16 * T
CH = 512
NCH = VOC // CH
QUART = D // 4


def cols(j):
    return pl.ds(pl.multiple_of(j * T, T), T)


def head_kernel(
    final, rows_t, table, table_other, goal, weights,
    grad_final, head_own, head_other, loss,
    fall, expo, tops, stat, stat_in, coef, coef_in, parts,
    part_a, part_b, whole_a, whole_b, sum_a, sum_b, part_a2, part_b2, whole_a2, whole_b2,
    g_s, g_r, st_s, st_r, co_s, co_r, a_s, b_s, pa_r, pb_r, wa_r, wb_r, a2_s, b2_s, a2_r, b2_r,
):
    me, y, xh, z = place()
    mine = y * 4 + z

    def dev(j):
        return flat(j // 4, xh, lax.rem(j, 4))

    barrier = pltpu.get_barrier_semaphore()

    def greet(k, carry):
        pl.semaphore_signal(
            barrier, inc=1, device_id={"wide": dev(lax.rem(mine + k, 16))}, device_id_type=MESH
        )
        return carry

    lax.fori_loop(1, 16, greet, 0)
    pl.semaphore_wait(barrier, 15)

    sent = []

    def send(src, dst, ssem, rsem, to):
        copy = remote(src, dst, ssem, rsem, wide=to)
        copy.start()
        sent.append(copy)

    def arrived(dst, rsem):
        remote(dst, dst, g_s.at[0], rsem, wide=dev(mine)).wait_recv()

    ring = Ring(
        lambda Y, Z, first, count: fall.at[pl.ds(first, count), cols(Y * 4 + Z)],
        lambda Y, Z, index: g_r.at[Y * 4 + Z, index],
        QUART,
        g_s,
        0,
    )
    ring.own(final)
    fall[:, cols(mine)] = final[...]

    def logits(j):
        seen = fall[:, cols(j)]
        goals = goal[j, 0:1, :]
        tip, weight, hit = [], [], jnp.zeros((1, T), F32)
        for c in range(NCH):
            part = jnp.dot(rows_t[c * CH : (c + 1) * CH, :], seen, preferred_element_type=F32)
            top = jnp.max(part, 0, keepdims=True)
            power = jnp.exp(part - top)
            spot = lax.broadcasted_iota(jnp.int32, (CH, T), 0) + c * CH
            hit = hit + jnp.sum(jnp.where(spot == goals, part, 0.0), 0, keepdims=True)
            expo[c * CH : (c + 1) * CH, cols(j)] = power.astype(BF)
            tip.append(top)
            weight.append(jnp.sum(power, 0, keepdims=True))
        top = functools.reduce(jnp.maximum, tip)
        total = sum(w * jnp.exp(t - top) for w, t in zip(weight, tip))
        zero = jnp.zeros((1, T), F32)
        tops[j] = jnp.concatenate(tip + [zero] * (8 - NCH), 0)
        stat[j] = jnp.concatenate([top, total, hit] + [zero] * 5, 0)

    def tell(j):
        return remote(stat.at[j], stat_in.at[mine], st_s.at[j], st_r.at[mine], wide=dev(j))

    def block(dy, dz):
        return turn4(y, dy) * 4 + turn4(z, dz)

    def forward(offsets):
        def one(k, carry):
            j = block(*offsets(k))
            logits(j)
            tell(j).start()
            return carry

        return one

    def odd(k):
        return 1 + 2 * lax.rem(k, 2)

    logits(mine)
    stat_in[mine] = stat[mine]
    ring.near()
    lax.fori_loop(0, 4, forward(lambda k: ((1 - k // 2) * odd(k), (k // 2) * odd(k))), 0)
    ring.far()
    lax.fori_loop(0, 2, forward(lambda k: (2 * (1 - k), 2 * k)), 0)
    ring.cross()
    lax.fori_loop(0, 4, forward(lambda k: (odd(k // 2), odd(k))), 0)
    ring.last()
    lax.fori_loop(
        0,
        4,
        forward(lambda k: (2 * (1 - k // 2) + odd(k) * (k // 2), odd(k) * (1 - k // 2) + 2 * (k // 2))),
        0,
    )
    forward(lambda k: (2, 2))(0, 0)

    def hear(k, carry):
        j = lax.rem(mine + k, 16)
        arrived(stat_in.at[j], st_r.at[j])
        return carry

    lax.fori_loop(1, 16, hear, 0)
    tip, weight, hit = stat_in[:, 0, :], stat_in[:, 1, :], stat_in[:, 2, :]
    top = jnp.max(tip, 0, keepdims=True)
    lse = top + jnp.log(jnp.sum(weight * jnp.exp(tip - top), 0, keepdims=True))
    picked = jnp.sum(hit, 0, keepdims=True)
    share, plain = weights[0:1, :], weights[1:2, :]
    zero = jnp.zeros((1, T), F32)
    coef[...] = jnp.concatenate(
        [lse, share * (1.0 + 2.0 * penalty_weight * lse), share] + [zero] * 5, 0
    )
    loss[...] = jnp.concatenate(
        [plain * (lse - picked + penalty_weight * lse * lse)] + [zero] * 7, 0
    )
    coef_in[mine] = coef[...]

    def spread(k):
        j = lax.rem(mine + k, 16)
        return remote(coef, coef_in.at[mine], co_s.at[k], co_r.at[mine], wide=dev(j))

    def spread_start(k, carry):
        spread(k).start()
        return carry

    lax.fori_loop(1, 16, spread_start, 0)

    up, down = 1, 3
    z_to = {step: flat(y, xh, turn4(z, step)) for step in (up, down)}
    y_to = {step: flat(turn4(y, step), xh, z) for step in (up, down)}

    def piece_a(j, index):
        row = j // 4
        return remote(
            parts.at[j, pl.ds(index * QUART, QUART)], part_a.at[index, row],
            a_s.at[j, index], pa_r.at[index, row], wide=z_to[(up, down)[index]],
        )

    def piece_b(j, index):
        column = lax.rem(j, 4)
        return remote(
            parts.at[j, pl.ds((2 + index) * QUART, QUART)], part_b.at[index, column],
            b_s.at[j, index], pb_r.at[index, column], wide=y_to[(up, down)[index]],
        )

    def half_a(j, index):
        row = j // 4
        return remote(
            parts.at[j, pl.ds(0, 2 * QUART)], whole_a.at[index, row],
            a_s.at[j, 0], wa_r.at[index, row], wide=z_to[(up, down)[index]],
        )

    def half_b(j, index):
        column = lax.rem(j, 4)
        return remote(
            parts.at[j, pl.ds(2 * QUART, 2 * QUART)], whole_b.at[index, column],
            b_s.at[j, 0], wb_r.at[index, column], wide=y_to[(up, down)[index]],
        )

    def offsets(k):
        return lax.rem(2 + k // 4, 4), lax.rem(2 + k, 4)

    def post(k):
        dy, dz = offsets(k)
        j = block(dy, dz)

        @pl.when(dz == 2)
        def _():
            piece_a(j, 0).start()
            piece_a(j, 1).start()

        @pl.when(dy == 2)
        def _():
            piece_b(j, 0).start()
            piece_b(j, 1).start()

        for index, step in enumerate((up, down)):

            @pl.when(dz == step)
            def _():
                row = j // 4
                arrived(part_a.at[index, row], pa_r.at[index, row])
                rows = pl.ds(index * QUART, QUART)
                total = parts[j, rows, :].astype(F32) + part_a[index, row].astype(F32)
                parts[j, rows, :] = total.astype(BF)
                half_a(j, index).start()

            @pl.when(dy == step)
            def _():
                column = lax.rem(j, 4)
                arrived(part_b.at[index, column], pb_r.at[index, column])
                rows = pl.ds((2 + index) * QUART, QUART)
                total = parts[j, rows, :].astype(F32) + part_b[index, column].astype(F32)
                parts[j, rows, :] = total.astype(BF)
                half_b(j, index).start()

    def backward(k, carry):
        j = block(*offsets(k))

        @pl.when(k != 10)
        def _():
            arrived(coef_in.at[j], co_r.at[j])

        lse, soft, pick = coef_in[j, 0:1, :], coef_in[j, 1:2, :], coef_in[j, 2:3, :]
        goals = goal[j, 0:1, :]
        for c in range(NCH):
            scale = soft * jnp.exp(tops[j, c : c + 1, :] - lse)
            power = expo[c * CH : (c + 1) * CH, cols(j)].astype(F32)
            spot = lax.broadcasted_iota(jnp.int32, (CH, T), 0) + c * CH
            grad = power * scale - jnp.where(spot == goals, pick, 0.0)
            expo[c * CH : (c + 1) * CH, cols(j)] = grad.astype(BF)
        product = jnp.dot(table[...], expo[0:SHARD, cols(j)], preferred_element_type=F32)
        product += jnp.dot(table_other[...], expo[SHARD:VOC, cols(j)], preferred_element_type=F32)
        parts[j] = product.astype(BF)

        @pl.when(k > 0)
        def _():
            post(k - 1)

        return carry

    lax.fori_loop(0, 16, backward, 0)
    post(15)

    def head_chunk(c):
        return lax.dot_general(
            fall[...],
            expo[pl.ds(pl.multiple_of(c * 256, 256), 256), :],
            (((1,), (1,)), ((), ())),
            preferred_element_type=F32,
        )

    def other_chunk(c, carry):
        head_other[:, cols(c)] = head_chunk(c + SHARD // 256).astype(BF)
        return carry

    def own_chunk(c, carry):
        head_own[:, cols(c)] = head_chunk(c)
        return carry

    lax.fori_loop(0, SHARD // 256, other_chunk, 0)

    kinds = (
        (whole_a, wa_r, sum_a, part_a2, whole_a2, a2_s, a2_r, y_to, 0),
        (whole_b, wb_r, sum_b, part_b2, whole_b2, b2_s, b2_r, z_to, 2 * QUART),
    )
    for d in (2, 1, 3, 0):
        for kind, (whole, w_r, total, part2, whole2, s2, r2, to, base) in enumerate(kinds):
            at = turn4(y if kind == 0 else z, d)
            j = at * 4 + z if kind == 0 else y * 4 + at
            acc = parts[j, base : base + 2 * QUART, :].astype(F32)
            for index in range(2):
                arrived(whole.at[index, at], w_r.at[index, at])
                acc = acc + whole[index, at].astype(F32)
            if d == 0:
                grad_final[base : base + 2 * QUART, :] = acc
            else:
                total[d - 1] = acc.astype(BF)
            if d == 2:
                for index, step in enumerate((up, down)):
                    piece = total.at[1, pl.ds(index * QUART, QUART)]
                    send(piece, part2.at[index], s2.at[index], r2.at[index], to[step])
    lax.fori_loop(0, SHARD // 512, own_chunk, 0)
    for kind, (whole, w_r, total, part2, whole2, s2, r2, to, base) in enumerate(kinds):
        for index, step in enumerate((up, down)):
            arrived(part2.at[index], r2.at[index])
            rows = pl.ds(index * QUART, QUART)
            added = total[step - 1, rows, :].astype(F32) + part2[index].astype(F32)
            total[step - 1, rows, :] = added.astype(BF)
            send(total.at[step - 1], whole2.at[index], s2.at[2 + index], r2.at[2 + index], to[step])
    lax.fori_loop(SHARD // 512, SHARD // 256, own_chunk, 0)
    for kind, (whole, w_r, total, part2, whole2, s2, r2, to, base) in enumerate(kinds):
        for index in range(2):
            arrived(whole2.at[index], r2.at[2 + index])
        grad_final[base : base + 2 * QUART, :] += whole2[0].astype(F32) + whole2[1].astype(F32)

    def finish(k, carry):
        j = lax.rem(mine + k, 16)
        tell(j).wait_send()
        spread(k).wait_send()
        return carry

    lax.fori_loop(1, 16, finish, 0)
    for copy in sent:
        copy.wait_send()
    ring.finish()

    def finish_pieces(k, carry):
        row, column = block(k, 2), block(2, k)
        piece_a(row, 0).wait_send()
        piece_a(row, 1).wait_send()
        piece_b(column, 0).wait_send()
        piece_b(column, 1).wait_send()
        for index, step in enumerate((up, down)):
            half_a(block(k, step), index).wait_send()
            half_b(block(step, k), index).wait_send()
        return carry

    lax.fori_loop(0, 4, finish_pieces, 0)


def head(final, rows_t, table, table_other, goal, weights):
    return pl.pallas_call(
        head_kernel,
        name="head",
        out_shape=(
            jax.ShapeDtypeStruct((D, T), F32),
            jax.ShapeDtypeStruct((D, SHARD), F32),
            jax.ShapeDtypeStruct((D, SHARD), BF),
            jax.ShapeDtypeStruct((8, T), F32),
        ),
        in_specs=[VMEM] * 6,
        out_specs=(VMEM,) * 4,
        scratch_shapes=[
            pltpu.VMEM((D, TOK), BF),
            pltpu.VMEM((VOC, TOK), BF),
            pltpu.VMEM((16, 8, T), F32),
            pltpu.VMEM((16, 8, T), F32),
            pltpu.VMEM((16, 8, T), F32),
            pltpu.VMEM((8, T), F32),
            pltpu.VMEM((16, 8, T), F32),
            pltpu.VMEM((16, D, T), BF),
            pltpu.VMEM((2, 4, QUART, T), BF),
            pltpu.VMEM((2, 4, QUART, T), BF),
            pltpu.VMEM((2, 4, 2 * QUART, T), BF),
            pltpu.VMEM((2, 4, 2 * QUART, T), BF),
            pltpu.VMEM((3, 2 * QUART, T), BF),
            pltpu.VMEM((3, 2 * QUART, T), BF),
            pltpu.VMEM((2, QUART, T), BF),
            pltpu.VMEM((2, QUART, T), BF),
            pltpu.VMEM((2, 2 * QUART, T), BF),
            pltpu.VMEM((2, 2 * QUART, T), BF),
            DMA((RING_SENDS,)),
            DMA((16, 4)),
            DMA((16,)),
            DMA((16,)),
            DMA((16,)),
            DMA((16,)),
            DMA((16, 2)),
            DMA((16, 2)),
            DMA((2, 4)),
            DMA((2, 4)),
            DMA((2, 4)),
            DMA((2, 4)),
            DMA((4,)),
            DMA((4,)),
            DMA((4,)),
            DMA((4,)),
        ],
        compiler_params=params(4, 61),
        cost_estimate=pl.CostEstimate(
            flops=6 * VOC * TOK * D, bytes_accessed=2 * 10**7, transcendentals=VOC * TOK
        ),
    )(final, rows_t, table, table_other, goal, weights)


class Reduce:
    def __init__(self, parts, base, quarter, along_z, refs):
        (
            self.first, self.part1, self.whole1, self.second, self.part2, self.whole2,
            self.third, self.stop, self.third_in, self.s, self.r,
        ) = refs
        self.parts, self.base, self.q, self.along_z = parts, base, quarter, along_z
        self.me, self.y, self.xh, self.z = place()
        self.sent = []

    def send(self, src, dst, at, **to):
        copy = remote(src, dst, self.s.at[at], self.r.at[at], **to)
        copy.start()
        self.sent.append(copy)

    def wait(self, dst, at):
        remote(dst, dst, self.s.at[at], self.r.at[at], wide=self.me).wait_recv()

    def item1(self, step, first, count):
        rows = pl.ds(self.base + first * self.q, count * self.q)
        if self.along_z:
            return (slice(None), slice(None), turn4(self.z, step), rows)
        return (turn4(self.y, step), slice(None), slice(None), rows)

    def item2(self, step, first, count):
        rows = pl.ds(first * self.q, count * self.q)
        if self.along_z:
            return (turn4(self.y, step), slice(None), rows)
        return (slice(None), turn4(self.z, step), rows)

    def to(self, stage, step):
        if self.along_z == (stage == 1):
            return flat(self.y, self.xh, turn4(self.z, step))
        return flat(turn4(self.y, step), self.xh, self.z)

    def split(self, stage, ref, item, part, base):
        for index, step in enumerate((1, 3)):
            self.send(ref.at[item(2, index, 1)], part.at[index], base + index, wide=self.to(stage, step))

    def join(self, stage, ref, item, part, whole, base):
        for index, step in enumerate((1, 3)):
            self.wait(part.at[index], base + index)
            at = item(step, index, 1)
            ref[at] = (ref[at].astype(F32) + part[index].astype(F32)).astype(BF)
            self.send(
                ref.at[item(step, 0, 2)], whole.at[index], base + 2 + index, wide=self.to(stage, step)
            )

    def add(self, ref, item, whole, base):
        acc = ref[item(0, 0, 2)].astype(F32)
        for index in range(2):
            self.wait(whole.at[index], base + 2 + index)
            acc = acc + whole[index].astype(F32)
        return acc

    def one(self):
        self.split(1, self.parts, self.item1, self.part1, 0)

    def two(self):
        self.join(1, self.parts, self.item1, self.part1, self.whole1, 0)

    def three(self):
        self.first[...] = self.add(self.parts, self.item1, self.whole1, 0).astype(BF)
        self.split(2, self.first, self.item2, self.part2, 4)

    def four(self):
        self.join(2, self.first, self.item2, self.part2, self.whole2, 4)

    def five(self):
        self.second[...] = self.add(self.first, self.item2, self.whole2, 4)
        self.third[...] = self.second[1 - self.xh].astype(BF)
        self.send(self.third, self.stop, 8, **beside(1 if self.along_z else 3))

    def six(self):
        self.wait(self.stop, 8)
        self.send(self.stop, self.third_in, 9, **beside(1 if self.along_z else 3))

    def total(self):
        self.wait(self.third_in, 9)
        return self.second[self.xh] + self.third_in[...].astype(F32)

    def finish(self):
        for copy in self.sent:
            copy.wait_send()


def reduce_scratch(half, lanes):
    shapes = []
    for group in ((4, 2), (2, 4)):
        quarter = half // 2
        shapes += [
            pltpu.VMEM(group + (half, lanes), BF),
            pltpu.VMEM((2,) + group + (quarter, lanes), BF),
            pltpu.VMEM((2,) + group + (half, lanes), BF),
            pltpu.VMEM((2, half, lanes), F32),
            pltpu.VMEM((2, 2, quarter, lanes), BF),
            pltpu.VMEM((2, 2, half, lanes), BF),
            pltpu.VMEM((half, lanes), BF),
            pltpu.VMEM((half, lanes), BF),
            pltpu.VMEM((half, lanes), BF),
            DMA((10,)),
            DMA((10,)),
        ]
    return shapes


def back_kernel(fa_in, wp_in, rows, head_other, extra, fa_sum, wp_sum, rows_in, head_in, extra_sum, *scratch):
    me, y, xh, z = place()
    greet_wide(me, sides=True)
    fa, wp, extra_in, stops, row_s, row_r, extra_s, extra_r, swap_s, swap_r, local = scratch[44:]
    loads = [
        pltpu.make_async_copy(fa_in, fa, local.at[0]),
        pltpu.make_async_copy(wp_in, wp, local.at[1]),
    ]
    for load in loads:
        load.start()
    halves = (pl.ds(0, D // 2), pl.ds(D // 2, D // 2))
    trade = Relay(
        [head_other.at[half] for half in halves],
        [stops.at[i] for i in range(2)],
        [head_in.at[half] for half in halves],
        swap_s,
        swap_r,
    )
    for load in loads:
        load.wait()
    streams = []
    for parts, rows_of, at in ((fa, FA_ROWS, 0), (wp, WP_ROWS, 22)):
        for half in range(2):
            refs = scratch[at + 11 * half : at + 11 * half + 11]
            streams.append(Reduce(parts, half * rows_of // 2, rows_of // 4, half == 0, refs))
    for stream in streams:
        stream.one()
    trade.start()
    give = Scatter(lambda p: rows.at[slots(p)], lambda p: rows_in.at[slots(p)], row_s, row_r, me)
    give.start()
    share = Scatter(lambda p: extra, lambda p: extra_in.at[p], extra_s, extra_r, me)
    share.start()
    rows_in[slots(me), :] = rows[slots(me), :]
    extra_in[me] = extra[...]
    for stream in streams:
        stream.two()
    trade.forward()
    for stream in streams:
        stream.three()
    for stream in streams:
        stream.four()
    for stream in streams:
        stream.five()
    share.wait_recv()
    total = extra_in[0]
    for w in range(1, NW):
        total = total + extra_in[w]
    extra_sum[...] = total
    for stream in streams:
        stream.six()
    for out, pair, half in ((fa_sum, streams[:2], FA_ROWS // 2), (wp_sum, streams[2:], WP_ROWS // 2)):
        out[0:half, :] = pair[0].total()
        out[half : 2 * half, :] = pair[1].total()
    give.wait_recv()
    trade.wait()
    for stream in streams:
        stream.finish()
    give.wait_send()
    share.wait_send()
    trade.finish()


def back(fa, wp, rows, head_other, extra):
    return pl.pallas_call(
        back_kernel,
        name="back",
        out_shape=(
            jax.ShapeDtypeStruct((FA_ROWS, D), F32),
            jax.ShapeDtypeStruct((WP_ROWS, 128), F32),
            jax.ShapeDtypeStruct((NW * CAP, D), BF),
            jax.ShapeDtypeStruct((D, SHARD), BF),
            jax.ShapeDtypeStruct((8, 640), F32),
        ),
        in_specs=[ANY, ANY, VMEM, ANY, VMEM],
        out_specs=(VMEM, VMEM, VMEM, ANY, VMEM),
        scratch_shapes=reduce_scratch(FA_ROWS // 2, D)
        + reduce_scratch(WP_ROWS // 2, 128)
        + [
            pltpu.VMEM((4, 2, 4, FA_ROWS, D), BF),
            pltpu.VMEM((4, 2, 4, WP_ROWS, 128), BF),
            pltpu.VMEM((NW, 8, 640), F32),
            pltpu.VMEM((2, D // 2, SHARD), BF),
        ]
        + [DMA((NW,))] * 4
        + [DMA((4,)), DMA((4,)), DMA((2,))],
        compiler_params=params(5, 48),
        cost_estimate=pl.CostEstimate(flops=10**8, bytes_accessed=3 * 10**7, transcendentals=0),
    )(fa, wp, rows, head_other, extra)


def norm_kernel(value, out, landing, s, r):
    me = lax.axis_index("wide")
    greet_wide(me)
    share = Scatter(lambda p: value, lambda p: landing.at[p], s, r, me)
    share.start()
    landing[me] = value[...]
    share.wait_recv()
    total = landing[0]
    for w in range(1, NW):
        total = total + landing[w]
    out[...] = total
    share.wait_send()


def norm_sum(value):
    return pl.pallas_call(
        norm_kernel,
        name="norm_sum",
        out_shape=jax.ShapeDtypeStruct((8, 128), F32),
        in_specs=[VMEM],
        out_specs=VMEM,
        scratch_shapes=[pltpu.VMEM((NW, 8, 128), F32), DMA((NW,)), DMA((NW,))],
        compiler_params=params(6, 16),
    )(value)


GRP_PARTS = ((D, SHARD), (FA_ROWS, D), (WP_ROWS, 128))


def group_kernel(*refs):
    values, gains = refs[0:3], refs[3]
    outs, gains_out = refs[4:7], refs[7]
    scratch = refs[8:]
    grp = lax.axis_index("grp")
    core, x = lax.rem(grp, 2), grp // 2
    near, far = x * 2 + 1 - core, (1 - x) * 2 + core
    barrier = pltpu.get_barrier_semaphore()
    for k in range(1, NG):
        pl.semaphore_signal(
            barrier, inc=1, device_id={"grp": lax.rem(grp + k, NG)}, device_id_type=MESH
        )
    pl.semaphore_wait(barrier, NG - 1)
    gains_in, gains_s, gains_r = scratch[15:18]
    told = []
    for k in range(1, NG):
        to = lax.rem(grp + k, NG)
        told.append(remote(gains, gains_in.at[grp], gains_s.at[k], gains_r.at[grp], grp=to))
        told[-1].start()
    gains_in[grp] = gains[...]
    sent = []
    for i, value in enumerate(values):
        half = value.shape[0] // 2
        one, one_in, two, two_in, sems = scratch[5 * i : 5 * i + 5]
        away = pl.ds(pl.multiple_of((1 - core) * half, 16), half)
        one[...] = value[away, :].astype(BF)
        copy = remote(one, one_in, sems.at[0], sems.at[1], grp=near)
        copy.start()
        sent.append(copy)
    for i, value in enumerate(values):
        half = value.shape[0] // 2
        one, one_in, two, two_in, sems = scratch[5 * i : 5 * i + 5]
        kept = pl.ds(pl.multiple_of(core * half, 16), half)
        sent[i].wait_recv()
        two[...] = (value[kept, :] + one_in[...].astype(F32)).astype(BF)
        copy = remote(two, two_in, sems.at[2], sems.at[3], grp=far)
        copy.start()
        sent.append(copy)
    for i, value in enumerate(values):
        half = value.shape[0] // 2
        one, one_in, two, two_in, sems = scratch[5 * i : 5 * i + 5]
        kept = pl.ds(pl.multiple_of(core * half, 16), half)
        sent[3 + i].wait_recv()
        outs[i][kept, :] = two[...].astype(F32) + two_in[...].astype(F32)
        piece = outs[i].at[kept]
        copy = remote(piece, piece, sems.at[4], sems.at[5], grp=near)
        copy.start()
        sent.append(copy)
    for k in range(1, NG):
        other = lax.rem(grp + k, NG)
        remote(gains, gains_in.at[other], gains_s.at[k], gains_r.at[other], grp=other).wait_recv()
    gains_out[...] = (gains_in[0] + gains_in[1]) + (gains_in[2] + gains_in[3])
    for i, value in enumerate(values):
        half = value.shape[0] // 2
        sems = scratch[5 * i + 4]
        away = outs[i].at[pl.ds(pl.multiple_of((1 - core) * half, 16), half)]
        remote(away, away, sems.at[4], sems.at[5], grp=near).wait_recv()
    for copy in sent + told:
        copy.wait_send()


def group_sum(*values):
    scratch = []
    for rows, lanes in GRP_PARTS:
        scratch += [pltpu.VMEM((rows // 2, lanes), BF)] * 4 + [DMA((6,))]
    shapes = GRP_PARTS + ((8, 640),)
    return pl.pallas_call(
        group_kernel,
        name="group_sum",
        out_shape=tuple(jax.ShapeDtypeStruct(shape, F32) for shape in shapes),
        in_specs=[VMEM] * 4,
        out_specs=(VMEM,) * 4,
        scratch_shapes=scratch + [pltpu.VMEM((NG, 8, 640), F32), DMA((NG,)), DMA((NG,))],
        compiler_params=params(7, 40),
        cost_estimate=pl.CostEstimate(flops=10**7, bytes_accessed=2 * 10**7, transcendentals=0),
    )(*values)


def dot(spec, a, b):
    return jnp.einsum(spec, a, b, preferred_element_type=F32)


def rms_normed(values, gain):
    scale = lax.rsqrt(jnp.mean(values * values, 0, keepdims=True) + norm_eps)
    return values * scale * gain[:, None]


def norm_back(values, gain, grad):
    scale = lax.rsqrt(jnp.mean(values * values, 0, keepdims=True) + norm_eps)
    pulled = grad * gain[:, None]
    middle = jnp.mean(values * pulled, 0, keepdims=True)
    return (
        scale * pulled - values * (scale * scale * scale) * middle,
        jnp.sum(grad * values * scale, 1),
    )


def rotary():
    half = HD // 2
    freqs = rope_base ** (-(jnp.arange(half, dtype=F32) * 2.0) / HD)
    angles = freqs[:, None] * jnp.arange(T, dtype=F32)[None, :]
    return (jnp.concatenate([jnp.cos(angles)] * 2, 0), jnp.concatenate([jnp.sin(angles)] * 2, 0))


def rotate(values, cosine, sine):
    half = HD // 2
    turned = jnp.concatenate([-values[..., half:, :], values[..., :half, :]], -2)
    return values * cosine + turned * sine


def unrotate(grad, cosine, sine):
    half = HD // 2
    part = grad * sine
    return grad * cosine + jnp.concatenate([part[..., half:, :], -part[..., :half, :]], -2)


def layer_forward(hidden0, gains, wa, wf, wp, allowed, cosine, sine):
    kv = KVH * HD
    group = H // KVH
    normed1 = rms_normed(hidden0, gains[0]).astype(BF)
    mixed = dot("ed,dt->et", wa, normed1)
    queries = rotate(mixed[:D].reshape(KVH, group, HD, T), cosine, sine).astype(BF)
    keys = rotate(mixed[D : D + kv].reshape(KVH, HD, T), cosine, sine).astype(BF)
    values = mixed[D + kv :].reshape(KVH, HD, T).astype(BF)
    scores = dot("kct,kgcq->kgtq", keys, queries) * HD ** (-0.5)
    scores = jnp.where(allowed, scores, masked_score)
    expo = jnp.exp(scores - jnp.max(scores, -2, keepdims=True))
    soft = expo / jnp.sum(expo, -2, keepdims=True)
    probs = soft.astype(BF)
    attended = dot("kct,kgtq->kgcq", values, probs).reshape(D, T).astype(BF)
    hidden1 = hidden0 + dot("de,et->dt", wp[:, :D], attended)
    normed2 = rms_normed(hidden1, gains[1]).astype(BF)
    gate_up = dot("ed,dt->et", wf, normed2)
    inner = (jax.nn.silu(gate_up[:FF]) * gate_up[FF:]).astype(BF)
    hidden2 = hidden1 + dot("df,ft->dt", wp[:, D:], inner)
    final = rms_normed(hidden2, gains[2]).astype(BF)
    kept = (
        hidden0, normed1, queries, keys, values, soft, probs,
        attended, hidden1, normed2, gate_up, inner, hidden2,
    )
    return final, kept


def layer_backward(grad_final, kept, gains, wa, wf, wp, cosine, sine):
    (
        hidden0, normed1, queries, keys, values, soft, probs,
        attended, hidden1, normed2, gate_up, inner, hidden2,
    ) = kept
    group = H // KVH
    grad_h2, grad_g3 = norm_back(hidden2, gains[2], grad_final)
    branch = grad_h2.astype(BF)
    grad_down = dot("dt,ft->df", branch, inner)
    grad_inner = dot("df,dt->ft", wp[:, D:], branch)
    gate, up = gate_up[:FF], gate_up[FF:]
    sigmoid = jax.nn.sigmoid(gate)
    slope = sigmoid * (1.0 + gate * (1.0 - sigmoid))
    grad_gate_up = jnp.concatenate(
        [grad_inner * up * slope, grad_inner * (gate * sigmoid)], 0
    ).astype(BF)
    grad_ffn = dot("et,dt->ed", grad_gate_up, normed2)
    grad_normed2 = dot("ed,et->dt", wf, grad_gate_up)
    grad_part, grad_g2 = norm_back(hidden1, gains[1], grad_normed2)
    grad_h1 = grad_h2 + grad_part
    branch = grad_h1.astype(BF)
    grad_wo = dot("dt,et->de", branch, attended)
    grad_att = dot("de,dt->et", wp[:, :D], branch).astype(BF).reshape(KVH, group, HD, T)
    grad_probs = dot("kct,kgcq->kgtq", values, grad_att)
    grad_scores = (
        soft * (grad_probs - jnp.sum(soft * grad_probs, -2, keepdims=True))
    ).astype(BF)
    grad_q = dot("kct,kgtq->kgcq", keys, grad_scores) * HD ** (-0.5)
    grad_k = dot("kgcq,kgtq->kct", queries, grad_scores) * HD ** (-0.5)
    grad_v = dot("kgcq,kgtq->kct", grad_att, probs)
    grad_q = unrotate(grad_q, cosine, sine).reshape(D, T)
    grad_k = unrotate(grad_k, cosine, sine).reshape(KVH * HD, T)
    grad_mixed = jnp.concatenate([grad_q, grad_k, grad_v.reshape(KVH * HD, T)], 0).astype(BF)
    grad_attn = dot("et,dt->ed", grad_mixed, normed1)
    grad_normed1 = dot("ed,et->dt", wa, grad_mixed)
    grad_part, grad_g1 = norm_back(hidden0, gains[0], grad_normed1)
    grad_proj = jnp.concatenate([grad_wo, grad_down], 1)
    return (
        (grad_h1 + grad_part).astype(BF),
        grad_attn,
        grad_ffn,
        grad_proj,
        jnp.stack([grad_g1, grad_g2, grad_g3]),
    )


def adam_update(weight, grad, first, second, rate, decay):
    first = beta_one * first + (1.0 - beta_one) * grad
    second = beta_two * second + (1.0 - beta_two) * grad * grad
    ratio = first / (1.0 - beta_one**STEP) / (jnp.sqrt(second / (1.0 - beta_two**STEP)) + adam_eps)
    return (weight - rate * (ratio + decay * weight), first, second)


def pack_fa(attn, ffn):
    pad = [(0, 0)] * (attn.ndim - 2) + [(0, FA_ROWS - 126), (0, 0)]
    return jnp.pad(jnp.concatenate([ffn, attn], -2), pad)


def pack_wp(proj):
    lead = proj.shape[:-2]
    pad = [(0, 0)] * len(lead) + [(0, WP_ROWS - 297), (0, 0)]
    return jnp.pad(proj.reshape(lead + (297, 128)), pad)


def on_device(
    token_ids,
    targets,
    segment_ids,
    row_counts,
    embed_table_master,
    embed_table_first,
    embed_table_second,
    embed_table_anchor,
    embed_table_momentum,
    attn_in_master,
    attn_in_first,
    attn_in_second,
    attn_in_anchor,
    attn_in_momentum,
    ffn_in_master,
    ffn_in_first,
    ffn_in_second,
    ffn_in_anchor,
    ffn_in_momentum,
    proj_out_master,
    proj_out_first,
    proj_out_second,
    proj_out_anchor,
    proj_out_momentum,
    norm_gains_master,
    norm_gains_first,
    norm_gains_second,
    norm_gains_anchor,
    norm_gains_momentum,
):
    me = lax.axis_index("wide")
    xh = lax.rem(me // 4, 2)
    other = flat(me // 8, 1 - xh, lax.rem(me, 4))
    ids = token_ids[0]
    gains = norm_gains_master[0]
    table = embed_table_master[0].T.astype(BF)
    weight = jnp.sum(row_counts[0, 0] * jnp.arange(1, 4))

    owner = ids // SHARD
    local = ids - owner * SHARD
    place_of = jnp.arange(T)
    same = ids[:, None] == ids[None, :]
    first_seen = ~jnp.any(same & (place_of[None, :] < place_of[:, None]), 1)
    rank = jnp.sum(
        (first_seen[None, :] & (owner[None, :] == owner[:, None]) & (ids[None, :] < ids[:, None])),
        1,
        dtype=jnp.int32,
    )
    most = jnp.max(rank) + 1
    slot_place = jnp.arange(NW * CAP)

    def slot_picks(turn):
        at = rank - turn * CAP
        slot = jnp.where((at >= 0) & (at < CAP), owner * CAP + at, -1)
        return slot_place[:, None] == slot[None, :]

    def message(picks):
        asked = jnp.max(jnp.where(picks, local[None, :], -1), 1).reshape(NW, 1, CAP)
        asked = jnp.pad(asked, ((0, 0), (0, 0), (0, 128 - CAP)), constant_values=-1)
        rest = jnp.concatenate(
            [
                targets[0].reshape(2, 128),
                jnp.broadcast_to(weight, (1, 128)),
                jnp.broadcast_to(most, (1, 128)),
                jnp.zeros((3, 128), jnp.int32),
            ],
            0,
        )
        return jnp.concatenate([asked, jnp.broadcast_to(rest[None], (NW, 7, 128))], 1)

    picks = slot_picks(0)
    fa = pack_fa(attn_in_master[0].T, ffn_in_master[0].T).astype(BF)
    wp = pack_wp(proj_out_master[0].T).astype(BF)
    got, rows, most_all, table_other, rows_t, fa_all, wp_all = front(message(picks), table, fa, wp)
    turns = (jnp.max(most_all) + CAP - 1) // CAP

    def to_tokens(rows, picks):
        return dot("sd,st->dt", rows, picks.astype(BF))

    def more_tokens(carry):
        turn, hidden = carry
        picks = slot_picks(turn)
        return turn + 1, hidden + to_tokens(more_rows(message(picks), table), picks)

    hidden0 = lax.while_loop(
        lambda carry: carry[0] < turns, more_tokens, (jnp.int32(1), to_tokens(rows, picks))
    )[1]

    wf_full = fa_all[:, :96].reshape(2 * FF, D)
    wa_full = fa_all[:, 96:126].reshape(QKV, D)
    wp_full = wp_all[:, :297].reshape(D, D + FF)
    segments = segment_ids[0]
    allowed = (place_of[:, None] <= place_of[None, :]) & (segments[:, None] == segments[None, :])
    cosine, sine = rotary()
    final, kept = layer_forward(hidden0, gains, wa_full, wf_full, wp_full, allowed, cosine, sine)

    total = jnp.sum(got[:, 3, 0]).astype(F32) * T
    goals = got[:, 1:3, :].reshape(4, 2, 4, T)
    goals = jnp.where(xh == 0, goals[:, 0], goals[:, 1]).reshape(16, 1, T)
    near, far = goals - me * SHARD, goals - other * SHARD
    goals = jnp.where(
        (near >= 0) & (near < SHARD), near, jnp.where((far >= 0) & (far < SHARD), far + SHARD, -1)
    )
    goals = jnp.broadcast_to(goals, (16, 8, T))
    plain = weight.astype(F32)
    weights = jnp.concatenate(
        [jnp.full((1, T), plain / total, F32), jnp.full((1, T), plain, F32), jnp.zeros((6, T), F32)], 0
    )
    grad_final, head_own, head_other, loss = head(final, rows_t, table, table_other, goals, weights)

    grad_embedded, grad_attn, grad_ffn, grad_proj, grad_gains = layer_backward(
        grad_final, kept, gains, wa_full, wf_full, wp_full, cosine, sine
    )
    fa_parts = pack_fa(
        grad_attn.astype(BF).reshape(NW, 30, D), grad_ffn.astype(BF).reshape(NW, 96, D)
    ).reshape(4, 2, 4, FA_ROWS, D)
    wp_parts = pack_wp(grad_proj.astype(BF).reshape(NW, 18, D + FF)).reshape(4, 2, 4, WP_ROWS, 128)
    extra = jnp.zeros((8, 640), F32).at[:3, :D].set(grad_gains).at[3, 0].set(jnp.sum(loss[0]))

    def to_slots(picks):
        return dot("st,dt->sd", picks.astype(BF), grad_embedded).astype(BF)

    fa_sum, wp_sum, rows_in, head_in, extra_sum = back(
        fa_parts, wp_parts, to_slots(picks), head_other, extra
    )

    def to_table(got, rows):
        asked = got[:, 0, :CAP].reshape(NW * CAP)
        hot = (asked[:, None] == jnp.arange(SHARD)[None, :]).astype(BF)
        return dot("sd,sv->dv", rows, hot)

    def more_table(carry):
        turn, grad = carry
        picks = slot_picks(turn)
        return turn + 1, grad + to_table(*more_grads(message(picks), to_slots(picks)))

    table_grad = lax.while_loop(
        lambda carry: carry[0] < turns,
        more_table,
        (jnp.int32(1), head_own + head_in.astype(F32) + to_table(got, rows_in)),
    )[1]

    sum_gains = extra_sum[:3, :D]
    loss_total = extra_sum[3, 0]
    squares = jnp.sum(table_grad * table_grad) + jnp.sum(fa_sum * fa_sum) + jnp.sum(wp_sum * wp_sum)
    squares = norm_sum(jnp.broadcast_to(squares, (8, 128)))[0, 0]
    norm = jnp.sqrt(squares + jnp.sum(sum_gains * sum_gains))
    factor = jnp.minimum(1.0, clip_norm / norm)

    sum_ffn, sum_attn = fa_sum[:96], fa_sum[96:126]
    sum_proj = wp_sum[:297].reshape(18, D + FF)
    kinds = (
        (
            embed_table_master[0].T,
            table_grad,
            embed_table_first[0].T,
            embed_table_second[0].T,
            embed_table_anchor.T,
            embed_table_momentum.T,
            inner_rate,
            weight_decay,
        ),
        (
            attn_in_master[0].T,
            sum_attn,
            attn_in_first[0].T,
            attn_in_second[0].T,
            attn_in_anchor.T,
            attn_in_momentum.T,
            inner_rate,
            weight_decay,
        ),
        (
            ffn_in_master[0].T,
            sum_ffn,
            ffn_in_first[0].T,
            ffn_in_second[0].T,
            ffn_in_anchor.T,
            ffn_in_momentum.T,
            inner_rate,
            weight_decay,
        ),
        (
            proj_out_master[0].T,
            sum_proj,
            proj_out_first[0].T,
            proj_out_second[0].T,
            proj_out_anchor.T,
            proj_out_momentum.T,
            inner_rate,
            weight_decay,
        ),
        (
            gains,
            sum_gains,
            norm_gains_first[0],
            norm_gains_second[0],
            norm_gains_anchor,
            norm_gains_momentum,
            gain_rate,
            0.0,
        ),
    )
    updated = [
        adam_update(kind[0], kind[1] * factor, kind[2], kind[3], kind[6], kind[7]) for kind in kinds
    ]
    diffs = [kinds[index][4] - updated[index][0] for index in range(5)]
    summed = group_sum(
        diffs[0],
        pack_fa(diffs[1], diffs[2]),
        pack_wp(diffs[3]),
        jnp.zeros((8, 640), F32).at[:3, :D].set(diffs[4]),
    )
    sums = (
        summed[0],
        summed[1][96:126],
        summed[1][:96],
        summed[2][:297].reshape(18, D + FF),
        summed[3][:3, :D],
    )
    results = [loss_total.reshape(1), total.reshape(1), norm.reshape(1)]
    for index in range(5):
        average = sums[index] / NG
        outer = outer_momentum * kinds[index][5] + average
        weight = kinds[index][4] - outer_rate * (average + outer_momentum * outer)
        values = [average, outer, weight, updated[index][1], updated[index][2]]
        if index < 4:
            values = [value.T for value in values]
        results += values[:3] + [values[3][None], values[4][None]]
    return tuple(results)


def solution(mesh):
    in_specs = (
        P("grp", "wide"),
        P("grp", "wide"),
        P("grp", "wide"),
        P("grp", "wide", None),
        P("grp", "wide", None),
        P("grp", "wide", None),
        P("grp", "wide", None),
        P("wide", None),
        P("wide", None),
        P("grp", None, "wide"),
        P("grp", None, "wide"),
        P("grp", None, "wide"),
        P(None, "wide"),
        P(None, "wide"),
        P("grp", None, "wide"),
        P("grp", None, "wide"),
        P("grp", None, "wide"),
        P(None, "wide"),
        P(None, "wide"),
        P("grp", None, "wide"),
        P("grp", None, "wide"),
        P("grp", None, "wide"),
        P(None, "wide"),
        P(None, "wide"),
        P("grp", None, None),
        P("grp", None, None),
        P("grp", None, None),
        P(),
        P(),
    )
    out_specs = (
        P("grp"),
        P("grp"),
        P("grp"),
        P("wide", None),
        P("wide", None),
        P("wide", None),
        P("grp", "wide", None),
        P("grp", "wide", None),
        P(None, "wide"),
        P(None, "wide"),
        P(None, "wide"),
        P("grp", None, "wide"),
        P("grp", None, "wide"),
        P(None, "wide"),
        P(None, "wide"),
        P(None, "wide"),
        P("grp", None, "wide"),
        P("grp", None, "wide"),
        P(None, "wide"),
        P(None, "wide"),
        P(None, "wide"),
        P("grp", None, "wide"),
        P("grp", None, "wide"),
        P(),
        P(),
        P(),
        P("grp", None, None),
        P("grp", None, None),
    )
    return jax.shard_map(
        on_device, mesh=mesh, in_specs=in_specs, out_specs=out_specs, check_vma=False
    )
```

```python
import functools

import jax
import jax.numpy as jnp
import numpy as np
from jax import lax
from jax.experimental import pallas as pl
from jax.experimental.pallas import tpu as pltpu
from jax.sharding import PartitionSpec as P

D = 576
H = 9
KVH = 3
HD = 64
FF = 1536
QKV = 960
STEP = 8
T = 256
SHARD = 1536
NW = 32
NG = 4
CAP = 32
FA_ROWS = 128
WP_ROWS = 320
FFN_AT, DOWN_AT, ATTN_AT, PACKED = 0, 96, 160, 208
SUMMED = 224

beta_one = 0.9
beta_two = 0.999
adam_eps = 1e-08
weight_decay = 0.1
inner_rate = 0.02
gain_rate = 0.2
clip_norm = 0.01
penalty_weight = 0.005
outer_rate = 0.7
outer_momentum = 0.9
rope_base = 100000.0
norm_eps = 1e-05
masked_score = -1e30

BF = jnp.bfloat16
F32 = jnp.float32
MESH = pl.DeviceIdType.MESH
VMEM = pl.BlockSpec(memory_space=pltpu.VMEM)
ANY = pl.BlockSpec(memory_space=pl.ANY)
DMA = pltpu.SemaphoreType.DMA
MIB = 1 << 20


def params(collective, mib):
    return pltpu.CompilerParams(
        collective_id=collective, has_side_effects=True, vmem_limit_bytes=mib * MIB
    )


def place():
    me = lax.axis_index("wide")
    return me, me // 8, lax.rem(me // 4, 2), lax.rem(me, 4)


def flat(y, xh, z):
    return y * 8 + xh * 4 + z


def turn4(at, by):
    return lax.rem(at + by, 4)


def remote(src, dst, ssem, rsem, **device):
    return pltpu.make_async_remote_copy(
        src_ref=src,
        dst_ref=dst,
        send_sem=ssem,
        recv_sem=rsem,
        device_id=device,
        device_id_type=MESH,
    )


def greet_wide(me, grp=None, sides=False, meanwhile=None):
    barrier = pltpu.get_barrier_semaphore()

    def one(k, carry):
        pl.semaphore_signal(
            barrier, inc=1, device_id={"wide": lax.rem(me + k, NW)}, device_id_type=MESH
        )
        return carry

    lax.fori_loop(1, NW, one, 0)
    count = NW - 1
    if grp is not None:
        for k in range(1, NG):
            pl.semaphore_signal(
                barrier, inc=1, device_id={"grp": lax.rem(grp + k, NG)}, device_id_type=MESH
            )
        count += NG - 1
    if sides:
        for step in (1, 3):
            pl.semaphore_signal(barrier, inc=1, device_id=beside(step), device_id_type=MESH)
        count += 2
    if meanwhile is not None:
        meanwhile()
    pl.semaphore_wait(barrier, count)


class Scatter:
    def __init__(self, src_at, dst_at, ssem, rsem, me):
        self.src_at, self.dst_at, self.ssem, self.rsem, self.me = src_at, dst_at, ssem, rsem, me

    def copy(self, k):
        peer = lax.rem(self.me + k, NW)
        return remote(
            self.src_at(peer), self.dst_at(self.me), self.ssem.at[k], self.rsem.at[self.me], wide=peer
        )

    def start(self):
        def one(k, carry):
            self.copy(k).start()
            return carry

        lax.fori_loop(1, NW, one, 0)

    def wait_recv(self):
        def one(k, carry):
            peer = lax.rem(self.me + k, NW)
            remote(
                self.src_at(peer), self.dst_at(peer), self.ssem.at[k], self.rsem.at[peer], wide=peer
            ).wait_recv()
            return carry

        lax.fori_loop(1, NW, one, 0)

    def wait_send(self):
        def one(k, carry):
            self.copy(k).wait_send()
            return carry

        lax.fori_loop(1, NW, one, 0)


class Ring:
    def __init__(self, view, sem, bounds, ssem):
        self.view, self.sem, self.bounds = view, sem, bounds
        self.ssem, self.used, self.sent = ssem, 0, []
        self.me, self.y, self.xh, self.z = place()

    def send(self, src, dst, rsem, to):
        copy = remote(src, dst, self.ssem.at[self.used], rsem, wide=flat(to[0], self.xh, to[1]))
        self.used += 1
        copy.start()
        self.sent.append(copy)

    def piece(self, y, z, first, count):
        return self.view(y, z, self.bounds[first], self.bounds[first + count] - self.bounds[first])

    def pass_on(self, y, z, first, count, index, *to):
        piece = self.piece(y, z, first, count)
        for one in to:
            self.send(piece, piece, self.sem(y, z, index), one)

    def landed(self, piece, sem):
        remote(piece, piece, self.ssem.at[0], sem, wide=self.me).wait_recv()

    def wait(self, y, z, first, count, index):
        self.landed(self.piece(y, z, first, count), self.sem(y, z, index))

    def around(self):
        y, z = self.y, self.z
        return y, z, (turn4(y, 1), z), (turn4(y, 3), z), (y, turn4(z, 1)), (y, turn4(z, 3))

    def own(self, src, dst, index):
        y, z, y_up, y_down, z_up, z_down = self.around()
        for to in (y_up, y_down, z_up, z_down):
            self.send(src, dst, self.sem(y, z, index), to)

    def near(self, parts=None):
        y, z, y_up, y_down, z_up, z_down = self.around()
        for at, far, turn, half, sides in (
            (y_down, y_up, 0, 0, (z_up, z_down)),
            (y_up, y_down, 1, 0, (z_up, z_down)),
            (z_down, z_up, 0, 2, (y_up, y_down)),
            (z_up, z_down, 1, 2, (y_up, y_down)),
        ):
            if parts is None:
                self.wait(*at, 0, 4, 0)
            else:
                for part, index in parts:
                    self.landed(part(*at), self.sem(*at, index))
            self.pass_on(*at, turn, 1, turn, far)
            self.pass_on(*at, 2 + turn, 1, 2 + turn, far)
            self.pass_on(*at, half, 2, half, *sides)

    def far(self):
        y, z, y_up, y_down, z_up, z_down = self.around()
        for at, half, sides in (
            ((turn4(y, 2), z), 0, (z_up, z_down)),
            ((y, turn4(z, 2)), 2, (y_up, y_down)),
        ):
            for index in range(4):
                self.wait(*at, index, 1, index)
            self.pass_on(*at, half, 2, half, *sides)

    def cross(self):
        y, z, y_up, y_down, z_up, z_down = self.around()
        for k in (1, 3, 2):
            row, column = turn4(y, k), turn4(z, k)
            self.wait(row, z_down[1], 0, 2, 0)
            self.pass_on(row, z_down[1], 0, 1, 0, z_up)
            self.wait(row, z_up[1], 0, 2, 0)
            self.pass_on(row, z_up[1], 1, 1, 1, z_down)
            self.wait(y_down[0], column, 2, 2, 2)
            self.pass_on(y_down[0], column, 2, 1, 2, y_up)
            self.wait(y_up[0], column, 2, 2, 2)
            self.pass_on(y_up[0], column, 3, 1, 3, y_down)

    def last(self):
        y, z = self.y, self.z
        for k in (1, 3, 2):
            row, column = turn4(y, k), turn4(z, k)
            for index in range(2):
                self.wait(row, turn4(z, 2), index, 1, index)
                self.wait(turn4(y, 2), column, 2 + index, 1, 2 + index)

    def finish(self):
        for copy in self.sent:
            copy.wait_send()


RING_SENDS = 36


def beside(step):
    me, y, xh, z = place()
    grp = lax.axis_index("grp")
    low = grp // 2
    side = lax.rem(xh + low + (0 if step == 1 else 1), 2)
    return {"grp": (1 - low) * 2 + lax.rem(grp, 2), "wide": flat(y, side, z)}


class Relay:
    def __init__(self, sources, stops, ends, ssem, rsem):
        self.sources, self.stops, self.ends, self.ssem, self.rsem = sources, stops, ends, ssem, rsem

    def copy(self, src, dst, at, step):
        return remote(src, dst, self.ssem.at[at], self.rsem.at[at], **beside(step))

    def legs(self, hop):
        for i, step in enumerate((1, 3)):
            src = self.sources[i] if hop == 0 else self.stops[i]
            dst = self.stops[i] if hop == 0 else self.ends[i]
            yield self.copy(src, dst, 2 * hop + i, step)

    def start(self):
        for copy in self.legs(0):
            copy.start()

    def forward(self):
        for first, second in zip(self.legs(0), self.legs(1)):
            first.wait_recv()
            second.start()

    def wait(self):
        for copy in self.legs(1):
            copy.wait_recv()

    def finish(self):
        for hop in (0, 1):
            for copy in self.legs(hop):
                copy.wait_send()


def look_up(got, table, hot, rows, slot_row):
    asked = got[:, slot_row, :].astype(F32)
    asked = jnp.concatenate([asked, jnp.zeros((128 - NW, 128), F32)], 0).T
    step = 8 * CAP
    for first in range(0, NW, 8):
        for d in range(8):
            column = asked[0:CAP, first + d : first + d + 1]
            lanes = lax.broadcasted_iota(jnp.int32, (CAP, SHARD), 1).astype(F32)
            hot[d * CAP : (d + 1) * CAP, :] = jnp.where(lanes == column, 1.0, 0.0).astype(BF)
        picked = lax.dot_general(
            hot[...], table[...], (((1,), (1,)), ((), ())), preferred_element_type=F32
        )
        rows[first * CAP : first * CAP + step, :] = picked.astype(BF)


def slots(at):
    return pl.ds(pl.multiple_of(at * CAP, CAP), CAP)


def turn_over(table, rows, first):
    for c in range(0, SHARD, 256):
        rows[first + c : first + c + 256, :] = table[:, c : c + 256].T


def owner_of(ids):
    return (((ids >> 9) * 171) >> 9).astype(jnp.int32)


def ask_rows(tok, msg, picks, slot_out):
    row = tok[0:1, :]
    column = jnp.broadcast_to(row.astype(F32), (128, T)).T[:, 0:1].astype(jnp.int32)
    row_owner, column_owner = owner_of(row), owner_of(column)
    down = lax.broadcasted_iota(jnp.int32, (T, T), 0)
    across = lax.broadcasted_iota(jnp.int32, (T, T), 1)
    same = row == column

    def count(which, axis):
        return jnp.sum(jnp.where(which, 1.0, 0.0), axis, keepdims=True)

    first_row = count(same & (down < across), 0) == 0.0
    first_column = count(same & (across < down), 1) == 0.0
    near = row_owner == column_owner
    rank_row = count(near & (column < row) & first_column, 0)
    rank_column = count(near & (row < column) & first_row, 1)
    slot_row = jnp.where(rank_row < CAP, row_owner.astype(F32) * CAP + rank_row, -1.0)
    slot_column = jnp.where(rank_column < CAP, column_owner.astype(F32) * CAP + rank_column, -1.0)
    lanes = lax.broadcasted_iota(jnp.int32, (T, NW * CAP), 1).astype(F32)
    hit = lanes == slot_column
    picks[...] = jnp.where(hit, 1.0, 0.0).astype(BF)
    slot_out[...] = jnp.broadcast_to(slot_row, (8, T)).astype(jnp.int32)
    local = (column - column_owner * SHARD).astype(F32)
    asked = jnp.max(jnp.where(hit, local, -1.0), 0, keepdims=True).astype(jnp.int32)
    most = (jnp.max(rank_row, 1, keepdims=True) + 1.0).astype(jnp.int32)
    rest = [
        tok[1:2, 0:128], tok[1:2, 128:256], tok[3:4, 0:128], jnp.broadcast_to(most, (1, 128)),
    ] + [jnp.zeros((1, 128), jnp.int32)] * 3
    for g in range(8):
        msg[g] = jnp.concatenate([asked[:, g * 128 : (g + 1) * 128]] + rest, 0)


def find_rows(got, table, asked_t, hot, rows, part):
    asked = got[:, 0, :].astype(F32)
    asked_t[...] = jnp.concatenate([asked, jnp.full((128 - NW, 128), -1.0, F32)], 0).T
    mine = asked_t[pl.ds(pl.multiple_of(part * CAP, CAP), CAP), :]
    lanes = lax.broadcasted_iota(jnp.int32, (CAP, SHARD), 1).astype(F32)
    for d in range(NW):
        hot[d * CAP : (d + 1) * CAP, :] = jnp.where(lanes == mine[:, d : d + 1], 1.0, 0.0).astype(BF)
    step = 8 * CAP
    for first in range(0, NW * CAP, step):
        picked = lax.dot_general(
            hot[first : first + step, :], table[...], (((1,), (1,)), ((), ())), preferred_element_type=F32
        )
        rows[first : first + step, :] = picked.astype(BF)


def turn_over(table, rows, first):
    for c in range(0, SHARD, 256):
        rows[first + c : first + c + 256, :] = table[:, c : c + 256].T


def front_kernel(
    tok, table, packed, got, emb, most, table_other, rows_t, packed_all, picks, slot_out, hot, goal, weights,
    msg, asked_t, rows, own_most, stops, msg_s, msg_r, emb_s, emb_r, most_s, most_r, swap_s, swap_r,
    ring_s, ring_r, x_sem, local,
):
    me, y, xh, z = place()
    grp = lax.axis_index("grp")
    other = flat(y, 1 - xh, z)
    greet_wide(me, grp, sides=True, meanwhile=lambda: ask_rows(tok, msg, picks, slot_out))
    over = remote(packed, packed_all.at[y, z, xh], x_sem.at[0], x_sem.at[1], wide=other)
    over.start()
    ask = Scatter(lambda p: msg.at[p // 4], lambda p: got.at[p], msg_s, msg_r, me)
    ask.start()
    got[me] = msg[me // 4]
    ring = Ring(
        lambda Y, Z, first, count: packed_all.at[Y, Z, :, pl.ds(first, count)],
        lambda Y, Z, index: ring_r.at[Y, Z, index],
        (0, 48, 96, 144, 208),
        ring_s,
    )
    ring.own(packed, packed_all.at[y, z, xh], 0)
    keep = pltpu.make_async_copy(packed, packed_all.at[y, z, xh], local.at[0])
    keep.start()
    ask.wait_recv()
    find_rows(got, table, asked_t, hot, rows, lax.rem(me, 4))
    reply = Scatter(lambda p: rows.at[slots(p)], lambda p: emb.at[slots(p)], emb_s, emb_r, me)
    reply.start()
    over.wait_recv()
    ring.own(packed_all.at[y, z, 1 - xh], packed_all.at[y, z, 1 - xh], 4)
    emb[slots(me), :] = rows[slots(me), :]
    halves = (pl.ds(0, D // 2), pl.ds(D // 2, D // 2))
    trade = Relay(
        [table.at[half] for half in halves],
        [stops.at[i] for i in range(2)],
        [table_other.at[half] for half in halves],
        swap_s,
        swap_r,
    )
    trade.start()
    ring.near(
        [
            (lambda Y, Z: packed_all.at[Y, Z, xh], 0),
            (lambda Y, Z: packed_all.at[Y, Z, 1 - xh], 4),
        ]
    )
    largest = jnp.max(got[:, 4, :], 0, keepdims=True)
    own_most[...] = jnp.broadcast_to(largest, (8, 128))
    most[grp] = own_most[...]
    told = []
    for k in range(1, NG):
        to = lax.rem(grp + k, NG)
        told.append(remote(own_most, most.at[grp], most_s.at[k], most_r.at[grp], grp=to))
        told[-1].start()
    total = jnp.sum(got[:, 3, :].astype(F32), 0, keepdims=True)
    total = jnp.concatenate([total, total], 1) * T
    plain = tok[3:4, :].astype(F32)
    weights[...] = jnp.concatenate([plain / total, plain, total] + [jnp.zeros((1, T), F32)] * 5, 0)

    def place_goal(j, carry):
        from_dev = flat(j // 4, xh, lax.rem(j, 4))
        goals = jnp.concatenate([got[from_dev, 1:2, :], got[from_dev, 2:3, :]], 1)
        near, far = goals - me * SHARD, goals - other * SHARD
        at = jnp.where((far >= 0) & (far < SHARD), far + SHARD, -1)
        at = jnp.where((near >= 0) & (near < SHARD), near, at)
        goal[j] = jnp.broadcast_to(at, (8, T))
        return carry

    lax.fori_loop(0, 16, place_goal, 0)
    ring.far()
    turn_over(table, rows_t, 0)
    ring.cross()
    trade.forward()
    reply.wait_recv()
    for k in range(1, NG):
        to = lax.rem(grp + k, NG)
        remote(own_most, most.at[to], most_s.at[k], most_r.at[to], grp=to).wait_recv()
    trade.wait()
    turn_over(table_other, rows_t, SHARD)
    ring.last()
    keep.wait()
    over.wait_send()
    ask.wait_send()
    reply.wait_send()
    trade.finish()
    for copy in told:
        copy.wait_send()
    ring.finish()


def front(tok, table, packed):
    return pl.pallas_call(
        front_kernel,
        name="front",
        out_shape=(
            jax.ShapeDtypeStruct((NW, 8, 128), jnp.int32),
            jax.ShapeDtypeStruct((NW * CAP, D), BF),
            jax.ShapeDtypeStruct((NG, 8, 128), jnp.int32),
            jax.ShapeDtypeStruct((D, SHARD), BF),
            jax.ShapeDtypeStruct((2 * SHARD, D), BF),
            jax.ShapeDtypeStruct((4, 4, 2, PACKED, D), BF),
            jax.ShapeDtypeStruct((T, NW * CAP), BF),
            jax.ShapeDtypeStruct((8, T), jnp.int32),
            jax.ShapeDtypeStruct((NW * CAP, SHARD), BF),
            jax.ShapeDtypeStruct((16, 8, T), jnp.int32),
            jax.ShapeDtypeStruct((8, T), F32),
        ),
        in_specs=[VMEM, VMEM, ANY],
        out_specs=(VMEM, VMEM, VMEM, VMEM, VMEM, ANY) + (VMEM,) * 5,
        scratch_shapes=[
            pltpu.VMEM((8, 8, 128), jnp.int32),
            pltpu.VMEM((128, 128), F32),
            pltpu.VMEM((NW * CAP, D), BF),
            pltpu.VMEM((8, 128), jnp.int32),
            pltpu.VMEM((2, D // 2, SHARD), BF),
            DMA((NW,)),
            DMA((NW,)),
            DMA((NW,)),
            DMA((NW,)),
            DMA((NG,)),
            DMA((NG,)),
            DMA((4,)),
            DMA((4,)),
            DMA((RING_SENDS + 4,)),
            DMA((4, 4, 5)),
            DMA((2,)),
            DMA((1,)),
        ],
        compiler_params=params(1, 48),
        cost_estimate=pl.CostEstimate(flops=2 * 10**9, bytes_accessed=3 * 10**7, transcendentals=0),
    )(tok, table, packed)


ORDER = tuple((i // 8) * 8 + (i % 2) * 4 + (i // 2) % 4 for i in range(NW))


def spread_rows(used, stride, at, repeat=1):
    picks = np.zeros((NW * stride, NW * used), np.float32)
    for i, w in enumerate(ORDER):
        for j in range(repeat):
            for r in range(used):
                picks[i * stride + at + j * used + r, w * used + r] = 1.0
    return picks


def rope():
    half = HD // 2
    freqs = np.float32(rope_base) ** (-(np.arange(half, dtype=np.float32) * np.float32(2.0)) / np.float32(HD))
    angles = freqs.astype(np.float32)[:, None] * np.arange(T, dtype=np.float32)[None, :]
    return np.concatenate([np.cos(angles), np.sin(angles)], 0).astype(np.float32)


def turned(values):
    return values.T


def gain_columns(gains):
    return jnp.concatenate([gains[...], jnp.zeros((120, D), F32)], 0).T


def rms(values, gain):
    scale = lax.rsqrt(jnp.mean(values * values, 0, keepdims=True) + norm_eps)
    return values * scale * gain


def rms_back(values, gain, grad):
    scale = lax.rsqrt(jnp.mean(values * values, 0, keepdims=True) + norm_eps)
    pulled = grad * gain
    middle = jnp.mean(values * pulled, 0, keepdims=True)
    back = scale * pulled - values * (scale * scale * scale) * middle
    return back, jnp.sum(grad * values * scale, 1, keepdims=True)


def mask_of(tok):
    row = tok[2:3, :]
    column = jnp.broadcast_to(row.astype(F32), (128, T)).T[:, 0:1].astype(jnp.int32)
    down = lax.broadcasted_iota(jnp.int32, (T, T), 0)
    across = lax.broadcasted_iota(jnp.int32, (T, T), 1)
    return (down <= across) & (row == column)


def mm(a, b):
    return jnp.dot(a, b, preferred_element_type=F32)


def mm_nt(a, b):
    return lax.dot_general(a, b, (((1,), (1,)), ((), ())), preferred_element_type=F32)


def mm_tn(a, b):
    return lax.dot_general(a, b, (((0,), (0,)), ((), ())), preferred_element_type=F32)


def rotated(x, rot):
    cosine, sine = rot[0:32, :], rot[32:64, :]
    one, two = x[0:32, :], x[32:64, :]
    return jnp.concatenate([one * cosine - two * sine, two * cosine + one * sine], 0)


def unrotated(x, rot):
    cosine, sine = rot[0:32, :], rot[32:64, :]
    one, two = x[0:32, :], x[32:64, :]
    return jnp.concatenate([one * cosine + two * sine, two * cosine - one * sine], 0)


def load_trunk(packed, ffn, down, attn, sem):
    loads = [
        pltpu.make_async_copy(packed.at[:, :, :, ATTN_AT:PACKED], attn, sem.at[0]),
        pltpu.make_async_copy(packed.at[:, :, :, FFN_AT:DOWN_AT], ffn, sem.at[1]),
        pltpu.make_async_copy(packed.at[:, :, :, DOWN_AT:ATTN_AT, 0:512], down, sem.at[2]),
    ]
    for load in loads:
        load.start()
    return loads


TRUNK_SCRATCH = [
    pltpu.VMEM((4, 4, 2, 96, D), BF),
    pltpu.VMEM((4, 4, 2, 64, 512), BF),
    pltpu.VMEM((4, 4, 2, 48, D), BF),
    DMA((3,)),
]


def forward_kernel(
    hidden, packed, gains, rot, tok,
    final, h0, n1, q, k, v, lse, att, h1, n2, gate_up, inner, h2,
    ffn, down, attn, sem, mixed,
):
    loads = load_trunk(packed, ffn, down, attn, sem)
    columns = gain_columns(gains)
    allowed = mask_of(tok)
    start = turned(hidden[...])
    h0[...] = start
    normed = rms(start, columns[:, 0:1]).astype(BF)
    n1[...] = normed
    loads[0].wait()
    rows48 = attn[...].reshape(NW * 48, D)
    product = mm(rows48, normed)
    for i, w in enumerate(ORDER):
        mixed[w * 30 : w * 30 + 30, :] = product[i * 48 : i * 48 + 30, :]
    for kv in range(KVH):
        k[kv * HD : (kv + 1) * HD, :] = rotated(
            mixed[D + kv * HD : D + (kv + 1) * HD, :], rot[...]
        ).astype(BF)
        at = D + (KVH + kv) * HD
        v[kv * HD : (kv + 1) * HD, :] = mixed[at : at + HD, :].astype(BF)
    logs = []
    for h in range(H):
        kv = h // (H // KVH)
        query = rotated(mixed[h * HD : (h + 1) * HD, :], rot[...]).astype(BF)
        q[h * HD : (h + 1) * HD, :] = query
        scores = mm_tn(k[kv * HD : (kv + 1) * HD, :], query) * HD ** (-0.5)
        scores = jnp.where(allowed, scores, masked_score)
        top = jnp.max(scores, 0, keepdims=True)
        power = jnp.exp(scores - top)
        total = jnp.sum(power, 0, keepdims=True)
        probs = (power / total).astype(BF)
        att[h * HD : (h + 1) * HD, :] = mm(v[kv * HD : (kv + 1) * HD, :], probs).astype(BF)
        logs.append(top + jnp.log(total))
    lse[...] = jnp.concatenate(logs + [jnp.zeros((16 - H, T), F32)], 0)
    product = mm(rows48, att[...])
    for i, w in enumerate(ORDER):
        mixed[w * 18 : w * 18 + 18, :] = product[i * 48 + 30 : i * 48 + 48, :]
    middle = start + mixed[0:D, :]
    h1[...] = middle
    normed = rms(middle, columns[:, 1:2]).astype(BF)
    n2[...] = normed
    loads[1].wait()
    gate_up[...] = mm(ffn[...].reshape(NW * 96, D), normed)
    for i in range(NW // 2):
        gate = gate_up[i * 96 : (i + 1) * 96, :]
        up = gate_up[FF + i * 96 : FF + (i + 1) * 96, :]
        w = ORDER[i]
        inner[w * 96 : (w + 1) * 96, :] = (gate / (1.0 + jnp.exp(-gate)) * up).astype(BF)
    loads[2].wait()
    rows64 = down[...].reshape(NW * 64, 512)
    for j in range(3):
        product = mm(rows64, inner[j * 512 : (j + 1) * 512, :])
        for i, w in enumerate(ORDER):
            piece = product[i * 64 + j * 18 : i * 64 + j * 18 + 18, :]
            if j:
                mixed[w * 18 : w * 18 + 18, :] += piece
            else:
                mixed[w * 18 : w * 18 + 18, :] = piece
    last = middle + mixed[0:D, :]
    h2[...] = last
    final[...] = rms(last, columns[:, 2:3]).astype(BF)


def forward(hidden, packed, gains, rot, tok):
    def out(rows, kind):
        return jax.ShapeDtypeStruct((rows, T), kind)

    return pl.pallas_call(
        forward_kernel,
        name="forward",
        out_shape=(
            out(D, BF), out(D, F32), out(D, BF), out(D, BF), out(KVH * HD, BF), out(KVH * HD, BF), out(16, F32),
            out(D, BF), out(D, F32), out(D, BF), out(2 * FF, F32), out(FF, BF), out(D, F32),
        ),
        in_specs=[VMEM, ANY, VMEM, VMEM, VMEM],
        out_specs=(VMEM,) * 13,
        scratch_shapes=TRUNK_SCRATCH + [pltpu.VMEM((QKV, T), F32)],
        compiler_params=pltpu.CompilerParams(vmem_limit_bytes=48 * MIB),
        cost_estimate=pl.CostEstimate(flops=4 * 10**9, bytes_accessed=2 * 10**7, transcendentals=10**6),
    )(hidden, packed, gains, rot, tok)


def more_rows_kernel(msg, table, got, emb, hot, rows, msg_s, msg_r, emb_s, emb_r):
    me = lax.axis_index("wide")
    greet_wide(me)
    ask = Scatter(lambda p: msg.at[p], lambda p: got.at[p], msg_s, msg_r, me)
    ask.start()
    got[me] = msg[me]
    ask.wait_recv()
    look_up(got, table, hot, rows, 0)
    reply = Scatter(lambda p: rows.at[slots(p)], lambda p: emb.at[slots(p)], emb_s, emb_r, me)
    reply.start()
    emb[slots(me), :] = rows[slots(me), :]
    reply.wait_recv()
    ask.wait_send()
    reply.wait_send()


def more_rows(msg, table):
    return pl.pallas_call(
        more_rows_kernel,
        name="more_rows",
        out_shape=(
            jax.ShapeDtypeStruct((NW, 8, 128), jnp.int32),
            jax.ShapeDtypeStruct((NW * CAP, D), BF),
        ),
        in_specs=[VMEM, VMEM],
        out_specs=(VMEM, VMEM),
        scratch_shapes=[pltpu.VMEM((8 * CAP, SHARD), BF), pltpu.VMEM((NW * CAP, D), BF)]
        + [DMA((NW,))] * 4,
        compiler_params=params(2, 40),
    )(msg, table)[1]


def more_grads_kernel(msg, rows, got, out, msg_s, msg_r, row_s, row_r):
    me = lax.axis_index("wide")
    greet_wide(me)
    ask = Scatter(lambda p: msg.at[p], lambda p: got.at[p], msg_s, msg_r, me)
    ask.start()
    give = Scatter(lambda p: rows.at[slots(p)], lambda p: out.at[slots(p)], row_s, row_r, me)
    give.start()
    got[me] = msg[me]
    out[slots(me), :] = rows[slots(me), :]
    ask.wait_recv()
    give.wait_recv()
    ask.wait_send()
    give.wait_send()


def more_grads(msg, rows):
    return pl.pallas_call(
        more_grads_kernel,
        name="more_grads",
        out_shape=(
            jax.ShapeDtypeStruct((NW, 8, 128), jnp.int32),
            jax.ShapeDtypeStruct((NW * CAP, D), BF),
        ),
        in_specs=[VMEM, VMEM],
        out_specs=(VMEM, VMEM),
        scratch_shapes=[DMA((NW,))] * 4,
        compiler_params=params(3, 20),
    )(msg, rows)


VOC = 2 * SHARD
TOK = 16 * T
CH = 512
NCH = VOC // CH
QUART = D // 4


def cols(j):
    return pl.ds(pl.multiple_of(j * T, T), T)


def head_kernel(
    final, rows_t, table, table_other, goal, weights,
    grad_final, head_own, head_other, loss,
    fall, expo, tops, stat, stat_in, coef, coef_in, parts,
    part_a, part_b, whole_a, whole_b, sum_a, sum_b, part_a2, part_b2, whole_a2, whole_b2,
    g_s, g_r, st_s, st_r, co_s, co_r, a_s, b_s, pa_r, pb_r, wa_r, wb_r, a2_s, b2_s, a2_r, b2_r,
):
    me, y, xh, z = place()
    mine = y * 4 + z

    def dev(j):
        return flat(j // 4, xh, lax.rem(j, 4))

    barrier = pltpu.get_barrier_semaphore()

    def greet(k, carry):
        pl.semaphore_signal(
            barrier, inc=1, device_id={"wide": dev(lax.rem(mine + k, 16))}, device_id_type=MESH
        )
        return carry

    lax.fori_loop(1, 16, greet, 0)
    pl.semaphore_wait(barrier, 15)

    sent = []

    def send(src, dst, ssem, rsem, to):
        copy = remote(src, dst, ssem, rsem, wide=to)
        copy.start()
        sent.append(copy)

    def arrived(dst, rsem):
        remote(dst, dst, g_s.at[0], rsem, wide=dev(mine)).wait_recv()

    ring = Ring(
        lambda Y, Z, first, count: fall.at[pl.ds(first, count), cols(Y * 4 + Z)],
        lambda Y, Z, index: g_r.at[Y * 4 + Z, index],
        tuple(QUART * k for k in range(5)),
        g_s,
    )
    ring.own(final, fall.at[:, cols(mine)], 0)
    fall[:, cols(mine)] = final[...]

    def logits(j):
        seen = fall[:, cols(j)]
        goals = goal[j, 0:1, :]
        tip, weight, hit = [], [], jnp.zeros((1, T), F32)
        for c in range(NCH):
            part = jnp.dot(rows_t[c * CH : (c + 1) * CH, :], seen, preferred_element_type=F32)
            top = jnp.max(part, 0, keepdims=True)
            power = jnp.exp(part - top)
            spot = lax.broadcasted_iota(jnp.int32, (CH, T), 0) + c * CH
            hit = hit + jnp.sum(jnp.where(spot == goals, part, 0.0), 0, keepdims=True)
            expo[c * CH : (c + 1) * CH, cols(j)] = power.astype(BF)
            tip.append(top)
            weight.append(jnp.sum(power, 0, keepdims=True))
        top = functools.reduce(jnp.maximum, tip)
        total = sum(w * jnp.exp(t - top) for w, t in zip(weight, tip))
        zero = jnp.zeros((1, T), F32)
        tops[j] = jnp.concatenate(tip + [zero] * (8 - NCH), 0)
        stat[j] = jnp.concatenate([top, total, hit] + [zero] * 5, 0)

    def tell(j):
        return remote(stat.at[j], stat_in.at[mine], st_s.at[j], st_r.at[mine], wide=dev(j))

    def block(dy, dz):
        return turn4(y, dy) * 4 + turn4(z, dz)

    def forward(offsets):
        def one(k, carry):
            j = block(*offsets(k))
            logits(j)
            tell(j).start()
            return carry

        return one

    def odd(k):
        return 1 + 2 * lax.rem(k, 2)

    logits(mine)
    stat_in[mine] = stat[mine]
    ring.near()
    lax.fori_loop(0, 4, forward(lambda k: ((1 - k // 2) * odd(k), (k // 2) * odd(k))), 0)
    ring.far()
    lax.fori_loop(0, 2, forward(lambda k: (2 * (1 - k), 2 * k)), 0)
    ring.cross()
    lax.fori_loop(0, 4, forward(lambda k: (odd(k // 2), odd(k))), 0)
    ring.last()
    lax.fori_loop(
        0,
        4,
        forward(lambda k: (2 * (1 - k // 2) + odd(k) * (k // 2), odd(k) * (1 - k // 2) + 2 * (k // 2))),
        0,
    )
    forward(lambda k: (2, 2))(0, 0)

    def hear(k, carry):
        j = lax.rem(mine + k, 16)
        arrived(stat_in.at[j], st_r.at[j])
        return carry

    lax.fori_loop(1, 16, hear, 0)
    tip, weight, hit = stat_in[:, 0, :], stat_in[:, 1, :], stat_in[:, 2, :]
    top = jnp.max(tip, 0, keepdims=True)
    lse = top + jnp.log(jnp.sum(weight * jnp.exp(tip - top), 0, keepdims=True))
    picked = jnp.sum(hit, 0, keepdims=True)
    share, plain = weights[0:1, :], weights[1:2, :]
    zero = jnp.zeros((1, T), F32)
    coef[...] = jnp.concatenate(
        [lse, share * (1.0 + 2.0 * penalty_weight * lse), share] + [zero] * 5, 0
    )
    loss[...] = jnp.concatenate(
        [plain * (lse - picked + penalty_weight * lse * lse)] + [zero] * 7, 0
    )
    coef_in[mine] = coef[...]

    def spread(k):
        j = lax.rem(mine + k, 16)
        return remote(coef, coef_in.at[mine], co_s.at[k], co_r.at[mine], wide=dev(j))

    def spread_start(k, carry):
        spread(k).start()
        return carry

    lax.fori_loop(1, 16, spread_start, 0)

    up, down = 1, 3
    z_to = {step: flat(y, xh, turn4(z, step)) for step in (up, down)}
    y_to = {step: flat(turn4(y, step), xh, z) for step in (up, down)}

    def piece_a(j, index):
        row = j // 4
        return remote(
            parts.at[j, pl.ds(index * QUART, QUART)], part_a.at[index, row],
            a_s.at[j, index], pa_r.at[index, row], wide=z_to[(up, down)[index]],
        )

    def piece_b(j, index):
        column = lax.rem(j, 4)
        return remote(
            parts.at[j, pl.ds((2 + index) * QUART, QUART)], part_b.at[index, column],
            b_s.at[j, index], pb_r.at[index, column], wide=y_to[(up, down)[index]],
        )

    def half_a(j, index):
        row = j // 4
        return remote(
            parts.at[j, pl.ds(0, 2 * QUART)], whole_a.at[index, row],
            a_s.at[j, 0], wa_r.at[index, row], wide=z_to[(up, down)[index]],
        )

    def half_b(j, index):
        column = lax.rem(j, 4)
        return remote(
            parts.at[j, pl.ds(2 * QUART, 2 * QUART)], whole_b.at[index, column],
            b_s.at[j, 0], wb_r.at[index, column], wide=y_to[(up, down)[index]],
        )

    def offsets(k):
        return lax.rem(2 + k // 4, 4), lax.rem(2 + k, 4)

    def post(k):
        dy, dz = offsets(k)
        j = block(dy, dz)

        @pl.when(dz == 2)
        def _():
            piece_a(j, 0).start()
            piece_a(j, 1).start()

        @pl.when(dy == 2)
        def _():
            piece_b(j, 0).start()
            piece_b(j, 1).start()

        for index, step in enumerate((up, down)):

            @pl.when(dz == step)
            def _():
                row = j // 4
                arrived(part_a.at[index, row], pa_r.at[index, row])
                rows = pl.ds(index * QUART, QUART)
                total = parts[j, rows, :].astype(F32) + part_a[index, row].astype(F32)
                parts[j, rows, :] = total.astype(BF)
                half_a(j, index).start()

            @pl.when(dy == step)
            def _():
                column = lax.rem(j, 4)
                arrived(part_b.at[index, column], pb_r.at[index, column])
                rows = pl.ds((2 + index) * QUART, QUART)
                total = parts[j, rows, :].astype(F32) + part_b[index, column].astype(F32)
                parts[j, rows, :] = total.astype(BF)
                half_b(j, index).start()

    def backward(k, carry):
        j = block(*offsets(k))

        @pl.when(k != 10)
        def _():
            arrived(coef_in.at[j], co_r.at[j])

        lse, soft, pick = coef_in[j, 0:1, :], coef_in[j, 1:2, :], coef_in[j, 2:3, :]
        goals = goal[j, 0:1, :]
        for c in range(NCH):
            scale = soft * jnp.exp(tops[j, c : c + 1, :] - lse)
            power = expo[c * CH : (c + 1) * CH, cols(j)].astype(F32)
            spot = lax.broadcasted_iota(jnp.int32, (CH, T), 0) + c * CH
            grad = power * scale - jnp.where(spot == goals, pick, 0.0)
            expo[c * CH : (c + 1) * CH, cols(j)] = grad.astype(BF)
        product = jnp.dot(table[...], expo[0:SHARD, cols(j)], preferred_element_type=F32)
        product += jnp.dot(table_other[...], expo[SHARD:VOC, cols(j)], preferred_element_type=F32)
        parts[j] = product.astype(BF)

        @pl.when(k > 0)
        def _():
            post(k - 1)

        return carry

    lax.fori_loop(0, 16, backward, 0)
    post(15)

    def head_chunk(c):
        return lax.dot_general(
            fall[...],
            expo[pl.ds(pl.multiple_of(c * 256, 256), 256), :],
            (((1,), (1,)), ((), ())),
            preferred_element_type=F32,
        )

    def other_chunk(c, carry):
        head_other[:, cols(c)] = head_chunk(c + SHARD // 256).astype(BF)
        return carry

    def own_chunk(c, carry):
        head_own[:, cols(c)] = head_chunk(c)
        return carry

    lax.fori_loop(0, SHARD // 256, other_chunk, 0)

    kinds = (
        (whole_a, wa_r, sum_a, part_a2, whole_a2, a2_s, a2_r, y_to, 0),
        (whole_b, wb_r, sum_b, part_b2, whole_b2, b2_s, b2_r, z_to, 2 * QUART),
    )
    for d in (2, 1, 3, 0):
        for kind, (whole, w_r, total, part2, whole2, s2, r2, to, base) in enumerate(kinds):
            at = turn4(y if kind == 0 else z, d)
            j = at * 4 + z if kind == 0 else y * 4 + at
            acc = parts[j, base : base + 2 * QUART, :].astype(F32)
            for index in range(2):
                arrived(whole.at[index, at], w_r.at[index, at])
                acc = acc + whole[index, at].astype(F32)
            if d == 0:
                grad_final[base : base + 2 * QUART, :] = acc
            else:
                total[d - 1] = acc.astype(BF)
            if d == 2:
                for index, step in enumerate((up, down)):
                    piece = total.at[1, pl.ds(index * QUART, QUART)]
                    send(piece, part2.at[index], s2.at[index], r2.at[index], to[step])
    lax.fori_loop(0, SHARD // 512, own_chunk, 0)
    for kind, (whole, w_r, total, part2, whole2, s2, r2, to, base) in enumerate(kinds):
        for index, step in enumerate((up, down)):
            arrived(part2.at[index], r2.at[index])
            rows = pl.ds(index * QUART, QUART)
            added = total[step - 1, rows, :].astype(F32) + part2[index].astype(F32)
            total[step - 1, rows, :] = added.astype(BF)
            send(total.at[step - 1], whole2.at[index], s2.at[2 + index], r2.at[2 + index], to[step])
    lax.fori_loop(SHARD // 512, SHARD // 256, own_chunk, 0)
    for kind, (whole, w_r, total, part2, whole2, s2, r2, to, base) in enumerate(kinds):
        for index in range(2):
            arrived(whole2.at[index], r2.at[2 + index])
        grad_final[base : base + 2 * QUART, :] += whole2[0].astype(F32) + whole2[1].astype(F32)

    def finish(k, carry):
        j = lax.rem(mine + k, 16)
        tell(j).wait_send()
        spread(k).wait_send()
        return carry

    lax.fori_loop(1, 16, finish, 0)
    for copy in sent:
        copy.wait_send()
    ring.finish()

    def finish_pieces(k, carry):
        row, column = block(k, 2), block(2, k)
        piece_a(row, 0).wait_send()
        piece_a(row, 1).wait_send()
        piece_b(column, 0).wait_send()
        piece_b(column, 1).wait_send()
        for index, step in enumerate((up, down)):
            half_a(block(k, step), index).wait_send()
            half_b(block(step, k), index).wait_send()
        return carry

    lax.fori_loop(0, 4, finish_pieces, 0)


def head(final, rows_t, table, table_other, goal, weights):
    return pl.pallas_call(
        head_kernel,
        name="head",
        out_shape=(
            jax.ShapeDtypeStruct((D, T), F32),
            jax.ShapeDtypeStruct((D, SHARD), F32),
            jax.ShapeDtypeStruct((D, SHARD), BF),
            jax.ShapeDtypeStruct((8, T), F32),
        ),
        in_specs=[VMEM] * 6,
        out_specs=(VMEM,) * 4,
        scratch_shapes=[
            pltpu.VMEM((D, TOK), BF),
            pltpu.VMEM((VOC, TOK), BF),
            pltpu.VMEM((16, 8, T), F32),
            pltpu.VMEM((16, 8, T), F32),
            pltpu.VMEM((16, 8, T), F32),
            pltpu.VMEM((8, T), F32),
            pltpu.VMEM((16, 8, T), F32),
            pltpu.VMEM((16, D, T), BF),
            pltpu.VMEM((2, 4, QUART, T), BF),
            pltpu.VMEM((2, 4, QUART, T), BF),
            pltpu.VMEM((2, 4, 2 * QUART, T), BF),
            pltpu.VMEM((2, 4, 2 * QUART, T), BF),
            pltpu.VMEM((3, 2 * QUART, T), BF),
            pltpu.VMEM((3, 2 * QUART, T), BF),
            pltpu.VMEM((2, QUART, T), BF),
            pltpu.VMEM((2, QUART, T), BF),
            pltpu.VMEM((2, 2 * QUART, T), BF),
            pltpu.VMEM((2, 2 * QUART, T), BF),
            DMA((RING_SENDS,)),
            DMA((16, 4)),
            DMA((16,)),
            DMA((16,)),
            DMA((16,)),
            DMA((16,)),
            DMA((16, 2)),
            DMA((16, 2)),
            DMA((2, 4)),
            DMA((2, 4)),
            DMA((2, 4)),
            DMA((2, 4)),
            DMA((4,)),
            DMA((4,)),
            DMA((4,)),
            DMA((4,)),
        ],
        compiler_params=params(4, 61),
        cost_estimate=pl.CostEstimate(
            flops=6 * VOC * TOK * D, bytes_accessed=2 * 10**7, transcendentals=VOC * TOK
        ),
    )(final, rows_t, table, table_other, goal, weights)


class Reduce:
    def __init__(self, parts, base, sizes, along_z, refs):
        (
            self.first, part_a, part_b, self.whole1, self.second, next_a, next_b, self.whole2,
            self.third, self.stop, self.third_in, self.s, self.r,
        ) = refs
        self.part1, self.part2 = (part_a, part_b), (next_a, next_b)
        self.parts, self.base, self.sizes, self.along_z = parts, base, sizes, along_z
        self.rows = (pl.ds(0, sizes[0]), pl.ds(sizes[0], sizes[1]), pl.ds(0, sum(sizes)))
        self.me, self.y, self.xh, self.z = place()
        self.sent = []

    def send(self, src, dst, at, **to):
        copy = remote(src, dst, self.s.at[at], self.r.at[at], **to)
        copy.start()
        self.sent.append(copy)

    def wait(self, dst, at):
        remote(dst, dst, self.s.at[at], self.r.at[at], wide=self.me).wait_recv()

    def item1(self, step, which):
        rows = pl.ds(self.base + self.rows[which].start, self.rows[which].size)
        if self.along_z:
            return (slice(None), turn4(self.z, step), slice(None), rows)
        return (turn4(self.y, step), slice(None), slice(None), rows)

    def item2(self, step, which):
        return (turn4(self.y if self.along_z else self.z, step), slice(None), self.rows[which])

    def to(self, stage, step):
        if self.along_z == (stage == 1):
            return flat(self.y, self.xh, turn4(self.z, step))
        return flat(turn4(self.y, step), self.xh, self.z)

    def split(self, stage, ref, item, part, base):
        for index, step in enumerate((1, 3)):
            self.send(ref.at[item(2, index)], part[index], base + index, wide=self.to(stage, step))

    def join(self, stage, ref, item, part, whole, base):
        for index, step in enumerate((1, 3)):
            self.wait(part[index], base + index)
            at = item(step, index)
            ref[at] = (ref[at].astype(F32) + part[index][...].astype(F32)).astype(BF)
            self.send(ref.at[item(step, 2)], whole.at[index], base + 2 + index, wide=self.to(stage, step))

    def add(self, ref, item, whole, base):
        acc = ref[item(0, 2)].astype(F32)
        for index in range(2):
            self.wait(whole.at[index], base + 2 + index)
            acc = acc + whole[index].astype(F32)
        return acc

    def one(self):
        self.split(1, self.parts, self.item1, self.part1, 0)

    def two(self):
        self.join(1, self.parts, self.item1, self.part1, self.whole1, 0)

    def three(self):
        self.first[...] = self.add(self.parts, self.item1, self.whole1, 0).astype(BF)
        self.split(2, self.first, self.item2, self.part2, 4)

    def four(self):
        self.join(2, self.first, self.item2, self.part2, self.whole2, 4)

    def five(self):
        self.second[...] = self.add(self.first, self.item2, self.whole2, 4)
        self.third[...] = self.second[1 - self.xh].astype(BF)
        self.send(self.third, self.stop, 8, **beside(1 if self.along_z else 3))

    def six(self):
        self.wait(self.stop, 8)
        self.send(self.stop, self.third_in, 9, **beside(1 if self.along_z else 3))

    def total(self):
        self.wait(self.third_in, 9)
        return self.second[self.xh] + self.third_in[...].astype(F32)

    def finish(self):
        for copy in self.sent:
            copy.wait_send()


STREAMS = ((0, (48, 32), True), (80, (48, 32), False), (160, (16, 16), True), (192, (16, 16), False))


def reduce_scratch():
    shapes = []
    for _, sizes, _ in STREAMS:
        half = sum(sizes)
        shapes += [
            pltpu.VMEM((4, 2, half, D), BF),
            pltpu.VMEM((4, 2, sizes[0], D), BF),
            pltpu.VMEM((4, 2, sizes[1], D), BF),
            pltpu.VMEM((2, 4, 2, half, D), BF),
            pltpu.VMEM((2, half, D), F32),
            pltpu.VMEM((2, sizes[0], D), BF),
            pltpu.VMEM((2, sizes[1], D), BF),
            pltpu.VMEM((2, 2, half, D), BF),
            pltpu.VMEM((half, D), BF),
            pltpu.VMEM((half, D), BF),
            pltpu.VMEM((half, D), BF),
            DMA((10,)),
            DMA((10,)),
        ]
    return shapes


def back_kernel(
    grad_final, h0, n1, q, k, v, lse, att, h1, n2, gate_up, inner, h2,
    packed, gains, rot, tok, slot_row, loss, head_other, lay_attn, lay_out, lay_down,
    summed, rows_in, head_in, extra_sum, grad_embedded,
    ffn, down, attn, sem, parts, rows, grad_up, grad_mixed, spread, extra, extra_in, stops,
    row_s, row_r, extra_s, extra_r, swap_s, swap_r, *reducers,
):
    me, y, xh, z = place()
    loads = load_trunk(packed, ffn, down, attn, sem)
    greet_wide(me, sides=True)
    halves = (pl.ds(0, D // 2), pl.ds(D // 2, D // 2))
    trade = Relay(
        [head_other.at[half] for half in halves],
        [stops.at[i] for i in range(2)],
        [head_in.at[half] for half in halves],
        swap_s,
        swap_r,
    )
    trade.start()
    streams = [
        Reduce(parts, base, sizes, along, reducers[13 * i : 13 * i + 13])
        for i, (base, sizes, along) in enumerate(STREAMS)
    ]
    early, late = streams[:2], streams[2:]
    columns = gain_columns(gains)

    grad_h2, gain3 = rms_back(h2[...], columns[:, 2:3], grad_final[...])
    spread[...] = mm(lay_down[...], grad_h2.astype(BF)).astype(BF)
    chunk = lax.broadcasted_iota(jnp.int32, (NW * 64, T), 0) & 63
    zero = jnp.zeros((NW * 64, T), BF)
    wide = jnp.concatenate(
        [
            jnp.where((chunk >= 18 * j) & (chunk < 18 * (j + 1)), spread[...].astype(F32), 0.0).astype(BF)
            for j in range(3)
        ],
        1,
    )
    inners = jnp.concatenate([inner[j * 512 : (j + 1) * 512, :] for j in range(3)], 1)
    grad_down = mm_nt(wide, inners).astype(BF).reshape(4, 4, 2, 64, 512)
    parts[:, :, :, DOWN_AT:ATTN_AT, 0:512] = grad_down
    parts[:, :, :, DOWN_AT:ATTN_AT, 512:D] = jnp.zeros((4, 4, 2, 64, D - 512), BF)
    loads[2].wait()
    grad_inner = mm_tn(down[...].reshape(NW * 64, 512), wide)
    for i in range(NW // 2):
        w = ORDER[i]
        gate = gate_up[i * 96 : (i + 1) * 96, :]
        up = gate_up[FF + i * 96 : FF + (i + 1) * 96, :]
        pieces = []
        for at in range(w * 96, w * 96 + 96, 32):
            j, r = at // 512, at % 512
            pieces.append(grad_inner[r : r + 32, j * T : (j + 1) * T])
        grad = jnp.concatenate(pieces, 0)
        sigmoid = 1.0 / (1.0 + jnp.exp(-gate))
        slope = sigmoid * (1.0 + gate * (1.0 - sigmoid))
        grad_up[i * 96 : (i + 1) * 96, :] = (grad * up * slope).astype(BF)
        grad_up[FF + i * 96 : FF + (i + 1) * 96, :] = (grad * (gate * sigmoid)).astype(BF)
    parts[:, :, :, FFN_AT:DOWN_AT, :] = mm_nt(grad_up[...], n2[...]).astype(BF).reshape(4, 4, 2, 96, D)
    for stream in early:
        stream.one()
    loads[1].wait()
    grad_normed = turned(mm_tn(grad_up[...], ffn[...].reshape(NW * 96, D)))
    part, gain2 = rms_back(h1[...], columns[:, 1:2], grad_normed)
    grad_h1 = grad_h2 + part
    out_rows = mm(lay_out[...], grad_h1.astype(BF)).astype(BF)
    loads[0].wait()
    rows48 = attn[...].reshape(NW * 48, D)
    grad_att = turned(mm_tn(out_rows, rows48)).astype(BF)
    for stream in early:
        stream.two()

    allowed = mask_of(tok)
    group = H // KVH
    for kv in range(KVH):
        keys = k[kv * HD : (kv + 1) * HD, :]
        values = v[kv * HD : (kv + 1) * HD, :]
        grad_k, grad_v = jnp.zeros((HD, T), F32), jnp.zeros((HD, T), F32)
        for h in range(kv * group, (kv + 1) * group):
            query = q[h * HD : (h + 1) * HD, :]
            grad_out = grad_att[h * HD : (h + 1) * HD, :]
            scores = mm_tn(keys, query) * HD ** (-0.5)
            scores = jnp.where(allowed, scores, masked_score)
            soft = jnp.exp(scores - lse[h : h + 1, :])
            grad_probs = mm_tn(values, grad_out)
            mean = jnp.sum(soft * grad_probs, 0, keepdims=True)
            grad_scores = (soft * (grad_probs - mean)).astype(BF)
            grad_q = mm(keys, grad_scores) * HD ** (-0.5)
            grad_mixed[h * HD : (h + 1) * HD, :] = unrotated(grad_q, rot[...]).astype(BF)
            grad_k = grad_k + mm_nt(query, grad_scores) * HD ** (-0.5)
            grad_v = grad_v + mm_nt(grad_out, soft.astype(BF))
        at = D + kv * HD
        grad_mixed[at : at + HD, :] = unrotated(grad_k, rot[...]).astype(BF)
        at = D + (KVH + kv) * HD
        grad_mixed[at : at + HD, :] = grad_v.astype(BF)
    for stream in early:
        stream.three()
    attn_rows = mm(lay_attn[...], grad_mixed[...]).astype(BF)
    both = jnp.concatenate([attn_rows, out_rows], 1)
    seen = jnp.concatenate([n1[...], att[...]], 1)
    parts[:, :, :, ATTN_AT:PACKED, :] = mm_nt(both, seen).astype(BF).reshape(4, 4, 2, 48, D)
    parts[:, :, :, PACKED:SUMMED, :] = jnp.zeros((4, 4, 2, SUMMED - PACKED, D), BF)
    for stream in late:
        stream.one()
    grad_normed = turned(mm_tn(attn_rows, rows48))
    part, gain1 = rms_back(h0[...], columns[:, 0:1], grad_normed)
    grad_h0 = (grad_h1 + part).astype(BF)
    grad_embedded[...] = grad_h0
    slot = lax.broadcasted_iota(jnp.int32, (NW * CAP, T), 0)
    picks = jnp.where(slot == slot_row[0:1, :], 1.0, 0.0).astype(BF)
    rows[...] = mm_nt(picks, grad_h0).astype(BF)
    give = Scatter(lambda p: rows.at[slots(p)], lambda p: rows_in.at[slots(p)], row_s, row_r, me)
    give.start()
    for stream in early:
        stream.four()
    trade.forward()
    lane = lax.broadcasted_iota(jnp.int32, (D, 128), 1)
    table = jnp.where(lane == 0, gain1, jnp.where(lane == 1, gain2, jnp.where(lane == 2, gain3, 0.0)))
    lost = jnp.sum(loss[0:1, :], 1, keepdims=True)
    table = table.T[0:8, :]
    extra[...] = jnp.where(lax.broadcasted_iota(jnp.int32, (8, D), 0) == 3, lost, table)
    share = Scatter(lambda p: extra, lambda p: extra_in.at[p], extra_s, extra_r, me)
    share.start()
    rows_in[slots(me), :] = rows[slots(me), :]
    extra_in[me] = extra[...]
    for stream in late:
        stream.two()
    for stream in early:
        stream.five()
    for stream in late:
        stream.three()
    for stream in late:
        stream.four()
    for stream in early:
        stream.six()
    for stream in late:
        stream.five()
    share.wait_recv()
    total = extra_in[0]
    for w in range(1, NW):
        total = total + extra_in[w]
    extra_sum[...] = total
    for stream in late:
        stream.six()
    for stream in streams:
        summed[stream.base : stream.base + sum(stream.sizes), :] = stream.total()
    give.wait_recv()
    trade.wait()
    for stream in streams:
        stream.finish()
    give.wait_send()
    share.wait_send()
    trade.finish()


def back(grad_final, kept, packed, gains, rot, tok, slot_row, loss, head_other):
    lays = [
        jnp.asarray(spread_rows(30, 48, 0), BF),
        jnp.asarray(spread_rows(18, 48, 30), BF),
        jnp.asarray(spread_rows(18, 64, 0, 3), BF),
    ]
    return pl.pallas_call(
        back_kernel,
        name="back",
        out_shape=(
            jax.ShapeDtypeStruct((SUMMED, D), F32),
            jax.ShapeDtypeStruct((NW * CAP, D), BF),
            jax.ShapeDtypeStruct((D, SHARD), BF),
            jax.ShapeDtypeStruct((8, D), F32),
            jax.ShapeDtypeStruct((D, T), BF),
        ),
        in_specs=[VMEM] * 13 + [ANY] + [VMEM] * 5 + [ANY] + [VMEM] * 3,
        out_specs=(VMEM, VMEM, ANY, VMEM, VMEM),
        scratch_shapes=TRUNK_SCRATCH
        + [
            pltpu.VMEM((4, 4, 2, SUMMED, D), BF),
            pltpu.VMEM((NW * CAP, D), BF),
            pltpu.VMEM((2 * FF, T), BF),
            pltpu.VMEM((QKV, T), BF),
            pltpu.VMEM((NW * 64, T), BF),
            pltpu.VMEM((8, D), F32),
            pltpu.VMEM((NW, 8, D), F32),
            pltpu.VMEM((2, D // 2, SHARD), BF),
        ]
        + [DMA((NW,))] * 4
        + [DMA((4,)), DMA((4,))]
        + reduce_scratch(),
        compiler_params=params(5, 60),
        cost_estimate=pl.CostEstimate(flops=10**10, bytes_accessed=3 * 10**7, transcendentals=10**6),
    )(grad_final, *kept, packed, gains, rot, tok, slot_row, loss, head_other, *lays)


def norm_kernel(value, out, landing, s, r):
    me = lax.axis_index("wide")
    greet_wide(me)
    share = Scatter(lambda p: value, lambda p: landing.at[p], s, r, me)
    share.start()
    landing[me] = value[...]
    share.wait_recv()
    total = landing[0]
    for w in range(1, NW):
        total = total + landing[w]
    out[...] = total
    share.wait_send()


def norm_sum(value):
    return pl.pallas_call(
        norm_kernel,
        name="norm_sum",
        out_shape=jax.ShapeDtypeStruct((8, 128), F32),
        in_specs=[VMEM],
        out_specs=VMEM,
        scratch_shapes=[pltpu.VMEM((NW, 8, 128), F32), DMA((NW,)), DMA((NW,))],
        compiler_params=params(6, 16),
    )(value)


GRP_PARTS = ((D, SHARD), (FA_ROWS, D), (WP_ROWS, 128))


def group_kernel(*refs):
    values, gains = refs[0:3], refs[3]
    outs, gains_out = refs[4:7], refs[7]
    scratch = refs[8:]
    grp = lax.axis_index("grp")
    core, x = lax.rem(grp, 2), grp // 2
    near, far = x * 2 + 1 - core, (1 - x) * 2 + core
    barrier = pltpu.get_barrier_semaphore()
    for k in range(1, NG):
        pl.semaphore_signal(
            barrier, inc=1, device_id={"grp": lax.rem(grp + k, NG)}, device_id_type=MESH
        )
    pl.semaphore_wait(barrier, NG - 1)
    gains_in, gains_s, gains_r = scratch[15:18]
    told = []
    for k in range(1, NG):
        to = lax.rem(grp + k, NG)
        told.append(remote(gains, gains_in.at[grp], gains_s.at[k], gains_r.at[grp], grp=to))
        told[-1].start()
    gains_in[grp] = gains[...]
    sent = []
    for i, value in enumerate(values):
        half = value.shape[0] // 2
        one, one_in, two, two_in, sems = scratch[5 * i : 5 * i + 5]
        away = pl.ds(pl.multiple_of((1 - core) * half, 16), half)
        one[...] = value[away, :].astype(BF)
        copy = remote(one, one_in, sems.at[0], sems.at[1], grp=near)
        copy.start()
        sent.append(copy)
    for i, value in enumerate(values):
        half = value.shape[0] // 2
        one, one_in, two, two_in, sems = scratch[5 * i : 5 * i + 5]
        kept = pl.ds(pl.multiple_of(core * half, 16), half)
        sent[i].wait_recv()
        two[...] = (value[kept, :] + one_in[...].astype(F32)).astype(BF)
        copy = remote(two, two_in, sems.at[2], sems.at[3], grp=far)
        copy.start()
        sent.append(copy)
    for i, value in enumerate(values):
        half = value.shape[0] // 2
        one, one_in, two, two_in, sems = scratch[5 * i : 5 * i + 5]
        kept = pl.ds(pl.multiple_of(core * half, 16), half)
        sent[3 + i].wait_recv()
        outs[i][kept, :] = two[...].astype(F32) + two_in[...].astype(F32)
        piece = outs[i].at[kept]
        copy = remote(piece, piece, sems.at[4], sems.at[5], grp=near)
        copy.start()
        sent.append(copy)
    for k in range(1, NG):
        other = lax.rem(grp + k, NG)
        remote(gains, gains_in.at[other], gains_s.at[k], gains_r.at[other], grp=other).wait_recv()
    gains_out[...] = (gains_in[0] + gains_in[1]) + (gains_in[2] + gains_in[3])
    for i, value in enumerate(values):
        half = value.shape[0] // 2
        sems = scratch[5 * i + 4]
        away = outs[i].at[pl.ds(pl.multiple_of((1 - core) * half, 16), half)]
        remote(away, away, sems.at[4], sems.at[5], grp=near).wait_recv()
    for copy in sent + told:
        copy.wait_send()


def group_sum(*values):
    scratch = []
    for rows, lanes in GRP_PARTS:
        scratch += [pltpu.VMEM((rows // 2, lanes), BF)] * 4 + [DMA((6,))]
    shapes = GRP_PARTS + ((8, 640),)
    return pl.pallas_call(
        group_kernel,
        name="group_sum",
        out_shape=tuple(jax.ShapeDtypeStruct(shape, F32) for shape in shapes),
        in_specs=[VMEM] * 4,
        out_specs=(VMEM,) * 4,
        scratch_shapes=scratch + [pltpu.VMEM((NG, 8, 640), F32), DMA((NG,)), DMA((NG,))],
        compiler_params=params(7, 40),
        cost_estimate=pl.CostEstimate(flops=10**7, bytes_accessed=2 * 10**7, transcendentals=0),
    )(*values)


def dot(spec, a, b):
    return jnp.einsum(spec, a, b, preferred_element_type=F32)


def adam_update(weight, grad, first, second, rate, decay):
    first = beta_one * first + (1.0 - beta_one) * grad
    second = beta_two * second + (1.0 - beta_two) * grad * grad
    ratio = first / (1.0 - beta_one**STEP) / (jnp.sqrt(second / (1.0 - beta_two**STEP)) + adam_eps)
    return (weight - rate * (ratio + decay * weight), first, second)


def pack_fa(attn, ffn):
    pad = [(0, 0)] * (attn.ndim - 2) + [(0, FA_ROWS - 126), (0, 0)]
    return jnp.pad(jnp.concatenate([ffn, attn], -2), pad)


def pack_wp(proj):
    lead = proj.shape[:-2]
    pad = [(0, 0)] * len(lead) + [(0, WP_ROWS - 297), (0, 0)]
    return jnp.pad(proj.reshape(lead + (297, 128)), pad)


def on_device(
    token_ids,
    targets,
    segment_ids,
    row_counts,
    embed_table_master,
    embed_table_first,
    embed_table_second,
    embed_table_anchor,
    embed_table_momentum,
    attn_in_master,
    attn_in_first,
    attn_in_second,
    attn_in_anchor,
    attn_in_momentum,
    ffn_in_master,
    ffn_in_first,
    ffn_in_second,
    ffn_in_anchor,
    ffn_in_momentum,
    proj_out_master,
    proj_out_first,
    proj_out_second,
    proj_out_anchor,
    proj_out_momentum,
    norm_gains_master,
    norm_gains_first,
    norm_gains_second,
    norm_gains_anchor,
    norm_gains_momentum,
):
    ids = token_ids[0]
    gains = norm_gains_master[0]
    table = embed_table_master[0].T.astype(BF)
    weight = jnp.sum(row_counts[0, 0] * jnp.arange(1, 4))
    proj = proj_out_master[0].T
    packed = jnp.concatenate(
        [
            ffn_in_master[0].T,
            jnp.pad(proj[:, D:].reshape(18, 3, 512).transpose(1, 0, 2).reshape(54, 512), ((0, 10), (0, D - 512))),
            attn_in_master[0].T,
            proj[:, :D],
        ],
        0,
    ).astype(BF)
    tok = jnp.concatenate(
        [
            token_ids, targets, segment_ids, jnp.broadcast_to(weight, (1, T)), jnp.zeros((4, T), jnp.int32),
        ],
        0,
    )
    got, rows, most_all, table_other, rows_t, packed_all, picks, slot_row, hot, goals, weights = front(
        tok, table, packed
    )
    turns = (jnp.max(most_all) + CAP - 1) // CAP

    def asked_in(turn):
        ids_now = jnp.where(turn > 0, ids, 0)
        owner = ids_now // SHARD
        same = ids_now[:, None] == ids_now[None, :]
        before = jnp.arange(T)[None, :] < jnp.arange(T)[:, None]
        first_seen = ~jnp.any(same & before, 1)
        smaller = (owner[None, :] == owner[:, None]) & (ids_now[None, :] < ids_now[:, None])
        rank = jnp.sum(first_seen[None, :] & smaller, 1, dtype=jnp.int32) - turn * CAP
        slot = jnp.where((rank >= 0) & (rank < CAP), owner * CAP + rank, -1)
        chosen = jnp.arange(NW * CAP)[:, None] == slot[None, :]
        asked = jnp.max(jnp.where(chosen, (ids_now - owner * SHARD)[None, :], -1), 1).reshape(NW, 1, CAP)
        asked = jnp.pad(asked, ((0, 0), (0, 0), (0, 128 - CAP)), constant_values=-1)
        return jnp.pad(asked, ((0, 0), (0, 7), (0, 0))), chosen.astype(BF)

    def more_tokens(carry):
        turn, hidden = carry
        message, chosen = asked_in(turn)
        return turn + 1, hidden + dot("sd,st->td", more_rows(message, table), chosen)

    hidden0 = lax.while_loop(
        lambda carry: carry[0] < turns, more_tokens, (jnp.int32(1), dot("ts,sd->td", picks, rows))
    )[1]

    gains8 = jnp.pad(gains, ((0, 5), (0, 0)))
    rot = jnp.asarray(rope())
    final, *kept = forward(hidden0, packed_all, gains8, rot, tok)
    total = weights[2, 0]
    grad_final, head_own, head_other, loss = head(final, rows_t, table, table_other, goals, weights)
    summed, rows_in, head_in, extra_sum, grad_embedded = back(
        grad_final, kept, packed_all, gains8, rot, tok, slot_row, loss, head_other
    )

    def more_table(carry):
        turn, grad = carry
        message, chosen = asked_in(turn)
        mine = dot("st,dt->sd", chosen, grad_embedded).astype(BF)
        got_now, rows_now = more_grads(message, mine)
        asked = got_now[:, 0, :CAP].reshape(NW * CAP)
        hot_now = (asked[:, None] == jnp.arange(SHARD)[None, :]).astype(BF)
        return turn + 1, grad + dot("sd,sv->dv", rows_now, hot_now)

    table_grad = lax.while_loop(
        lambda carry: carry[0] < turns,
        more_table,
        (jnp.int32(1), head_own + head_in.astype(F32) + dot("sd,sv->dv", rows_in, hot)),
    )[1]

    sum_gains = extra_sum[:3, :D]
    loss_total = extra_sum[3, 0]
    squares = jnp.sum(table_grad * table_grad) + jnp.sum(summed * summed)
    squares = norm_sum(jnp.broadcast_to(squares, (8, 128)))[0, 0]
    norm = jnp.sqrt(squares + jnp.sum(sum_gains * sum_gains))
    factor = jnp.minimum(1.0, clip_norm / norm)

    sum_ffn, sum_attn = summed[FFN_AT:DOWN_AT], summed[ATTN_AT : ATTN_AT + 30]
    sum_down = summed[DOWN_AT : DOWN_AT + 54, :512].reshape(3, 18, 512).transpose(1, 0, 2).reshape(18, FF)
    sum_proj = jnp.concatenate([summed[ATTN_AT + 30 : PACKED], sum_down], 1)
    kinds = (
        (
            embed_table_master[0].T,
            table_grad,
            embed_table_first[0].T,
            embed_table_second[0].T,
            embed_table_anchor.T,
            embed_table_momentum.T,
            inner_rate,
            weight_decay,
        ),
        (
            attn_in_master[0].T,
            sum_attn,
            attn_in_first[0].T,
            attn_in_second[0].T,
            attn_in_anchor.T,
            attn_in_momentum.T,
            inner_rate,
            weight_decay,
        ),
        (
            ffn_in_master[0].T,
            sum_ffn,
            ffn_in_first[0].T,
            ffn_in_second[0].T,
            ffn_in_anchor.T,
            ffn_in_momentum.T,
            inner_rate,
            weight_decay,
        ),
        (
            proj_out_master[0].T,
            sum_proj,
            proj_out_first[0].T,
            proj_out_second[0].T,
            proj_out_anchor.T,
            proj_out_momentum.T,
            inner_rate,
            weight_decay,
        ),
        (
            gains,
            sum_gains,
            norm_gains_first[0],
            norm_gains_second[0],
            norm_gains_anchor,
            norm_gains_momentum,
            gain_rate,
            0.0,
        ),
    )
    updated = [
        adam_update(kind[0], kind[1] * factor, kind[2], kind[3], kind[6], kind[7]) for kind in kinds
    ]
    diffs = [kinds[index][4] - updated[index][0] for index in range(5)]
    summed = group_sum(
        diffs[0],
        pack_fa(diffs[1], diffs[2]),
        pack_wp(diffs[3]),
        jnp.zeros((8, 640), F32).at[:3, :D].set(diffs[4]),
    )
    sums = (
        summed[0],
        summed[1][96:126],
        summed[1][:96],
        summed[2][:297].reshape(18, D + FF),
        summed[3][:3, :D],
    )
    results = [loss_total.reshape(1), total.reshape(1), norm.reshape(1)]
    for index in range(5):
        average = sums[index] / NG
        outer = outer_momentum * kinds[index][5] + average
        weight = kinds[index][4] - outer_rate * (average + outer_momentum * outer)
        values = [average, outer, weight, updated[index][1], updated[index][2]]
        if index < 4:
            values = [value.T for value in values]
        results += values[:3] + [values[3][None], values[4][None]]
    return tuple(results)


def solution(mesh):
    in_specs = (
        P("grp", "wide"),
        P("grp", "wide"),
        P("grp", "wide"),
        P("grp", "wide", None),
        P("grp", "wide", None),
        P("grp", "wide", None),
        P("grp", "wide", None),
        P("wide", None),
        P("wide", None),
        P("grp", None, "wide"),
        P("grp", None, "wide"),
        P("grp", None, "wide"),
        P(None, "wide"),
        P(None, "wide"),
        P("grp", None, "wide"),
        P("grp", None, "wide"),
        P("grp", None, "wide"),
        P(None, "wide"),
        P(None, "wide"),
        P("grp", None, "wide"),
        P("grp", None, "wide"),
        P("grp", None, "wide"),
        P(None, "wide"),
        P(None, "wide"),
        P("grp", None, None),
        P("grp", None, None),
        P("grp", None, None),
        P(),
        P(),
    )
    out_specs = (
        P("grp"),
        P("grp"),
        P("grp"),
        P("wide", None),
        P("wide", None),
        P("wide", None),
        P("grp", "wide", None),
        P("grp", "wide", None),
        P(None, "wide"),
        P(None, "wide"),
        P(None, "wide"),
        P("grp", None, "wide"),
        P("grp", None, "wide"),
        P(None, "wide"),
        P(None, "wide"),
        P(None, "wide"),
        P("grp", None, "wide"),
        P("grp", None, "wide"),
        P(None, "wide"),
        P(None, "wide"),
        P(None, "wide"),
        P("grp", None, "wide"),
        P("grp", None, "wide"),
        P(),
        P(),
        P(),
        P("grp", None, None),
        P("grp", None, None),
    )
    return jax.shard_map(
        on_device, mesh=mesh, in_specs=in_specs, out_specs=out_specs, check_vma=False
    )
```

```python
import functools

import jax
import jax.numpy as jnp
import numpy as np
from jax import lax
from jax.experimental import pallas as pl
from jax.experimental.pallas import tpu as pltpu
from jax.sharding import PartitionSpec as P

D = 576
H = 9
KVH = 3
HD = 64
FF = 1536
QKV = 960
STEP = 8
T = 256
SHARD = 1536
NW = 32
NG = 4
CAP = 32
FFN_AT, DOWN_AT, ATTN_AT, PACKED = 0, 96, 160, 208
SUMMED = 224

beta_one = 0.9
beta_two = 0.999
adam_eps = 1e-08
weight_decay = 0.1
inner_rate = 0.02
gain_rate = 0.2
clip_norm = 0.01
penalty_weight = 0.005
outer_rate = 0.7
outer_momentum = 0.9
rope_base = 100000.0
norm_eps = 1e-05
masked_score = -1e30

BF = jnp.bfloat16
F32 = jnp.float32
MESH = pl.DeviceIdType.MESH
VMEM = pl.BlockSpec(memory_space=pltpu.VMEM)
ANY = pl.BlockSpec(memory_space=pl.ANY)
DMA = pltpu.SemaphoreType.DMA
MIB = 1 << 20


def params(collective, mib):
    return pltpu.CompilerParams(
        collective_id=collective, has_side_effects=True, vmem_limit_bytes=mib * MIB
    )


def place():
    me = lax.axis_index("wide")
    return me, me // 8, lax.rem(me // 4, 2), lax.rem(me, 4)


def flat(y, xh, z):
    return y * 8 + xh * 4 + z


def turn4(at, by):
    return lax.rem(at + by, 4)


def remote(src, dst, ssem, rsem, **device):
    return pltpu.make_async_remote_copy(
        src_ref=src,
        dst_ref=dst,
        send_sem=ssem,
        recv_sem=rsem,
        device_id=device,
        device_id_type=MESH,
    )


def greet_wide(me, grp=None, sides=False, meanwhile=None):
    barrier = pltpu.get_barrier_semaphore()

    def one(k, carry):
        pl.semaphore_signal(
            barrier, inc=1, device_id={"wide": lax.rem(me + k, NW)}, device_id_type=MESH
        )
        return carry

    lax.fori_loop(1, NW, one, 0)
    count = NW - 1
    if grp is not None:
        for k in range(1, NG):
            pl.semaphore_signal(
                barrier, inc=1, device_id={"grp": lax.rem(grp + k, NG)}, device_id_type=MESH
            )
        count += NG - 1
    if sides:
        for step in (1, 3):
            pl.semaphore_signal(barrier, inc=1, device_id=beside(step), device_id_type=MESH)
        count += 2
    if meanwhile is not None:
        meanwhile()
    pl.semaphore_wait(barrier, count)


def near_peers(me, y, xh, z):
    peers = [flat(y, xh, turn4(z, k)) for k in (1, 2, 3)] + [flat(turn4(y, k), xh, z) for k in (1, 2, 3)]
    return peers + [flat(y, 1 - xh, z)]


class Tree:
    def __init__(self, hold, land_z, land_y, land_x, ssem, rsem):
        self.hold, self.lands = hold, (land_z, land_y, land_x)
        self.ssem, self.rsem = ssem, rsem
        me, self.y, self.xh, self.z = place()
        self.sent = []

    def send(self, stage):
        y, xh, z = self.y, self.xh, self.z
        at = (z, y, xh)[stage]
        land, src = self.lands[stage], self.hold.at[stage]
        for k in range(1, 2 if stage == 2 else 4):
            if stage == 0:
                to = flat(y, xh, turn4(z, k))
            elif stage == 1:
                to = flat(turn4(y, k), xh, z)
            else:
                to = flat(y, 1 - xh, z)
            copy = remote(src, land.at[at], self.ssem.at[stage, k], self.rsem.at[stage, at], wide=to)
            copy.start()
            self.sent.append(copy)
        land[at] = self.hold[stage]

    def start(self, value):
        self.hold[0] = value
        self.send(0)

    def collect(self, stage):
        at = (self.z, self.y, self.xh)[stage]
        land = self.lands[stage]
        size = 2 if stage == 2 else 4
        for k in range(1, size):
            other = lax.rem(at + k, size)
            remote(
                land.at[other], land.at[other], self.ssem.at[stage, k], self.rsem.at[stage, other],
                wide=flat(self.y, self.xh, self.z),
            ).wait_recv()
        total = land[0]
        for k in range(1, size):
            total = total + land[k]
        return total

    def next(self, stage):
        self.hold[stage + 1] = self.collect(stage)
        self.send(stage + 1)

    def finish(self):
        for copy in self.sent:
            copy.wait_send()


def tree_scratch(lanes):
    return [
        pltpu.VMEM((3, 8, lanes), F32),
        pltpu.VMEM((4, 8, lanes), F32),
        pltpu.VMEM((4, 8, lanes), F32),
        pltpu.VMEM((2, 8, lanes), F32),
        DMA((3, 4)),
        DMA((3, 4)),
    ]


class Scatter:
    def __init__(self, src_at, dst_at, ssem, rsem, me):
        self.src_at, self.dst_at, self.ssem, self.rsem, self.me = src_at, dst_at, ssem, rsem, me

    def copy(self, k):
        peer = lax.rem(self.me + k, NW)
        return remote(
            self.src_at(peer), self.dst_at(self.me), self.ssem.at[k], self.rsem.at[self.me], wide=peer
        )

    def start(self):
        def one(k, carry):
            self.copy(k).start()
            return carry

        lax.fori_loop(1, NW, one, 0)

    def wait_recv(self):
        def one(k, carry):
            peer = lax.rem(self.me + k, NW)
            remote(
                self.src_at(peer), self.dst_at(peer), self.ssem.at[k], self.rsem.at[peer], wide=peer
            ).wait_recv()
            return carry

        lax.fori_loop(1, NW, one, 0)

    def wait_send(self):
        def one(k, carry):
            self.copy(k).wait_send()
            return carry

        lax.fori_loop(1, NW, one, 0)


class Ring:
    def __init__(self, view, sem, bounds, ssem):
        self.view, self.sem, self.bounds = view, sem, bounds
        self.ssem, self.used, self.sent = ssem, 0, []
        self.me, self.y, self.xh, self.z = place()

    def send(self, src, dst, rsem, to):
        copy = remote(src, dst, self.ssem.at[self.used], rsem, wide=flat(to[0], self.xh, to[1]))
        self.used += 1
        copy.start()
        self.sent.append(copy)

    def piece(self, y, z, first, count):
        return self.view(y, z, self.bounds[first], self.bounds[first + count] - self.bounds[first])

    def pass_on(self, y, z, first, count, index, *to):
        piece = self.piece(y, z, first, count)
        for one in to:
            self.send(piece, piece, self.sem(y, z, index), one)

    def landed(self, piece, sem):
        remote(piece, piece, self.ssem.at[0], sem, wide=self.me).wait_recv()

    def wait(self, y, z, first, count, index):
        self.landed(self.piece(y, z, first, count), self.sem(y, z, index))

    def around(self):
        y, z = self.y, self.z
        return y, z, (turn4(y, 1), z), (turn4(y, 3), z), (y, turn4(z, 1)), (y, turn4(z, 3))

    def own(self, src, dst, index):
        y, z, y_up, y_down, z_up, z_down = self.around()
        for to in (y_up, y_down, z_up, z_down):
            self.send(src, dst, self.sem(y, z, index), to)

    def near(self, parts=None):
        y, z, y_up, y_down, z_up, z_down = self.around()
        for at, far, turn, half, sides in (
            (y_down, y_up, 0, 0, (z_up, z_down)),
            (y_up, y_down, 1, 0, (z_up, z_down)),
            (z_down, z_up, 0, 2, (y_up, y_down)),
            (z_up, z_down, 1, 2, (y_up, y_down)),
        ):
            if parts is None:
                self.wait(*at, 0, 4, 0)
            else:
                for part, index in parts:
                    self.landed(part(*at), self.sem(*at, index))
            self.pass_on(*at, turn, 1, turn, far)
            self.pass_on(*at, 2 + turn, 1, 2 + turn, far)
            self.pass_on(*at, half, 2, half, *sides)

    def far(self):
        y, z, y_up, y_down, z_up, z_down = self.around()
        for at, half, sides in (
            ((turn4(y, 2), z), 0, (z_up, z_down)),
            ((y, turn4(z, 2)), 2, (y_up, y_down)),
        ):
            for index in range(4):
                self.wait(*at, index, 1, index)
            self.pass_on(*at, half, 2, half, *sides)

    def cross(self):
        y, z, y_up, y_down, z_up, z_down = self.around()
        for k in (1, 3, 2):
            row, column = turn4(y, k), turn4(z, k)
            self.wait(row, z_down[1], 0, 2, 0)
            self.pass_on(row, z_down[1], 0, 1, 0, z_up)
            self.wait(row, z_up[1], 0, 2, 0)
            self.pass_on(row, z_up[1], 1, 1, 1, z_down)
            self.wait(y_down[0], column, 2, 2, 2)
            self.pass_on(y_down[0], column, 2, 1, 2, y_up)
            self.wait(y_up[0], column, 2, 2, 2)
            self.pass_on(y_up[0], column, 3, 1, 3, y_down)

    def last(self):
        y, z = self.y, self.z
        for k in (1, 3, 2):
            row, column = turn4(y, k), turn4(z, k)
            for index in range(2):
                self.wait(row, turn4(z, 2), index, 1, index)
                self.wait(turn4(y, 2), column, 2 + index, 1, 2 + index)

    def finish(self):
        for copy in self.sent:
            copy.wait_send()


RING_SENDS = 36


def beside(step):
    me, y, xh, z = place()
    grp = lax.axis_index("grp")
    low = grp // 2
    side = lax.rem(xh + low + (0 if step == 1 else 1), 2)
    return {"grp": (1 - low) * 2 + lax.rem(grp, 2), "wide": flat(y, side, z)}


class Relay:
    def __init__(self, sources, stops, ends, ssem, rsem):
        self.sources, self.stops, self.ends, self.ssem, self.rsem = sources, stops, ends, ssem, rsem

    def copy(self, src, dst, at, step):
        return remote(src, dst, self.ssem.at[at], self.rsem.at[at], **beside(step))

    def legs(self, hop):
        for i, step in enumerate((1, 3)):
            src = self.sources[i] if hop == 0 else self.stops[i]
            dst = self.stops[i] if hop == 0 else self.ends[i]
            yield self.copy(src, dst, 2 * hop + i, step)

    def start(self):
        for copy in self.legs(0):
            copy.start()

    def forward(self):
        for first, second in zip(self.legs(0), self.legs(1)):
            first.wait_recv()
            second.start()

    def wait(self):
        for copy in self.legs(1):
            copy.wait_recv()

    def finish(self):
        for hop in (0, 1):
            for copy in self.legs(hop):
                copy.wait_send()


def look_up(got, table, hot, rows, slot_row):
    asked = got[:, slot_row, :].astype(F32)
    asked = jnp.concatenate([asked, jnp.zeros((128 - NW, 128), F32)], 0).T
    step = 8 * CAP
    for first in range(0, NW, 8):
        for d in range(8):
            column = asked[0:CAP, first + d : first + d + 1]
            lanes = lax.broadcasted_iota(jnp.int32, (CAP, SHARD), 1).astype(F32)
            hot[d * CAP : (d + 1) * CAP, :] = jnp.where(lanes == column, 1.0, 0.0).astype(BF)
        picked = lax.dot_general(
            hot[...], table[...], (((1,), (1,)), ((), ())), preferred_element_type=F32
        )
        rows[first * CAP : first * CAP + step, :] = picked.astype(BF)


def slots(at):
    return pl.ds(pl.multiple_of(at * CAP, CAP), CAP)


def turn_over(table, rows, first):
    for c in range(0, SHARD, 256):
        rows[first + c : first + c + 256, :] = table[:, c : c + 256].T


def owner_of(ids):
    return (((ids >> 9) * 171) >> 9).astype(jnp.int32)


def ask_rows(tok, msg, picks, slot_out):
    row = tok[0:1, :]
    column = jnp.broadcast_to(row.astype(F32), (128, T)).T[:, 0:1].astype(jnp.int32)
    row_owner, column_owner = owner_of(row), owner_of(column)
    down = lax.broadcasted_iota(jnp.int32, (T, T), 0)
    across = lax.broadcasted_iota(jnp.int32, (T, T), 1)
    same = row == column

    def count(which, axis):
        return jnp.sum(jnp.where(which, 1.0, 0.0), axis, keepdims=True)

    first_row = count(same & (down < across), 0) == 0.0
    first_column = count(same & (across < down), 1) == 0.0
    near = row_owner == column_owner
    rank_row = count(near & (column < row) & first_column, 0)
    rank_column = count(near & (row < column) & first_row, 1)
    slot_row = jnp.where(rank_row < CAP, row_owner.astype(F32) * CAP + rank_row, -1.0)
    slot_column = jnp.where(rank_column < CAP, column_owner.astype(F32) * CAP + rank_column, -1.0)
    lanes = lax.broadcasted_iota(jnp.int32, (T, NW * CAP), 1).astype(F32)
    hit = lanes == slot_column
    picks[...] = jnp.where(hit, 1.0, 0.0).astype(BF)
    slot_out[...] = jnp.broadcast_to(slot_row, (8, T)).astype(jnp.int32)
    local = (column - column_owner * SHARD).astype(F32)
    asked = jnp.max(jnp.where(hit, local, -1.0), 0, keepdims=True).astype(jnp.int32)
    most = (jnp.max(rank_row, 1, keepdims=True) + 1.0).astype(jnp.int32)
    rest = [
        tok[1:2, 0:128], tok[1:2, 128:256], tok[3:4, 0:128], jnp.broadcast_to(most, (1, 128)),
    ] + [jnp.zeros((1, 128), jnp.int32)] * 3
    for g in range(8):
        msg[g] = jnp.concatenate([asked[:, g * 128 : (g + 1) * 128]] + rest, 0)


def find_rows(got, table, asked_t, hot, rows, part):
    asked = got[:, 0, :].astype(F32)
    asked_t[...] = jnp.concatenate([asked, jnp.full((128 - NW, 128), -1.0, F32)], 0).T
    mine = asked_t[pl.ds(pl.multiple_of(part * CAP, CAP), CAP), :]
    lanes = lax.broadcasted_iota(jnp.int32, (CAP, SHARD), 1).astype(F32)
    for d in range(NW):
        hot[d * CAP : (d + 1) * CAP, :] = jnp.where(lanes == mine[:, d : d + 1], 1.0, 0.0).astype(BF)
    step = 8 * CAP
    for first in range(0, NW * CAP, step):
        picked = lax.dot_general(
            hot[first : first + step, :], table[...], (((1,), (1,)), ((), ())), preferred_element_type=F32
        )
        rows[first : first + step, :] = picked.astype(BF)


def turn_over(table, rows, first):
    for c in range(0, SHARD, 256):
        rows[first + c : first + c + 256, :] = table[:, c : c + 256].T


def front_kernel(
    tok, table, packed, got, emb, most, table_other, rows_t, packed_all, picks, slot_out, hot, goal, weights,
    msg, asked_t, rows, own_most, stops, msg_s, msg_r, emb_s, emb_r, most_s, most_r, swap_s, swap_r,
    ring_s, ring_r, x_sem, local,
):
    me, y, xh, z = place()
    grp = lax.axis_index("grp")
    other = flat(y, 1 - xh, z)
    greet_wide(me, grp, sides=True, meanwhile=lambda: ask_rows(tok, msg, picks, slot_out))
    over = remote(packed, packed_all.at[y, z, xh], x_sem.at[0], x_sem.at[1], wide=other)
    over.start()
    ask = Scatter(lambda p: msg.at[p // 4], lambda p: got.at[p], msg_s, msg_r, me)
    ask.start()
    got[me] = msg[me // 4]
    ring = Ring(
        lambda Y, Z, first, count: packed_all.at[Y, Z, :, pl.ds(first, count)],
        lambda Y, Z, index: ring_r.at[Y, Z, index],
        (0, 48, 96, 144, 208),
        ring_s,
    )
    ring.own(packed, packed_all.at[y, z, xh], 0)
    keep = pltpu.make_async_copy(packed, packed_all.at[y, z, xh], local.at[0])
    keep.start()
    halves = (pl.ds(0, D // 2), pl.ds(D // 2, D // 2))
    trade = Relay(
        [table.at[half] for half in halves],
        [stops.at[i] for i in range(2)],
        [table_other.at[half] for half in halves],
        swap_s,
        swap_r,
    )
    trade.start()
    turn_over(table, rows_t, 0)
    ask.wait_recv()
    find_rows(got, table, asked_t, hot, rows, lax.rem(me, 4))
    reply = Scatter(lambda p: rows.at[slots(p)], lambda p: emb.at[slots(p)], emb_s, emb_r, me)
    reply.start()
    over.wait_recv()
    ring.own(packed_all.at[y, z, 1 - xh], packed_all.at[y, z, 1 - xh], 4)
    emb[slots(me), :] = rows[slots(me), :]
    ring.near(
        [
            (lambda Y, Z: packed_all.at[Y, Z, xh], 0),
            (lambda Y, Z: packed_all.at[Y, Z, 1 - xh], 4),
        ]
    )
    largest = jnp.max(got[:, 4, :], 0, keepdims=True)
    own_most[...] = jnp.broadcast_to(largest, (8, 128))
    most[grp] = own_most[...]
    told = []
    for k in range(1, NG):
        to = lax.rem(grp + k, NG)
        told.append(remote(own_most, most.at[grp], most_s.at[k], most_r.at[grp], grp=to))
        told[-1].start()
    total = jnp.sum(got[:, 3, :].astype(F32), 0, keepdims=True)
    total = jnp.concatenate([total, total], 1) * T
    plain = tok[3:4, :].astype(F32)
    weights[...] = jnp.concatenate([plain / total, plain, total] + [jnp.zeros((1, T), F32)] * 5, 0)

    def place_goal(j, carry):
        from_dev = flat(j // 4, xh, lax.rem(j, 4))
        goals = jnp.concatenate([got[from_dev, 1:2, :], got[from_dev, 2:3, :]], 1)
        near, far = goals - me * SHARD, goals - other * SHARD
        at = jnp.where((far >= 0) & (far < SHARD), far + SHARD, -1)
        at = jnp.where((near >= 0) & (near < SHARD), near, at)
        goal[j] = jnp.broadcast_to(at, (8, T))
        return carry

    lax.fori_loop(0, 16, place_goal, 0)
    ring.far()
    trade.forward()
    ring.cross()
    reply.wait_recv()
    for k in range(1, NG):
        to = lax.rem(grp + k, NG)
        remote(own_most, most.at[to], most_s.at[k], most_r.at[to], grp=to).wait_recv()
    trade.wait()
    turn_over(table_other, rows_t, SHARD)
    ring.last()
    keep.wait()
    over.wait_send()
    ask.wait_send()
    reply.wait_send()
    trade.finish()
    for copy in told:
        copy.wait_send()
    ring.finish()


def front(tok, table, packed):
    return pl.pallas_call(
        front_kernel,
        name="front",
        out_shape=(
            jax.ShapeDtypeStruct((NW, 8, 128), jnp.int32),
            jax.ShapeDtypeStruct((NW * CAP, D), BF),
            jax.ShapeDtypeStruct((NG, 8, 128), jnp.int32),
            jax.ShapeDtypeStruct((D, SHARD), BF),
            jax.ShapeDtypeStruct((2 * SHARD, D), BF),
            jax.ShapeDtypeStruct((4, 4, 2, PACKED, D), BF),
            jax.ShapeDtypeStruct((T, NW * CAP), BF),
            jax.ShapeDtypeStruct((8, T), jnp.int32),
            jax.ShapeDtypeStruct((NW * CAP, SHARD), BF),
            jax.ShapeDtypeStruct((16, 8, T), jnp.int32),
            jax.ShapeDtypeStruct((8, T), F32),
        ),
        in_specs=[VMEM, VMEM, ANY],
        out_specs=(VMEM, VMEM, VMEM, VMEM, VMEM, ANY) + (VMEM,) * 5,
        scratch_shapes=[
            pltpu.VMEM((8, 8, 128), jnp.int32),
            pltpu.VMEM((128, 128), F32),
            pltpu.VMEM((NW * CAP, D), BF),
            pltpu.VMEM((8, 128), jnp.int32),
            pltpu.VMEM((2, D // 2, SHARD), BF),
            DMA((NW,)),
            DMA((NW,)),
            DMA((NW,)),
            DMA((NW,)),
            DMA((NG,)),
            DMA((NG,)),
            DMA((4,)),
            DMA((4,)),
            DMA((RING_SENDS + 4,)),
            DMA((4, 4, 5)),
            DMA((2,)),
            DMA((1,)),
        ],
        compiler_params=params(1, 60),
        cost_estimate=pl.CostEstimate(flops=2 * 10**9, bytes_accessed=3 * 10**7, transcendentals=0),
    )(tok, table, packed)


ORDER = tuple((i // 8) * 8 + (i % 2) * 4 + (i // 2) % 4 for i in range(NW))


def spread_rows(used, stride, at, repeat=1):
    picks = np.zeros((NW * stride, NW * used), np.float32)
    for i, w in enumerate(ORDER):
        for j in range(repeat):
            for r in range(used):
                picks[i * stride + at + j * used + r, w * used + r] = 1.0
    return picks


def rope():
    half = HD // 2
    freqs = np.float32(rope_base) ** (-(np.arange(half, dtype=np.float32) * np.float32(2.0)) / np.float32(HD))
    angles = freqs.astype(np.float32)[:, None] * np.arange(T, dtype=np.float32)[None, :]
    return np.concatenate([np.cos(angles), np.sin(angles)], 0).astype(np.float32)


def turned(values):
    return values.T


def gain_columns(gains):
    return jnp.concatenate([gains[...], jnp.zeros((120, D), F32)], 0).T


def rms(values, gain):
    scale = lax.rsqrt(jnp.mean(values * values, 0, keepdims=True) + norm_eps)
    return values * scale * gain


def rms_back(values, gain, grad):
    scale = lax.rsqrt(jnp.mean(values * values, 0, keepdims=True) + norm_eps)
    pulled = grad * gain
    middle = jnp.mean(values * pulled, 0, keepdims=True)
    back = scale * pulled - values * (scale * scale * scale) * middle
    return back, jnp.sum(grad * values * scale, 1, keepdims=True)


def mask_of(tok):
    row = tok[2:3, :]
    column = jnp.broadcast_to(row.astype(F32), (128, T)).T[:, 0:1].astype(jnp.int32)
    down = lax.broadcasted_iota(jnp.int32, (T, T), 0)
    across = lax.broadcasted_iota(jnp.int32, (T, T), 1)
    return (down <= across) & (row == column)


def mm(a, b):
    return jnp.dot(a, b, preferred_element_type=F32)


def mm_nt(a, b):
    return lax.dot_general(a, b, (((1,), (1,)), ((), ())), preferred_element_type=F32)


def mm_tn(a, b):
    return lax.dot_general(a, b, (((0,), (0,)), ((), ())), preferred_element_type=F32)


def rotated(x, rot):
    cosine, sine = rot[0:32, :], rot[32:64, :]
    one, two = x[0:32, :], x[32:64, :]
    return jnp.concatenate([one * cosine - two * sine, two * cosine + one * sine], 0)


def unrotated(x, rot):
    cosine, sine = rot[0:32, :], rot[32:64, :]
    one, two = x[0:32, :], x[32:64, :]
    return jnp.concatenate([one * cosine + two * sine, two * cosine - one * sine], 0)


def load_trunk(packed, ffn, down, attn, sem):
    loads = [
        pltpu.make_async_copy(packed.at[:, :, :, ATTN_AT:PACKED], attn, sem.at[0]),
        pltpu.make_async_copy(packed.at[:, :, :, FFN_AT:DOWN_AT], ffn, sem.at[1]),
        pltpu.make_async_copy(packed.at[:, :, :, DOWN_AT:ATTN_AT, 0:512], down, sem.at[2]),
    ]
    for load in loads:
        load.start()
    return loads


TRUNK_SCRATCH = [
    pltpu.VMEM((4, 4, 2, 96, D), BF),
    pltpu.VMEM((4, 4, 2, 64, 512), BF),
    pltpu.VMEM((4, 4, 2, 48, D), BF),
    DMA((3,)),
]


def forward_kernel(
    hidden, packed, gains, rot, tok,
    final, h0, n1, q, k, v, lse, att, h1, n2, gate_up, inner, h2,
    ffn, down, attn, sem, mixed,
):
    loads = load_trunk(packed, ffn, down, attn, sem)
    columns = gain_columns(gains)
    allowed = mask_of(tok)
    start = turned(hidden[...])
    h0[...] = start
    normed = rms(start, columns[:, 0:1]).astype(BF)
    n1[...] = normed
    loads[0].wait()
    rows48 = attn[...].reshape(NW * 48, D)
    product = mm(rows48, normed)
    for i, w in enumerate(ORDER):
        mixed[w * 30 : w * 30 + 30, :] = product[i * 48 : i * 48 + 30, :]
    for kv in range(KVH):
        k[kv * HD : (kv + 1) * HD, :] = rotated(
            mixed[D + kv * HD : D + (kv + 1) * HD, :], rot[...]
        ).astype(BF)
        at = D + (KVH + kv) * HD
        v[kv * HD : (kv + 1) * HD, :] = mixed[at : at + HD, :].astype(BF)
    logs = []
    for h in range(H):
        kv = h // (H // KVH)
        query = rotated(mixed[h * HD : (h + 1) * HD, :], rot[...]).astype(BF)
        q[h * HD : (h + 1) * HD, :] = query
        scores = mm_tn(k[kv * HD : (kv + 1) * HD, :], query) * HD ** (-0.5)
        scores = jnp.where(allowed, scores, masked_score)
        top = jnp.max(scores, 0, keepdims=True)
        power = jnp.exp(scores - top)
        total = jnp.sum(power, 0, keepdims=True)
        probs = (power / total).astype(BF)
        att[h * HD : (h + 1) * HD, :] = mm(v[kv * HD : (kv + 1) * HD, :], probs).astype(BF)
        logs.append(top + jnp.log(total))
    lse[...] = jnp.concatenate(logs + [jnp.zeros((16 - H, T), F32)], 0)
    product = mm(rows48, att[...])
    for i, w in enumerate(ORDER):
        mixed[w * 18 : w * 18 + 18, :] = product[i * 48 + 30 : i * 48 + 48, :]
    middle = start + mixed[0:D, :]
    h1[...] = middle
    normed = rms(middle, columns[:, 1:2]).astype(BF)
    n2[...] = normed
    loads[1].wait()
    gate_up[...] = mm(ffn[...].reshape(NW * 96, D), normed)
    for i in range(NW // 2):
        gate = gate_up[i * 96 : (i + 1) * 96, :]
        up = gate_up[FF + i * 96 : FF + (i + 1) * 96, :]
        w = ORDER[i]
        inner[w * 96 : (w + 1) * 96, :] = (gate / (1.0 + jnp.exp(-gate)) * up).astype(BF)
    loads[2].wait()
    rows64 = down[...].reshape(NW * 64, 512)
    for j in range(3):
        product = mm(rows64, inner[j * 512 : (j + 1) * 512, :])
        for i, w in enumerate(ORDER):
            piece = product[i * 64 + j * 18 : i * 64 + j * 18 + 18, :]
            if j:
                mixed[w * 18 : w * 18 + 18, :] += piece
            else:
                mixed[w * 18 : w * 18 + 18, :] = piece
    last = middle + mixed[0:D, :]
    h2[...] = last
    final[...] = rms(last, columns[:, 2:3]).astype(BF)


def forward(hidden, packed, gains, rot, tok):
    def out(rows, kind):
        return jax.ShapeDtypeStruct((rows, T), kind)

    return pl.pallas_call(
        forward_kernel,
        name="forward",
        out_shape=(
            out(D, BF), out(D, F32), out(D, BF), out(D, BF), out(KVH * HD, BF), out(KVH * HD, BF), out(16, F32),
            out(D, BF), out(D, F32), out(D, BF), out(2 * FF, F32), out(FF, BF), out(D, F32),
        ),
        in_specs=[VMEM, ANY, VMEM, VMEM, VMEM],
        out_specs=(VMEM,) * 13,
        scratch_shapes=TRUNK_SCRATCH + [pltpu.VMEM((QKV, T), F32)],
        compiler_params=pltpu.CompilerParams(vmem_limit_bytes=60 * MIB),
        cost_estimate=pl.CostEstimate(flops=4 * 10**9, bytes_accessed=2 * 10**7, transcendentals=10**6),
    )(hidden, packed, gains, rot, tok)


def more_rows_kernel(msg, table, got, emb, hot, rows, msg_s, msg_r, emb_s, emb_r):
    me = lax.axis_index("wide")
    greet_wide(me)
    ask = Scatter(lambda p: msg.at[p], lambda p: got.at[p], msg_s, msg_r, me)
    ask.start()
    got[me] = msg[me]
    ask.wait_recv()
    look_up(got, table, hot, rows, 0)
    reply = Scatter(lambda p: rows.at[slots(p)], lambda p: emb.at[slots(p)], emb_s, emb_r, me)
    reply.start()
    emb[slots(me), :] = rows[slots(me), :]
    reply.wait_recv()
    ask.wait_send()
    reply.wait_send()


def more_rows(msg, table):
    return pl.pallas_call(
        more_rows_kernel,
        name="more_rows",
        out_shape=(
            jax.ShapeDtypeStruct((NW, 8, 128), jnp.int32),
            jax.ShapeDtypeStruct((NW * CAP, D), BF),
        ),
        in_specs=[VMEM, VMEM],
        out_specs=(VMEM, VMEM),
        scratch_shapes=[pltpu.VMEM((8 * CAP, SHARD), BF), pltpu.VMEM((NW * CAP, D), BF)]
        + [DMA((NW,))] * 4,
        compiler_params=params(2, 40),
    )(msg, table)[1]


def more_grads_kernel(msg, rows, got, out, msg_s, msg_r, row_s, row_r):
    me = lax.axis_index("wide")
    greet_wide(me)
    ask = Scatter(lambda p: msg.at[p], lambda p: got.at[p], msg_s, msg_r, me)
    ask.start()
    give = Scatter(lambda p: rows.at[slots(p)], lambda p: out.at[slots(p)], row_s, row_r, me)
    give.start()
    got[me] = msg[me]
    out[slots(me), :] = rows[slots(me), :]
    ask.wait_recv()
    give.wait_recv()
    ask.wait_send()
    give.wait_send()


def more_grads(msg, rows):
    return pl.pallas_call(
        more_grads_kernel,
        name="more_grads",
        out_shape=(
            jax.ShapeDtypeStruct((NW, 8, 128), jnp.int32),
            jax.ShapeDtypeStruct((NW * CAP, D), BF),
        ),
        in_specs=[VMEM, VMEM],
        out_specs=(VMEM, VMEM),
        scratch_shapes=[DMA((NW,))] * 4,
        compiler_params=params(3, 20),
    )(msg, rows)


VOC = 2 * SHARD
TOK = 16 * T
CH = 512
NCH = VOC // CH
QUART = D // 4


def cols(j):
    return pl.ds(pl.multiple_of(j * T, T), T)


def head_kernel(
    final, rows_t, table, table_other, goal, weights,
    grad_final, head_own, head_other, loss,
    fall, expo, tops, stat, stat_in, coef, coef_in, parts,
    part_a, part_b, whole_a, whole_b, sum_a, sum_b, part_a2, part_b2, whole_a2, whole_b2,
    g_s, g_r, st_s, st_r, co_s, co_r, a_s, b_s, pa_r, pb_r, wa_r, wb_r, a2_s, b2_s, a2_r, b2_r,
):
    me, y, xh, z = place()
    mine = y * 4 + z

    def dev(j):
        return flat(j // 4, xh, lax.rem(j, 4))

    barrier = pltpu.get_barrier_semaphore()

    def greet(k, carry):
        pl.semaphore_signal(
            barrier, inc=1, device_id={"wide": dev(lax.rem(mine + k, 16))}, device_id_type=MESH
        )
        return carry

    lax.fori_loop(1, 16, greet, 0)
    pl.semaphore_wait(barrier, 15)

    sent = []

    def send(src, dst, ssem, rsem, to):
        copy = remote(src, dst, ssem, rsem, wide=to)
        copy.start()
        sent.append(copy)

    def arrived(dst, rsem):
        remote(dst, dst, g_s.at[0], rsem, wide=dev(mine)).wait_recv()

    ring = Ring(
        lambda Y, Z, first, count: fall.at[pl.ds(first, count), cols(Y * 4 + Z)],
        lambda Y, Z, index: g_r.at[Y * 4 + Z, index],
        tuple(QUART * k for k in range(5)),
        g_s,
    )
    ring.own(final, fall.at[:, cols(mine)], 0)
    fall[:, cols(mine)] = final[...]

    def logits(j):
        seen = fall[:, cols(j)]
        goals = goal[j]
        group, hit = goals >> 3, jnp.zeros((8, T), F32)
        tip, weight = [], []
        for c in range(NCH):
            part = jnp.dot(rows_t[c * CH : (c + 1) * CH, :], seen, preferred_element_type=F32)
            top = jnp.max(part, 0, keepdims=True)
            power = jnp.exp(part - top)
            for r in range(CH // 8):
                hit = jnp.where(group == c * (CH // 8) + r, part[8 * r : 8 * r + 8, :], hit)
            expo[c * CH : (c + 1) * CH, cols(j)] = power.astype(BF)
            tip.append(top)
            weight.append(jnp.sum(power, 0, keepdims=True))
        spot = lax.broadcasted_iota(jnp.int32, (8, T), 0)
        hit = jnp.sum(jnp.where(spot == (goals & 7), hit, 0.0), 0, keepdims=True)
        top = functools.reduce(jnp.maximum, tip)
        total = sum(w * jnp.exp(t - top) for w, t in zip(weight, tip))
        zero = jnp.zeros((1, T), F32)
        tops[j] = jnp.concatenate(tip + [zero] * (8 - NCH), 0)
        stat[j] = jnp.concatenate([top, total, hit] + [zero] * 5, 0)

    def tell(j):
        return remote(stat.at[j], stat_in.at[mine], st_s.at[j], st_r.at[mine], wide=dev(j))

    def block(dy, dz):
        return turn4(y, dy) * 4 + turn4(z, dz)

    def forward(offsets):
        def one(k, carry):
            j = block(*offsets(k))
            logits(j)
            tell(j).start()
            return carry

        return one

    def odd(k):
        return 1 + 2 * lax.rem(k, 2)

    logits(mine)
    stat_in[mine] = stat[mine]
    ring.near()
    lax.fori_loop(0, 4, forward(lambda k: ((1 - k // 2) * odd(k), (k // 2) * odd(k))), 0)
    ring.far()
    lax.fori_loop(0, 2, forward(lambda k: (2 * (1 - k), 2 * k)), 0)
    ring.cross()
    lax.fori_loop(0, 4, forward(lambda k: (odd(k // 2), odd(k))), 0)
    ring.last()
    lax.fori_loop(
        0,
        4,
        forward(lambda k: (2 * (1 - k // 2) + odd(k) * (k // 2), odd(k) * (1 - k // 2) + 2 * (k // 2))),
        0,
    )
    forward(lambda k: (2, 2))(0, 0)

    def hear(k, carry):
        j = lax.rem(mine + k, 16)
        arrived(stat_in.at[j], st_r.at[j])
        return carry

    lax.fori_loop(1, 16, hear, 0)
    tip, weight, hit = stat_in[:, 0, :], stat_in[:, 1, :], stat_in[:, 2, :]
    top = jnp.max(tip, 0, keepdims=True)
    lse = top + jnp.log(jnp.sum(weight * jnp.exp(tip - top), 0, keepdims=True))
    picked = jnp.sum(hit, 0, keepdims=True)
    share, plain = weights[0:1, :], weights[1:2, :]
    zero = jnp.zeros((1, T), F32)
    coef[...] = jnp.concatenate(
        [lse, share * (1.0 + 2.0 * penalty_weight * lse), share] + [zero] * 5, 0
    )
    loss[...] = jnp.concatenate(
        [plain * (lse - picked + penalty_weight * lse * lse)] + [zero] * 7, 0
    )
    coef_in[mine] = coef[...]

    def spread(k):
        j = lax.rem(mine + k, 16)
        return remote(coef, coef_in.at[mine], co_s.at[k], co_r.at[mine], wide=dev(j))

    def spread_start(k, carry):
        spread(k).start()
        return carry

    lax.fori_loop(1, 16, spread_start, 0)

    up, down = 1, 3
    z_to = {step: flat(y, xh, turn4(z, step)) for step in (up, down)}
    y_to = {step: flat(turn4(y, step), xh, z) for step in (up, down)}

    def piece_a(j, index):
        row = j // 4
        return remote(
            parts.at[j, pl.ds(index * QUART, QUART)], part_a.at[index, row],
            a_s.at[j, index], pa_r.at[index, row], wide=z_to[(up, down)[index]],
        )

    def piece_b(j, index):
        column = lax.rem(j, 4)
        return remote(
            parts.at[j, pl.ds((2 + index) * QUART, QUART)], part_b.at[index, column],
            b_s.at[j, index], pb_r.at[index, column], wide=y_to[(up, down)[index]],
        )

    def half_a(j, index):
        row = j // 4
        return remote(
            parts.at[j, pl.ds(0, 2 * QUART)], whole_a.at[index, row],
            a_s.at[j, 0], wa_r.at[index, row], wide=z_to[(up, down)[index]],
        )

    def half_b(j, index):
        column = lax.rem(j, 4)
        return remote(
            parts.at[j, pl.ds(2 * QUART, 2 * QUART)], whole_b.at[index, column],
            b_s.at[j, 0], wb_r.at[index, column], wide=y_to[(up, down)[index]],
        )

    def offsets(k):
        return lax.rem(2 + k // 4, 4), lax.rem(2 + k, 4)

    def post(k):
        dy, dz = offsets(k)
        j = block(dy, dz)

        @pl.when(dz == 2)
        def _():
            piece_a(j, 0).start()
            piece_a(j, 1).start()

        @pl.when(dy == 2)
        def _():
            piece_b(j, 0).start()
            piece_b(j, 1).start()

        for index, step in enumerate((up, down)):

            @pl.when(dz == step)
            def _():
                row = j // 4
                arrived(part_a.at[index, row], pa_r.at[index, row])
                rows = pl.ds(index * QUART, QUART)
                total = parts[j, rows, :].astype(F32) + part_a[index, row].astype(F32)
                parts[j, rows, :] = total.astype(BF)
                half_a(j, index).start()

            @pl.when(dy == step)
            def _():
                column = lax.rem(j, 4)
                arrived(part_b.at[index, column], pb_r.at[index, column])
                rows = pl.ds((2 + index) * QUART, QUART)
                total = parts[j, rows, :].astype(F32) + part_b[index, column].astype(F32)
                parts[j, rows, :] = total.astype(BF)
                half_b(j, index).start()

    def backward(k, carry):
        j = block(*offsets(k))

        @pl.when(k != 10)
        def _():
            arrived(coef_in.at[j], co_r.at[j])

        lse, soft, pick = coef_in[j, 0:1, :], coef_in[j, 1:2, :], coef_in[j, 2:3, :]
        goals = goal[j]
        group = goals >> 3
        pick = jnp.where(lax.broadcasted_iota(jnp.int32, (8, T), 0) == (goals & 7), pick, 0.0)
        for c in range(NCH):
            scale = soft * jnp.exp(tops[j, c : c + 1, :] - lse)
            power = expo[c * CH : (c + 1) * CH, cols(j)].astype(F32)
            spot = lax.broadcasted_iota(jnp.int32, (CH // 8, 8, T), 0) + c * (CH // 8)
            drop = jnp.where(spot == group[None], pick[None], 0.0).reshape(CH, T)
            expo[c * CH : (c + 1) * CH, cols(j)] = (power * scale - drop).astype(BF)
        product = jnp.dot(table[...], expo[0:SHARD, cols(j)], preferred_element_type=F32)
        product += jnp.dot(table_other[...], expo[SHARD:VOC, cols(j)], preferred_element_type=F32)
        parts[j] = product.astype(BF)

        @pl.when(k > 0)
        def _():
            post(k - 1)

        return carry

    lax.fori_loop(0, 16, backward, 0)
    post(15)

    def head_chunk(c):
        return lax.dot_general(
            fall[...],
            expo[pl.ds(pl.multiple_of(c * 256, 256), 256), :],
            (((1,), (1,)), ((), ())),
            preferred_element_type=F32,
        )

    def other_chunk(c, carry):
        head_other[:, cols(c)] = head_chunk(c + SHARD // 256).astype(BF)
        return carry

    def own_chunk(c, carry):
        head_own[:, cols(c)] = head_chunk(c)
        return carry

    lax.fori_loop(0, SHARD // 256, other_chunk, 0)

    kinds = (
        (whole_a, wa_r, sum_a, part_a2, whole_a2, a2_s, a2_r, y_to, 0),
        (whole_b, wb_r, sum_b, part_b2, whole_b2, b2_s, b2_r, z_to, 2 * QUART),
    )
    for d in (2, 1, 3, 0):
        for kind, (whole, w_r, total, part2, whole2, s2, r2, to, base) in enumerate(kinds):
            at = turn4(y if kind == 0 else z, d)
            j = at * 4 + z if kind == 0 else y * 4 + at
            acc = parts[j, base : base + 2 * QUART, :].astype(F32)
            for index in range(2):
                arrived(whole.at[index, at], w_r.at[index, at])
                acc = acc + whole[index, at].astype(F32)
            if d == 0:
                grad_final[base : base + 2 * QUART, :] = acc
            else:
                total[d - 1] = acc.astype(BF)
            if d == 2:
                for index, step in enumerate((up, down)):
                    piece = total.at[1, pl.ds(index * QUART, QUART)]
                    send(piece, part2.at[index], s2.at[index], r2.at[index], to[step])
    lax.fori_loop(0, SHARD // 512, own_chunk, 0)
    for kind, (whole, w_r, total, part2, whole2, s2, r2, to, base) in enumerate(kinds):
        for index, step in enumerate((up, down)):
            arrived(part2.at[index], r2.at[index])
            rows = pl.ds(index * QUART, QUART)
            added = total[step - 1, rows, :].astype(F32) + part2[index].astype(F32)
            total[step - 1, rows, :] = added.astype(BF)
            send(total.at[step - 1], whole2.at[index], s2.at[2 + index], r2.at[2 + index], to[step])
    lax.fori_loop(SHARD // 512, SHARD // 256, own_chunk, 0)
    for kind, (whole, w_r, total, part2, whole2, s2, r2, to, base) in enumerate(kinds):
        for index in range(2):
            arrived(whole2.at[index], r2.at[2 + index])
        grad_final[base : base + 2 * QUART, :] += whole2[0].astype(F32) + whole2[1].astype(F32)

    def finish(k, carry):
        j = lax.rem(mine + k, 16)
        tell(j).wait_send()
        spread(k).wait_send()
        return carry

    lax.fori_loop(1, 16, finish, 0)
    for copy in sent:
        copy.wait_send()
    ring.finish()

    def finish_pieces(k, carry):
        row, column = block(k, 2), block(2, k)
        piece_a(row, 0).wait_send()
        piece_a(row, 1).wait_send()
        piece_b(column, 0).wait_send()
        piece_b(column, 1).wait_send()
        for index, step in enumerate((up, down)):
            half_a(block(k, step), index).wait_send()
            half_b(block(step, k), index).wait_send()
        return carry

    lax.fori_loop(0, 4, finish_pieces, 0)


def head(final, rows_t, table, table_other, goal, weights):
    return pl.pallas_call(
        head_kernel,
        name="head",
        out_shape=(
            jax.ShapeDtypeStruct((D, T), F32),
            jax.ShapeDtypeStruct((D, SHARD), F32),
            jax.ShapeDtypeStruct((D, SHARD), BF),
            jax.ShapeDtypeStruct((8, T), F32),
        ),
        in_specs=[VMEM] * 6,
        out_specs=(VMEM,) * 4,
        scratch_shapes=[
            pltpu.VMEM((D, TOK), BF),
            pltpu.VMEM((VOC, TOK), BF),
            pltpu.VMEM((16, 8, T), F32),
            pltpu.VMEM((16, 8, T), F32),
            pltpu.VMEM((16, 8, T), F32),
            pltpu.VMEM((8, T), F32),
            pltpu.VMEM((16, 8, T), F32),
            pltpu.VMEM((16, D, T), BF),
            pltpu.VMEM((2, 4, QUART, T), BF),
            pltpu.VMEM((2, 4, QUART, T), BF),
            pltpu.VMEM((2, 4, 2 * QUART, T), BF),
            pltpu.VMEM((2, 4, 2 * QUART, T), BF),
            pltpu.VMEM((3, 2 * QUART, T), BF),
            pltpu.VMEM((3, 2 * QUART, T), BF),
            pltpu.VMEM((2, QUART, T), BF),
            pltpu.VMEM((2, QUART, T), BF),
            pltpu.VMEM((2, 2 * QUART, T), BF),
            pltpu.VMEM((2, 2 * QUART, T), BF),
            DMA((RING_SENDS,)),
            DMA((16, 4)),
            DMA((16,)),
            DMA((16,)),
            DMA((16,)),
            DMA((16,)),
            DMA((16, 2)),
            DMA((16, 2)),
            DMA((2, 4)),
            DMA((2, 4)),
            DMA((2, 4)),
            DMA((2, 4)),
            DMA((4,)),
            DMA((4,)),
            DMA((4,)),
            DMA((4,)),
        ],
        compiler_params=params(4, 61),
        cost_estimate=pl.CostEstimate(
            flops=6 * VOC * TOK * D, bytes_accessed=2 * 10**7, transcendentals=VOC * TOK
        ),
    )(final, rows_t, table, table_other, goal, weights)


class Reduce:
    def __init__(self, parts, base, sizes, along_z, refs):
        (
            self.first, part_a, part_b, self.whole1, self.second, next_a, next_b, self.whole2,
            self.third, self.stop, self.third_in, self.s, self.r,
        ) = refs
        self.part1, self.part2 = (part_a, part_b), (next_a, next_b)
        self.parts, self.base, self.sizes, self.along_z = parts, base, sizes, along_z
        self.rows = (pl.ds(0, sizes[0]), pl.ds(sizes[0], sizes[1]), pl.ds(0, sum(sizes)))
        self.me, self.y, self.xh, self.z = place()
        self.sent = []

    def send(self, src, dst, at, **to):
        copy = remote(src, dst, self.s.at[at], self.r.at[at], **to)
        copy.start()
        self.sent.append(copy)

    def wait(self, dst, at):
        remote(dst, dst, self.s.at[at], self.r.at[at], wide=self.me).wait_recv()

    def item1(self, step, which):
        rows = pl.ds(self.base + self.rows[which].start, self.rows[which].size)
        if self.along_z:
            return (slice(None), turn4(self.z, step), slice(None), rows)
        return (turn4(self.y, step), slice(None), slice(None), rows)

    def item2(self, step, which):
        return (turn4(self.y if self.along_z else self.z, step), slice(None), self.rows[which])

    def to(self, stage, step):
        if self.along_z == (stage == 1):
            return flat(self.y, self.xh, turn4(self.z, step))
        return flat(turn4(self.y, step), self.xh, self.z)

    def split(self, stage, ref, item, part, base):
        for index, step in enumerate((1, 3)):
            self.send(ref.at[item(2, index)], part[index], base + index, wide=self.to(stage, step))

    def join(self, stage, ref, item, part, whole, base):
        for index, step in enumerate((1, 3)):
            self.wait(part[index], base + index)
            at = item(step, index)
            ref[at] = (ref[at].astype(F32) + part[index][...].astype(F32)).astype(BF)
            self.send(ref.at[item(step, 2)], whole.at[index], base + 2 + index, wide=self.to(stage, step))

    def add(self, ref, item, whole, base):
        acc = ref[item(0, 2)].astype(F32)
        for index in range(2):
            self.wait(whole.at[index], base + 2 + index)
            acc = acc + whole[index].astype(F32)
        return acc

    def one(self):
        self.split(1, self.parts, self.item1, self.part1, 0)

    def two(self):
        self.join(1, self.parts, self.item1, self.part1, self.whole1, 0)

    def three(self):
        self.first[...] = self.add(self.parts, self.item1, self.whole1, 0).astype(BF)
        self.split(2, self.first, self.item2, self.part2, 4)

    def four(self):
        self.join(2, self.first, self.item2, self.part2, self.whole2, 4)

    def five(self):
        self.second[...] = self.add(self.first, self.item2, self.whole2, 4)
        self.third[...] = self.second[1 - self.xh].astype(BF)
        self.send(self.third, self.stop, 8, **beside(1 if self.along_z else 3))

    def six(self):
        self.wait(self.stop, 8)
        self.send(self.stop, self.third_in, 9, **beside(1 if self.along_z else 3))

    def total(self):
        self.wait(self.third_in, 9)
        return self.second[self.xh] + self.third_in[...].astype(F32)

    def finish(self):
        for copy in self.sent:
            copy.wait_send()


STREAMS = ((0, (48, 32), True), (80, (48, 32), False), (160, (16, 16), True), (192, (16, 16), False))


def reduce_scratch():
    shapes = []
    for _, sizes, _ in STREAMS:
        half = sum(sizes)
        shapes += [
            pltpu.VMEM((4, 2, half, D), BF),
            pltpu.VMEM((4, 2, sizes[0], D), BF),
            pltpu.VMEM((4, 2, sizes[1], D), BF),
            pltpu.VMEM((2, 4, 2, half, D), BF),
            pltpu.VMEM((2, half, D), F32),
            pltpu.VMEM((2, sizes[0], D), BF),
            pltpu.VMEM((2, sizes[1], D), BF),
            pltpu.VMEM((2, 2, half, D), BF),
            pltpu.VMEM((half, D), BF),
            pltpu.VMEM((half, D), BF),
            pltpu.VMEM((half, D), BF),
            DMA((10,)),
            DMA((10,)),
        ]
    return shapes


def back_kernel(
    grad_final, h0, n1, q, k, v, lse, att, h1, n2, gate_up, inner, h2,
    packed, gains, rot, tok, slot_row, loss, head_other, lay_attn, lay_out, lay_down,
    summed, rows_in, head_in, extra_sum, grad_embedded,
    ffn, down, attn, sem, parts, rows, grad_up, grad_mixed, spread, stops,
    row_s, row_r, swap_s, swap_r, hold, land_z, land_y, land_x, tree_s, tree_r, *reducers,
):
    me, y, xh, z = place()
    loads = load_trunk(packed, ffn, down, attn, sem)
    greet_wide(me, sides=True)
    halves = (pl.ds(0, D // 2), pl.ds(D // 2, D // 2))
    trade = Relay(
        [head_other.at[half] for half in halves],
        [stops.at[i] for i in range(2)],
        [head_in.at[half] for half in halves],
        swap_s,
        swap_r,
    )
    trade.start()
    streams = [
        Reduce(parts, base, sizes, along, reducers[13 * i : 13 * i + 13])
        for i, (base, sizes, along) in enumerate(STREAMS)
    ]
    early, late = streams[:2], streams[2:]
    columns = gain_columns(gains)

    grad_h2, gain3 = rms_back(h2[...], columns[:, 2:3], grad_final[...])
    spread[...] = mm(lay_down[...], grad_h2.astype(BF)).astype(BF)
    chunk = lax.broadcasted_iota(jnp.int32, (NW * 64, T), 0) & 63
    zero = jnp.zeros((NW * 64, T), BF)
    wide = jnp.concatenate(
        [
            jnp.where((chunk >= 18 * j) & (chunk < 18 * (j + 1)), spread[...].astype(F32), 0.0).astype(BF)
            for j in range(3)
        ],
        1,
    )
    inners = jnp.concatenate([inner[j * 512 : (j + 1) * 512, :] for j in range(3)], 1)
    grad_down = mm_nt(wide, inners).astype(BF).reshape(4, 4, 2, 64, 512)
    parts[:, :, :, DOWN_AT:ATTN_AT, 0:512] = grad_down
    parts[:, :, :, DOWN_AT:ATTN_AT, 512:D] = jnp.zeros((4, 4, 2, 64, D - 512), BF)
    loads[2].wait()
    grad_inner = mm_tn(down[...].reshape(NW * 64, 512), wide)
    for i in range(NW // 2):
        w = ORDER[i]
        gate = gate_up[i * 96 : (i + 1) * 96, :]
        up = gate_up[FF + i * 96 : FF + (i + 1) * 96, :]
        pieces = []
        for at in range(w * 96, w * 96 + 96, 32):
            j, r = at // 512, at % 512
            pieces.append(grad_inner[r : r + 32, j * T : (j + 1) * T])
        grad = jnp.concatenate(pieces, 0)
        sigmoid = 1.0 / (1.0 + jnp.exp(-gate))
        slope = sigmoid * (1.0 + gate * (1.0 - sigmoid))
        grad_up[i * 96 : (i + 1) * 96, :] = (grad * up * slope).astype(BF)
        grad_up[FF + i * 96 : FF + (i + 1) * 96, :] = (grad * (gate * sigmoid)).astype(BF)
    parts[:, :, :, FFN_AT:DOWN_AT, :] = mm_nt(grad_up[...], n2[...]).astype(BF).reshape(4, 4, 2, 96, D)
    for stream in early:
        stream.one()
    loads[1].wait()
    grad_normed = turned(mm_tn(grad_up[...], ffn[...].reshape(NW * 96, D)))
    part, gain2 = rms_back(h1[...], columns[:, 1:2], grad_normed)
    grad_h1 = grad_h2 + part
    out_rows = mm(lay_out[...], grad_h1.astype(BF)).astype(BF)
    loads[0].wait()
    rows48 = attn[...].reshape(NW * 48, D)
    grad_att = turned(mm_tn(out_rows, rows48)).astype(BF)
    for stream in early:
        stream.two()

    allowed = mask_of(tok)
    group = H // KVH
    for kv in range(KVH):
        keys = k[kv * HD : (kv + 1) * HD, :]
        values = v[kv * HD : (kv + 1) * HD, :]
        grad_k, grad_v = jnp.zeros((HD, T), F32), jnp.zeros((HD, T), F32)
        for h in range(kv * group, (kv + 1) * group):
            query = q[h * HD : (h + 1) * HD, :]
            grad_out = grad_att[h * HD : (h + 1) * HD, :]
            scores = mm_tn(keys, query) * HD ** (-0.5)
            scores = jnp.where(allowed, scores, masked_score)
            soft = jnp.exp(scores - lse[h : h + 1, :])
            grad_probs = mm_tn(values, grad_out)
            mean = jnp.sum(soft * grad_probs, 0, keepdims=True)
            grad_scores = (soft * (grad_probs - mean)).astype(BF)
            grad_q = mm(keys, grad_scores) * HD ** (-0.5)
            grad_mixed[h * HD : (h + 1) * HD, :] = unrotated(grad_q, rot[...]).astype(BF)
            grad_k = grad_k + mm_nt(query, grad_scores) * HD ** (-0.5)
            grad_v = grad_v + mm_nt(grad_out, soft.astype(BF))
        at = D + kv * HD
        grad_mixed[at : at + HD, :] = unrotated(grad_k, rot[...]).astype(BF)
        at = D + (KVH + kv) * HD
        grad_mixed[at : at + HD, :] = grad_v.astype(BF)
    for stream in early:
        stream.three()
    attn_rows = mm(lay_attn[...], grad_mixed[...]).astype(BF)
    both = jnp.concatenate([attn_rows, out_rows], 1)
    seen = jnp.concatenate([n1[...], att[...]], 1)
    parts[:, :, :, ATTN_AT:PACKED, :] = mm_nt(both, seen).astype(BF).reshape(4, 4, 2, 48, D)
    parts[:, :, :, PACKED:SUMMED, :] = jnp.zeros((4, 4, 2, SUMMED - PACKED, D), BF)
    for stream in late:
        stream.one()
    grad_normed = turned(mm_tn(attn_rows, rows48))
    part, gain1 = rms_back(h0[...], columns[:, 0:1], grad_normed)
    grad_h0 = (grad_h1 + part).astype(BF)
    grad_embedded[...] = grad_h0
    slot = lax.broadcasted_iota(jnp.int32, (NW * CAP, T), 0)
    picks = jnp.where(slot == slot_row[0:1, :], 1.0, 0.0).astype(BF)
    rows[...] = mm_nt(picks, grad_h0).astype(BF)
    give = Scatter(lambda p: rows.at[slots(p)], lambda p: rows_in.at[slots(p)], row_s, row_r, me)
    give.start()
    for stream in early:
        stream.four()
    trade.forward()
    lane = lax.broadcasted_iota(jnp.int32, (D, 128), 1)
    table = jnp.where(lane == 0, gain1, jnp.where(lane == 1, gain2, jnp.where(lane == 2, gain3, 0.0)))
    lost = jnp.sum(loss[0:1, :], 1, keepdims=True)
    table = table.T[0:8, :]
    tree = Tree(hold, land_z, land_y, land_x, tree_s, tree_r)
    tree.start(jnp.where(lax.broadcasted_iota(jnp.int32, (8, D), 0) == 3, lost, table))
    rows_in[slots(me), :] = rows[slots(me), :]
    for stream in late:
        stream.two()
    for stream in early:
        stream.five()
    tree.next(0)
    for stream in late:
        stream.three()
    for stream in late:
        stream.four()
    tree.next(1)
    for stream in early:
        stream.six()
    for stream in late:
        stream.five()
    extra_sum[...] = tree.collect(2)
    for stream in late:
        stream.six()
    for stream in streams:
        summed[stream.base : stream.base + sum(stream.sizes), :] = stream.total()
    give.wait_recv()
    trade.wait()
    for stream in streams:
        stream.finish()
    give.wait_send()
    tree.finish()
    trade.finish()


def back(grad_final, kept, packed, gains, rot, tok, slot_row, loss, head_other):
    lays = [
        jnp.asarray(spread_rows(30, 48, 0), BF),
        jnp.asarray(spread_rows(18, 48, 30), BF),
        jnp.asarray(spread_rows(18, 64, 0, 3), BF),
    ]
    return pl.pallas_call(
        back_kernel,
        name="back",
        out_shape=(
            jax.ShapeDtypeStruct((SUMMED, D), F32),
            jax.ShapeDtypeStruct((NW * CAP, D), BF),
            jax.ShapeDtypeStruct((D, SHARD), BF),
            jax.ShapeDtypeStruct((8, D), F32),
            jax.ShapeDtypeStruct((D, T), BF),
        ),
        in_specs=[VMEM] * 13 + [ANY] + [VMEM] * 5 + [ANY] + [VMEM] * 3,
        out_specs=(VMEM, VMEM, ANY, VMEM, VMEM),
        scratch_shapes=TRUNK_SCRATCH
        + [
            pltpu.VMEM((4, 4, 2, SUMMED, D), BF),
            pltpu.VMEM((NW * CAP, D), BF),
            pltpu.VMEM((2 * FF, T), BF),
            pltpu.VMEM((QKV, T), BF),
            pltpu.VMEM((NW * 64, T), BF),
            pltpu.VMEM((2, D // 2, SHARD), BF),
        ]
        + [DMA((NW,)), DMA((NW,)), DMA((4,)), DMA((4,))]
        + tree_scratch(D)
        + reduce_scratch(),
        compiler_params=params(5, 60),
        cost_estimate=pl.CostEstimate(flops=10**10, bytes_accessed=3 * 10**7, transcendentals=10**6),
    )(grad_final, *kept, packed, gains, rot, tok, slot_row, loss, head_other, *lays)


def adam_update(weight, grad, first, second, rate, decay):
    first = beta_one * first + (1.0 - beta_one) * grad
    second = beta_two * second + (1.0 - beta_two) * grad * grad
    ratio = first / (1.0 - beta_one**STEP) / (jnp.sqrt(second / (1.0 - beta_two**STEP)) + adam_eps)
    return (weight - rate * (ratio + decay * weight), first, second)


def adam_diff(weight, grad, first, second, anchor, rate, decay):
    return anchor - adam_update(weight, grad, first, second, rate, decay)[0]


PIECES = ((0, 0, 96), (0, 96, 96), (0, 192, 96), (1, 0, 112))


def update_kernel(
    rows, hot, head, head_in, summed, extra, gains, tm, tf, ts, ta, km, kf, ks, ka,
    table_grad, total_t, total_k, total_g, norms,
    v_rows, v_hot, v_head, v_head_in, vm, vf, vs, va, flipped,
    one_t, one_t_in, two_t, two_t_in, one_k, one_k_in, two_k, two_k_in, gains_out, gains_in,
    load_sem, one_s, one_r, two_s, two_r, three_s, three_r, gains_s, gains_r,
    hold, land_z, land_y, land_x, tree_s, tree_r,
):
    me, y, xh, z = place()
    grp = lax.axis_index("grp")
    core, x = lax.rem(grp, 2), grp // 2
    near, far = x * 2 + 1 - core, (1 - x) * 2 + core
    loads = [
        pltpu.make_async_copy(src, dst, load_sem.at[i])
        for i, (src, dst) in enumerate(
            zip((rows, hot, head, head_in, tm, tf, ts, ta), (v_rows, v_hot, v_head, v_head_in, vm, vf, vs, va))
        )
    ]
    for load in loads:
        load.start()
    barrier = pltpu.get_barrier_semaphore()
    for peer in near_peers(me, y, xh, z):
        pl.semaphore_signal(barrier, inc=1, device_id={"wide": peer}, device_id_type=MESH)
    for k in range(1, NG):
        pl.semaphore_signal(
            barrier, inc=1, device_id={"grp": lax.rem(grp + k, NG)}, device_id_type=MESH
        )
    pl.semaphore_wait(barrier, 7 + NG - 1)
    for load in loads[:4]:
        load.wait()
    for c in range(0, NW * CAP, 256):
        flipped[:, c : c + 256] = v_rows[c : c + 256, :].T
    squares = jnp.zeros((1, 256), F32)
    for c in range(0, SHARD, 256):
        part = v_head[:, c : c + 256] + v_head_in[:, c : c + 256].astype(F32)
        part = part + mm(flipped[...], v_hot[:, c : c + 256])
        table_grad[:, c : c + 256] = part
        squares = squares + jnp.sum(part * part, 0, keepdims=True)
    squares = jnp.sum(squares, 1, keepdims=True)
    trunk = jnp.sum(summed[...] * summed[...], 0, keepdims=True)
    squares = squares + jnp.sum(trunk, 1, keepdims=True)
    tree = Tree(hold, land_z, land_y, land_x, tree_s, tree_r)
    tree.start(jnp.broadcast_to(squares, (8, 128)))
    gain_grads = extra[0:3, :]
    gain_squares = jnp.sum(jnp.sum(gain_grads * gain_grads, 0, keepdims=True), 1, keepdims=True)
    tree.next(0)
    for load in loads[4:]:
        load.wait()
    tree.next(1)
    norm = jnp.sqrt(tree.collect(2)[0:1, 0:1] + gain_squares)
    factor = jnp.minimum(1.0, clip_norm / norm)
    down = lax.broadcasted_iota(jnp.int32, (8, 128), 0)
    norms[...] = jnp.where(down == 0, norm, factor)

    parts = (
        (vm, table_grad, vf, vs, va, total_t, D // 2, one_t, one_t_in, two_t, two_t_in),
        (km, summed, kf, ks, ka, total_k, SUMMED // 2, one_k, one_k_in, two_k, two_k_in),
    )
    sent = []

    def span(which, at, count, side):
        half = parts[which][6]
        return pl.ds(pl.multiple_of(side * half + at, 16), count)

    def diff(which, at, count, side):
        m, g, f, s2, a = parts[which][:5]
        rows = span(which, at, count, side)
        return adam_diff(
            m[rows, :], g[rows, :] * factor, f[rows, :], s2[rows, :], a[rows, :], inner_rate, weight_decay
        )

    for i, (which, at, count) in enumerate(PIECES):
        one, one_in = parts[which][7:9]
        rows = pl.ds(at, count)
        one[rows, :] = diff(which, at, count, 1 - core).astype(BF)
        copy = remote(one.at[rows], one_in.at[rows], one_s.at[i], one_r.at[i], grp=near)
        copy.start()
        sent.append(copy)
    for i, (which, at, count) in enumerate(PIECES):
        one, one_in, two, two_in = parts[which][7:11]
        rows = pl.ds(at, count)
        own = diff(which, at, count, core)
        sent[i].wait_recv()
        two[rows, :] = (own + one_in[rows, :].astype(F32)).astype(BF)
        copy = remote(two.at[rows], two_in.at[rows], two_s.at[i], two_r.at[i], grp=far)
        copy.start()
        sent.append(copy)
    gains_out[0:3, :] = adam_diff(
        gains[0:3, :], gain_grads * factor, gains[8:11, :], gains[16:19, :], gains[24:27, :], gain_rate, 0.0
    )
    gains_out[3:8, :] = jnp.zeros((5, D), F32)
    told = []
    for k in range(1, NG):
        to = lax.rem(grp + k, NG)
        told.append(remote(gains_out, gains_in.at[grp], gains_s.at[k], gains_r.at[grp], grp=to))
        told[-1].start()
    gains_in[grp] = gains_out[...]
    for i, (which, at, count) in enumerate(PIECES):
        total, two, two_in = parts[which][5], parts[which][9], parts[which][10]
        rows = pl.ds(at, count)
        sent[len(PIECES) + i].wait_recv()
        kept = span(which, at, count, core)
        total[kept, :] = two[rows, :].astype(F32) + two_in[rows, :].astype(F32)
        copy = remote(total.at[kept], total.at[kept], three_s.at[i], three_r.at[i], grp=near)
        copy.start()
        sent.append(copy)
    for k in range(1, NG):
        other = lax.rem(grp + k, NG)
        remote(
            gains_out, gains_in.at[other], gains_s.at[k], gains_r.at[other], grp=other
        ).wait_recv()
    total_g[...] = (gains_in[0] + gains_in[1]) + (gains_in[2] + gains_in[3])
    for i, (which, at, count) in enumerate(PIECES):
        away = parts[which][5].at[span(which, at, count, 1 - core)]
        remote(away, away, three_s.at[i], three_r.at[i], grp=near).wait_recv()
    for copy in sent + told:
        copy.wait_send()
    tree.finish()


def update(rows, hot, head, head_in, summed, extra, gains, table, trunk):
    def exchange(size, lanes):
        return [pltpu.VMEM((size // 2, lanes), BF)] * 4

    table_f32 = pltpu.VMEM((D, SHARD), F32)
    pieces = DMA((len(PIECES),))
    return pl.pallas_call(
        update_kernel,
        name="update",
        out_shape=(
            jax.ShapeDtypeStruct((D, SHARD), F32),
            jax.ShapeDtypeStruct((D, SHARD), F32),
            jax.ShapeDtypeStruct((SUMMED, D), F32),
            jax.ShapeDtypeStruct((8, D), F32),
            jax.ShapeDtypeStruct((8, 128), F32),
        ),
        in_specs=[ANY] * 4 + [VMEM] * 3 + [ANY] * 4 + [VMEM] * 4,
        out_specs=(VMEM,) * 5,
        scratch_shapes=[
            pltpu.VMEM((NW * CAP, D), BF),
            pltpu.VMEM((NW * CAP, SHARD), BF),
            table_f32,
            pltpu.VMEM((D, SHARD), BF),
            table_f32,
            table_f32,
            table_f32,
            table_f32,
            pltpu.VMEM((D, NW * CAP), BF),
        ]
        + exchange(D, SHARD)
        + exchange(SUMMED, D)
        + [pltpu.VMEM((8, D), F32), pltpu.VMEM((NG, 8, D), F32), DMA((8,))]
        + [pieces] * 6
        + [DMA((NG,)), DMA((NG,))]
        + tree_scratch(128),
        compiler_params=params(6, 48),
        cost_estimate=pl.CostEstimate(flops=2 * 10**9, bytes_accessed=3 * 10**7, transcendentals=10**6),
    )(rows, hot, head, head_in, summed, extra, gains, *table, *trunk)


def dot(spec, a, b):
    return jnp.einsum(spec, a, b, preferred_element_type=F32)


def pack(attn, ffn, proj, rows):
    down = proj[:, D:].reshape(18, 3, 512).transpose(1, 0, 2).reshape(54, 512)
    down = jnp.pad(down, ((0, 10), (0, D - 512)))
    return jnp.pad(jnp.concatenate([ffn, down, attn, proj[:, :D]], 0), ((0, rows - PACKED), (0, 0)))


def unpack(packed):
    down = packed[DOWN_AT : DOWN_AT + 54, :512].reshape(3, 18, 512).transpose(1, 0, 2).reshape(18, FF)
    proj = jnp.concatenate([packed[ATTN_AT + 30 : PACKED], down], 1)
    return packed[ATTN_AT : ATTN_AT + 30], packed[FFN_AT:DOWN_AT], proj


def on_device(
    token_ids,
    targets,
    segment_ids,
    row_counts,
    embed_table_master,
    embed_table_first,
    embed_table_second,
    embed_table_anchor,
    embed_table_momentum,
    attn_in_master,
    attn_in_first,
    attn_in_second,
    attn_in_anchor,
    attn_in_momentum,
    ffn_in_master,
    ffn_in_first,
    ffn_in_second,
    ffn_in_anchor,
    ffn_in_momentum,
    proj_out_master,
    proj_out_first,
    proj_out_second,
    proj_out_anchor,
    proj_out_momentum,
    norm_gains_master,
    norm_gains_first,
    norm_gains_second,
    norm_gains_anchor,
    norm_gains_momentum,
):
    ids = token_ids[0]
    gains = norm_gains_master[0]
    table = embed_table_master[0].T.astype(BF)
    weight = jnp.sum(row_counts[0, 0] * jnp.arange(1, 4))
    trunk = tuple(
        (attn.T, ffn.T, proj.T)
        for attn, ffn, proj in (
            (attn_in_master[0], ffn_in_master[0], proj_out_master[0]),
            (attn_in_first[0], ffn_in_first[0], proj_out_first[0]),
            (attn_in_second[0], ffn_in_second[0], proj_out_second[0]),
            (attn_in_anchor, ffn_in_anchor, proj_out_anchor),
            (attn_in_momentum, ffn_in_momentum, proj_out_momentum),
        )
    )
    packed = pack(*trunk[0], PACKED).astype(BF)
    tok = jnp.concatenate(
        [
            token_ids, targets, segment_ids, jnp.broadcast_to(weight, (1, T)), jnp.zeros((4, T), jnp.int32),
        ],
        0,
    )
    got, rows, most_all, table_other, rows_t, packed_all, picks, slot_row, hot, goals, weights = front(
        tok, table, packed
    )
    turns = (jnp.max(most_all) + CAP - 1) // CAP

    def asked_in(turn):
        ids_now = jnp.where(turn > 0, ids, 0)
        owner = ids_now // SHARD
        same = ids_now[:, None] == ids_now[None, :]
        before = jnp.arange(T)[None, :] < jnp.arange(T)[:, None]
        first_seen = ~jnp.any(same & before, 1)
        smaller = (owner[None, :] == owner[:, None]) & (ids_now[None, :] < ids_now[:, None])
        rank = jnp.sum(first_seen[None, :] & smaller, 1, dtype=jnp.int32) - turn * CAP
        slot = jnp.where((rank >= 0) & (rank < CAP), owner * CAP + rank, -1)
        chosen = jnp.arange(NW * CAP)[:, None] == slot[None, :]
        asked = jnp.max(jnp.where(chosen, (ids_now - owner * SHARD)[None, :], -1), 1).reshape(NW, 1, CAP)
        asked = jnp.pad(asked, ((0, 0), (0, 0), (0, 128 - CAP)), constant_values=-1)
        return jnp.pad(asked, ((0, 0), (0, 7), (0, 0))), chosen.astype(BF)

    def more_tokens(carry):
        turn, hidden = carry
        message, chosen = asked_in(turn)
        return turn + 1, hidden + dot("sd,st->td", more_rows(message, table), chosen)

    hidden0 = lax.while_loop(
        lambda carry: carry[0] < turns, more_tokens, (jnp.int32(1), dot("ts,sd->td", picks, rows))
    )[1]

    gains8 = jnp.pad(gains, ((0, 5), (0, 0)))
    rot = jnp.asarray(rope())
    final, *kept = forward(hidden0, packed_all, gains8, rot, tok)
    total = weights[2, 0]
    grad_final, head_own, head_other, loss = head(final, rows_t, table, table_other, goals, weights)
    summed, rows_in, head_in, extra_sum, grad_embedded = back(
        grad_final, kept, packed_all, gains8, rot, tok, slot_row, loss, head_other
    )

    def more_table(carry):
        turn, grad = carry
        message, chosen = asked_in(turn)
        mine = dot("st,dt->sd", chosen, grad_embedded).astype(BF)
        got_now, rows_now = more_grads(message, mine)
        asked = got_now[:, 0, :CAP].reshape(NW * CAP)
        hot_now = (asked[:, None] == jnp.arange(SHARD)[None, :]).astype(BF)
        return turn + 1, grad + dot("sd,sv->dv", rows_now, hot_now)

    head_grad = lax.while_loop(lambda carry: carry[0] < turns, more_table, (jnp.int32(1), head_own))[1]
    kinds = [
        (
            embed_table_master[0].T,
            embed_table_first[0].T,
            embed_table_second[0].T,
            embed_table_anchor.T,
            embed_table_momentum.T,
        )
    ]
    kinds += [tuple(arrays[index] for arrays in trunk) for index in range(3)]
    kinds.append(
        (gains, norm_gains_first[0], norm_gains_second[0], norm_gains_anchor, norm_gains_momentum)
    )
    table_grad, total_t, total_k, total_g, norms = update(
        rows_in,
        hot,
        head_grad,
        head_in,
        summed,
        extra_sum,
        jnp.concatenate([jnp.pad(value, ((0, 5), (0, 0))) for value in kinds[4][:4]], 0),
        kinds[0][:4],
        [pack(*arrays, SUMMED) for arrays in trunk[:4]],
    )
    grads = (table_grad,) + unpack(summed) + (extra_sum[:3],)
    sums = (total_t,) + unpack(total_k) + (total_g[:3],)
    loss_total, norm, factor = extra_sum[3, 0], norms[0, 0], norms[1, 0]
    results = [loss_total.reshape(1), total.reshape(1), norm.reshape(1)]
    for index in range(5):
        _, first, second, anchor, momentum = kinds[index]
        average = sums[index] / NG
        outer = outer_momentum * momentum + average
        weight = anchor - outer_rate * (average + outer_momentum * outer)
        grad = grads[index] * factor
        first = beta_one * first + (1.0 - beta_one) * grad
        second = beta_two * second + (1.0 - beta_two) * grad * grad
        values = [average, outer, weight, first, second]
        if index < 4:
            values = [value.T for value in values]
        results += values[:3] + [values[3][None], values[4][None]]
    return tuple(results)


def solution(mesh):
    in_specs = (
        P("grp", "wide"),
        P("grp", "wide"),
        P("grp", "wide"),
        P("grp", "wide", None),
        P("grp", "wide", None),
        P("grp", "wide", None),
        P("grp", "wide", None),
        P("wide", None),
        P("wide", None),
        P("grp", None, "wide"),
        P("grp", None, "wide"),
        P("grp", None, "wide"),
        P(None, "wide"),
        P(None, "wide"),
        P("grp", None, "wide"),
        P("grp", None, "wide"),
        P("grp", None, "wide"),
        P(None, "wide"),
        P(None, "wide"),
        P("grp", None, "wide"),
        P("grp", None, "wide"),
        P("grp", None, "wide"),
        P(None, "wide"),
        P(None, "wide"),
        P("grp", None, None),
        P("grp", None, None),
        P("grp", None, None),
        P(),
        P(),
    )
    out_specs = (
        P("grp"),
        P("grp"),
        P("grp"),
        P("wide", None),
        P("wide", None),
        P("wide", None),
        P("grp", "wide", None),
        P("grp", "wide", None),
        P(None, "wide"),
        P(None, "wide"),
        P(None, "wide"),
        P("grp", None, "wide"),
        P("grp", None, "wide"),
        P(None, "wide"),
        P(None, "wide"),
        P(None, "wide"),
        P("grp", None, "wide"),
        P("grp", None, "wide"),
        P(None, "wide"),
        P(None, "wide"),
        P(None, "wide"),
        P("grp", None, "wide"),
        P("grp", None, "wide"),
        P(),
        P(),
        P(),
        P("grp", None, None),
        P("grp", None, None),
    )
    return jax.shard_map(
        on_device, mesh=mesh, in_specs=in_specs, out_specs=out_specs, check_vma=False
    )
```

```python
import functools

import jax
import jax.numpy as jnp
import numpy as np
from jax import lax
from jax.experimental import pallas as pl
from jax.experimental.pallas import tpu as pltpu
from jax.sharding import PartitionSpec as P

D = 576
H = 9
KVH = 3
HD = 64
FF = 1536
QKV = 960
STEP = 8
T = 256
SHARD = 1536
NW = 32
NG = 4
CAP = 32
FFN_AT, DOWN_AT, ATTN_AT, PACKED = 0, 96, 160, 208
SUMMED = 224

beta_one = 0.9
beta_two = 0.999
adam_eps = 1e-08
weight_decay = 0.1
inner_rate = 0.02
gain_rate = 0.2
clip_norm = 0.01
penalty_weight = 0.005
outer_rate = 0.7
outer_momentum = 0.9
rope_base = 100000.0
norm_eps = 1e-05
masked_score = -1e30

BF = jnp.bfloat16
F32 = jnp.float32
MESH = pl.DeviceIdType.MESH
VMEM = pl.BlockSpec(memory_space=pltpu.VMEM)
ANY = pl.BlockSpec(memory_space=pl.ANY)
DMA = pltpu.SemaphoreType.DMA
MIB = 1 << 20


def params(collective, mib):
    return pltpu.CompilerParams(
        collective_id=collective, has_side_effects=True, vmem_limit_bytes=mib * MIB
    )


def place():
    me = lax.axis_index("wide")
    return me, me // 8, lax.rem(me // 4, 2), lax.rem(me, 4)


def flat(y, xh, z):
    return y * 8 + xh * 4 + z


def turn4(at, by):
    return lax.rem(at + by, 4)


def remote(src, dst, ssem, rsem, **device):
    return pltpu.make_async_remote_copy(
        src_ref=src,
        dst_ref=dst,
        send_sem=ssem,
        recv_sem=rsem,
        device_id=device,
        device_id_type=MESH,
    )


def greet_wide(me, grp=None, sides=False, meanwhile=None):
    barrier = pltpu.get_barrier_semaphore()

    def one(k, carry):
        pl.semaphore_signal(
            barrier, inc=1, device_id={"wide": lax.rem(me + k, NW)}, device_id_type=MESH
        )
        return carry

    lax.fori_loop(1, NW, one, 0)
    count = NW - 1
    if grp is not None:
        for k in range(1, NG):
            pl.semaphore_signal(
                barrier, inc=1, device_id={"grp": lax.rem(grp + k, NG)}, device_id_type=MESH
            )
        count += NG - 1
    if sides:
        for step in (1, 3):
            pl.semaphore_signal(barrier, inc=1, device_id=beside(step), device_id_type=MESH)
        count += 2
    if meanwhile is not None:
        meanwhile()
    pl.semaphore_wait(barrier, count)


def near_peers(me, y, xh, z):
    peers = [flat(y, xh, turn4(z, k)) for k in (1, 2, 3)] + [flat(turn4(y, k), xh, z) for k in (1, 2, 3)]
    return peers + [flat(y, 1 - xh, z)]


class Tree:
    def __init__(self, hold, land_z, land_y, land_x, ssem, rsem):
        self.hold, self.lands = hold, (land_z, land_y, land_x)
        self.ssem, self.rsem = ssem, rsem
        me, self.y, self.xh, self.z = place()
        self.sent = []

    def send(self, stage):
        y, xh, z = self.y, self.xh, self.z
        at = (z, y, xh)[stage]
        land, src = self.lands[stage], self.hold.at[stage]
        for k in range(1, 2 if stage == 2 else 4):
            if stage == 0:
                to = flat(y, xh, turn4(z, k))
            elif stage == 1:
                to = flat(turn4(y, k), xh, z)
            else:
                to = flat(y, 1 - xh, z)
            copy = remote(src, land.at[at], self.ssem.at[stage, k], self.rsem.at[stage, at], wide=to)
            copy.start()
            self.sent.append(copy)
        land[at] = self.hold[stage]

    def start(self, value):
        self.hold[0] = value
        self.send(0)

    def collect(self, stage):
        at = (self.z, self.y, self.xh)[stage]
        land = self.lands[stage]
        size = 2 if stage == 2 else 4
        for k in range(1, size):
            other = lax.rem(at + k, size)
            remote(
                land.at[other], land.at[other], self.ssem.at[stage, k], self.rsem.at[stage, other],
                wide=flat(self.y, self.xh, self.z),
            ).wait_recv()
        total = land[0]
        for k in range(1, size):
            total = total + land[k]
        return total

    def next(self, stage):
        self.hold[stage + 1] = self.collect(stage)
        self.send(stage + 1)

    def finish(self):
        for copy in self.sent:
            copy.wait_send()


def tree_scratch(lanes):
    return [
        pltpu.VMEM((3, 8, lanes), F32),
        pltpu.VMEM((4, 8, lanes), F32),
        pltpu.VMEM((4, 8, lanes), F32),
        pltpu.VMEM((2, 8, lanes), F32),
        DMA((3, 4)),
        DMA((3, 4)),
    ]


class Scatter:
    def __init__(self, src_at, dst_at, ssem, rsem, me):
        self.src_at, self.dst_at, self.ssem, self.rsem, self.me = src_at, dst_at, ssem, rsem, me

    def copy(self, k):
        peer = lax.rem(self.me + k, NW)
        return remote(
            self.src_at(peer), self.dst_at(self.me), self.ssem.at[k], self.rsem.at[self.me], wide=peer
        )

    def start(self):
        def one(k, carry):
            self.copy(k).start()
            return carry

        lax.fori_loop(1, NW, one, 0)

    def wait_recv(self):
        def one(k, carry):
            peer = lax.rem(self.me + k, NW)
            remote(
                self.src_at(peer), self.dst_at(peer), self.ssem.at[k], self.rsem.at[peer], wide=peer
            ).wait_recv()
            return carry

        lax.fori_loop(1, NW, one, 0)

    def wait_send(self):
        def one(k, carry):
            self.copy(k).wait_send()
            return carry

        lax.fori_loop(1, NW, one, 0)


class Ring:
    def __init__(self, view, sem, bounds, ssem):
        self.view, self.sem, self.bounds = view, sem, bounds
        self.ssem, self.used, self.sent = ssem, 0, []
        self.me, self.y, self.xh, self.z = place()

    def send(self, src, dst, rsem, to):
        copy = remote(src, dst, self.ssem.at[self.used], rsem, wide=flat(to[0], self.xh, to[1]))
        self.used += 1
        copy.start()
        self.sent.append(copy)

    def piece(self, y, z, first, count):
        return self.view(y, z, self.bounds[first], self.bounds[first + count] - self.bounds[first])

    def pass_on(self, y, z, first, count, index, *to):
        piece = self.piece(y, z, first, count)
        for one in to:
            self.send(piece, piece, self.sem(y, z, index), one)

    def landed(self, piece, sem):
        remote(piece, piece, self.ssem.at[0], sem, wide=self.me).wait_recv()

    def wait(self, y, z, first, count, index):
        self.landed(self.piece(y, z, first, count), self.sem(y, z, index))

    def around(self):
        y, z = self.y, self.z
        return y, z, (turn4(y, 1), z), (turn4(y, 3), z), (y, turn4(z, 1)), (y, turn4(z, 3))

    def own(self, src, dst, index):
        y, z, y_up, y_down, z_up, z_down = self.around()
        for to in (y_up, y_down, z_up, z_down):
            self.send(src, dst, self.sem(y, z, index), to)

    def near(self, parts=None):
        y, z, y_up, y_down, z_up, z_down = self.around()
        for at, far, turn, half, sides in (
            (y_down, y_up, 0, 0, (z_up, z_down)),
            (y_up, y_down, 1, 0, (z_up, z_down)),
            (z_down, z_up, 0, 2, (y_up, y_down)),
            (z_up, z_down, 1, 2, (y_up, y_down)),
        ):
            if parts is None:
                self.wait(*at, 0, 4, 0)
            else:
                for part, index in parts:
                    self.landed(part(*at), self.sem(*at, index))
            self.pass_on(*at, turn, 1, turn, far)
            self.pass_on(*at, 2 + turn, 1, 2 + turn, far)
            self.pass_on(*at, half, 2, half, *sides)

    def far(self):
        y, z, y_up, y_down, z_up, z_down = self.around()
        for at, half, sides in (
            ((turn4(y, 2), z), 0, (z_up, z_down)),
            ((y, turn4(z, 2)), 2, (y_up, y_down)),
        ):
            for index in range(4):
                self.wait(*at, index, 1, index)
            self.pass_on(*at, half, 2, half, *sides)

    def cross(self):
        y, z, y_up, y_down, z_up, z_down = self.around()
        for k in (1, 3, 2):
            row, column = turn4(y, k), turn4(z, k)
            self.wait(row, z_down[1], 0, 2, 0)
            self.pass_on(row, z_down[1], 0, 1, 0, z_up)
            self.wait(row, z_up[1], 0, 2, 0)
            self.pass_on(row, z_up[1], 1, 1, 1, z_down)
            self.wait(y_down[0], column, 2, 2, 2)
            self.pass_on(y_down[0], column, 2, 1, 2, y_up)
            self.wait(y_up[0], column, 2, 2, 2)
            self.pass_on(y_up[0], column, 3, 1, 3, y_down)

    def last(self):
        y, z = self.y, self.z
        for k in (1, 3, 2):
            row, column = turn4(y, k), turn4(z, k)
            for index in range(2):
                self.wait(row, turn4(z, 2), index, 1, index)
                self.wait(turn4(y, 2), column, 2 + index, 1, 2 + index)

    def finish(self):
        for copy in self.sent:
            copy.wait_send()


RING_SENDS = 36


def beside(step):
    me, y, xh, z = place()
    grp = lax.axis_index("grp")
    low = grp // 2
    side = lax.rem(xh + low + (0 if step == 1 else 1), 2)
    return {"grp": (1 - low) * 2 + lax.rem(grp, 2), "wide": flat(y, side, z)}


class Relay:
    def __init__(self, sources, stops, ends, ssem, rsem):
        self.sources, self.stops, self.ends, self.ssem, self.rsem = sources, stops, ends, ssem, rsem

    def copy(self, src, dst, at, step):
        return remote(src, dst, self.ssem.at[at], self.rsem.at[at], **beside(step))

    def legs(self, hop):
        for i, step in enumerate((1, 3)):
            src = self.sources[i] if hop == 0 else self.stops[i]
            dst = self.stops[i] if hop == 0 else self.ends[i]
            yield self.copy(src, dst, 2 * hop + i, step)

    def start(self):
        for copy in self.legs(0):
            copy.start()

    def forward(self):
        for first, second in zip(self.legs(0), self.legs(1)):
            first.wait_recv()
            second.start()

    def wait(self):
        for copy in self.legs(1):
            copy.wait_recv()

    def finish(self):
        for hop in (0, 1):
            for copy in self.legs(hop):
                copy.wait_send()


def look_up(got, table, hot, rows, slot_row):
    asked = got[:, slot_row, :].astype(F32)
    asked = jnp.concatenate([asked, jnp.zeros((128 - NW, 128), F32)], 0).T
    step = 8 * CAP
    for first in range(0, NW, 8):
        for d in range(8):
            column = asked[0:CAP, first + d : first + d + 1]
            lanes = lax.broadcasted_iota(jnp.int32, (CAP, SHARD), 1).astype(F32)
            hot[d * CAP : (d + 1) * CAP, :] = jnp.where(lanes == column, 1.0, 0.0).astype(BF)
        picked = lax.dot_general(
            hot[...], table[...], (((1,), (1,)), ((), ())), preferred_element_type=F32
        )
        rows[first * CAP : first * CAP + step, :] = picked.astype(BF)


def slots(at):
    return pl.ds(pl.multiple_of(at * CAP, CAP), CAP)


def turn_over(table, rows, first):
    for c in range(0, SHARD, 256):
        rows[first + c : first + c + 256, :] = table[:, c : c + 256].T


def owner_of(ids):
    return (((ids >> 9) * 171) >> 9).astype(jnp.int32)


def ask_rows(tok, msg, picks, slot_out):
    row = tok[0:1, :]
    column = jnp.broadcast_to(row.astype(F32), (128, T)).T[:, 0:1].astype(jnp.int32)
    row_owner, column_owner = owner_of(row), owner_of(column)
    down = lax.broadcasted_iota(jnp.int32, (T, T), 0)
    across = lax.broadcasted_iota(jnp.int32, (T, T), 1)
    same = row == column

    def count(which, axis):
        return jnp.sum(jnp.where(which, 1.0, 0.0), axis, keepdims=True)

    first_row = count(same & (down < across), 0) == 0.0
    first_column = count(same & (across < down), 1) == 0.0
    near = row_owner == column_owner
    rank_row = count(near & (column < row) & first_column, 0)
    rank_column = count(near & (row < column) & first_row, 1)
    slot_row = jnp.where(rank_row < CAP, row_owner.astype(F32) * CAP + rank_row, -1.0)
    slot_column = jnp.where(rank_column < CAP, column_owner.astype(F32) * CAP + rank_column, -1.0)
    lanes = lax.broadcasted_iota(jnp.int32, (T, NW * CAP), 1).astype(F32)
    hit = lanes == slot_column
    picks[...] = jnp.where(hit, 1.0, 0.0).astype(BF)
    slot_out[...] = jnp.broadcast_to(slot_row, (8, T)).astype(jnp.int32)
    local = (column - column_owner * SHARD).astype(F32)
    asked = jnp.max(jnp.where(hit, local, -1.0), 0, keepdims=True).astype(jnp.int32)
    most = (jnp.max(rank_row, 1, keepdims=True) + 1.0).astype(jnp.int32)
    rest = [
        tok[1:2, 0:128], tok[1:2, 128:256], tok[3:4, 0:128], jnp.broadcast_to(most, (1, 128)),
    ] + [jnp.zeros((1, 128), jnp.int32)] * 3
    for g in range(8):
        msg[g] = jnp.concatenate([asked[:, g * 128 : (g + 1) * 128]] + rest, 0)


def find_rows(got, table, asked_t, hot, rows, part):
    asked = got[:, 0, :].astype(F32)
    asked_t[...] = jnp.concatenate([asked, jnp.full((128 - NW, 128), -1.0, F32)], 0).T
    mine = asked_t[pl.ds(pl.multiple_of(part * CAP, CAP), CAP), :]
    lanes = lax.broadcasted_iota(jnp.int32, (CAP, SHARD), 1).astype(F32)
    for d in range(NW):
        hot[d * CAP : (d + 1) * CAP, :] = jnp.where(lanes == mine[:, d : d + 1], 1.0, 0.0).astype(BF)
    step = 8 * CAP
    for first in range(0, NW * CAP, step):
        picked = lax.dot_general(
            hot[first : first + step, :], table[...], (((1,), (1,)), ((), ())), preferred_element_type=F32
        )
        rows[first : first + step, :] = picked.astype(BF)


def turn_over(table, rows, first):
    for c in range(0, SHARD, 256):
        rows[first + c : first + c + 256, :] = table[:, c : c + 256].T


def front_kernel(
    tok, table, packed, got, emb, most, table_other, rows_t, packed_all, picks, slot_out, hot, goal, weights,
    msg, asked_t, rows, own_most, stops, msg_s, msg_r, emb_s, emb_r, most_s, most_r, swap_s, swap_r,
    ring_s, ring_r, x_sem, local,
):
    me, y, xh, z = place()
    grp = lax.axis_index("grp")
    other = flat(y, 1 - xh, z)
    greet_wide(me, grp, sides=True, meanwhile=lambda: ask_rows(tok, msg, picks, slot_out))
    over = remote(packed, packed_all.at[y, z, xh], x_sem.at[0], x_sem.at[1], wide=other)
    over.start()
    ask = Scatter(lambda p: msg.at[p // 4], lambda p: got.at[p], msg_s, msg_r, me)
    ask.start()
    got[me] = msg[me // 4]
    ring = Ring(
        lambda Y, Z, first, count: packed_all.at[Y, Z, :, pl.ds(first, count)],
        lambda Y, Z, index: ring_r.at[Y, Z, index],
        (0, 48, 96, 144, 208),
        ring_s,
    )
    ring.own(packed, packed_all.at[y, z, xh], 0)
    keep = pltpu.make_async_copy(packed, packed_all.at[y, z, xh], local.at[0])
    keep.start()
    halves = (pl.ds(0, D // 2), pl.ds(D // 2, D // 2))
    trade = Relay(
        [table.at[half] for half in halves],
        [stops.at[i] for i in range(2)],
        [table_other.at[half] for half in halves],
        swap_s,
        swap_r,
    )
    trade.start()
    over.wait_recv()
    ring.own(packed_all.at[y, z, 1 - xh], packed_all.at[y, z, 1 - xh], 4)
    ask.wait_recv()
    find_rows(got, table, asked_t, hot, rows, lax.rem(me, 4))
    ring.near(
        [
            (lambda Y, Z: packed_all.at[Y, Z, xh], 0),
            (lambda Y, Z: packed_all.at[Y, Z, 1 - xh], 4),
        ]
    )
    reply = Scatter(lambda p: rows.at[slots(p)], lambda p: emb.at[slots(p)], emb_s, emb_r, me)
    reply.start()
    emb[slots(me), :] = rows[slots(me), :]
    turn_over(table, rows_t, 0)
    largest = jnp.max(got[:, 4, :], 0, keepdims=True)
    own_most[...] = jnp.broadcast_to(largest, (8, 128))
    most[grp] = own_most[...]
    told = []
    for k in range(1, NG):
        to = lax.rem(grp + k, NG)
        told.append(remote(own_most, most.at[grp], most_s.at[k], most_r.at[grp], grp=to))
        told[-1].start()
    total = jnp.sum(got[:, 3, :].astype(F32), 0, keepdims=True)
    total = jnp.concatenate([total, total], 1) * T
    plain = tok[3:4, :].astype(F32)
    weights[...] = jnp.concatenate([plain / total, plain, total] + [jnp.zeros((1, T), F32)] * 5, 0)

    def place_goal(j, carry):
        from_dev = flat(j // 4, xh, lax.rem(j, 4))
        goals = jnp.concatenate([got[from_dev, 1:2, :], got[from_dev, 2:3, :]], 1)
        near, far = goals - me * SHARD, goals - other * SHARD
        at = jnp.where((far >= 0) & (far < SHARD), far + SHARD, -1)
        at = jnp.where((near >= 0) & (near < SHARD), near, at)
        goal[j] = jnp.broadcast_to(at, (8, T))
        return carry

    lax.fori_loop(0, 16, place_goal, 0)
    ring.far()
    trade.forward()
    ring.cross()
    reply.wait_recv()
    for k in range(1, NG):
        to = lax.rem(grp + k, NG)
        remote(own_most, most.at[to], most_s.at[k], most_r.at[to], grp=to).wait_recv()
    trade.wait()
    turn_over(table_other, rows_t, SHARD)
    ring.last()
    keep.wait()
    over.wait_send()
    ask.wait_send()
    reply.wait_send()
    trade.finish()
    for copy in told:
        copy.wait_send()
    ring.finish()


def front(tok, table, packed):
    return pl.pallas_call(
        front_kernel,
        name="front",
        out_shape=(
            jax.ShapeDtypeStruct((NW, 8, 128), jnp.int32),
            jax.ShapeDtypeStruct((NW * CAP, D), BF),
            jax.ShapeDtypeStruct((NG, 8, 128), jnp.int32),
            jax.ShapeDtypeStruct((D, SHARD), BF),
            jax.ShapeDtypeStruct((2 * SHARD, D), BF),
            jax.ShapeDtypeStruct((4, 4, 2, PACKED, D), BF),
            jax.ShapeDtypeStruct((T, NW * CAP), BF),
            jax.ShapeDtypeStruct((8, T), jnp.int32),
            jax.ShapeDtypeStruct((NW * CAP, SHARD), BF),
            jax.ShapeDtypeStruct((16, 8, T), jnp.int32),
            jax.ShapeDtypeStruct((8, T), F32),
        ),
        in_specs=[VMEM, VMEM, ANY],
        out_specs=(VMEM, VMEM, VMEM, VMEM, VMEM, ANY) + (VMEM,) * 5,
        scratch_shapes=[
            pltpu.VMEM((8, 8, 128), jnp.int32),
            pltpu.VMEM((128, 128), F32),
            pltpu.VMEM((NW * CAP, D), BF),
            pltpu.VMEM((8, 128), jnp.int32),
            pltpu.VMEM((2, D // 2, SHARD), BF),
            DMA((NW,)),
            DMA((NW,)),
            DMA((NW,)),
            DMA((NW,)),
            DMA((NG,)),
            DMA((NG,)),
            DMA((4,)),
            DMA((4,)),
            DMA((RING_SENDS + 4,)),
            DMA((4, 4, 5)),
            DMA((2,)),
            DMA((1,)),
        ],
        compiler_params=params(1, 60),
        cost_estimate=pl.CostEstimate(flops=2 * 10**9, bytes_accessed=3 * 10**7, transcendentals=0),
    )(tok, table, packed)


ORDER = tuple((i // 8) * 8 + (i % 2) * 4 + (i // 2) % 4 for i in range(NW))


def spread_rows(used, stride, at, repeat=1):
    picks = np.zeros((NW * stride, NW * used), np.float32)
    for i, w in enumerate(ORDER):
        for j in range(repeat):
            for r in range(used):
                picks[i * stride + at + j * used + r, w * used + r] = 1.0
    return picks


def rope():
    half = HD // 2
    freqs = np.float32(rope_base) ** (-(np.arange(half, dtype=np.float32) * np.float32(2.0)) / np.float32(HD))
    angles = freqs.astype(np.float32)[:, None] * np.arange(T, dtype=np.float32)[None, :]
    return np.concatenate([np.cos(angles), np.sin(angles)], 0).astype(np.float32)


def turned(values):
    return values.T


def gain_columns(gains):
    return jnp.concatenate([gains[...], jnp.zeros((120, D), F32)], 0).T


def rms(values, gain):
    scale = lax.rsqrt(jnp.mean(values * values, 0, keepdims=True) + norm_eps)
    return values * scale * gain


def rms_back(values, gain, grad):
    scale = lax.rsqrt(jnp.mean(values * values, 0, keepdims=True) + norm_eps)
    pulled = grad * gain
    middle = jnp.mean(values * pulled, 0, keepdims=True)
    back = scale * pulled - values * (scale * scale * scale) * middle
    return back, jnp.sum(grad * values * scale, 1, keepdims=True)


def mask_of(tok):
    row = tok[2:3, :]
    column = jnp.broadcast_to(row.astype(F32), (128, T)).T[:, 0:1].astype(jnp.int32)
    down = lax.broadcasted_iota(jnp.int32, (T, T), 0)
    across = lax.broadcasted_iota(jnp.int32, (T, T), 1)
    return (down <= across) & (row == column)


def mm(a, b):
    return jnp.dot(a, b, preferred_element_type=F32)


def mm_nt(a, b):
    return lax.dot_general(a, b, (((1,), (1,)), ((), ())), preferred_element_type=F32)


def mm_tn(a, b):
    return lax.dot_general(a, b, (((0,), (0,)), ((), ())), preferred_element_type=F32)


def rotated(x, rot):
    cosine, sine = rot[0:32, :], rot[32:64, :]
    one, two = x[0:32, :], x[32:64, :]
    return jnp.concatenate([one * cosine - two * sine, two * cosine + one * sine], 0)


def unrotated(x, rot):
    cosine, sine = rot[0:32, :], rot[32:64, :]
    one, two = x[0:32, :], x[32:64, :]
    return jnp.concatenate([one * cosine + two * sine, two * cosine - one * sine], 0)


def load_trunk(packed, ffn, down, attn, sem):
    loads = [
        pltpu.make_async_copy(packed.at[:, :, :, ATTN_AT:PACKED], attn, sem.at[0]),
        pltpu.make_async_copy(packed.at[:, :, :, FFN_AT:DOWN_AT], ffn, sem.at[1]),
        pltpu.make_async_copy(packed.at[:, :, :, DOWN_AT:ATTN_AT, 0:512], down, sem.at[2]),
    ]
    for load in loads:
        load.start()
    return loads


TRUNK_SCRATCH = [
    pltpu.VMEM((4, 4, 2, 96, D), BF),
    pltpu.VMEM((4, 4, 2, 64, 512), BF),
    pltpu.VMEM((4, 4, 2, 48, D), BF),
    DMA((3,)),
]


def forward_kernel(
    more, emb, picks, packed, gains, rot, tok,
    final, h0, n1, q, k, v, lse, att, h1, n2, gate_up, inner, h2,
    ffn, down, attn, sem, mixed,
):
    loads = load_trunk(packed, ffn, down, attn, sem)
    columns = gain_columns(gains)
    allowed = mask_of(tok)
    start = turned(mm(picks[...], emb[...]) + more[...])
    h0[...] = start
    normed = rms(start, columns[:, 0:1]).astype(BF)
    n1[...] = normed
    loads[0].wait()
    rows48 = attn[...].reshape(NW * 48, D)
    product = mm(rows48, normed)
    for i, w in enumerate(ORDER):
        mixed[w * 30 : w * 30 + 30, :] = product[i * 48 : i * 48 + 30, :]
    for kv in range(KVH):
        k[kv * HD : (kv + 1) * HD, :] = rotated(
            mixed[D + kv * HD : D + (kv + 1) * HD, :], rot[...]
        ).astype(BF)
        at = D + (KVH + kv) * HD
        v[kv * HD : (kv + 1) * HD, :] = mixed[at : at + HD, :].astype(BF)
    logs = []
    for h in range(H):
        kv = h // (H // KVH)
        query = rotated(mixed[h * HD : (h + 1) * HD, :], rot[...]).astype(BF)
        q[h * HD : (h + 1) * HD, :] = query
        scores = mm_tn(k[kv * HD : (kv + 1) * HD, :], query) * HD ** (-0.5)
        scores = jnp.where(allowed, scores, masked_score)
        top = jnp.max(scores, 0, keepdims=True)
        power = jnp.exp(scores - top)
        total = jnp.sum(power, 0, keepdims=True)
        probs = (power / total).astype(BF)
        att[h * HD : (h + 1) * HD, :] = mm(v[kv * HD : (kv + 1) * HD, :], probs).astype(BF)
        logs.append(top + jnp.log(total))
    lse[...] = jnp.concatenate(logs + [jnp.zeros((16 - H, T), F32)], 0)
    product = mm(rows48, att[...])
    for i, w in enumerate(ORDER):
        mixed[w * 18 : w * 18 + 18, :] = product[i * 48 + 30 : i * 48 + 48, :]
    middle = start + mixed[0:D, :]
    h1[...] = middle
    normed = rms(middle, columns[:, 1:2]).astype(BF)
    n2[...] = normed
    loads[1].wait()
    gate_up[...] = mm(ffn[...].reshape(NW * 96, D), normed)
    for i in range(NW // 2):
        gate = gate_up[i * 96 : (i + 1) * 96, :]
        up = gate_up[FF + i * 96 : FF + (i + 1) * 96, :]
        w = ORDER[i]
        inner[w * 96 : (w + 1) * 96, :] = (gate / (1.0 + jnp.exp(-gate)) * up).astype(BF)
    loads[2].wait()
    rows64 = down[...].reshape(NW * 64, 512)
    for j in range(3):
        product = mm(rows64, inner[j * 512 : (j + 1) * 512, :])
        for i, w in enumerate(ORDER):
            piece = product[i * 64 + j * 18 : i * 64 + j * 18 + 18, :]
            if j:
                mixed[w * 18 : w * 18 + 18, :] += piece
            else:
                mixed[w * 18 : w * 18 + 18, :] = piece
    last = middle + mixed[0:D, :]
    h2[...] = last
    final[...] = rms(last, columns[:, 2:3]).astype(BF)


def forward(more, emb, picks, packed, gains, rot, tok):
    def out(rows, kind):
        return jax.ShapeDtypeStruct((rows, T), kind)

    return pl.pallas_call(
        forward_kernel,
        name="forward",
        out_shape=(
            out(D, BF), out(D, F32), out(D, BF), out(D, BF), out(KVH * HD, BF), out(KVH * HD, BF), out(16, F32),
            out(D, BF), out(D, F32), out(D, BF), out(2 * FF, F32), out(FF, BF), out(D, F32),
        ),
        in_specs=[VMEM, VMEM, VMEM, ANY, VMEM, VMEM, VMEM],
        out_specs=(VMEM,) * 13,
        scratch_shapes=TRUNK_SCRATCH + [pltpu.VMEM((QKV, T), F32)],
        compiler_params=pltpu.CompilerParams(vmem_limit_bytes=60 * MIB),
        cost_estimate=pl.CostEstimate(flops=4 * 10**9, bytes_accessed=2 * 10**7, transcendentals=10**6),
    )(more, emb, picks, packed, gains, rot, tok)


def more_rows_kernel(msg, table, got, emb, hot, rows, msg_s, msg_r, emb_s, emb_r):
    me = lax.axis_index("wide")
    greet_wide(me)
    ask = Scatter(lambda p: msg.at[p], lambda p: got.at[p], msg_s, msg_r, me)
    ask.start()
    got[me] = msg[me]
    ask.wait_recv()
    look_up(got, table, hot, rows, 0)
    reply = Scatter(lambda p: rows.at[slots(p)], lambda p: emb.at[slots(p)], emb_s, emb_r, me)
    reply.start()
    emb[slots(me), :] = rows[slots(me), :]
    reply.wait_recv()
    ask.wait_send()
    reply.wait_send()


def more_rows(msg, table):
    return pl.pallas_call(
        more_rows_kernel,
        name="more_rows",
        out_shape=(
            jax.ShapeDtypeStruct((NW, 8, 128), jnp.int32),
            jax.ShapeDtypeStruct((NW * CAP, D), BF),
        ),
        in_specs=[VMEM, VMEM],
        out_specs=(VMEM, VMEM),
        scratch_shapes=[pltpu.VMEM((8 * CAP, SHARD), BF), pltpu.VMEM((NW * CAP, D), BF)]
        + [DMA((NW,))] * 4,
        compiler_params=params(2, 40),
    )(msg, table)[1]


def more_grads_kernel(msg, rows, got, out, msg_s, msg_r, row_s, row_r):
    me = lax.axis_index("wide")
    greet_wide(me)
    ask = Scatter(lambda p: msg.at[p], lambda p: got.at[p], msg_s, msg_r, me)
    ask.start()
    give = Scatter(lambda p: rows.at[slots(p)], lambda p: out.at[slots(p)], row_s, row_r, me)
    give.start()
    got[me] = msg[me]
    out[slots(me), :] = rows[slots(me), :]
    ask.wait_recv()
    give.wait_recv()
    ask.wait_send()
    give.wait_send()


def more_grads(msg, rows):
    return pl.pallas_call(
        more_grads_kernel,
        name="more_grads",
        out_shape=(
            jax.ShapeDtypeStruct((NW, 8, 128), jnp.int32),
            jax.ShapeDtypeStruct((NW * CAP, D), BF),
        ),
        in_specs=[VMEM, VMEM],
        out_specs=(VMEM, VMEM),
        scratch_shapes=[DMA((NW,))] * 4,
        compiler_params=params(3, 20),
    )(msg, rows)


VOC = 2 * SHARD
TOK = 16 * T
CH = 512
NCH = VOC // CH
QUART = D // 4


def cols(j):
    return pl.ds(pl.multiple_of(j * T, T), T)


def head_kernel(
    final, rows_t, table, table_other, goal, weights,
    grad_final, head_own, head_other, loss,
    fall, expo, even, odd_grad, tops, stat, stat_in, coef, coef_in, parts,
    part_a, part_b, whole_a, whole_b, sum_a, sum_b, part_a2, part_b2, whole_a2, whole_b2,
    g_s, g_r, st_s, st_r, co_s, co_r, a_s, b_s, pa_r, pb_r, wa_r, wb_r, a2_s, b2_s, a2_r, b2_r,
):
    me, y, xh, z = place()
    mine = y * 4 + z

    def dev(j):
        return flat(j // 4, xh, lax.rem(j, 4))

    barrier = pltpu.get_barrier_semaphore()

    def greet(k, carry):
        pl.semaphore_signal(
            barrier, inc=1, device_id={"wide": dev(lax.rem(mine + k, 16))}, device_id_type=MESH
        )
        return carry

    lax.fori_loop(1, 16, greet, 0)
    pl.semaphore_wait(barrier, 15)

    sent = []

    def send(src, dst, ssem, rsem, to):
        copy = remote(src, dst, ssem, rsem, wide=to)
        copy.start()
        sent.append(copy)

    def arrived(dst, rsem):
        remote(dst, dst, g_s.at[0], rsem, wide=dev(mine)).wait_recv()

    ring = Ring(
        lambda Y, Z, first, count: fall.at[pl.ds(first, count), cols(Y * 4 + Z)],
        lambda Y, Z, index: g_r.at[Y * 4 + Z, index],
        tuple(QUART * k for k in range(5)),
        g_s,
    )
    ring.own(final, fall.at[:, cols(mine)], 0)
    fall[:, cols(mine)] = final[...]

    def logits(j):
        seen = fall[:, cols(j)]
        goals = goal[j]
        group, hit = goals >> 3, jnp.zeros((8, T), F32)
        tip, weight = [], []
        ahead = mm(rows_t[0:CH, :], seen)
        for c in range(NCH):
            part = ahead
            if c + 1 < NCH:
                ahead = mm(rows_t[(c + 1) * CH : (c + 2) * CH, :], seen)
            top = jnp.max(part, 0, keepdims=True)
            power = jnp.exp(part - top)
            for r in range(CH // 8):
                hit = jnp.where(group == c * (CH // 8) + r, part[8 * r : 8 * r + 8, :], hit)
            expo[c * CH : (c + 1) * CH, cols(j)] = power.astype(BF)
            tip.append(top)
            weight.append(jnp.sum(power, 0, keepdims=True))
        spot = lax.broadcasted_iota(jnp.int32, (8, T), 0)
        hit = jnp.sum(jnp.where(spot == (goals & 7), hit, 0.0), 0, keepdims=True)
        top = functools.reduce(jnp.maximum, tip)
        total = sum(w * jnp.exp(t - top) for w, t in zip(weight, tip))
        zero = jnp.zeros((1, T), F32)
        tops[j] = jnp.concatenate(tip + [zero] * (8 - NCH), 0)
        stat[j] = jnp.concatenate([top, total, hit] + [zero] * 5, 0)

    def tell(j):
        return remote(stat.at[j], stat_in.at[mine], st_s.at[j], st_r.at[mine], wide=dev(j))

    def block(dy, dz):
        return turn4(y, dy) * 4 + turn4(z, dz)

    def forward(offsets):
        def one(k, carry):
            j = block(*offsets(k))
            logits(j)
            tell(j).start()
            return carry

        return one

    def odd(k):
        return 1 + 2 * lax.rem(k, 2)

    logits(mine)
    stat_in[mine] = stat[mine]
    ring.near()
    lax.fori_loop(0, 4, forward(lambda k: ((1 - k // 2) * odd(k), (k // 2) * odd(k))), 0)
    ring.far()
    lax.fori_loop(0, 2, forward(lambda k: (2 * (1 - k), 2 * k)), 0)
    ring.cross()
    lax.fori_loop(0, 4, forward(lambda k: (odd(k // 2), odd(k))), 0)
    ring.last()
    lax.fori_loop(
        0,
        4,
        forward(lambda k: (2 * (1 - k // 2) + odd(k) * (k // 2), odd(k) * (1 - k // 2) + 2 * (k // 2))),
        0,
    )
    forward(lambda k: (2, 2))(0, 0)

    def hear(k, carry):
        j = lax.rem(mine + k, 16)
        arrived(stat_in.at[j], st_r.at[j])
        return carry

    lax.fori_loop(1, 16, hear, 0)
    tip, weight, hit = stat_in[:, 0, :], stat_in[:, 1, :], stat_in[:, 2, :]
    top = jnp.max(tip, 0, keepdims=True)
    lse = top + jnp.log(jnp.sum(weight * jnp.exp(tip - top), 0, keepdims=True))
    picked = jnp.sum(hit, 0, keepdims=True)
    share, plain = weights[0:1, :], weights[1:2, :]
    zero = jnp.zeros((1, T), F32)
    coef[...] = jnp.concatenate(
        [lse, share * (1.0 + 2.0 * penalty_weight * lse), share] + [zero] * 5, 0
    )
    loss[...] = jnp.concatenate(
        [plain * (lse - picked + penalty_weight * lse * lse)] + [zero] * 7, 0
    )
    coef_in[mine] = coef[...]

    def spread(k):
        j = lax.rem(mine + k, 16)
        return remote(coef, coef_in.at[mine], co_s.at[k], co_r.at[mine], wide=dev(j))

    def spread_start(k, carry):
        spread(k).start()
        return carry

    lax.fori_loop(1, 16, spread_start, 0)

    up, down = 1, 3
    z_to = {step: flat(y, xh, turn4(z, step)) for step in (up, down)}
    y_to = {step: flat(turn4(y, step), xh, z) for step in (up, down)}

    def piece_a(j, index):
        row = j // 4
        return remote(
            parts.at[j, pl.ds(index * QUART, QUART)], part_a.at[index, row],
            a_s.at[j, index], pa_r.at[index, row], wide=z_to[(up, down)[index]],
        )

    def piece_b(j, index):
        column = lax.rem(j, 4)
        return remote(
            parts.at[j, pl.ds((2 + index) * QUART, QUART)], part_b.at[index, column],
            b_s.at[j, index], pb_r.at[index, column], wide=y_to[(up, down)[index]],
        )

    def half_a(j, index):
        row = j // 4
        return remote(
            parts.at[j, pl.ds(0, 2 * QUART)], whole_a.at[index, row],
            a_s.at[j, 0], wa_r.at[index, row], wide=z_to[(up, down)[index]],
        )

    def half_b(j, index):
        column = lax.rem(j, 4)
        return remote(
            parts.at[j, pl.ds(2 * QUART, 2 * QUART)], whole_b.at[index, column],
            b_s.at[j, 0], wb_r.at[index, column], wide=y_to[(up, down)[index]],
        )

    def offsets(k):
        return lax.rem(2 + k // 4, 4), lax.rem(2 + k, 4)

    def post(k):
        dy, dz = offsets(k)
        j = block(dy, dz)

        @pl.when(dz == 2)
        def _():
            piece_a(j, 0).start()
            piece_a(j, 1).start()

        @pl.when(dy == 2)
        def _():
            piece_b(j, 0).start()
            piece_b(j, 1).start()

        for index, step in enumerate((up, down)):

            @pl.when(dz == step)
            def _():
                row = j // 4
                arrived(part_a.at[index, row], pa_r.at[index, row])
                rows = pl.ds(index * QUART, QUART)
                total = parts[j, rows, :].astype(F32) + part_a[index, row].astype(F32)
                parts[j, rows, :] = total.astype(BF)
                half_a(j, index).start()

            @pl.when(dy == step)
            def _():
                column = lax.rem(j, 4)
                arrived(part_b.at[index, column], pb_r.at[index, column])
                rows = pl.ds((2 + index) * QUART, QUART)
                total = parts[j, rows, :].astype(F32) + part_b[index, column].astype(F32)
                parts[j, rows, :] = total.astype(BF)
                half_b(j, index).start()

    def await_coef(k):
        j = block(*offsets(k))

        @pl.when(k != 10)
        def _():
            arrived(coef_in.at[j], co_r.at[j])

    def grad_logits(k, out):
        j = block(*offsets(k))
        lse, soft, pick = coef_in[j, 0:1, :], coef_in[j, 1:2, :], coef_in[j, 2:3, :]
        goals = goal[j]
        group = goals >> 3
        pick = jnp.where(lax.broadcasted_iota(jnp.int32, (8, T), 0) == (goals & 7), pick, 0.0)
        for c in range(NCH):
            scale = soft * jnp.exp(tops[j, c : c + 1, :] - lse)
            power = expo[c * CH : (c + 1) * CH, cols(j)].astype(F32)
            spot = lax.broadcasted_iota(jnp.int32, (CH // 8, 8, T), 0) + c * (CH // 8)
            drop = jnp.where(spot == group[None], pick[None], 0.0).reshape(CH, T)
            grad = (power * scale - drop).astype(BF)
            out[c * CH : (c + 1) * CH, :] = grad
            expo[c * CH : (c + 1) * CH, cols(j)] = grad

    def to_tokens(k, grad):
        product = mm(table[...], grad[0:SHARD, :]) + mm(table_other[...], grad[SHARD:VOC, :])
        parts[block(*offsets(k))] = product.astype(BF)

    def backward(i, carry):
        for k, now, ahead in ((2 * i, even, odd_grad), (2 * i + 1, odd_grad, even)):
            await_coef(k + 1)
            to_tokens(k, now)
            grad_logits(k + 1, ahead)

            @pl.when(k > 0)
            def _():
                post(k - 1)

        return carry

    await_coef(0)
    grad_logits(0, even)
    lax.fori_loop(0, 7, backward, 0)
    await_coef(15)
    to_tokens(14, even)
    grad_logits(15, odd_grad)
    post(13)
    to_tokens(15, odd_grad)
    post(14)
    post(15)

    def head_chunk(c):
        return lax.dot_general(
            fall[...],
            expo[pl.ds(pl.multiple_of(c * 256, 256), 256), :],
            (((1,), (1,)), ((), ())),
            preferred_element_type=F32,
        )

    def other_chunk(c, carry):
        head_other[:, cols(c)] = head_chunk(c + SHARD // 256).astype(BF)
        return carry

    def own_chunk(c, carry):
        head_own[:, cols(c)] = head_chunk(c)
        return carry

    lax.fori_loop(0, SHARD // 256, other_chunk, 0)

    kinds = (
        (whole_a, wa_r, sum_a, part_a2, whole_a2, a2_s, a2_r, y_to, 0),
        (whole_b, wb_r, sum_b, part_b2, whole_b2, b2_s, b2_r, z_to, 2 * QUART),
    )
    for d in (2, 1, 3, 0):
        for kind, (whole, w_r, total, part2, whole2, s2, r2, to, base) in enumerate(kinds):
            at = turn4(y if kind == 0 else z, d)
            j = at * 4 + z if kind == 0 else y * 4 + at
            acc = parts[j, base : base + 2 * QUART, :].astype(F32)
            for index in range(2):
                arrived(whole.at[index, at], w_r.at[index, at])
                acc = acc + whole[index, at].astype(F32)
            if d == 0:
                grad_final[base : base + 2 * QUART, :] = acc
            else:
                total[d - 1] = acc.astype(BF)
            if d == 2:
                for index, step in enumerate((up, down)):
                    piece = total.at[1, pl.ds(index * QUART, QUART)]
                    send(piece, part2.at[index], s2.at[index], r2.at[index], to[step])
    lax.fori_loop(0, SHARD // 512, own_chunk, 0)
    for kind, (whole, w_r, total, part2, whole2, s2, r2, to, base) in enumerate(kinds):
        for index, step in enumerate((up, down)):
            arrived(part2.at[index], r2.at[index])
            rows = pl.ds(index * QUART, QUART)
            added = total[step - 1, rows, :].astype(F32) + part2[index].astype(F32)
            total[step - 1, rows, :] = added.astype(BF)
            send(total.at[step - 1], whole2.at[index], s2.at[2 + index], r2.at[2 + index], to[step])
    lax.fori_loop(SHARD // 512, SHARD // 256, own_chunk, 0)
    for kind, (whole, w_r, total, part2, whole2, s2, r2, to, base) in enumerate(kinds):
        for index in range(2):
            arrived(whole2.at[index], r2.at[2 + index])
        grad_final[base : base + 2 * QUART, :] += whole2[0].astype(F32) + whole2[1].astype(F32)

    def finish(k, carry):
        j = lax.rem(mine + k, 16)
        tell(j).wait_send()
        spread(k).wait_send()
        return carry

    lax.fori_loop(1, 16, finish, 0)
    for copy in sent:
        copy.wait_send()
    ring.finish()

    def finish_pieces(k, carry):
        row, column = block(k, 2), block(2, k)
        piece_a(row, 0).wait_send()
        piece_a(row, 1).wait_send()
        piece_b(column, 0).wait_send()
        piece_b(column, 1).wait_send()
        for index, step in enumerate((up, down)):
            half_a(block(k, step), index).wait_send()
            half_b(block(step, k), index).wait_send()
        return carry

    lax.fori_loop(0, 4, finish_pieces, 0)


def head(final, rows_t, table, table_other, goal, weights):
    return pl.pallas_call(
        head_kernel,
        name="head",
        out_shape=(
            jax.ShapeDtypeStruct((D, T), F32),
            jax.ShapeDtypeStruct((D, SHARD), F32),
            jax.ShapeDtypeStruct((D, SHARD), BF),
            jax.ShapeDtypeStruct((8, T), F32),
        ),
        in_specs=[VMEM] * 6,
        out_specs=(VMEM,) * 4,
        scratch_shapes=[
            pltpu.VMEM((D, TOK), BF),
            pltpu.VMEM((VOC, TOK), BF),
            pltpu.VMEM((VOC, T), BF),
            pltpu.VMEM((VOC, T), BF),
            pltpu.VMEM((16, 8, T), F32),
            pltpu.VMEM((16, 8, T), F32),
            pltpu.VMEM((16, 8, T), F32),
            pltpu.VMEM((8, T), F32),
            pltpu.VMEM((16, 8, T), F32),
            pltpu.VMEM((16, D, T), BF),
            pltpu.VMEM((2, 4, QUART, T), BF),
            pltpu.VMEM((2, 4, QUART, T), BF),
            pltpu.VMEM((2, 4, 2 * QUART, T), BF),
            pltpu.VMEM((2, 4, 2 * QUART, T), BF),
            pltpu.VMEM((3, 2 * QUART, T), BF),
            pltpu.VMEM((3, 2 * QUART, T), BF),
            pltpu.VMEM((2, QUART, T), BF),
            pltpu.VMEM((2, QUART, T), BF),
            pltpu.VMEM((2, 2 * QUART, T), BF),
            pltpu.VMEM((2, 2 * QUART, T), BF),
            DMA((RING_SENDS,)),
            DMA((16, 4)),
            DMA((16,)),
            DMA((16,)),
            DMA((16,)),
            DMA((16,)),
            DMA((16, 2)),
            DMA((16, 2)),
            DMA((2, 4)),
            DMA((2, 4)),
            DMA((2, 4)),
            DMA((2, 4)),
            DMA((4,)),
            DMA((4,)),
            DMA((4,)),
            DMA((4,)),
        ],
        compiler_params=params(4, 61),
        cost_estimate=pl.CostEstimate(
            flops=6 * VOC * TOK * D, bytes_accessed=2 * 10**7, transcendentals=VOC * TOK
        ),
    )(final, rows_t, table, table_other, goal, weights)


class Reduce:
    def __init__(self, parts, base, sizes, along_z, refs):
        (
            self.first, part_a, part_b, self.whole1, self.second, next_a, next_b, self.whole2,
            self.third, self.stop, self.third_in, self.s, self.r,
        ) = refs
        self.part1, self.part2 = (part_a, part_b), (next_a, next_b)
        self.parts, self.base, self.sizes, self.along_z = parts, base, sizes, along_z
        self.rows = (pl.ds(0, sizes[0]), pl.ds(sizes[0], sizes[1]), pl.ds(0, sum(sizes)))
        self.me, self.y, self.xh, self.z = place()
        self.sent = []

    def send(self, src, dst, at, **to):
        copy = remote(src, dst, self.s.at[at], self.r.at[at], **to)
        copy.start()
        self.sent.append(copy)

    def wait(self, dst, at):
        remote(dst, dst, self.s.at[at], self.r.at[at], wide=self.me).wait_recv()

    def item1(self, step, which):
        rows = pl.ds(self.base + self.rows[which].start, self.rows[which].size)
        if self.along_z:
            return (slice(None), turn4(self.z, step), slice(None), rows)
        return (turn4(self.y, step), slice(None), slice(None), rows)

    def item2(self, step, which):
        return (turn4(self.y if self.along_z else self.z, step), slice(None), self.rows[which])

    def to(self, stage, step):
        if self.along_z == (stage == 1):
            return flat(self.y, self.xh, turn4(self.z, step))
        return flat(turn4(self.y, step), self.xh, self.z)

    def split(self, stage, ref, item, part, base):
        for index, step in enumerate((1, 3)):
            self.send(ref.at[item(2, index)], part[index], base + index, wide=self.to(stage, step))

    def join(self, stage, ref, item, part, whole, base):
        for index, step in enumerate((1, 3)):
            self.wait(part[index], base + index)
            at = item(step, index)
            ref[at] = (ref[at].astype(F32) + part[index][...].astype(F32)).astype(BF)
            self.send(ref.at[item(step, 2)], whole.at[index], base + 2 + index, wide=self.to(stage, step))

    def add(self, ref, item, whole, base):
        acc = ref[item(0, 2)].astype(F32)
        for index in range(2):
            self.wait(whole.at[index], base + 2 + index)
            acc = acc + whole[index].astype(F32)
        return acc

    def one(self):
        self.split(1, self.parts, self.item1, self.part1, 0)

    def two(self):
        self.join(1, self.parts, self.item1, self.part1, self.whole1, 0)

    def three(self):
        self.first[...] = self.add(self.parts, self.item1, self.whole1, 0).astype(BF)
        self.split(2, self.first, self.item2, self.part2, 4)

    def four(self):
        self.join(2, self.first, self.item2, self.part2, self.whole2, 4)

    def five(self):
        self.second[...] = self.add(self.first, self.item2, self.whole2, 4)
        self.third[...] = self.second[1 - self.xh].astype(BF)
        self.send(self.third, self.stop, 8, **beside(1 if self.along_z else 3))

    def six(self):
        self.wait(self.stop, 8)
        self.send(self.stop, self.third_in, 9, **beside(1 if self.along_z else 3))

    def total(self):
        self.wait(self.third_in, 9)
        return self.second[self.xh] + self.third_in[...].astype(F32)

    def finish(self):
        for copy in self.sent:
            copy.wait_send()


STREAMS = ((0, (48, 32), True), (80, (48, 32), False), (160, (16, 16), True), (192, (16, 16), False))


def reduce_scratch():
    shapes = []
    for _, sizes, _ in STREAMS:
        half = sum(sizes)
        shapes += [
            pltpu.VMEM((4, 2, half, D), BF),
            pltpu.VMEM((4, 2, sizes[0], D), BF),
            pltpu.VMEM((4, 2, sizes[1], D), BF),
            pltpu.VMEM((2, 4, 2, half, D), BF),
            pltpu.VMEM((2, half, D), F32),
            pltpu.VMEM((2, sizes[0], D), BF),
            pltpu.VMEM((2, sizes[1], D), BF),
            pltpu.VMEM((2, 2, half, D), BF),
            pltpu.VMEM((half, D), BF),
            pltpu.VMEM((half, D), BF),
            pltpu.VMEM((half, D), BF),
            DMA((10,)),
            DMA((10,)),
        ]
    return shapes


def back_kernel(
    grad_final, h0, n1, q, k, v, lse, att, h1, n2, gate_up, inner, h2,
    packed, gains, rot, tok, slot_row, loss, head_other, lay_attn_in, lay_out_in, lay_down_in,
    summed, rows_in, head_in, extra_sum, grad_embedded,
    ffn, down, attn, sem, lay_attn, lay_out, lay_down, lay_sem, parts, rows, grad_up, grad_mixed, spread, stops,
    row_s, row_r, swap_s, swap_r, hold, land_z, land_y, land_x, tree_s, tree_r, *reducers,
):
    me, y, xh, z = place()
    lays = [
        pltpu.make_async_copy(src, dst, lay_sem.at[i])
        for i, (src, dst) in enumerate(
            ((lay_down_in, lay_down), (lay_out_in, lay_out), (lay_attn_in, lay_attn))
        )
    ]
    lays[0].start()
    loads = load_trunk(packed, ffn, down, attn, sem)
    lays[1].start()
    lays[2].start()
    greet_wide(me, sides=True)
    halves = (pl.ds(0, D // 2), pl.ds(D // 2, D // 2))
    trade = Relay(
        [head_other.at[half] for half in halves],
        [stops.at[i] for i in range(2)],
        [head_in.at[half] for half in halves],
        swap_s,
        swap_r,
    )
    trade.start()
    streams = [
        Reduce(parts, base, sizes, along, reducers[13 * i : 13 * i + 13])
        for i, (base, sizes, along) in enumerate(STREAMS)
    ]
    early, late = streams[:2], streams[2:]
    columns = gain_columns(gains)

    grad_h2, gain3 = rms_back(h2[...], columns[:, 2:3], grad_final[...])
    lays[0].wait()
    spread[...] = mm(lay_down[...], grad_h2.astype(BF)).astype(BF)
    chunk = lax.broadcasted_iota(jnp.int32, (NW * 64, T), 0) & 63
    zero = jnp.zeros((NW * 64, T), BF)
    wide = jnp.concatenate(
        [
            jnp.where((chunk >= 18 * j) & (chunk < 18 * (j + 1)), spread[...].astype(F32), 0.0).astype(BF)
            for j in range(3)
        ],
        1,
    )
    inners = jnp.concatenate([inner[j * 512 : (j + 1) * 512, :] for j in range(3)], 1)
    grad_down = mm_nt(wide, inners).astype(BF).reshape(4, 4, 2, 64, 512)
    parts[:, :, :, DOWN_AT:ATTN_AT, 0:512] = grad_down
    parts[:, :, :, DOWN_AT:ATTN_AT, 512:D] = jnp.zeros((4, 4, 2, 64, D - 512), BF)
    loads[2].wait()
    grad_inner = mm_tn(down[...].reshape(NW * 64, 512), wide)
    for i in range(NW // 2):
        w = ORDER[i]
        gate = gate_up[i * 96 : (i + 1) * 96, :]
        up = gate_up[FF + i * 96 : FF + (i + 1) * 96, :]
        pieces = []
        for at in range(w * 96, w * 96 + 96, 32):
            j, r = at // 512, at % 512
            pieces.append(grad_inner[r : r + 32, j * T : (j + 1) * T])
        grad = jnp.concatenate(pieces, 0)
        sigmoid = 1.0 / (1.0 + jnp.exp(-gate))
        slope = sigmoid * (1.0 + gate * (1.0 - sigmoid))
        grad_up[i * 96 : (i + 1) * 96, :] = (grad * up * slope).astype(BF)
        grad_up[FF + i * 96 : FF + (i + 1) * 96, :] = (grad * (gate * sigmoid)).astype(BF)
    parts[:, :, :, FFN_AT:DOWN_AT, :] = mm_nt(grad_up[...], n2[...]).astype(BF).reshape(4, 4, 2, 96, D)
    for stream in early:
        stream.one()
    loads[1].wait()
    grad_normed = turned(mm_tn(grad_up[...], ffn[...].reshape(NW * 96, D)))
    part, gain2 = rms_back(h1[...], columns[:, 1:2], grad_normed)
    grad_h1 = grad_h2 + part
    lays[1].wait()
    out_rows = mm(lay_out[...], grad_h1.astype(BF)).astype(BF)
    loads[0].wait()
    rows48 = attn[...].reshape(NW * 48, D)
    grad_att = turned(mm_tn(out_rows, rows48)).astype(BF)
    for stream in early:
        stream.two()

    allowed = mask_of(tok)
    group = H // KVH
    for kv in range(KVH):
        keys = k[kv * HD : (kv + 1) * HD, :]
        values = v[kv * HD : (kv + 1) * HD, :]
        grad_k, grad_v = jnp.zeros((HD, T), F32), jnp.zeros((HD, T), F32)
        for h in range(kv * group, (kv + 1) * group):
            query = q[h * HD : (h + 1) * HD, :]
            grad_out = grad_att[h * HD : (h + 1) * HD, :]
            scores = mm_tn(keys, query) * HD ** (-0.5)
            scores = jnp.where(allowed, scores, masked_score)
            soft = jnp.exp(scores - lse[h : h + 1, :])
            grad_probs = mm_tn(values, grad_out)
            mean = jnp.sum(soft * grad_probs, 0, keepdims=True)
            grad_scores = (soft * (grad_probs - mean)).astype(BF)
            grad_q = mm(keys, grad_scores) * HD ** (-0.5)
            grad_mixed[h * HD : (h + 1) * HD, :] = unrotated(grad_q, rot[...]).astype(BF)
            grad_k = grad_k + mm_nt(query, grad_scores) * HD ** (-0.5)
            grad_v = grad_v + mm_nt(grad_out, soft.astype(BF))
        at = D + kv * HD
        grad_mixed[at : at + HD, :] = unrotated(grad_k, rot[...]).astype(BF)
        at = D + (KVH + kv) * HD
        grad_mixed[at : at + HD, :] = grad_v.astype(BF)
    for stream in early:
        stream.three()
    lays[2].wait()
    attn_rows = mm(lay_attn[...], grad_mixed[...]).astype(BF)
    both = jnp.concatenate([attn_rows, out_rows], 1)
    seen = jnp.concatenate([n1[...], att[...]], 1)
    parts[:, :, :, ATTN_AT:PACKED, :] = mm_nt(both, seen).astype(BF).reshape(4, 4, 2, 48, D)
    parts[:, :, :, PACKED:SUMMED, :] = jnp.zeros((4, 4, 2, SUMMED - PACKED, D), BF)
    for stream in late:
        stream.one()
    grad_normed = turned(mm_tn(attn_rows, rows48))
    part, gain1 = rms_back(h0[...], columns[:, 0:1], grad_normed)
    grad_h0 = (grad_h1 + part).astype(BF)
    grad_embedded[...] = grad_h0
    slot = lax.broadcasted_iota(jnp.int32, (NW * CAP, T), 0)
    picks = jnp.where(slot == slot_row[0:1, :], 1.0, 0.0).astype(BF)
    rows[...] = mm_nt(picks, grad_h0).astype(BF)
    give = Scatter(lambda p: rows.at[slots(p)], lambda p: rows_in.at[slots(p)], row_s, row_r, me)
    give.start()
    for stream in early:
        stream.four()
    trade.forward()
    lane = lax.broadcasted_iota(jnp.int32, (D, 128), 1)
    table = jnp.where(lane == 0, gain1, jnp.where(lane == 1, gain2, jnp.where(lane == 2, gain3, 0.0)))
    lost = jnp.sum(loss[0:1, :], 1, keepdims=True)
    table = table.T[0:8, :]
    tree = Tree(hold, land_z, land_y, land_x, tree_s, tree_r)
    tree.start(jnp.where(lax.broadcasted_iota(jnp.int32, (8, D), 0) == 3, lost, table))
    rows_in[slots(me), :] = rows[slots(me), :]
    for stream in late:
        stream.two()
    for stream in early:
        stream.five()
    tree.next(0)
    for stream in late:
        stream.three()
    for stream in late:
        stream.four()
    tree.next(1)
    for stream in early:
        stream.six()
    for stream in late:
        stream.five()
    extra_sum[...] = tree.collect(2)
    for stream in late:
        stream.six()
    for stream in streams:
        summed[stream.base : stream.base + sum(stream.sizes), :] = stream.total()
    give.wait_recv()
    trade.wait()
    for stream in streams:
        stream.finish()
    give.wait_send()
    tree.finish()
    trade.finish()


def back(grad_final, kept, packed, gains, rot, tok, slot_row, loss, head_other):
    lays = [
        jnp.asarray(spread_rows(30, 48, 0), BF),
        jnp.asarray(spread_rows(18, 48, 30), BF),
        jnp.asarray(spread_rows(18, 64, 0, 3), BF),
    ]
    return pl.pallas_call(
        back_kernel,
        name="back",
        out_shape=(
            jax.ShapeDtypeStruct((SUMMED, D), F32),
            jax.ShapeDtypeStruct((NW * CAP, D), BF),
            jax.ShapeDtypeStruct((D, SHARD), BF),
            jax.ShapeDtypeStruct((8, D), F32),
            jax.ShapeDtypeStruct((D, T), BF),
        ),
        in_specs=[VMEM] * 13 + [ANY] + [VMEM] * 5 + [ANY] * 4,
        out_specs=(VMEM, VMEM, ANY, VMEM, VMEM),
        scratch_shapes=TRUNK_SCRATCH
        + [
            pltpu.VMEM((NW * 48, QKV), BF),
            pltpu.VMEM((NW * 48, D), BF),
            pltpu.VMEM((NW * 64, D), BF),
            DMA((3,)),
            pltpu.VMEM((4, 4, 2, SUMMED, D), BF),
            pltpu.VMEM((NW * CAP, D), BF),
            pltpu.VMEM((2 * FF, T), BF),
            pltpu.VMEM((QKV, T), BF),
            pltpu.VMEM((NW * 64, T), BF),
            pltpu.VMEM((2, D // 2, SHARD), BF),
        ]
        + [DMA((NW,)), DMA((NW,)), DMA((4,)), DMA((4,))]
        + tree_scratch(D)
        + reduce_scratch(),
        compiler_params=params(5, 60),
        cost_estimate=pl.CostEstimate(flops=10**10, bytes_accessed=3 * 10**7, transcendentals=10**6),
    )(grad_final, *kept, packed, gains, rot, tok, slot_row, loss, head_other, *lays)


def adam_update(weight, grad, first, second, rate, decay):
    first = beta_one * first + (1.0 - beta_one) * grad
    second = beta_two * second + (1.0 - beta_two) * grad * grad
    ratio = first / (1.0 - beta_one**STEP) / (jnp.sqrt(second / (1.0 - beta_two**STEP)) + adam_eps)
    return (weight - rate * (ratio + decay * weight), first, second)


def adam_diff(weight, grad, first, second, anchor, rate, decay):
    return anchor - adam_update(weight, grad, first, second, rate, decay)[0]


PIECES = ((0, 0, 96), (0, 96, 96), (0, 192, 96), (1, 0, 112))


def update_kernel(
    rows, hot, head, head_in, summed, extra, gains, tm, tf, ts, ta, km, kf, ks, ka,
    table_grad, total_t, total_k, total_g, norms,
    v_rows, v_hot, v_head, v_head_in, vm, vf, vs, va, flipped,
    one_t, one_t_in, two_t, two_t_in, one_k, one_k_in, two_k, two_k_in, gains_out, gains_in,
    load_sem, one_s, one_r, two_s, two_r, three_s, three_r, gains_s, gains_r,
    hold, land_z, land_y, land_x, tree_s, tree_r,
):
    me, y, xh, z = place()
    grp = lax.axis_index("grp")
    core, x = lax.rem(grp, 2), grp // 2
    near, far = x * 2 + 1 - core, (1 - x) * 2 + core
    loads = [
        pltpu.make_async_copy(src, dst, load_sem.at[i])
        for i, (src, dst) in enumerate(
            zip((rows, hot, head, head_in, tm, tf, ts, ta), (v_rows, v_hot, v_head, v_head_in, vm, vf, vs, va))
        )
    ]
    for load in loads:
        load.start()
    barrier = pltpu.get_barrier_semaphore()
    for peer in near_peers(me, y, xh, z):
        pl.semaphore_signal(barrier, inc=1, device_id={"wide": peer}, device_id_type=MESH)
    for k in range(1, NG):
        pl.semaphore_signal(
            barrier, inc=1, device_id={"grp": lax.rem(grp + k, NG)}, device_id_type=MESH
        )
    pl.semaphore_wait(barrier, 7 + NG - 1)
    for load in loads[:4]:
        load.wait()
    for c in range(0, NW * CAP, 256):
        flipped[:, c : c + 256] = v_rows[c : c + 256, :].T
    squares = jnp.zeros((1, 256), F32)
    for c in range(0, SHARD, 256):
        part = v_head[:, c : c + 256] + v_head_in[:, c : c + 256].astype(F32)
        part = part + mm(flipped[...], v_hot[:, c : c + 256])
        table_grad[:, c : c + 256] = part
        squares = squares + jnp.sum(part * part, 0, keepdims=True)
    squares = jnp.sum(squares, 1, keepdims=True)
    trunk = jnp.sum(summed[...] * summed[...], 0, keepdims=True)
    squares = squares + jnp.sum(trunk, 1, keepdims=True)
    tree = Tree(hold, land_z, land_y, land_x, tree_s, tree_r)
    tree.start(jnp.broadcast_to(squares, (8, 128)))
    gain_grads = extra[0:3, :]
    gain_squares = jnp.sum(jnp.sum(gain_grads * gain_grads, 0, keepdims=True), 1, keepdims=True)
    tree.next(0)
    for load in loads[4:]:
        load.wait()
    tree.next(1)
    norm = jnp.sqrt(tree.collect(2)[0:1, 0:1] + gain_squares)
    factor = jnp.minimum(1.0, clip_norm / norm)
    down = lax.broadcasted_iota(jnp.int32, (8, 128), 0)
    norms[...] = jnp.where(down == 0, norm, factor)

    parts = (
        (vm, table_grad, vf, vs, va, total_t, D // 2, one_t, one_t_in, two_t, two_t_in),
        (km, summed, kf, ks, ka, total_k, SUMMED // 2, one_k, one_k_in, two_k, two_k_in),
    )
    sent = []

    def span(which, at, count, side):
        half = parts[which][6]
        return pl.ds(pl.multiple_of(side * half + at, 16), count)

    def diff(which, at, count, side):
        m, g, f, s2, a = parts[which][:5]
        rows = span(which, at, count, side)
        return adam_diff(
            m[rows, :], g[rows, :] * factor, f[rows, :], s2[rows, :], a[rows, :], inner_rate, weight_decay
        )

    for i, (which, at, count) in enumerate(PIECES):
        one, one_in = parts[which][7:9]
        rows = pl.ds(at, count)
        one[rows, :] = diff(which, at, count, 1 - core).astype(BF)
        copy = remote(one.at[rows], one_in.at[rows], one_s.at[i], one_r.at[i], grp=near)
        copy.start()
        sent.append(copy)
    for i, (which, at, count) in enumerate(PIECES):
        one, one_in, two, two_in = parts[which][7:11]
        rows = pl.ds(at, count)
        own = diff(which, at, count, core)
        sent[i].wait_recv()
        two[rows, :] = (own + one_in[rows, :].astype(F32)).astype(BF)
        copy = remote(two.at[rows], two_in.at[rows], two_s.at[i], two_r.at[i], grp=far)
        copy.start()
        sent.append(copy)
    gains_out[0:3, :] = adam_diff(
        gains[0:3, :], gain_grads * factor, gains[8:11, :], gains[16:19, :], gains[24:27, :], gain_rate, 0.0
    )
    gains_out[3:8, :] = jnp.zeros((5, D), F32)
    told = []
    for k in range(1, NG):
        to = lax.rem(grp + k, NG)
        told.append(remote(gains_out, gains_in.at[grp], gains_s.at[k], gains_r.at[grp], grp=to))
        told[-1].start()
    gains_in[grp] = gains_out[...]
    for i, (which, at, count) in enumerate(PIECES):
        total, two, two_in = parts[which][5], parts[which][9], parts[which][10]
        rows = pl.ds(at, count)
        sent[len(PIECES) + i].wait_recv()
        kept = span(which, at, count, core)
        total[kept, :] = two[rows, :].astype(F32) + two_in[rows, :].astype(F32)
        copy = remote(total.at[kept], total.at[kept], three_s.at[i], three_r.at[i], grp=near)
        copy.start()
        sent.append(copy)
    for k in range(1, NG):
        other = lax.rem(grp + k, NG)
        remote(
            gains_out, gains_in.at[other], gains_s.at[k], gains_r.at[other], grp=other
        ).wait_recv()
    total_g[...] = (gains_in[0] + gains_in[1]) + (gains_in[2] + gains_in[3])
    for i, (which, at, count) in enumerate(PIECES):
        away = parts[which][5].at[span(which, at, count, 1 - core)]
        remote(away, away, three_s.at[i], three_r.at[i], grp=near).wait_recv()
    for copy in sent + told:
        copy.wait_send()
    tree.finish()


def update(rows, hot, head, head_in, summed, extra, gains, table, trunk):
    def exchange(size, lanes):
        return [pltpu.VMEM((size // 2, lanes), BF)] * 4

    table_f32 = pltpu.VMEM((D, SHARD), F32)
    pieces = DMA((len(PIECES),))
    return pl.pallas_call(
        update_kernel,
        name="update",
        out_shape=(
            jax.ShapeDtypeStruct((D, SHARD), F32),
            jax.ShapeDtypeStruct((D, SHARD), F32),
            jax.ShapeDtypeStruct((SUMMED, D), F32),
            jax.ShapeDtypeStruct((8, D), F32),
            jax.ShapeDtypeStruct((8, 128), F32),
        ),
        in_specs=[ANY] * 4 + [VMEM] * 3 + [ANY] * 4 + [VMEM] * 4,
        out_specs=(VMEM,) * 5,
        scratch_shapes=[
            pltpu.VMEM((NW * CAP, D), BF),
            pltpu.VMEM((NW * CAP, SHARD), BF),
            table_f32,
            pltpu.VMEM((D, SHARD), BF),
            table_f32,
            table_f32,
            table_f32,
            table_f32,
            pltpu.VMEM((D, NW * CAP), BF),
        ]
        + exchange(D, SHARD)
        + exchange(SUMMED, D)
        + [pltpu.VMEM((8, D), F32), pltpu.VMEM((NG, 8, D), F32), DMA((8,))]
        + [pieces] * 6
        + [DMA((NG,)), DMA((NG,))]
        + tree_scratch(128),
        compiler_params=params(6, 48),
        cost_estimate=pl.CostEstimate(flops=2 * 10**9, bytes_accessed=3 * 10**7, transcendentals=10**6),
    )(rows, hot, head, head_in, summed, extra, gains, *table, *trunk)


def dot(spec, a, b):
    return jnp.einsum(spec, a, b, preferred_element_type=F32)


def pack(attn, ffn, proj, rows):
    down = proj[:, D:].reshape(18, 3, 512).transpose(1, 0, 2).reshape(54, 512)
    down = jnp.pad(down, ((0, 10), (0, D - 512)))
    return jnp.pad(jnp.concatenate([ffn, down, attn, proj[:, :D]], 0), ((0, rows - PACKED), (0, 0)))


def unpack(packed):
    down = packed[DOWN_AT : DOWN_AT + 54, :512].reshape(3, 18, 512).transpose(1, 0, 2).reshape(18, FF)
    proj = jnp.concatenate([packed[ATTN_AT + 30 : PACKED], down], 1)
    return packed[ATTN_AT : ATTN_AT + 30], packed[FFN_AT:DOWN_AT], proj


def on_device(
    token_ids,
    targets,
    segment_ids,
    row_counts,
    embed_table_master,
    embed_table_first,
    embed_table_second,
    embed_table_anchor,
    embed_table_momentum,
    attn_in_master,
    attn_in_first,
    attn_in_second,
    attn_in_anchor,
    attn_in_momentum,
    ffn_in_master,
    ffn_in_first,
    ffn_in_second,
    ffn_in_anchor,
    ffn_in_momentum,
    proj_out_master,
    proj_out_first,
    proj_out_second,
    proj_out_anchor,
    proj_out_momentum,
    norm_gains_master,
    norm_gains_first,
    norm_gains_second,
    norm_gains_anchor,
    norm_gains_momentum,
):
    ids = token_ids[0]
    gains = norm_gains_master[0]
    table = embed_table_master[0].T.astype(BF)
    weight = jnp.sum(row_counts[0, 0] * jnp.arange(1, 4))
    trunk = tuple(
        (attn.T, ffn.T, proj.T)
        for attn, ffn, proj in (
            (attn_in_master[0], ffn_in_master[0], proj_out_master[0]),
            (attn_in_first[0], ffn_in_first[0], proj_out_first[0]),
            (attn_in_second[0], ffn_in_second[0], proj_out_second[0]),
            (attn_in_anchor, ffn_in_anchor, proj_out_anchor),
            (attn_in_momentum, ffn_in_momentum, proj_out_momentum),
        )
    )
    packed = pack(*trunk[0], PACKED).astype(BF)
    tok = jnp.concatenate(
        [
            token_ids, targets, segment_ids, jnp.broadcast_to(weight, (1, T)), jnp.zeros((4, T), jnp.int32),
        ],
        0,
    )
    got, rows, most_all, table_other, rows_t, packed_all, picks, slot_row, hot, goals, weights = front(
        tok, table, packed
    )
    turns = (jnp.max(most_all) + CAP - 1) // CAP

    def asked_in(turn):
        ids_now = jnp.where(turn > 0, ids, 0)
        owner = ids_now // SHARD
        same = ids_now[:, None] == ids_now[None, :]
        before = jnp.arange(T)[None, :] < jnp.arange(T)[:, None]
        first_seen = ~jnp.any(same & before, 1)
        smaller = (owner[None, :] == owner[:, None]) & (ids_now[None, :] < ids_now[:, None])
        rank = jnp.sum(first_seen[None, :] & smaller, 1, dtype=jnp.int32) - turn * CAP
        slot = jnp.where((rank >= 0) & (rank < CAP), owner * CAP + rank, -1)
        chosen = jnp.arange(NW * CAP)[:, None] == slot[None, :]
        asked = jnp.max(jnp.where(chosen, (ids_now - owner * SHARD)[None, :], -1), 1).reshape(NW, 1, CAP)
        asked = jnp.pad(asked, ((0, 0), (0, 0), (0, 128 - CAP)), constant_values=-1)
        return jnp.pad(asked, ((0, 0), (0, 7), (0, 0))), chosen.astype(BF)

    def more_tokens(carry):
        turn, hidden = carry
        message, chosen = asked_in(turn)
        return turn + 1, hidden + dot("sd,st->td", more_rows(message, table), chosen)

    more = lax.while_loop(
        lambda carry: carry[0] < turns, more_tokens, (jnp.int32(1), jnp.zeros((T, D), F32))
    )[1]

    gains8 = jnp.pad(gains, ((0, 5), (0, 0)))
    rot = jnp.asarray(rope())
    final, *kept = forward(more, rows, picks, packed_all, gains8, rot, tok)
    total = weights[2, 0]
    grad_final, head_own, head_other, loss = head(final, rows_t, table, table_other, goals, weights)
    summed, rows_in, head_in, extra_sum, grad_embedded = back(
        grad_final, kept, packed_all, gains8, rot, tok, slot_row, loss, head_other
    )

    def more_table(carry):
        turn, grad = carry
        message, chosen = asked_in(turn)
        mine = dot("st,dt->sd", chosen, grad_embedded).astype(BF)
        got_now, rows_now = more_grads(message, mine)
        asked = got_now[:, 0, :CAP].reshape(NW * CAP)
        hot_now = (asked[:, None] == jnp.arange(SHARD)[None, :]).astype(BF)
        return turn + 1, grad + dot("sd,sv->dv", rows_now, hot_now)

    head_grad = lax.while_loop(lambda carry: carry[0] < turns, more_table, (jnp.int32(1), head_own))[1]
    kinds = [
        (
            embed_table_master[0].T,
            embed_table_first[0].T,
            embed_table_second[0].T,
            embed_table_anchor.T,
            embed_table_momentum.T,
        )
    ]
    kinds += [tuple(arrays[index] for arrays in trunk) for index in range(3)]
    kinds.append(
        (gains, norm_gains_first[0], norm_gains_second[0], norm_gains_anchor, norm_gains_momentum)
    )
    table_grad, total_t, total_k, total_g, norms = update(
        rows_in,
        hot,
        head_grad,
        head_in,
        summed,
        extra_sum,
        jnp.concatenate([jnp.pad(value, ((0, 5), (0, 0))) for value in kinds[4][:4]], 0),
        kinds[0][:4],
        [pack(*arrays, SUMMED) for arrays in trunk[:4]],
    )
    grads = (table_grad,) + unpack(summed) + (extra_sum[:3],)
    sums = (total_t,) + unpack(total_k) + (total_g[:3],)
    loss_total, norm, factor = extra_sum[3, 0], norms[0, 0], norms[1, 0]
    results = [loss_total.reshape(1), total.reshape(1), norm.reshape(1)]
    for index in range(5):
        _, first, second, anchor, momentum = kinds[index]
        average = sums[index] / NG
        outer = outer_momentum * momentum + average
        weight = anchor - outer_rate * (average + outer_momentum * outer)
        grad = grads[index] * factor
        first = beta_one * first + (1.0 - beta_one) * grad
        second = beta_two * second + (1.0 - beta_two) * grad * grad
        values = [average, outer, weight, first, second]
        if index < 4:
            values = [value.T for value in values]
        results += values[:3] + [values[3][None], values[4][None]]
    return tuple(results)


def solution(mesh):
    in_specs = (
        P("grp", "wide"),
        P("grp", "wide"),
        P("grp", "wide"),
        P("grp", "wide", None),
        P("grp", "wide", None),
        P("grp", "wide", None),
        P("grp", "wide", None),
        P("wide", None),
        P("wide", None),
        P("grp", None, "wide"),
        P("grp", None, "wide"),
        P("grp", None, "wide"),
        P(None, "wide"),
        P(None, "wide"),
        P("grp", None, "wide"),
        P("grp", None, "wide"),
        P("grp", None, "wide"),
        P(None, "wide"),
        P(None, "wide"),
        P("grp", None, "wide"),
        P("grp", None, "wide"),
        P("grp", None, "wide"),
        P(None, "wide"),
        P(None, "wide"),
        P("grp", None, None),
        P("grp", None, None),
        P("grp", None, None),
        P(),
        P(),
    )
    out_specs = (
        P("grp"),
        P("grp"),
        P("grp"),
        P("wide", None),
        P("wide", None),
        P("wide", None),
        P("grp", "wide", None),
        P("grp", "wide", None),
        P(None, "wide"),
        P(None, "wide"),
        P(None, "wide"),
        P("grp", None, "wide"),
        P("grp", None, "wide"),
        P(None, "wide"),
        P(None, "wide"),
        P(None, "wide"),
        P("grp", None, "wide"),
        P("grp", None, "wide"),
        P(None, "wide"),
        P(None, "wide"),
        P(None, "wide"),
        P("grp", None, "wide"),
        P("grp", None, "wide"),
        P(),
        P(),
        P(),
        P("grp", None, None),
        P("grp", None, None),
    )
    return jax.shard_map(
        on_device, mesh=mesh, in_specs=in_specs, out_specs=out_specs, check_vma=False
    )
```

```python
import functools

import jax
import jax.numpy as jnp
import numpy as np
from jax import lax
from jax.experimental import pallas as pl
from jax.experimental.pallas import tpu as pltpu
from jax.sharding import PartitionSpec as P

D = 576
H = 9
KVH = 3
HD = 64
FF = 1536
QKV = 960
STEP = 8
T = 256
SHARD = 1536
NW = 32
NG = 4
CAP = 32
FFN_AT, DOWN_AT, ATTN_AT, PACKED = 0, 96, 160, 208
SUMMED = 224

beta_one = 0.9
beta_two = 0.999
adam_eps = 1e-08
weight_decay = 0.1
inner_rate = 0.02
gain_rate = 0.2
clip_norm = 0.01
penalty_weight = 0.005
outer_rate = 0.7
outer_momentum = 0.9
rope_base = 100000.0
norm_eps = 1e-05
masked_score = -1e30

BF = jnp.bfloat16
F32 = jnp.float32
MESH = pl.DeviceIdType.MESH
VMEM = pl.BlockSpec(memory_space=pltpu.VMEM)
ANY = pl.BlockSpec(memory_space=pl.ANY)
DMA = pltpu.SemaphoreType.DMA
MIB = 1 << 20


def params(collective, mib):
    return pltpu.CompilerParams(
        collective_id=collective, has_side_effects=True, vmem_limit_bytes=mib * MIB
    )


def place():
    me = lax.axis_index("wide")
    return me, me // 8, lax.rem(me // 4, 2), lax.rem(me, 4)


def flat(y, xh, z):
    return y * 8 + xh * 4 + z


def turn4(at, by):
    return lax.rem(at + by, 4)


def remote(src, dst, ssem, rsem, **device):
    return pltpu.make_async_remote_copy(
        src_ref=src,
        dst_ref=dst,
        send_sem=ssem,
        recv_sem=rsem,
        device_id=device,
        device_id_type=MESH,
    )


def greet_wide(me, grp=None, sides=False, meanwhile=None):
    barrier = pltpu.get_barrier_semaphore()

    def one(k, carry):
        pl.semaphore_signal(
            barrier, inc=1, device_id={"wide": lax.rem(me + k, NW)}, device_id_type=MESH
        )
        return carry

    lax.fori_loop(1, NW, one, 0)
    count = NW - 1
    if grp is not None:
        for k in range(1, NG):
            pl.semaphore_signal(
                barrier, inc=1, device_id={"grp": lax.rem(grp + k, NG)}, device_id_type=MESH
            )
        count += NG - 1
    if sides:
        for step in (1, 3):
            pl.semaphore_signal(barrier, inc=1, device_id=beside(step), device_id_type=MESH)
        count += 2
    if meanwhile is not None:
        meanwhile()
    pl.semaphore_wait(barrier, count)


def near_peers(me, y, xh, z):
    peers = [flat(y, xh, turn4(z, k)) for k in (1, 2, 3)] + [flat(turn4(y, k), xh, z) for k in (1, 2, 3)]
    return peers + [flat(y, 1 - xh, z)]


class Tree:
    def __init__(self, hold, land_z, land_y, land_x, ssem, rsem):
        self.hold, self.lands = hold, (land_z, land_y, land_x)
        self.ssem, self.rsem = ssem, rsem
        me, self.y, self.xh, self.z = place()
        self.sent = []

    def send(self, stage):
        y, xh, z = self.y, self.xh, self.z
        at = (z, y, xh)[stage]
        land, src = self.lands[stage], self.hold.at[stage]
        for k in range(1, 2 if stage == 2 else 4):
            if stage == 0:
                to = flat(y, xh, turn4(z, k))
            elif stage == 1:
                to = flat(turn4(y, k), xh, z)
            else:
                to = flat(y, 1 - xh, z)
            copy = remote(src, land.at[at], self.ssem.at[stage, k], self.rsem.at[stage, at], wide=to)
            copy.start()
            self.sent.append(copy)
        land[at] = self.hold[stage]

    def start(self, value):
        self.hold[0] = value
        self.send(0)

    def collect(self, stage):
        at = (self.z, self.y, self.xh)[stage]
        land = self.lands[stage]
        size = 2 if stage == 2 else 4
        for k in range(1, size):
            other = lax.rem(at + k, size)
            remote(
                land.at[other], land.at[other], self.ssem.at[stage, k], self.rsem.at[stage, other],
                wide=flat(self.y, self.xh, self.z),
            ).wait_recv()
        total = land[0]
        for k in range(1, size):
            total = total + land[k]
        return total

    def next(self, stage):
        self.hold[stage + 1] = self.collect(stage)
        self.send(stage + 1)

    def finish(self):
        for copy in self.sent:
            copy.wait_send()


def tree_scratch(lanes):
    return [
        pltpu.VMEM((3, 8, lanes), F32),
        pltpu.VMEM((4, 8, lanes), F32),
        pltpu.VMEM((4, 8, lanes), F32),
        pltpu.VMEM((2, 8, lanes), F32),
        DMA((3, 4)),
        DMA((3, 4)),
    ]


class Scatter:
    def __init__(self, src_at, dst_at, ssem, rsem, me):
        self.src_at, self.dst_at, self.ssem, self.rsem, self.me = src_at, dst_at, ssem, rsem, me

    def copy(self, k):
        peer = lax.rem(self.me + k, NW)
        return remote(
            self.src_at(peer), self.dst_at(self.me), self.ssem.at[k], self.rsem.at[self.me], wide=peer
        )

    def start(self):
        def one(k, carry):
            self.copy(k).start()
            return carry

        lax.fori_loop(1, NW, one, 0)

    def wait_recv(self):
        def one(k, carry):
            peer = lax.rem(self.me + k, NW)
            remote(
                self.src_at(peer), self.dst_at(peer), self.ssem.at[k], self.rsem.at[peer], wide=peer
            ).wait_recv()
            return carry

        lax.fori_loop(1, NW, one, 0)

    def wait_send(self):
        def one(k, carry):
            self.copy(k).wait_send()
            return carry

        lax.fori_loop(1, NW, one, 0)


class Ring:
    def __init__(self, view, sem, bounds, ssem):
        self.view, self.sem, self.bounds = view, sem, bounds
        self.ssem, self.used, self.sent = ssem, 0, []
        self.me, self.y, self.xh, self.z = place()

    def send(self, src, dst, rsem, to):
        copy = remote(src, dst, self.ssem.at[self.used], rsem, wide=flat(to[0], self.xh, to[1]))
        self.used += 1
        copy.start()
        self.sent.append(copy)

    def piece(self, y, z, first, count):
        return self.view(y, z, self.bounds[first], self.bounds[first + count] - self.bounds[first])

    def pass_on(self, y, z, first, count, index, *to):
        piece = self.piece(y, z, first, count)
        for one in to:
            self.send(piece, piece, self.sem(y, z, index), one)

    def landed(self, piece, sem):
        remote(piece, piece, self.ssem.at[0], sem, wide=self.me).wait_recv()

    def wait(self, y, z, first, count, index):
        self.landed(self.piece(y, z, first, count), self.sem(y, z, index))

    def around(self):
        y, z = self.y, self.z
        return y, z, (turn4(y, 1), z), (turn4(y, 3), z), (y, turn4(z, 1)), (y, turn4(z, 3))

    def own(self, src, dst, index):
        y, z, y_up, y_down, z_up, z_down = self.around()
        for to in (y_up, y_down, z_up, z_down):
            self.send(src, dst, self.sem(y, z, index), to)

    def near(self, parts=None):
        y, z, y_up, y_down, z_up, z_down = self.around()
        for at, far, turn, half, sides in (
            (y_down, y_up, 0, 0, (z_up, z_down)),
            (y_up, y_down, 1, 0, (z_up, z_down)),
            (z_down, z_up, 0, 2, (y_up, y_down)),
            (z_up, z_down, 1, 2, (y_up, y_down)),
        ):
            if parts is None:
                self.wait(*at, 0, 4, 0)
            else:
                for part, index in parts:
                    self.landed(part(*at), self.sem(*at, index))
            self.pass_on(*at, turn, 1, turn, far)
            self.pass_on(*at, 2 + turn, 1, 2 + turn, far)
            self.pass_on(*at, half, 2, half, *sides)

    def far(self):
        y, z, y_up, y_down, z_up, z_down = self.around()
        for at, half, sides in (
            ((turn4(y, 2), z), 0, (z_up, z_down)),
            ((y, turn4(z, 2)), 2, (y_up, y_down)),
        ):
            for index in range(4):
                self.wait(*at, index, 1, index)
            self.pass_on(*at, half, 2, half, *sides)

    def cross(self):
        y, z, y_up, y_down, z_up, z_down = self.around()
        for k in (1, 3, 2):
            row, column = turn4(y, k), turn4(z, k)
            self.wait(row, z_down[1], 0, 2, 0)
            self.pass_on(row, z_down[1], 0, 1, 0, z_up)
            self.wait(row, z_up[1], 0, 2, 0)
            self.pass_on(row, z_up[1], 1, 1, 1, z_down)
            self.wait(y_down[0], column, 2, 2, 2)
            self.pass_on(y_down[0], column, 2, 1, 2, y_up)
            self.wait(y_up[0], column, 2, 2, 2)
            self.pass_on(y_up[0], column, 3, 1, 3, y_down)

    def last(self):
        y, z = self.y, self.z
        for k in (1, 3, 2):
            row, column = turn4(y, k), turn4(z, k)
            for index in range(2):
                self.wait(row, turn4(z, 2), index, 1, index)
                self.wait(turn4(y, 2), column, 2 + index, 1, 2 + index)

    def finish(self):
        for copy in self.sent:
            copy.wait_send()


RING_SENDS = 36


def beside(step):
    me, y, xh, z = place()
    grp = lax.axis_index("grp")
    low = grp // 2
    side = lax.rem(xh + low + (0 if step == 1 else 1), 2)
    return {"grp": (1 - low) * 2 + lax.rem(grp, 2), "wide": flat(y, side, z)}


class Relay:
    def __init__(self, sources, stops, ends, ssem, rsem):
        self.sources, self.stops, self.ends, self.ssem, self.rsem = sources, stops, ends, ssem, rsem

    def copy(self, src, dst, at, step):
        return remote(src, dst, self.ssem.at[at], self.rsem.at[at], **beside(step))

    def legs(self, hop):
        for i, step in enumerate((1, 3)):
            src = self.sources[i] if hop == 0 else self.stops[i]
            dst = self.stops[i] if hop == 0 else self.ends[i]
            yield self.copy(src, dst, 2 * hop + i, step)

    def start(self):
        for copy in self.legs(0):
            copy.start()

    def forward(self):
        for first, second in zip(self.legs(0), self.legs(1)):
            first.wait_recv()
            second.start()

    def wait(self):
        for copy in self.legs(1):
            copy.wait_recv()

    def finish(self):
        for hop in (0, 1):
            for copy in self.legs(hop):
                copy.wait_send()


def look_up(got, table, hot, rows, slot_row):
    asked = got[:, slot_row, :].astype(F32)
    asked = jnp.concatenate([asked, jnp.zeros((128 - NW, 128), F32)], 0).T
    step = 8 * CAP
    for first in range(0, NW, 8):
        for d in range(8):
            column = asked[0:CAP, first + d : first + d + 1]
            lanes = lax.broadcasted_iota(jnp.int32, (CAP, SHARD), 1).astype(F32)
            hot[d * CAP : (d + 1) * CAP, :] = jnp.where(lanes == column, 1.0, 0.0).astype(BF)
        picked = lax.dot_general(
            hot[...], table[...], (((1,), (1,)), ((), ())), preferred_element_type=F32
        )
        rows[first * CAP : first * CAP + step, :] = picked.astype(BF)


def slots(at):
    return pl.ds(pl.multiple_of(at * CAP, CAP), CAP)


def turn_over(table, rows, first):
    for c in range(0, SHARD, 256):
        rows[first + c : first + c + 256, :] = table[:, c : c + 256].T


def owner_of(ids):
    return (((ids >> 9) * 171) >> 9).astype(jnp.int32)


def ask_rows(tok, msg, picks, slot_out):
    row = tok[0:1, :]
    column = jnp.broadcast_to(row.astype(F32), (128, T)).T[:, 0:1].astype(jnp.int32)
    row_owner, column_owner = owner_of(row), owner_of(column)
    down = lax.broadcasted_iota(jnp.int32, (T, T), 0)
    across = lax.broadcasted_iota(jnp.int32, (T, T), 1)
    same = row == column

    def count(which, axis):
        return jnp.sum(jnp.where(which, 1.0, 0.0), axis, keepdims=True)

    first_row = count(same & (down < across), 0) == 0.0
    first_column = count(same & (across < down), 1) == 0.0
    near = row_owner == column_owner
    rank_row = count(near & (column < row) & first_column, 0)
    rank_column = count(near & (row < column) & first_row, 1)
    slot_row = jnp.where(rank_row < CAP, row_owner.astype(F32) * CAP + rank_row, -1.0)
    slot_column = jnp.where(rank_column < CAP, column_owner.astype(F32) * CAP + rank_column, -1.0)
    lanes = lax.broadcasted_iota(jnp.int32, (T, NW * CAP), 1).astype(F32)
    hit = lanes == slot_column
    picks[...] = jnp.where(hit, 1.0, 0.0).astype(BF)
    slot_out[...] = jnp.broadcast_to(slot_row, (8, T)).astype(jnp.int32)
    local = (column - column_owner * SHARD).astype(F32)
    asked = jnp.max(jnp.where(hit, local, -1.0), 0, keepdims=True).astype(jnp.int32)
    most = (jnp.max(rank_row, 1, keepdims=True) + 1.0).astype(jnp.int32)
    rest = [
        tok[1:2, 0:128], tok[1:2, 128:256], tok[3:4, 0:128], jnp.broadcast_to(most, (1, 128)),
    ] + [jnp.zeros((1, 128), jnp.int32)] * 3
    for g in range(8):
        msg[g] = jnp.concatenate([asked[:, g * 128 : (g + 1) * 128]] + rest, 0)


def find_rows(got, table, asked_t, hot, rows, part):
    asked = got[:, 0, :].astype(F32)
    asked_t[...] = jnp.concatenate([asked, jnp.full((128 - NW, 128), -1.0, F32)], 0).T
    mine = asked_t[pl.ds(pl.multiple_of(part * CAP, CAP), CAP), :]
    lanes = lax.broadcasted_iota(jnp.int32, (CAP, SHARD), 1).astype(F32)
    for d in range(NW):
        hot[d * CAP : (d + 1) * CAP, :] = jnp.where(lanes == mine[:, d : d + 1], 1.0, 0.0).astype(BF)
    step = 16 * CAP
    for first in range(0, NW * CAP, step):
        picked = lax.dot_general(
            hot[first : first + step, :], table[...], (((1,), (1,)), ((), ())), preferred_element_type=F32
        )
        rows[first : first + step, :] = picked.astype(BF)


def turn_over(table, rows, first):
    for c in range(0, SHARD, 256):
        rows[first + c : first + c + 256, :] = table[:, c : c + 256].T


def front_kernel(
    tok, table, packed, got, emb, most, table_other, rows_t, packed_all, picks, slot_out, hot, goal, weights,
    msg, asked_t, rows, own_most, stops, msg_s, msg_r, emb_s, emb_r, most_s, most_r, swap_s, swap_r,
    ring_s, ring_r, x_sem, local,
):
    me, y, xh, z = place()
    grp = lax.axis_index("grp")
    other = flat(y, 1 - xh, z)
    greet_wide(me, grp, sides=True, meanwhile=lambda: ask_rows(tok, msg, picks, slot_out))
    over = remote(packed, packed_all.at[y, z, xh], x_sem.at[0], x_sem.at[1], wide=other)
    over.start()
    ask = Scatter(lambda p: msg.at[p // 4], lambda p: got.at[p], msg_s, msg_r, me)
    ask.start()
    got[me] = msg[me // 4]
    ring = Ring(
        lambda Y, Z, first, count: packed_all.at[Y, Z, :, pl.ds(first, count)],
        lambda Y, Z, index: ring_r.at[Y, Z, index],
        (0, 48, 96, 144, 208),
        ring_s,
    )
    ring.own(packed, packed_all.at[y, z, xh], 0)
    keep = pltpu.make_async_copy(packed, packed_all.at[y, z, xh], local.at[0])
    keep.start()
    halves = (pl.ds(0, D // 2), pl.ds(D // 2, D // 2))
    trade = Relay(
        [table.at[half] for half in halves],
        [stops.at[i] for i in range(2)],
        [table_other.at[half] for half in halves],
        swap_s,
        swap_r,
    )
    trade.start()
    over.wait_recv()
    ring.own(packed_all.at[y, z, 1 - xh], packed_all.at[y, z, 1 - xh], 4)
    ask.wait_recv()
    find_rows(got, table, asked_t, hot, rows, lax.rem(me, 4))
    ring.near(
        [
            (lambda Y, Z: packed_all.at[Y, Z, xh], 0),
            (lambda Y, Z: packed_all.at[Y, Z, 1 - xh], 4),
        ]
    )
    reply = Scatter(lambda p: rows.at[slots(p)], lambda p: emb.at[slots(p)], emb_s, emb_r, me)
    reply.start()
    emb[slots(me), :] = rows[slots(me), :]
    turn_over(table, rows_t, 0)
    largest = jnp.max(got[:, 4, :], 0, keepdims=True)
    own_most[...] = jnp.broadcast_to(largest, (8, 128))
    most[grp] = own_most[...]
    told = []
    for k in range(1, NG):
        to = lax.rem(grp + k, NG)
        told.append(remote(own_most, most.at[grp], most_s.at[k], most_r.at[grp], grp=to))
        told[-1].start()
    total = jnp.sum(got[:, 3, :].astype(F32), 0, keepdims=True)
    total = jnp.concatenate([total, total], 1) * T
    plain = tok[3:4, :].astype(F32)
    weights[...] = jnp.concatenate([plain / total, plain, total] + [jnp.zeros((1, T), F32)] * 5, 0)

    def place_goal(j, carry):
        from_dev = flat(j // 4, xh, lax.rem(j, 4))
        goals = jnp.concatenate([got[from_dev, 1:2, :], got[from_dev, 2:3, :]], 1)
        near, far = goals - me * SHARD, goals - other * SHARD
        at = jnp.where((far >= 0) & (far < SHARD), far + SHARD, -1)
        at = jnp.where((near >= 0) & (near < SHARD), near, at)
        goal[j] = jnp.broadcast_to(at, (8, T))
        return carry

    lax.fori_loop(0, 16, place_goal, 0)
    ring.far()
    trade.forward()
    ring.cross()
    reply.wait_recv()
    for k in range(1, NG):
        to = lax.rem(grp + k, NG)
        remote(own_most, most.at[to], most_s.at[k], most_r.at[to], grp=to).wait_recv()
    trade.wait()
    turn_over(table_other, rows_t, SHARD)
    ring.last()
    keep.wait()
    over.wait_send()
    ask.wait_send()
    reply.wait_send()
    trade.finish()
    for copy in told:
        copy.wait_send()
    ring.finish()


def front(tok, table, packed):
    return pl.pallas_call(
        front_kernel,
        name="front",
        out_shape=(
            jax.ShapeDtypeStruct((NW, 8, 128), jnp.int32),
            jax.ShapeDtypeStruct((NW * CAP, D), BF),
            jax.ShapeDtypeStruct((NG, 8, 128), jnp.int32),
            jax.ShapeDtypeStruct((D, SHARD), BF),
            jax.ShapeDtypeStruct((2 * SHARD, D), BF),
            jax.ShapeDtypeStruct((4, 4, 2, PACKED, D), BF),
            jax.ShapeDtypeStruct((T, NW * CAP), BF),
            jax.ShapeDtypeStruct((8, T), jnp.int32),
            jax.ShapeDtypeStruct((NW * CAP, SHARD), BF),
            jax.ShapeDtypeStruct((16, 8, T), jnp.int32),
            jax.ShapeDtypeStruct((8, T), F32),
        ),
        in_specs=[VMEM, VMEM, ANY],
        out_specs=(VMEM, VMEM, VMEM, VMEM, VMEM, ANY) + (VMEM,) * 5,
        scratch_shapes=[
            pltpu.VMEM((8, 8, 128), jnp.int32),
            pltpu.VMEM((128, 128), F32),
            pltpu.VMEM((NW * CAP, D), BF),
            pltpu.VMEM((8, 128), jnp.int32),
            pltpu.VMEM((2, D // 2, SHARD), BF),
            DMA((NW,)),
            DMA((NW,)),
            DMA((NW,)),
            DMA((NW,)),
            DMA((NG,)),
            DMA((NG,)),
            DMA((4,)),
            DMA((4,)),
            DMA((RING_SENDS + 4,)),
            DMA((4, 4, 5)),
            DMA((2,)),
            DMA((1,)),
        ],
        compiler_params=params(1, 60),
        cost_estimate=pl.CostEstimate(flops=2 * 10**9, bytes_accessed=3 * 10**7, transcendentals=0),
    )(tok, table, packed)


ORDER = tuple((i // 8) * 8 + (i % 2) * 4 + (i // 2) % 4 for i in range(NW))


def spread_rows(used, stride, at, repeat=1):
    picks = np.zeros((NW * stride, NW * used), np.float32)
    for i, w in enumerate(ORDER):
        for j in range(repeat):
            for r in range(used):
                picks[i * stride + at + j * used + r, w * used + r] = 1.0
    return picks


def rope():
    half = HD // 2
    freqs = np.float32(rope_base) ** (-(np.arange(half, dtype=np.float32) * np.float32(2.0)) / np.float32(HD))
    angles = freqs.astype(np.float32)[:, None] * np.arange(T, dtype=np.float32)[None, :]
    return np.concatenate([np.cos(angles), np.sin(angles)], 0).astype(np.float32)


def turned(values):
    return values.T


def gain_columns(gains):
    return jnp.concatenate([gains[...], jnp.zeros((120, D), F32)], 0).T


def rms(values, gain):
    scale = lax.rsqrt(jnp.mean(values * values, 0, keepdims=True) + norm_eps)
    return values * scale * gain


def rms_back(values, gain, grad):
    scale = lax.rsqrt(jnp.mean(values * values, 0, keepdims=True) + norm_eps)
    pulled = grad * gain
    middle = jnp.mean(values * pulled, 0, keepdims=True)
    back = scale * pulled - values * (scale * scale * scale) * middle
    return back, jnp.sum(grad * values * scale, 1, keepdims=True)


def mask_of(tok):
    row = tok[2:3, :]
    column = jnp.broadcast_to(row.astype(F32), (128, T)).T[:, 0:1].astype(jnp.int32)
    down = lax.broadcasted_iota(jnp.int32, (T, T), 0)
    across = lax.broadcasted_iota(jnp.int32, (T, T), 1)
    return (down <= across) & (row == column)


def mm(a, b):
    return jnp.dot(a, b, preferred_element_type=F32)


def mm_nt(a, b):
    return lax.dot_general(a, b, (((1,), (1,)), ((), ())), preferred_element_type=F32)


def mm_tn(a, b):
    return lax.dot_general(a, b, (((0,), (0,)), ((), ())), preferred_element_type=F32)


def rotated(x, rot):
    cosine, sine = rot[0:32, :], rot[32:64, :]
    one, two = x[0:32, :], x[32:64, :]
    return jnp.concatenate([one * cosine - two * sine, two * cosine + one * sine], 0)


def unrotated(x, rot):
    cosine, sine = rot[0:32, :], rot[32:64, :]
    one, two = x[0:32, :], x[32:64, :]
    return jnp.concatenate([one * cosine + two * sine, two * cosine - one * sine], 0)


def load_trunk(packed, ffn, down, attn, sem):
    loads = [
        pltpu.make_async_copy(packed.at[:, :, :, ATTN_AT:PACKED], attn, sem.at[0]),
        pltpu.make_async_copy(packed.at[:, :, :, FFN_AT:DOWN_AT], ffn, sem.at[1]),
        pltpu.make_async_copy(packed.at[:, :, :, DOWN_AT:ATTN_AT, 0:512], down, sem.at[2]),
    ]
    for load in loads:
        load.start()
    return loads


TRUNK_SCRATCH = [
    pltpu.VMEM((4, 4, 2, 96, D), BF),
    pltpu.VMEM((4, 4, 2, 64, 512), BF),
    pltpu.VMEM((4, 4, 2, 48, D), BF),
    DMA((3,)),
]


def forward_kernel(
    more, emb, picks, packed, gains, rot, tok,
    final, h0, n1, q, k, v, lse, att, h1, n2, gate_up, inner, h2,
    ffn, down, attn, sem, mixed,
):
    loads = load_trunk(packed, ffn, down, attn, sem)
    columns = gain_columns(gains)
    allowed = mask_of(tok)
    start = turned(mm(picks[...], emb[...]) + more[...])
    h0[...] = start
    normed = rms(start, columns[:, 0:1]).astype(BF)
    n1[...] = normed
    loads[0].wait()
    rows48 = attn[...].reshape(NW * 48, D)
    product = mm(rows48, normed)
    for i, w in enumerate(ORDER):
        mixed[w * 30 : w * 30 + 30, :] = product[i * 48 : i * 48 + 30, :]
    for kv in range(KVH):
        k[kv * HD : (kv + 1) * HD, :] = rotated(
            mixed[D + kv * HD : D + (kv + 1) * HD, :], rot[...]
        ).astype(BF)
        at = D + (KVH + kv) * HD
        v[kv * HD : (kv + 1) * HD, :] = mixed[at : at + HD, :].astype(BF)
    logs = []
    for h in range(H):
        kv = h // (H // KVH)
        query = rotated(mixed[h * HD : (h + 1) * HD, :], rot[...]).astype(BF)
        q[h * HD : (h + 1) * HD, :] = query
        scores = mm_tn(k[kv * HD : (kv + 1) * HD, :], query) * HD ** (-0.5)
        scores = jnp.where(allowed, scores, masked_score)
        top = jnp.max(scores, 0, keepdims=True)
        power = jnp.exp(scores - top)
        total = jnp.sum(power, 0, keepdims=True)
        probs = (power / total).astype(BF)
        att[h * HD : (h + 1) * HD, :] = mm(v[kv * HD : (kv + 1) * HD, :], probs).astype(BF)
        logs.append(top + jnp.log(total))
    lse[...] = jnp.concatenate(logs + [jnp.zeros((16 - H, T), F32)], 0)
    product = mm(rows48, att[...])
    for i, w in enumerate(ORDER):
        mixed[w * 18 : w * 18 + 18, :] = product[i * 48 + 30 : i * 48 + 48, :]
    middle = start + mixed[0:D, :]
    h1[...] = middle
    normed = rms(middle, columns[:, 1:2]).astype(BF)
    n2[...] = normed
    loads[1].wait()
    gate_up[...] = mm(ffn[...].reshape(NW * 96, D), normed)
    for i in range(NW // 2):
        gate = gate_up[i * 96 : (i + 1) * 96, :]
        up = gate_up[FF + i * 96 : FF + (i + 1) * 96, :]
        w = ORDER[i]
        inner[w * 96 : (w + 1) * 96, :] = (gate / (1.0 + jnp.exp(-gate)) * up).astype(BF)
    loads[2].wait()
    rows64 = down[...].reshape(NW * 64, 512)
    for j in range(3):
        product = mm(rows64, inner[j * 512 : (j + 1) * 512, :])
        for i, w in enumerate(ORDER):
            piece = product[i * 64 + j * 18 : i * 64 + j * 18 + 18, :]
            if j:
                mixed[w * 18 : w * 18 + 18, :] += piece
            else:
                mixed[w * 18 : w * 18 + 18, :] = piece
    last = middle + mixed[0:D, :]
    h2[...] = last
    final[...] = rms(last, columns[:, 2:3]).astype(BF)


def forward(more, emb, picks, packed, gains, rot, tok):
    def out(rows, kind):
        return jax.ShapeDtypeStruct((rows, T), kind)

    return pl.pallas_call(
        forward_kernel,
        name="forward",
        out_shape=(
            out(D, BF), out(D, F32), out(D, BF), out(D, BF), out(KVH * HD, BF), out(KVH * HD, BF), out(16, F32),
            out(D, BF), out(D, F32), out(D, BF), out(2 * FF, F32), out(FF, BF), out(D, F32),
        ),
        in_specs=[VMEM, VMEM, VMEM, ANY, VMEM, VMEM, VMEM],
        out_specs=(VMEM,) * 13,
        scratch_shapes=TRUNK_SCRATCH + [pltpu.VMEM((QKV, T), F32)],
        compiler_params=pltpu.CompilerParams(vmem_limit_bytes=60 * MIB),
        cost_estimate=pl.CostEstimate(flops=4 * 10**9, bytes_accessed=2 * 10**7, transcendentals=10**6),
    )(more, emb, picks, packed, gains, rot, tok)


def more_rows_kernel(msg, table, got, emb, hot, rows, msg_s, msg_r, emb_s, emb_r):
    me = lax.axis_index("wide")
    greet_wide(me)
    ask = Scatter(lambda p: msg.at[p], lambda p: got.at[p], msg_s, msg_r, me)
    ask.start()
    got[me] = msg[me]
    ask.wait_recv()
    look_up(got, table, hot, rows, 0)
    reply = Scatter(lambda p: rows.at[slots(p)], lambda p: emb.at[slots(p)], emb_s, emb_r, me)
    reply.start()
    emb[slots(me), :] = rows[slots(me), :]
    reply.wait_recv()
    ask.wait_send()
    reply.wait_send()


def more_rows(msg, table):
    return pl.pallas_call(
        more_rows_kernel,
        name="more_rows",
        out_shape=(
            jax.ShapeDtypeStruct((NW, 8, 128), jnp.int32),
            jax.ShapeDtypeStruct((NW * CAP, D), BF),
        ),
        in_specs=[VMEM, VMEM],
        out_specs=(VMEM, VMEM),
        scratch_shapes=[pltpu.VMEM((8 * CAP, SHARD), BF), pltpu.VMEM((NW * CAP, D), BF)]
        + [DMA((NW,))] * 4,
        compiler_params=params(2, 40),
    )(msg, table)[1]


def more_grads_kernel(msg, rows, got, out, msg_s, msg_r, row_s, row_r):
    me = lax.axis_index("wide")
    greet_wide(me)
    ask = Scatter(lambda p: msg.at[p], lambda p: got.at[p], msg_s, msg_r, me)
    ask.start()
    give = Scatter(lambda p: rows.at[slots(p)], lambda p: out.at[slots(p)], row_s, row_r, me)
    give.start()
    got[me] = msg[me]
    out[slots(me), :] = rows[slots(me), :]
    ask.wait_recv()
    give.wait_recv()
    ask.wait_send()
    give.wait_send()


def more_grads(msg, rows):
    return pl.pallas_call(
        more_grads_kernel,
        name="more_grads",
        out_shape=(
            jax.ShapeDtypeStruct((NW, 8, 128), jnp.int32),
            jax.ShapeDtypeStruct((NW * CAP, D), BF),
        ),
        in_specs=[VMEM, VMEM],
        out_specs=(VMEM, VMEM),
        scratch_shapes=[DMA((NW,))] * 4,
        compiler_params=params(3, 20),
    )(msg, rows)


VOC = 2 * SHARD
TOK = 16 * T
CH = 512
NCH = VOC // CH
QUART = D // 4


def cols(j):
    return pl.ds(pl.multiple_of(j * T, T), T)


def pair_cols(p):
    return pl.ds(pl.multiple_of(p * 2 * T, 2 * T), 2 * T)


def side_by_side(ref, p, rows):
    return jnp.concatenate([ref[2 * p, rows, :], ref[2 * p + 1, rows, :]], 1)


def head_kernel(
    final, rows_t, table, table_other, goal, weights,
    grad_final, head_own, head_other, loss,
    fall, expo, tops, stat, stat_in, coef, coef_in, parts,
    part_a, part_b, whole_a, whole_b, sum_a, sum_b, part_a2, part_b2, whole_a2, whole_b2,
    g_s, g_r, st_s, st_r, co_s, co_r, a_s, b_s, pa_r, pb_r, wa_r, wb_r, a2_s, b2_s, a2_r, b2_r,
):
    me, y, xh, z = place()
    mine = y * 4 + z

    def dev(j):
        return flat(j // 4, xh, lax.rem(j, 4))

    barrier = pltpu.get_barrier_semaphore()

    def greet(k, carry):
        pl.semaphore_signal(
            barrier, inc=1, device_id={"wide": dev(lax.rem(mine + k, 16))}, device_id_type=MESH
        )
        return carry

    lax.fori_loop(1, 16, greet, 0)
    pl.semaphore_wait(barrier, 15)

    sent = []

    def send(src, dst, ssem, rsem, to):
        copy = remote(src, dst, ssem, rsem, wide=to)
        copy.start()
        sent.append(copy)

    def arrived(dst, rsem):
        remote(dst, dst, g_s.at[0], rsem, wide=dev(mine)).wait_recv()

    ring = Ring(
        lambda Y, Z, first, count: fall.at[pl.ds(first, count), cols(Y * 4 + Z)],
        lambda Y, Z, index: g_r.at[Y * 4 + Z, index],
        tuple(QUART * k for k in range(5)),
        g_s,
    )
    ring.own(final, fall.at[:, cols(mine)], 0)
    fall[:, cols(mine)] = final[...]

    def logits(p):
        seen = fall[:, pair_cols(p)]
        goals = side_by_side(goal, p, slice(0, 8))
        group, hit = goals >> 3, jnp.zeros((8, 2 * T), F32)
        tip, weight = [], []
        for c in range(NCH):
            part = mm(rows_t[c * CH : (c + 1) * CH, :], seen)
            top = jnp.max(part, 0, keepdims=True)
            power = jnp.exp(part - top)
            for r in range(CH // 8):
                hit = jnp.where(group == c * (CH // 8) + r, part[8 * r : 8 * r + 8, :], hit)
            expo[c * CH : (c + 1) * CH, pair_cols(p)] = power.astype(BF)
            tip.append(top)
            weight.append(jnp.sum(power, 0, keepdims=True))
        spot = lax.broadcasted_iota(jnp.int32, (8, 2 * T), 0)
        hit = jnp.sum(jnp.where(spot == (goals & 7), hit, 0.0), 0, keepdims=True)
        top = functools.reduce(jnp.maximum, tip)
        total = sum(w * jnp.exp(t - top) for w, t in zip(weight, tip))
        zero = jnp.zeros((1, 2 * T), F32)
        tops[p] = jnp.concatenate(tip + [zero] * (8 - NCH), 0)
        stats = jnp.concatenate([top, total, hit] + [zero] * 5, 0)
        stat[2 * p] = stats[:, 0:T]
        stat[2 * p + 1] = stats[:, T : 2 * T]

    def tell(j):
        return remote(stat.at[j], stat_in.at[mine], st_s.at[j], st_r.at[mine], wide=dev(j))

    def block(dy, dz):
        return turn4(y, dy) * 4 + turn4(z, dz)

    half = z // 2

    def pair(dy, away):
        return turn4(y, dy) * 2 + lax.rem(half + away, 2)

    def forward(at):
        def one(k, carry):
            p = pair(*at(k))
            logits(p)
            tell(2 * p).start()
            tell(2 * p + 1).start()
            return carry

        return one

    ring.near()
    logits(pair(0, 0))
    stat_in[mine] = stat[mine]
    tell(2 * (mine // 2) + 1 - lax.rem(mine, 2)).start()
    ring.far()
    forward(lambda k: (0, 1))(0, 0)
    ring.cross()
    lax.fori_loop(0, 2, forward(lambda k: (1 + 2 * k, 0)), 0)
    ring.last()
    lax.fori_loop(
        0,
        4,
        forward(
            lambda k: (
                (1 + 2 * lax.rem(k, 2)) * (1 - k // 2) + 2 * (k // 2),
                1 - (k // 2) * (1 - lax.rem(k, 2)),
            )
        ),
        0,
    )

    def hear(k, carry):
        j = lax.rem(mine + k, 16)
        arrived(stat_in.at[j], st_r.at[j])
        return carry

    lax.fori_loop(1, 16, hear, 0)
    tip, weight, hit = stat_in[:, 0, :], stat_in[:, 1, :], stat_in[:, 2, :]
    top = jnp.max(tip, 0, keepdims=True)
    lse = top + jnp.log(jnp.sum(weight * jnp.exp(tip - top), 0, keepdims=True))
    picked = jnp.sum(hit, 0, keepdims=True)
    share, plain = weights[0:1, :], weights[1:2, :]
    zero = jnp.zeros((1, T), F32)
    coef[...] = jnp.concatenate(
        [lse, share * (1.0 + 2.0 * penalty_weight * lse), share] + [zero] * 5, 0
    )
    loss[...] = jnp.concatenate(
        [plain * (lse - picked + penalty_weight * lse * lse)] + [zero] * 7, 0
    )
    coef_in[mine] = coef[...]

    def spread(k):
        j = lax.rem(mine + k, 16)
        return remote(coef, coef_in.at[mine], co_s.at[k], co_r.at[mine], wide=dev(j))

    def spread_start(k, carry):
        spread(k).start()
        return carry

    lax.fori_loop(1, 16, spread_start, 0)

    up, down = 1, 3
    z_to = {step: flat(y, xh, turn4(z, step)) for step in (up, down)}
    y_to = {step: flat(turn4(y, step), xh, z) for step in (up, down)}

    def piece_a(j, index):
        row = j // 4
        return remote(
            parts.at[j, pl.ds(index * QUART, QUART)], part_a.at[index, row],
            a_s.at[j, index], pa_r.at[index, row], wide=z_to[(up, down)[index]],
        )

    def piece_b(j, index):
        column = lax.rem(j, 4)
        return remote(
            parts.at[j, pl.ds((2 + index) * QUART, QUART)], part_b.at[index, column],
            b_s.at[j, index], pb_r.at[index, column], wide=y_to[(up, down)[index]],
        )

    def half_a(j, index):
        row = j // 4
        return remote(
            parts.at[j, pl.ds(0, 2 * QUART)], whole_a.at[index, row],
            a_s.at[j, 0], wa_r.at[index, row], wide=z_to[(up, down)[index]],
        )

    def half_b(j, index):
        column = lax.rem(j, 4)
        return remote(
            parts.at[j, pl.ds(2 * QUART, 2 * QUART)], whole_b.at[index, column],
            b_s.at[j, 0], wb_r.at[index, column], wide=y_to[(up, down)[index]],
        )

    def pair_at(k):
        return pair(lax.rem(2 + k // 2, 4), lax.rem(k + 1, 2))

    def post(k):
        p = pair_at(k)
        for j in (2 * p, 2 * p + 1):
            dy, dz = lax.rem(j // 4 - y + 4, 4), lax.rem(lax.rem(j, 4) - z + 4, 4)

            @pl.when(dz == 2)
            def _(j=j):
                piece_a(j, 0).start()
                piece_a(j, 1).start()

            @pl.when(dy == 2)
            def _(j=j):
                piece_b(j, 0).start()
                piece_b(j, 1).start()

        for j in (2 * p, 2 * p + 1):
            dy, dz = lax.rem(j // 4 - y + 4, 4), lax.rem(lax.rem(j, 4) - z + 4, 4)
            for index, step in enumerate((up, down)):

                @pl.when(dz == step)
                def _(j=j, index=index):
                    row = j // 4
                    arrived(part_a.at[index, row], pa_r.at[index, row])
                    rows = pl.ds(index * QUART, QUART)
                    total = parts[j, rows, :].astype(F32) + part_a[index, row].astype(F32)
                    parts[j, rows, :] = total.astype(BF)
                    half_a(j, index).start()

                @pl.when(dy == step)
                def _(j=j, index=index):
                    column = lax.rem(j, 4)
                    arrived(part_b.at[index, column], pb_r.at[index, column])
                    rows = pl.ds((2 + index) * QUART, QUART)
                    total = parts[j, rows, :].astype(F32) + part_b[index, column].astype(F32)
                    parts[j, rows, :] = total.astype(BF)
                    half_b(j, index).start()

    def backward(k, carry):
        p = pair_at(k)
        for j in (2 * p, 2 * p + 1):

            @pl.when(j != mine)
            def _(j=j):
                arrived(coef_in.at[j], co_r.at[j])

        lse, soft, pick = (side_by_side(coef_in, p, slice(i, i + 1)) for i in range(3))
        goals = side_by_side(goal, p, slice(0, 8))
        group = goals >> 3
        pick = jnp.where(lax.broadcasted_iota(jnp.int32, (8, 2 * T), 0) == (goals & 7), pick, 0.0)
        for c in range(NCH):
            scale = soft * jnp.exp(tops[p, c : c + 1, :] - lse)
            power = expo[c * CH : (c + 1) * CH, pair_cols(p)].astype(F32)
            spot = lax.broadcasted_iota(jnp.int32, (CH // 8, 8, 2 * T), 0) + c * (CH // 8)
            drop = jnp.where(spot == group[None], pick[None], 0.0).reshape(CH, 2 * T)
            expo[c * CH : (c + 1) * CH, pair_cols(p)] = (power * scale - drop).astype(BF)
        product = mm(table[...], expo[0:SHARD, pair_cols(p)])
        product += mm(table_other[...], expo[SHARD:VOC, pair_cols(p)])
        parts[2 * p] = product[:, 0:T].astype(BF)
        parts[2 * p + 1] = product[:, T : 2 * T].astype(BF)

        @pl.when(k > 0)
        def _():
            post(k - 1)

        return carry

    lax.fori_loop(0, 8, backward, 0)
    post(7)

    def head_chunk(c):
        return mm_nt(fall[...], expo[pl.ds(pl.multiple_of(c * 512, 512), 512), :])

    def other_chunk(c, carry):
        head_other[:, pair_cols(c)] = head_chunk(c + SHARD // 512).astype(BF)
        return carry

    def own_chunk(c, carry):
        head_own[:, pair_cols(c)] = head_chunk(c)
        return carry

    lax.fori_loop(0, SHARD // 512, other_chunk, 0)

    kinds = (
        (whole_a, wa_r, sum_a, part_a2, whole_a2, a2_s, a2_r, y_to, 0),
        (whole_b, wb_r, sum_b, part_b2, whole_b2, b2_s, b2_r, z_to, 2 * QUART),
    )
    for d in (2, 1, 3, 0):
        for kind, (whole, w_r, total, part2, whole2, s2, r2, to, base) in enumerate(kinds):
            at = turn4(y if kind == 0 else z, d)
            j = at * 4 + z if kind == 0 else y * 4 + at
            acc = parts[j, base : base + 2 * QUART, :].astype(F32)
            for index in range(2):
                arrived(whole.at[index, at], w_r.at[index, at])
                acc = acc + whole[index, at].astype(F32)
            if d == 0:
                grad_final[base : base + 2 * QUART, :] = acc
            else:
                total[d - 1] = acc.astype(BF)
            if d == 2:
                for index, step in enumerate((up, down)):
                    piece = total.at[1, pl.ds(index * QUART, QUART)]
                    send(piece, part2.at[index], s2.at[index], r2.at[index], to[step])
    lax.fori_loop(0, 2, own_chunk, 0)
    for kind, (whole, w_r, total, part2, whole2, s2, r2, to, base) in enumerate(kinds):
        for index, step in enumerate((up, down)):
            arrived(part2.at[index], r2.at[index])
            rows = pl.ds(index * QUART, QUART)
            added = total[step - 1, rows, :].astype(F32) + part2[index].astype(F32)
            total[step - 1, rows, :] = added.astype(BF)
            send(total.at[step - 1], whole2.at[index], s2.at[2 + index], r2.at[2 + index], to[step])
    lax.fori_loop(2, SHARD // 512, own_chunk, 0)
    for kind, (whole, w_r, total, part2, whole2, s2, r2, to, base) in enumerate(kinds):
        for index in range(2):
            arrived(whole2.at[index], r2.at[2 + index])
        grad_final[base : base + 2 * QUART, :] += whole2[0].astype(F32) + whole2[1].astype(F32)

    def finish(k, carry):
        j = lax.rem(mine + k, 16)
        tell(j).wait_send()
        spread(k).wait_send()
        return carry

    lax.fori_loop(1, 16, finish, 0)
    for copy in sent:
        copy.wait_send()
    ring.finish()

    def finish_pieces(k, carry):
        row, column = block(k, 2), block(2, k)
        piece_a(row, 0).wait_send()
        piece_a(row, 1).wait_send()
        piece_b(column, 0).wait_send()
        piece_b(column, 1).wait_send()
        for index, step in enumerate((up, down)):
            half_a(block(k, step), index).wait_send()
            half_b(block(step, k), index).wait_send()
        return carry

    lax.fori_loop(0, 4, finish_pieces, 0)


def head(final, rows_t, table, table_other, goal, weights):
    return pl.pallas_call(
        head_kernel,
        name="head",
        out_shape=(
            jax.ShapeDtypeStruct((D, T), F32),
            jax.ShapeDtypeStruct((D, SHARD), F32),
            jax.ShapeDtypeStruct((D, SHARD), BF),
            jax.ShapeDtypeStruct((8, T), F32),
        ),
        in_specs=[VMEM] * 6,
        out_specs=(VMEM,) * 4,
        scratch_shapes=[
            pltpu.VMEM((D, TOK), BF),
            pltpu.VMEM((VOC, TOK), BF),
            pltpu.VMEM((8, 8, 2 * T), F32),
            pltpu.VMEM((16, 8, T), F32),
            pltpu.VMEM((16, 8, T), F32),
            pltpu.VMEM((8, T), F32),
            pltpu.VMEM((16, 8, T), F32),
            pltpu.VMEM((16, D, T), BF),
            pltpu.VMEM((2, 4, QUART, T), BF),
            pltpu.VMEM((2, 4, QUART, T), BF),
            pltpu.VMEM((2, 4, 2 * QUART, T), BF),
            pltpu.VMEM((2, 4, 2 * QUART, T), BF),
            pltpu.VMEM((3, 2 * QUART, T), BF),
            pltpu.VMEM((3, 2 * QUART, T), BF),
            pltpu.VMEM((2, QUART, T), BF),
            pltpu.VMEM((2, QUART, T), BF),
            pltpu.VMEM((2, 2 * QUART, T), BF),
            pltpu.VMEM((2, 2 * QUART, T), BF),
            DMA((RING_SENDS,)),
            DMA((16, 4)),
            DMA((16,)),
            DMA((16,)),
            DMA((16,)),
            DMA((16,)),
            DMA((16, 2)),
            DMA((16, 2)),
            DMA((2, 4)),
            DMA((2, 4)),
            DMA((2, 4)),
            DMA((2, 4)),
            DMA((4,)),
            DMA((4,)),
            DMA((4,)),
            DMA((4,)),
        ],
        compiler_params=params(4, 61),
        cost_estimate=pl.CostEstimate(
            flops=6 * VOC * TOK * D, bytes_accessed=2 * 10**7, transcendentals=VOC * TOK
        ),
    )(final, rows_t, table, table_other, goal, weights)


class Reduce:
    def __init__(self, parts, base, sizes, along_z, refs):
        (
            self.first, part_a, part_b, self.whole1, self.second, next_a, next_b, self.whole2,
            self.third, self.stop, self.third_in, self.s, self.r,
        ) = refs
        self.part1, self.part2 = (part_a, part_b), (next_a, next_b)
        self.parts, self.base, self.sizes, self.along_z = parts, base, sizes, along_z
        self.rows = (pl.ds(0, sizes[0]), pl.ds(sizes[0], sizes[1]), pl.ds(0, sum(sizes)))
        self.me, self.y, self.xh, self.z = place()
        self.sent = []

    def send(self, src, dst, at, **to):
        copy = remote(src, dst, self.s.at[at], self.r.at[at], **to)
        copy.start()
        self.sent.append(copy)

    def wait(self, dst, at):
        remote(dst, dst, self.s.at[at], self.r.at[at], wide=self.me).wait_recv()

    def item1(self, step, which):
        rows = pl.ds(self.base + self.rows[which].start, self.rows[which].size)
        if self.along_z:
            return (slice(None), turn4(self.z, step), slice(None), rows)
        return (turn4(self.y, step), slice(None), slice(None), rows)

    def item2(self, step, which):
        return (turn4(self.y if self.along_z else self.z, step), slice(None), self.rows[which])

    def to(self, stage, step):
        if self.along_z == (stage == 1):
            return flat(self.y, self.xh, turn4(self.z, step))
        return flat(turn4(self.y, step), self.xh, self.z)

    def split(self, stage, ref, item, part, base):
        for index, step in enumerate((1, 3)):
            self.send(ref.at[item(2, index)], part[index], base + index, wide=self.to(stage, step))

    def join(self, stage, ref, item, part, whole, base):
        for index, step in enumerate((1, 3)):
            self.wait(part[index], base + index)
            at = item(step, index)
            ref[at] = (ref[at].astype(F32) + part[index][...].astype(F32)).astype(BF)
            self.send(ref.at[item(step, 2)], whole.at[index], base + 2 + index, wide=self.to(stage, step))

    def add(self, ref, item, whole, base):
        acc = ref[item(0, 2)].astype(F32)
        for index in range(2):
            self.wait(whole.at[index], base + 2 + index)
            acc = acc + whole[index].astype(F32)
        return acc

    def one(self):
        self.split(1, self.parts, self.item1, self.part1, 0)

    def two(self):
        self.join(1, self.parts, self.item1, self.part1, self.whole1, 0)

    def three(self):
        self.first[...] = self.add(self.parts, self.item1, self.whole1, 0).astype(BF)
        self.split(2, self.first, self.item2, self.part2, 4)

    def four(self):
        self.join(2, self.first, self.item2, self.part2, self.whole2, 4)

    def five(self):
        self.second[...] = self.add(self.first, self.item2, self.whole2, 4)
        self.third[...] = self.second[1 - self.xh].astype(BF)
        self.send(self.third, self.stop, 8, **beside(1 if self.along_z else 3))

    def six(self):
        self.wait(self.stop, 8)
        self.send(self.stop, self.third_in, 9, **beside(1 if self.along_z else 3))

    def total(self):
        self.wait(self.third_in, 9)
        return self.second[self.xh] + self.third_in[...].astype(F32)

    def finish(self):
        for copy in self.sent:
            copy.wait_send()


STREAMS = ((0, (48, 32), True), (80, (48, 32), False), (160, (16, 16), True), (192, (16, 16), False))


def reduce_scratch():
    shapes = []
    for _, sizes, _ in STREAMS:
        half = sum(sizes)
        shapes += [
            pltpu.VMEM((4, 2, half, D), BF),
            pltpu.VMEM((4, 2, sizes[0], D), BF),
            pltpu.VMEM((4, 2, sizes[1], D), BF),
            pltpu.VMEM((2, 4, 2, half, D), BF),
            pltpu.VMEM((2, half, D), F32),
            pltpu.VMEM((2, sizes[0], D), BF),
            pltpu.VMEM((2, sizes[1], D), BF),
            pltpu.VMEM((2, 2, half, D), BF),
            pltpu.VMEM((half, D), BF),
            pltpu.VMEM((half, D), BF),
            pltpu.VMEM((half, D), BF),
            DMA((10,)),
            DMA((10,)),
        ]
    return shapes


def back_kernel(
    grad_final, h0, n1, q, k, v, lse, att, h1, n2, gate_up, inner, h2,
    packed, gains, rot, tok, slot_row, loss, head_other, lay_attn_in, lay_out_in, lay_down_in,
    summed, rows_in, head_in, extra_sum, grad_embedded,
    ffn, down, attn, sem, lay_attn, lay_out, lay_down, lay_sem, parts, rows, grad_up, grad_mixed, spread, stops,
    row_s, row_r, swap_s, swap_r, hold, land_z, land_y, land_x, tree_s, tree_r, *reducers,
):
    me, y, xh, z = place()
    lays = [
        pltpu.make_async_copy(src, dst, lay_sem.at[i])
        for i, (src, dst) in enumerate(
            ((lay_down_in, lay_down), (lay_out_in, lay_out), (lay_attn_in, lay_attn))
        )
    ]
    lays[0].start()
    loads = load_trunk(packed, ffn, down, attn, sem)
    lays[1].start()
    lays[2].start()
    greet_wide(me, sides=True)
    halves = (pl.ds(0, D // 2), pl.ds(D // 2, D // 2))
    trade = Relay(
        [head_other.at[half] for half in halves],
        [stops.at[i] for i in range(2)],
        [head_in.at[half] for half in halves],
        swap_s,
        swap_r,
    )
    trade.start()
    streams = [
        Reduce(parts, base, sizes, along, reducers[13 * i : 13 * i + 13])
        for i, (base, sizes, along) in enumerate(STREAMS)
    ]
    early, late = streams[:2], streams[2:]
    columns = gain_columns(gains)

    grad_h2, gain3 = rms_back(h2[...], columns[:, 2:3], grad_final[...])
    lays[0].wait()
    spread[...] = mm(lay_down[...], grad_h2.astype(BF)).astype(BF)
    chunk = lax.broadcasted_iota(jnp.int32, (NW * 64, T), 0) & 63
    zero = jnp.zeros((NW * 64, T), BF)
    wide = jnp.concatenate(
        [
            jnp.where((chunk >= 18 * j) & (chunk < 18 * (j + 1)), spread[...].astype(F32), 0.0).astype(BF)
            for j in range(3)
        ],
        1,
    )
    inners = jnp.concatenate([inner[j * 512 : (j + 1) * 512, :] for j in range(3)], 1)
    grad_down = mm_nt(wide, inners).astype(BF).reshape(4, 4, 2, 64, 512)
    parts[:, :, :, DOWN_AT:ATTN_AT, 0:512] = grad_down
    parts[:, :, :, DOWN_AT:ATTN_AT, 512:D] = jnp.zeros((4, 4, 2, 64, D - 512), BF)
    loads[2].wait()
    grad_inner = mm_tn(down[...].reshape(NW * 64, 512), wide)
    for i in range(NW // 2):
        w = ORDER[i]
        gate = gate_up[i * 96 : (i + 1) * 96, :]
        up = gate_up[FF + i * 96 : FF + (i + 1) * 96, :]
        pieces = []
        for at in range(w * 96, w * 96 + 96, 32):
            j, r = at // 512, at % 512
            pieces.append(grad_inner[r : r + 32, j * T : (j + 1) * T])
        grad = jnp.concatenate(pieces, 0)
        sigmoid = 1.0 / (1.0 + jnp.exp(-gate))
        slope = sigmoid * (1.0 + gate * (1.0 - sigmoid))
        grad_up[i * 96 : (i + 1) * 96, :] = (grad * up * slope).astype(BF)
        grad_up[FF + i * 96 : FF + (i + 1) * 96, :] = (grad * (gate * sigmoid)).astype(BF)
    parts[:, :, :, FFN_AT:DOWN_AT, :] = mm_nt(grad_up[...], n2[...]).astype(BF).reshape(4, 4, 2, 96, D)
    for stream in early:
        stream.one()
    loads[1].wait()
    grad_normed = turned(mm_tn(grad_up[...], ffn[...].reshape(NW * 96, D)))
    part, gain2 = rms_back(h1[...], columns[:, 1:2], grad_normed)
    grad_h1 = grad_h2 + part
    lays[1].wait()
    out_rows = mm(lay_out[...], grad_h1.astype(BF)).astype(BF)
    loads[0].wait()
    rows48 = attn[...].reshape(NW * 48, D)
    grad_att = turned(mm_tn(out_rows, rows48)).astype(BF)
    for stream in early:
        stream.two()

    allowed = mask_of(tok)
    group = H // KVH
    for kv in range(KVH):
        keys = k[kv * HD : (kv + 1) * HD, :]
        values = v[kv * HD : (kv + 1) * HD, :]
        grad_k, grad_v = jnp.zeros((HD, T), F32), jnp.zeros((HD, T), F32)
        for h in range(kv * group, (kv + 1) * group):
            query = q[h * HD : (h + 1) * HD, :]
            grad_out = grad_att[h * HD : (h + 1) * HD, :]
            scores = mm_tn(keys, query) * HD ** (-0.5)
            scores = jnp.where(allowed, scores, masked_score)
            soft = jnp.exp(scores - lse[h : h + 1, :])
            grad_probs = mm_tn(values, grad_out)
            mean = jnp.sum(soft * grad_probs, 0, keepdims=True)
            grad_scores = (soft * (grad_probs - mean)).astype(BF)
            grad_q = mm(keys, grad_scores) * HD ** (-0.5)
            grad_mixed[h * HD : (h + 1) * HD, :] = unrotated(grad_q, rot[...]).astype(BF)
            grad_k = grad_k + mm_nt(query, grad_scores) * HD ** (-0.5)
            grad_v = grad_v + mm_nt(grad_out, soft.astype(BF))
        at = D + kv * HD
        grad_mixed[at : at + HD, :] = unrotated(grad_k, rot[...]).astype(BF)
        at = D + (KVH + kv) * HD
        grad_mixed[at : at + HD, :] = grad_v.astype(BF)
    for stream in early:
        stream.three()
    lays[2].wait()
    attn_rows = mm(lay_attn[...], grad_mixed[...]).astype(BF)
    both = jnp.concatenate([attn_rows, out_rows], 1)
    seen = jnp.concatenate([n1[...], att[...]], 1)
    parts[:, :, :, ATTN_AT:PACKED, :] = mm_nt(both, seen).astype(BF).reshape(4, 4, 2, 48, D)
    parts[:, :, :, PACKED:SUMMED, :] = jnp.zeros((4, 4, 2, SUMMED - PACKED, D), BF)
    for stream in late:
        stream.one()
    grad_normed = turned(mm_tn(attn_rows, rows48))
    part, gain1 = rms_back(h0[...], columns[:, 0:1], grad_normed)
    grad_h0 = (grad_h1 + part).astype(BF)
    grad_embedded[...] = grad_h0
    slot = lax.broadcasted_iota(jnp.int32, (NW * CAP, T), 0)
    picks = jnp.where(slot == slot_row[0:1, :], 1.0, 0.0).astype(BF)
    rows[...] = mm_nt(picks, grad_h0).astype(BF)
    give = Scatter(lambda p: rows.at[slots(p)], lambda p: rows_in.at[slots(p)], row_s, row_r, me)
    give.start()
    for stream in early:
        stream.four()
    trade.forward()
    lane = lax.broadcasted_iota(jnp.int32, (D, 128), 1)
    table = jnp.where(lane == 0, gain1, jnp.where(lane == 1, gain2, jnp.where(lane == 2, gain3, 0.0)))
    lost = jnp.sum(loss[0:1, :], 1, keepdims=True)
    table = table.T[0:8, :]
    tree = Tree(hold, land_z, land_y, land_x, tree_s, tree_r)
    tree.start(jnp.where(lax.broadcasted_iota(jnp.int32, (8, D), 0) == 3, lost, table))
    rows_in[slots(me), :] = rows[slots(me), :]
    for stream in late:
        stream.two()
    for stream in early:
        stream.five()
    tree.next(0)
    for stream in late:
        stream.three()
    for stream in late:
        stream.four()
    tree.next(1)
    for stream in early:
        stream.six()
    for stream in late:
        stream.five()
    extra_sum[...] = tree.collect(2)
    for stream in late:
        stream.six()
    for stream in streams:
        summed[stream.base : stream.base + sum(stream.sizes), :] = stream.total()
    give.wait_recv()
    trade.wait()
    for stream in streams:
        stream.finish()
    give.wait_send()
    tree.finish()
    trade.finish()


def back(grad_final, kept, packed, gains, rot, tok, slot_row, loss, head_other):
    lays = [
        jnp.asarray(spread_rows(30, 48, 0), BF),
        jnp.asarray(spread_rows(18, 48, 30), BF),
        jnp.asarray(spread_rows(18, 64, 0, 3), BF),
    ]
    return pl.pallas_call(
        back_kernel,
        name="back",
        out_shape=(
            jax.ShapeDtypeStruct((SUMMED, D), F32),
            jax.ShapeDtypeStruct((NW * CAP, D), BF),
            jax.ShapeDtypeStruct((D, SHARD), BF),
            jax.ShapeDtypeStruct((8, D), F32),
            jax.ShapeDtypeStruct((D, T), BF),
        ),
        in_specs=[VMEM] * 13 + [ANY] + [VMEM] * 5 + [ANY] * 4,
        out_specs=(VMEM, VMEM, ANY, VMEM, VMEM),
        scratch_shapes=TRUNK_SCRATCH
        + [
            pltpu.VMEM((NW * 48, QKV), BF),
            pltpu.VMEM((NW * 48, D), BF),
            pltpu.VMEM((NW * 64, D), BF),
            DMA((3,)),
            pltpu.VMEM((4, 4, 2, SUMMED, D), BF),
            pltpu.VMEM((NW * CAP, D), BF),
            pltpu.VMEM((2 * FF, T), BF),
            pltpu.VMEM((QKV, T), BF),
            pltpu.VMEM((NW * 64, T), BF),
            pltpu.VMEM((2, D // 2, SHARD), BF),
        ]
        + [DMA((NW,)), DMA((NW,)), DMA((4,)), DMA((4,))]
        + tree_scratch(D)
        + reduce_scratch(),
        compiler_params=params(5, 60),
        cost_estimate=pl.CostEstimate(flops=10**10, bytes_accessed=3 * 10**7, transcendentals=10**6),
    )(grad_final, *kept, packed, gains, rot, tok, slot_row, loss, head_other, *lays)


def adam_update(weight, grad, first, second, rate, decay):
    first = beta_one * first + (1.0 - beta_one) * grad
    second = beta_two * second + (1.0 - beta_two) * grad * grad
    ratio = first / (1.0 - beta_one**STEP) / (jnp.sqrt(second / (1.0 - beta_two**STEP)) + adam_eps)
    return (weight - rate * (ratio + decay * weight), first, second)


def adam_diff(weight, grad, first, second, anchor, rate, decay):
    return anchor - adam_update(weight, grad, first, second, rate, decay)[0]


PIECES = ((0, 0, 96), (0, 96, 96), (0, 192, 96), (1, 0, 112))


def update_kernel(
    rows, hot, head, head_in, summed, extra, gains, tm, tf, ts, ta, km, kf, ks, ka,
    table_grad, total_t, total_k, total_g, norms,
    v_rows, v_hot, v_head, v_head_in, vm, vf, vs, va, flipped,
    one_t, one_t_in, two_t, two_t_in, one_k, one_k_in, two_k, two_k_in, gains_out, gains_in,
    load_sem, one_s, one_r, two_s, two_r, three_s, three_r, gains_s, gains_r,
    hold, land_z, land_y, land_x, tree_s, tree_r,
):
    me, y, xh, z = place()
    grp = lax.axis_index("grp")
    core, x = lax.rem(grp, 2), grp // 2
    near, far = x * 2 + 1 - core, (1 - x) * 2 + core
    loads = [
        pltpu.make_async_copy(src, dst, load_sem.at[i])
        for i, (src, dst) in enumerate(
            zip((rows, hot, head, head_in, tm, tf, ts, ta), (v_rows, v_hot, v_head, v_head_in, vm, vf, vs, va))
        )
    ]
    for load in loads:
        load.start()
    barrier = pltpu.get_barrier_semaphore()
    for peer in near_peers(me, y, xh, z):
        pl.semaphore_signal(barrier, inc=1, device_id={"wide": peer}, device_id_type=MESH)
    for k in range(1, NG):
        pl.semaphore_signal(
            barrier, inc=1, device_id={"grp": lax.rem(grp + k, NG)}, device_id_type=MESH
        )
    pl.semaphore_wait(barrier, 7 + NG - 1)
    for load in loads[:4]:
        load.wait()
    for c in range(0, NW * CAP, 256):
        flipped[:, c : c + 256] = v_rows[c : c + 256, :].T
    squares = jnp.zeros((1, 512), F32)
    for c in range(0, SHARD, 512):
        part = v_head[:, c : c + 512] + v_head_in[:, c : c + 512].astype(F32)
        part = part + mm(flipped[...], v_hot[:, c : c + 512])
        table_grad[:, c : c + 512] = part
        squares = squares + jnp.sum(part * part, 0, keepdims=True)
    squares = jnp.sum(squares, 1, keepdims=True)
    trunk = jnp.sum(summed[...] * summed[...], 0, keepdims=True)
    squares = squares + jnp.sum(trunk, 1, keepdims=True)
    tree = Tree(hold, land_z, land_y, land_x, tree_s, tree_r)
    tree.start(jnp.broadcast_to(squares, (8, 128)))
    gain_grads = extra[0:3, :]
    gain_squares = jnp.sum(jnp.sum(gain_grads * gain_grads, 0, keepdims=True), 1, keepdims=True)
    tree.next(0)
    for load in loads[4:]:
        load.wait()
    tree.next(1)
    norm = jnp.sqrt(tree.collect(2)[0:1, 0:1] + gain_squares)
    factor = jnp.minimum(1.0, clip_norm / norm)
    down = lax.broadcasted_iota(jnp.int32, (8, 128), 0)
    norms[...] = jnp.where(down == 0, norm, factor)

    parts = (
        (vm, table_grad, vf, vs, va, total_t, D // 2, one_t, one_t_in, two_t, two_t_in),
        (km, summed, kf, ks, ka, total_k, SUMMED // 2, one_k, one_k_in, two_k, two_k_in),
    )
    sent = []

    def span(which, at, count, side):
        half = parts[which][6]
        return pl.ds(pl.multiple_of(side * half + at, 16), count)

    def diff(which, at, count, side):
        m, g, f, s2, a = parts[which][:5]
        rows = span(which, at, count, side)
        return adam_diff(
            m[rows, :], g[rows, :] * factor, f[rows, :], s2[rows, :], a[rows, :], inner_rate, weight_decay
        )

    for i, (which, at, count) in enumerate(PIECES):
        one, one_in = parts[which][7:9]
        rows = pl.ds(at, count)
        one[rows, :] = diff(which, at, count, 1 - core).astype(BF)
        copy = remote(one.at[rows], one_in.at[rows], one_s.at[i], one_r.at[i], grp=near)
        copy.start()
        sent.append(copy)
    for i, (which, at, count) in enumerate(PIECES):
        one, one_in, two, two_in = parts[which][7:11]
        rows = pl.ds(at, count)
        own = diff(which, at, count, core)
        sent[i].wait_recv()
        two[rows, :] = (own + one_in[rows, :].astype(F32)).astype(BF)
        copy = remote(two.at[rows], two_in.at[rows], two_s.at[i], two_r.at[i], grp=far)
        copy.start()
        sent.append(copy)
    gains_out[0:3, :] = adam_diff(
        gains[0:3, :], gain_grads * factor, gains[8:11, :], gains[16:19, :], gains[24:27, :], gain_rate, 0.0
    )
    gains_out[3:8, :] = jnp.zeros((5, D), F32)
    told = []
    for k in range(1, NG):
        to = lax.rem(grp + k, NG)
        told.append(remote(gains_out, gains_in.at[grp], gains_s.at[k], gains_r.at[grp], grp=to))
        told[-1].start()
    gains_in[grp] = gains_out[...]
    for i, (which, at, count) in enumerate(PIECES):
        total, two, two_in = parts[which][5], parts[which][9], parts[which][10]
        rows = pl.ds(at, count)
        sent[len(PIECES) + i].wait_recv()
        kept = span(which, at, count, core)
        total[kept, :] = two[rows, :].astype(F32) + two_in[rows, :].astype(F32)
        copy = remote(total.at[kept], total.at[kept], three_s.at[i], three_r.at[i], grp=near)
        copy.start()
        sent.append(copy)
    for k in range(1, NG):
        other = lax.rem(grp + k, NG)
        remote(
            gains_out, gains_in.at[other], gains_s.at[k], gains_r.at[other], grp=other
        ).wait_recv()
    total_g[...] = (gains_in[0] + gains_in[1]) + (gains_in[2] + gains_in[3])
    for i, (which, at, count) in enumerate(PIECES):
        away = parts[which][5].at[span(which, at, count, 1 - core)]
        remote(away, away, three_s.at[i], three_r.at[i], grp=near).wait_recv()
    for copy in sent + told:
        copy.wait_send()
    tree.finish()


def update(rows, hot, head, head_in, summed, extra, gains, table, trunk):
    def exchange(size, lanes):
        return [pltpu.VMEM((size // 2, lanes), BF)] * 4

    table_f32 = pltpu.VMEM((D, SHARD), F32)
    pieces = DMA((len(PIECES),))
    return pl.pallas_call(
        update_kernel,
        name="update",
        out_shape=(
            jax.ShapeDtypeStruct((D, SHARD), F32),
            jax.ShapeDtypeStruct((D, SHARD), F32),
            jax.ShapeDtypeStruct((SUMMED, D), F32),
            jax.ShapeDtypeStruct((8, D), F32),
            jax.ShapeDtypeStruct((8, 128), F32),
        ),
        in_specs=[ANY] * 4 + [VMEM] * 3 + [ANY] * 4 + [VMEM] * 4,
        out_specs=(VMEM,) * 5,
        scratch_shapes=[
            pltpu.VMEM((NW * CAP, D), BF),
            pltpu.VMEM((NW * CAP, SHARD), BF),
            table_f32,
            pltpu.VMEM((D, SHARD), BF),
            table_f32,
            table_f32,
            table_f32,
            table_f32,
            pltpu.VMEM((D, NW * CAP), BF),
        ]
        + exchange(D, SHARD)
        + exchange(SUMMED, D)
        + [pltpu.VMEM((8, D), F32), pltpu.VMEM((NG, 8, D), F32), DMA((8,))]
        + [pieces] * 6
        + [DMA((NG,)), DMA((NG,))]
        + tree_scratch(128),
        compiler_params=params(6, 48),
        cost_estimate=pl.CostEstimate(flops=2 * 10**9, bytes_accessed=3 * 10**7, transcendentals=10**6),
    )(rows, hot, head, head_in, summed, extra, gains, *table, *trunk)


def dot(spec, a, b):
    return jnp.einsum(spec, a, b, preferred_element_type=F32)


def pack(attn, ffn, proj, rows):
    down = proj[:, D:].reshape(18, 3, 512).transpose(1, 0, 2).reshape(54, 512)
    down = jnp.pad(down, ((0, 10), (0, D - 512)))
    return jnp.pad(jnp.concatenate([ffn, down, attn, proj[:, :D]], 0), ((0, rows - PACKED), (0, 0)))


def unpack(packed):
    down = packed[DOWN_AT : DOWN_AT + 54, :512].reshape(3, 18, 512).transpose(1, 0, 2).reshape(18, FF)
    proj = jnp.concatenate([packed[ATTN_AT + 30 : PACKED], down], 1)
    return packed[ATTN_AT : ATTN_AT + 30], packed[FFN_AT:DOWN_AT], proj


def on_device(
    token_ids,
    targets,
    segment_ids,
    row_counts,
    embed_table_master,
    embed_table_first,
    embed_table_second,
    embed_table_anchor,
    embed_table_momentum,
    attn_in_master,
    attn_in_first,
    attn_in_second,
    attn_in_anchor,
    attn_in_momentum,
    ffn_in_master,
    ffn_in_first,
    ffn_in_second,
    ffn_in_anchor,
    ffn_in_momentum,
    proj_out_master,
    proj_out_first,
    proj_out_second,
    proj_out_anchor,
    proj_out_momentum,
    norm_gains_master,
    norm_gains_first,
    norm_gains_second,
    norm_gains_anchor,
    norm_gains_momentum,
):
    ids = token_ids[0]
    gains = norm_gains_master[0]
    table = embed_table_master[0].T.astype(BF)
    weight = jnp.sum(row_counts[0, 0] * jnp.arange(1, 4))
    trunk = tuple(
        (attn.T, ffn.T, proj.T)
        for attn, ffn, proj in (
            (attn_in_master[0], ffn_in_master[0], proj_out_master[0]),
            (attn_in_first[0], ffn_in_first[0], proj_out_first[0]),
            (attn_in_second[0], ffn_in_second[0], proj_out_second[0]),
            (attn_in_anchor, ffn_in_anchor, proj_out_anchor),
            (attn_in_momentum, ffn_in_momentum, proj_out_momentum),
        )
    )
    packed = pack(*trunk[0], PACKED).astype(BF)
    tok = jnp.concatenate(
        [
            token_ids, targets, segment_ids, jnp.broadcast_to(weight, (1, T)), jnp.zeros((4, T), jnp.int32),
        ],
        0,
    )
    got, rows, most_all, table_other, rows_t, packed_all, picks, slot_row, hot, goals, weights = front(
        tok, table, packed
    )
    turns = (jnp.max(most_all) + CAP - 1) // CAP

    def asked_in(turn):
        ids_now = jnp.where(turn > 0, ids, 0)
        owner = ids_now // SHARD
        same = ids_now[:, None] == ids_now[None, :]
        before = jnp.arange(T)[None, :] < jnp.arange(T)[:, None]
        first_seen = ~jnp.any(same & before, 1)
        smaller = (owner[None, :] == owner[:, None]) & (ids_now[None, :] < ids_now[:, None])
        rank = jnp.sum(first_seen[None, :] & smaller, 1, dtype=jnp.int32) - turn * CAP
        slot = jnp.where((rank >= 0) & (rank < CAP), owner * CAP + rank, -1)
        chosen = jnp.arange(NW * CAP)[:, None] == slot[None, :]
        asked = jnp.max(jnp.where(chosen, (ids_now - owner * SHARD)[None, :], -1), 1).reshape(NW, 1, CAP)
        asked = jnp.pad(asked, ((0, 0), (0, 0), (0, 128 - CAP)), constant_values=-1)
        return jnp.pad(asked, ((0, 0), (0, 7), (0, 0))), chosen.astype(BF)

    def more_tokens(carry):
        turn, hidden = carry
        message, chosen = asked_in(turn)
        return turn + 1, hidden + dot("sd,st->td", more_rows(message, table), chosen)

    more = lax.while_loop(
        lambda carry: carry[0] < turns, more_tokens, (jnp.int32(1), jnp.zeros((T, D), F32))
    )[1]

    gains8 = jnp.pad(gains, ((0, 5), (0, 0)))
    rot = jnp.asarray(rope())
    final, *kept = forward(more, rows, picks, packed_all, gains8, rot, tok)
    total = weights[2, 0]
    grad_final, head_own, head_other, loss = head(final, rows_t, table, table_other, goals, weights)
    summed, rows_in, head_in, extra_sum, grad_embedded = back(
        grad_final, kept, packed_all, gains8, rot, tok, slot_row, loss, head_other
    )

    def more_table(carry):
        turn, grad = carry
        message, chosen = asked_in(turn)
        mine = dot("st,dt->sd", chosen, grad_embedded).astype(BF)
        got_now, rows_now = more_grads(message, mine)
        asked = got_now[:, 0, :CAP].reshape(NW * CAP)
        hot_now = (asked[:, None] == jnp.arange(SHARD)[None, :]).astype(BF)
        return turn + 1, grad + dot("sd,sv->dv", rows_now, hot_now)

    head_grad = lax.while_loop(lambda carry: carry[0] < turns, more_table, (jnp.int32(1), head_own))[1]
    kinds = [
        (
            embed_table_master[0].T,
            embed_table_first[0].T,
            embed_table_second[0].T,
            embed_table_anchor.T,
            embed_table_momentum.T,
        )
    ]
    kinds += [tuple(arrays[index] for arrays in trunk) for index in range(3)]
    kinds.append(
        (gains, norm_gains_first[0], norm_gains_second[0], norm_gains_anchor, norm_gains_momentum)
    )
    table_grad, total_t, total_k, total_g, norms = update(
        rows_in,
        hot,
        head_grad,
        head_in,
        summed,
        extra_sum,
        jnp.concatenate([jnp.pad(value, ((0, 5), (0, 0))) for value in kinds[4][:4]], 0),
        kinds[0][:4],
        [pack(*arrays, SUMMED) for arrays in trunk[:4]],
    )
    grads = (table_grad,) + unpack(summed) + (extra_sum[:3],)
    sums = (total_t,) + unpack(total_k) + (total_g[:3],)
    loss_total, norm, factor = extra_sum[3, 0], norms[0, 0], norms[1, 0]
    results = [loss_total.reshape(1), total.reshape(1), norm.reshape(1)]
    for index in range(5):
        _, first, second, anchor, momentum = kinds[index]
        average = sums[index] / NG
        outer = outer_momentum * momentum + average
        weight = anchor - outer_rate * (average + outer_momentum * outer)
        grad = grads[index] * factor
        first = beta_one * first + (1.0 - beta_one) * grad
        second = beta_two * second + (1.0 - beta_two) * grad * grad
        values = [average, outer, weight, first, second]
        if index < 4:
            values = [value.T for value in values]
        results += values[:3] + [values[3][None], values[4][None]]
    return tuple(results)


def solution(mesh):
    in_specs = (
        P("grp", "wide"),
        P("grp", "wide"),
        P("grp", "wide"),
        P("grp", "wide", None),
        P("grp", "wide", None),
        P("grp", "wide", None),
        P("grp", "wide", None),
        P("wide", None),
        P("wide", None),
        P("grp", None, "wide"),
        P("grp", None, "wide"),
        P("grp", None, "wide"),
        P(None, "wide"),
        P(None, "wide"),
        P("grp", None, "wide"),
        P("grp", None, "wide"),
        P("grp", None, "wide"),
        P(None, "wide"),
        P(None, "wide"),
        P("grp", None, "wide"),
        P("grp", None, "wide"),
        P("grp", None, "wide"),
        P(None, "wide"),
        P(None, "wide"),
        P("grp", None, None),
        P("grp", None, None),
        P("grp", None, None),
        P(),
        P(),
    )
    out_specs = (
        P("grp"),
        P("grp"),
        P("grp"),
        P("wide", None),
        P("wide", None),
        P("wide", None),
        P("grp", "wide", None),
        P("grp", "wide", None),
        P(None, "wide"),
        P(None, "wide"),
        P(None, "wide"),
        P("grp", None, "wide"),
        P("grp", None, "wide"),
        P(None, "wide"),
        P(None, "wide"),
        P(None, "wide"),
        P("grp", None, "wide"),
        P("grp", None, "wide"),
        P(None, "wide"),
        P(None, "wide"),
        P(None, "wide"),
        P("grp", None, "wide"),
        P("grp", None, "wide"),
        P(),
        P(),
        P(),
        P("grp", None, None),
        P("grp", None, None),
    )
    return jax.shard_map(
        on_device, mesh=mesh, in_specs=in_specs, out_specs=out_specs, check_vma=False
    )
```

```python
import functools

import jax
import jax.numpy as jnp
import numpy as np
from jax import lax
from jax.experimental import pallas as pl
from jax.experimental.pallas import tpu as pltpu
from jax.sharding import PartitionSpec as P

D = 576
H = 9
KVH = 3
HD = 64
FF = 1536
QKV = 960
STEP = 8
T = 256
SHARD = 1536
NW = 32
NG = 4
CAP = 32
FFN_AT, DOWN_AT, ATTN_AT, PACKED = 0, 96, 160, 208
SUMMED = 224

beta_one = 0.9
beta_two = 0.999
adam_eps = 1e-08
weight_decay = 0.1
inner_rate = 0.02
gain_rate = 0.2
clip_norm = 0.01
penalty_weight = 0.005
outer_rate = 0.7
outer_momentum = 0.9
rope_base = 100000.0
norm_eps = 1e-05
masked_score = -1e30

BF = jnp.bfloat16
F32 = jnp.float32
MESH = pl.DeviceIdType.MESH
VMEM = pl.BlockSpec(memory_space=pltpu.VMEM)
ANY = pl.BlockSpec(memory_space=pl.ANY)
DMA = pltpu.SemaphoreType.DMA
MIB = 1 << 20


def params(collective, mib):
    return pltpu.CompilerParams(
        collective_id=collective, has_side_effects=True, vmem_limit_bytes=mib * MIB
    )


def place():
    me = lax.axis_index("wide")
    return me, me // 8, lax.rem(me // 4, 2), lax.rem(me, 4)


def flat(y, xh, z):
    return y * 8 + xh * 4 + z


def turn4(at, by):
    return lax.rem(at + by, 4)


def remote(src, dst, ssem, rsem, **device):
    return pltpu.make_async_remote_copy(
        src_ref=src,
        dst_ref=dst,
        send_sem=ssem,
        recv_sem=rsem,
        device_id=device,
        device_id_type=MESH,
    )


def greet_wide(me, grp=None, sides=False, meanwhile=None):
    barrier = pltpu.get_barrier_semaphore()

    def one(k, carry):
        pl.semaphore_signal(
            barrier, inc=1, device_id={"wide": lax.rem(me + k, NW)}, device_id_type=MESH
        )
        return carry

    lax.fori_loop(1, NW, one, 0)
    count = NW - 1
    if grp is not None:
        for k in range(1, NG):
            pl.semaphore_signal(
                barrier, inc=1, device_id={"grp": lax.rem(grp + k, NG)}, device_id_type=MESH
            )
        count += NG - 1
    if sides:
        for step in (1, 3):
            pl.semaphore_signal(barrier, inc=1, device_id=beside(step), device_id_type=MESH)
        count += 2
    if meanwhile is not None:
        meanwhile()
    pl.semaphore_wait(barrier, count)


def near_peers(me, y, xh, z):
    peers = [flat(y, xh, turn4(z, k)) for k in (1, 2, 3)] + [flat(turn4(y, k), xh, z) for k in (1, 2, 3)]
    return peers + [flat(y, 1 - xh, z)]


class Tree:
    def __init__(self, hold, land_z, land_y, land_x, ssem, rsem):
        self.hold, self.lands = hold, (land_z, land_y, land_x)
        self.ssem, self.rsem = ssem, rsem
        me, self.y, self.xh, self.z = place()
        self.sent = []

    def send(self, stage):
        y, xh, z = self.y, self.xh, self.z
        at = (z, y, xh)[stage]
        land, src = self.lands[stage], self.hold.at[stage]
        for k in range(1, 2 if stage == 2 else 4):
            if stage == 0:
                to = flat(y, xh, turn4(z, k))
            elif stage == 1:
                to = flat(turn4(y, k), xh, z)
            else:
                to = flat(y, 1 - xh, z)
            copy = remote(src, land.at[at], self.ssem.at[stage, k], self.rsem.at[stage, at], wide=to)
            copy.start()
            self.sent.append(copy)
        land[at] = self.hold[stage]

    def start(self, value):
        self.hold[0] = value
        self.send(0)

    def collect(self, stage):
        at = (self.z, self.y, self.xh)[stage]
        land = self.lands[stage]
        size = 2 if stage == 2 else 4
        for k in range(1, size):
            other = lax.rem(at + k, size)
            remote(
                land.at[other], land.at[other], self.ssem.at[stage, k], self.rsem.at[stage, other],
                wide=flat(self.y, self.xh, self.z),
            ).wait_recv()
        total = land[0]
        for k in range(1, size):
            total = total + land[k]
        return total

    def next(self, stage):
        self.hold[stage + 1] = self.collect(stage)
        self.send(stage + 1)

    def finish(self):
        for copy in self.sent:
            copy.wait_send()


def tree_scratch(lanes):
    return [
        pltpu.VMEM((3, 8, lanes), F32),
        pltpu.VMEM((4, 8, lanes), F32),
        pltpu.VMEM((4, 8, lanes), F32),
        pltpu.VMEM((2, 8, lanes), F32),
        DMA((3, 4)),
        DMA((3, 4)),
    ]


class Scatter:
    def __init__(self, src_at, dst_at, ssem, rsem, me):
        self.src_at, self.dst_at, self.ssem, self.rsem, self.me = src_at, dst_at, ssem, rsem, me

    def copy(self, k):
        peer = lax.rem(self.me + k, NW)
        return remote(
            self.src_at(peer), self.dst_at(self.me), self.ssem.at[k], self.rsem.at[self.me], wide=peer
        )

    def start(self):
        def one(k, carry):
            self.copy(k).start()
            return carry

        lax.fori_loop(1, NW, one, 0)

    def wait_recv(self):
        def one(k, carry):
            peer = lax.rem(self.me + k, NW)
            remote(
                self.src_at(peer), self.dst_at(peer), self.ssem.at[k], self.rsem.at[peer], wide=peer
            ).wait_recv()
            return carry

        lax.fori_loop(1, NW, one, 0)

    def wait_send(self):
        def one(k, carry):
            self.copy(k).wait_send()
            return carry

        lax.fori_loop(1, NW, one, 0)


class Ring:
    def __init__(self, view, sem, bounds, ssem):
        self.view, self.sem, self.bounds = view, sem, bounds
        self.ssem, self.used, self.sent = ssem, 0, []
        self.me, self.y, self.xh, self.z = place()

    def send(self, src, dst, rsem, to):
        copy = remote(src, dst, self.ssem.at[self.used], rsem, wide=flat(to[0], self.xh, to[1]))
        self.used += 1
        copy.start()
        self.sent.append(copy)

    def piece(self, y, z, first, count):
        return self.view(y, z, self.bounds[first], self.bounds[first + count] - self.bounds[first])

    def pass_on(self, y, z, first, count, index, *to):
        piece = self.piece(y, z, first, count)
        for one in to:
            self.send(piece, piece, self.sem(y, z, index), one)

    def landed(self, piece, sem):
        remote(piece, piece, self.ssem.at[0], sem, wide=self.me).wait_recv()

    def wait(self, y, z, first, count, index):
        self.landed(self.piece(y, z, first, count), self.sem(y, z, index))

    def around(self):
        y, z = self.y, self.z
        return y, z, (turn4(y, 1), z), (turn4(y, 3), z), (y, turn4(z, 1)), (y, turn4(z, 3))

    def own(self, src, dst, index):
        y, z, y_up, y_down, z_up, z_down = self.around()
        for to in (y_up, y_down, z_up, z_down):
            self.send(src, dst, self.sem(y, z, index), to)

    def near(self, parts=None):
        y, z, y_up, y_down, z_up, z_down = self.around()
        for at, far, turn, half, sides in (
            (y_down, y_up, 0, 0, (z_up, z_down)),
            (y_up, y_down, 1, 0, (z_up, z_down)),
            (z_down, z_up, 0, 2, (y_up, y_down)),
            (z_up, z_down, 1, 2, (y_up, y_down)),
        ):
            if parts is None:
                self.wait(*at, 0, 4, 0)
            else:
                for part, index in parts:
                    self.landed(part(*at), self.sem(*at, index))
            self.pass_on(*at, turn, 1, turn, far)
            self.pass_on(*at, 2 + turn, 1, 2 + turn, far)
            self.pass_on(*at, half, 2, half, *sides)

    def far(self):
        y, z, y_up, y_down, z_up, z_down = self.around()
        for at, half, sides in (
            ((turn4(y, 2), z), 0, (z_up, z_down)),
            ((y, turn4(z, 2)), 2, (y_up, y_down)),
        ):
            for index in range(4):
                self.wait(*at, index, 1, index)
            self.pass_on(*at, half, 2, half, *sides)

    def cross(self):
        y, z, y_up, y_down, z_up, z_down = self.around()
        for k in (1, 3, 2):
            row, column = turn4(y, k), turn4(z, k)
            self.wait(row, z_down[1], 0, 2, 0)
            self.pass_on(row, z_down[1], 0, 1, 0, z_up)
            self.wait(row, z_up[1], 0, 2, 0)
            self.pass_on(row, z_up[1], 1, 1, 1, z_down)
            self.wait(y_down[0], column, 2, 2, 2)
            self.pass_on(y_down[0], column, 2, 1, 2, y_up)
            self.wait(y_up[0], column, 2, 2, 2)
            self.pass_on(y_up[0], column, 3, 1, 3, y_down)

    def last(self):
        y, z = self.y, self.z
        for k in (1, 3, 2):
            row, column = turn4(y, k), turn4(z, k)
            for index in range(2):
                self.wait(row, turn4(z, 2), index, 1, index)
                self.wait(turn4(y, 2), column, 2 + index, 1, 2 + index)

    def finish(self):
        for copy in self.sent:
            copy.wait_send()


RING_SENDS = 36


def beside(step):
    me, y, xh, z = place()
    grp = lax.axis_index("grp")
    low = grp // 2
    side = lax.rem(xh + low + (0 if step == 1 else 1), 2)
    return {"grp": (1 - low) * 2 + lax.rem(grp, 2), "wide": flat(y, side, z)}


class Relay:
    def __init__(self, sources, stops, ends, ssem, rsem):
        self.sources, self.stops, self.ends, self.ssem, self.rsem = sources, stops, ends, ssem, rsem

    def copy(self, src, dst, at, step):
        return remote(src, dst, self.ssem.at[at], self.rsem.at[at], **beside(step))

    def legs(self, hop):
        for i, step in enumerate((1, 3)):
            src = self.sources[i] if hop == 0 else self.stops[i]
            dst = self.stops[i] if hop == 0 else self.ends[i]
            yield self.copy(src, dst, 2 * hop + i, step)

    def start(self):
        for copy in self.legs(0):
            copy.start()

    def forward(self):
        for first, second in zip(self.legs(0), self.legs(1)):
            first.wait_recv()
            second.start()

    def wait(self):
        for copy in self.legs(1):
            copy.wait_recv()

    def finish(self):
        for hop in (0, 1):
            for copy in self.legs(hop):
                copy.wait_send()


def look_up(got, table, hot, rows, slot_row):
    asked = got[:, slot_row, :].astype(F32)
    asked = jnp.concatenate([asked, jnp.zeros((128 - NW, 128), F32)], 0).T
    step = 8 * CAP
    for first in range(0, NW, 8):
        for d in range(8):
            column = asked[0:CAP, first + d : first + d + 1]
            lanes = lax.broadcasted_iota(jnp.int32, (CAP, SHARD), 1).astype(F32)
            hot[d * CAP : (d + 1) * CAP, :] = jnp.where(lanes == column, 1.0, 0.0).astype(BF)
        picked = lax.dot_general(
            hot[...], table[...], (((1,), (1,)), ((), ())), preferred_element_type=F32
        )
        rows[first * CAP : first * CAP + step, :] = picked.astype(BF)


def slots(at):
    return pl.ds(pl.multiple_of(at * CAP, CAP), CAP)


def turn_over(table, rows, first):
    for c in range(0, SHARD, 256):
        rows[first + c : first + c + 256, :] = table[:, c : c + 256].T


def owner_of(ids):
    return (((ids >> 9) * 171) >> 9).astype(jnp.int32)


def pack_rows(out, attn, ffn, proj):
    out[FFN_AT:DOWN_AT, :] = ffn
    out[DOWN_AT:ATTN_AT, :] = jnp.zeros((ATTN_AT - DOWN_AT, D), F32)
    for j in range(3):
        at = DOWN_AT + 18 * j
        out[at : at + 18, 0:512] = proj[:, D + 512 * j : D + 512 * (j + 1)]
    out[ATTN_AT : ATTN_AT + 30, :] = attn
    out[ATTN_AT + 30 : PACKED, :] = proj[:, 0:D]


def ask_rows(ids, targets, weight, msg, picks, slot_out):
    row = ids[0:1, :]
    column = jnp.broadcast_to(row.astype(F32), (128, T)).T[:, 0:1].astype(jnp.int32)
    row_owner, column_owner = owner_of(row), owner_of(column)
    down = lax.broadcasted_iota(jnp.int32, (T, T), 0)
    across = lax.broadcasted_iota(jnp.int32, (T, T), 1)
    same = row == column

    def count(which, axis):
        return jnp.sum(jnp.where(which, 1.0, 0.0), axis, keepdims=True)

    first_row = count(same & (down < across), 0) == 0.0
    first_column = count(same & (across < down), 1) == 0.0
    near = row_owner == column_owner
    rank_row = count(near & (column < row) & first_column, 0)
    rank_column = count(near & (row < column) & first_row, 1)
    slot_row = jnp.where(rank_row < CAP, row_owner.astype(F32) * CAP + rank_row, -1.0)
    slot_column = jnp.where(rank_column < CAP, column_owner.astype(F32) * CAP + rank_column, -1.0)
    lanes = lax.broadcasted_iota(jnp.int32, (T, NW * CAP), 1).astype(F32)
    hit = lanes == slot_column
    picks[...] = jnp.where(hit, 1.0, 0.0).astype(BF)
    slot_out[...] = jnp.broadcast_to(slot_row, (8, T)).astype(jnp.int32)
    local = (column - column_owner * SHARD).astype(F32)
    asked = jnp.max(jnp.where(hit, local, -1.0), 0, keepdims=True).astype(jnp.int32)
    most = (jnp.max(rank_row, 1, keepdims=True) + 1.0).astype(jnp.int32)
    rest = [
        targets[0:1, 0:128], targets[0:1, 128:256], weight[:, 0:128], jnp.broadcast_to(most, (1, 128)),
    ] + [jnp.zeros((1, 128), jnp.int32)] * 3
    for g in range(8):
        msg[g] = jnp.concatenate([asked[:, g * 128 : (g + 1) * 128]] + rest, 0)


def find_rows(got, table, asked_t, hot, rows, part):
    asked = got[:, 0, :].astype(F32)
    asked_t[...] = jnp.concatenate([asked, jnp.full((128 - NW, 128), -1.0, F32)], 0).T
    mine = asked_t[pl.ds(pl.multiple_of(part * CAP, CAP), CAP), :]
    lanes = lax.broadcasted_iota(jnp.int32, (CAP, SHARD), 1).astype(F32)
    for d in range(NW):
        hot[d * CAP : (d + 1) * CAP, :] = jnp.where(lanes == mine[:, d : d + 1], 1.0, 0.0).astype(BF)
    step = 16 * CAP
    for first in range(0, NW * CAP, step):
        picked = lax.dot_general(
            hot[first : first + step, :], table[...], (((1,), (1,)), ((), ())), preferred_element_type=F32
        )
        rows[first : first + step, :] = picked.astype(BF)


def turn_over(table, rows, first):
    for c in range(0, SHARD, 256):
        rows[first + c : first + c + 256, :] = table[:, c : c + 256].T


def front_kernel(
    ids, targets, counts, master, attn, ffn, proj,
    got, emb, most_out, table_out, other_out, rows_t_out, packed_all, picks, slot_out, hot_out, goal, weights,
    wide, table, table_other, rows_t, hot, long, packed, most, msg, asked_t, rows, own_most, stops, msg_s, msg_r, emb_s, emb_r, most_s, most_r, swap_s, swap_r,
    ring_s, ring_r, x_sem, local,
):
    me, y, xh, z = place()
    grp = lax.axis_index("grp")
    other = flat(y, 1 - xh, z)
    load = pltpu.make_async_copy(master, wide, local.at[1])
    load.start()
    by_source = lax.broadcasted_iota(jnp.int32, (1, 3), 1) + 1
    weight = jnp.sum((counts[...] * by_source).astype(F32), 1, keepdims=True)
    weight = jnp.broadcast_to(weight, (1, T)).astype(jnp.int32)

    def prepare():
        pack_rows(long, attn[:, 0, :], ffn[...], proj[:, 0, :])
        packed[...] = long[...].astype(BF)
        ask_rows(ids, targets, weight, msg, picks, slot_out)
        load.wait()
        table[...] = wide[...].astype(BF)

    greet_wide(me, grp, sides=True, meanwhile=prepare)
    saves = [pltpu.make_async_copy(table, table_out, local.at[1])]
    saves[0].start()
    over = remote(packed, packed_all.at[y, z, xh], x_sem.at[0], x_sem.at[1], wide=other)
    over.start()
    ask = Scatter(lambda p: msg.at[p // 4], lambda p: got.at[p], msg_s, msg_r, me)
    ask.start()
    got[me] = msg[me // 4]
    ring = Ring(
        lambda Y, Z, first, count: packed_all.at[Y, Z, :, pl.ds(first, count)],
        lambda Y, Z, index: ring_r.at[Y, Z, index],
        (0, 48, 96, 144, 208),
        ring_s,
    )
    ring.own(packed, packed_all.at[y, z, xh], 0)
    keep = pltpu.make_async_copy(packed, packed_all.at[y, z, xh], local.at[0])
    keep.start()
    halves = (pl.ds(0, D // 2), pl.ds(D // 2, D // 2))
    trade = Relay(
        [table.at[half] for half in halves],
        [stops.at[i] for i in range(2)],
        [table_other.at[half] for half in halves],
        swap_s,
        swap_r,
    )
    trade.start()
    over.wait_recv()
    ring.own(packed_all.at[y, z, 1 - xh], packed_all.at[y, z, 1 - xh], 4)
    ask.wait_recv()
    find_rows(got, table, asked_t, hot, rows, lax.rem(me, 4))
    saves.append(pltpu.make_async_copy(hot, hot_out, local.at[2]))
    saves[-1].start()
    ring.near(
        [
            (lambda Y, Z: packed_all.at[Y, Z, xh], 0),
            (lambda Y, Z: packed_all.at[Y, Z, 1 - xh], 4),
        ]
    )
    reply = Scatter(lambda p: rows.at[slots(p)], lambda p: emb.at[slots(p)], emb_s, emb_r, me)
    reply.start()
    emb[slots(me), :] = rows[slots(me), :]
    turn_over(table, rows_t, 0)
    saves.append(pltpu.make_async_copy(rows_t.at[0:SHARD], rows_t_out.at[0:SHARD], local.at[3]))
    saves[-1].start()
    largest = jnp.max(got[:, 4, :], 0, keepdims=True)
    own_most[...] = jnp.broadcast_to(largest, (8, 128))
    most[grp] = own_most[...]
    told = []
    for k in range(1, NG):
        to = lax.rem(grp + k, NG)
        told.append(remote(own_most, most.at[grp], most_s.at[k], most_r.at[grp], grp=to))
        told[-1].start()
    total = jnp.sum(got[:, 3, :].astype(F32), 0, keepdims=True)
    total = jnp.concatenate([total, total], 1) * T
    plain = weight.astype(F32)
    weights[...] = jnp.concatenate([plain / total, plain, total] + [jnp.zeros((1, T), F32)] * 5, 0)

    def place_goal(j, carry):
        from_dev = flat(j // 4, xh, lax.rem(j, 4))
        goals = jnp.concatenate([got[from_dev, 1:2, :], got[from_dev, 2:3, :]], 1)
        near, far = goals - me * SHARD, goals - other * SHARD
        at = jnp.where((far >= 0) & (far < SHARD), far + SHARD, -1)
        at = jnp.where((near >= 0) & (near < SHARD), near, at)
        goal[j] = jnp.broadcast_to(at, (8, T))
        return carry

    lax.fori_loop(0, 16, place_goal, 0)
    ring.far()
    trade.forward()
    ring.cross()
    reply.wait_recv()
    for k in range(1, NG):
        to = lax.rem(grp + k, NG)
        remote(own_most, most.at[to], most_s.at[k], most_r.at[to], grp=to).wait_recv()
    most_out[...] = jnp.maximum(jnp.maximum(most[0], most[1]), jnp.maximum(most[2], most[3]))
    trade.wait()
    saves.append(pltpu.make_async_copy(table_other, other_out, local.at[4]))
    saves[-1].start()
    turn_over(table_other, rows_t, SHARD)
    rest = pl.ds(SHARD, SHARD)
    saves.append(pltpu.make_async_copy(rows_t.at[rest], rows_t_out.at[rest], local.at[5]))
    saves[-1].start()
    ring.last()
    keep.wait()
    for save in saves:
        save.wait()
    over.wait_send()
    ask.wait_send()
    reply.wait_send()
    trade.finish()
    for copy in told:
        copy.wait_send()
    ring.finish()


def front(*args):
    return pl.pallas_call(
        front_kernel,
        name="front",
        out_shape=(
            jax.ShapeDtypeStruct((NW, 8, 128), jnp.int32),
            jax.ShapeDtypeStruct((NW * CAP, D), BF),
            jax.ShapeDtypeStruct((8, 128), jnp.int32),
            jax.ShapeDtypeStruct((D, SHARD), BF),
            jax.ShapeDtypeStruct((D, SHARD), BF),
            jax.ShapeDtypeStruct((2 * SHARD, D), BF),
            jax.ShapeDtypeStruct((4, 4, 2, PACKED, D), BF),
            jax.ShapeDtypeStruct((T, NW * CAP), BF),
            jax.ShapeDtypeStruct((8, T), jnp.int32),
            jax.ShapeDtypeStruct((NW * CAP, SHARD), BF),
            jax.ShapeDtypeStruct((16, 8, T), jnp.int32),
            jax.ShapeDtypeStruct((8, T), F32),
        ),
        in_specs=[VMEM, VMEM, VMEM, ANY, VMEM, VMEM, VMEM],
        out_specs=(VMEM, VMEM, VMEM, ANY, ANY, ANY, ANY, VMEM, VMEM, ANY, VMEM, VMEM),
        scratch_shapes=[
            pltpu.VMEM((D, SHARD), F32),
            pltpu.VMEM((D, SHARD), BF),
            pltpu.VMEM((D, SHARD), BF),
            pltpu.VMEM((2 * SHARD, D), BF),
            pltpu.VMEM((NW * CAP, SHARD), BF),
            pltpu.VMEM((PACKED, D), F32),
            pltpu.VMEM((PACKED, D), BF),
            pltpu.VMEM((NG, 8, 128), jnp.int32),
            pltpu.VMEM((8, 8, 128), jnp.int32),
            pltpu.VMEM((128, 128), F32),
            pltpu.VMEM((NW * CAP, D), BF),
            pltpu.VMEM((8, 128), jnp.int32),
            pltpu.VMEM((2, D // 2, SHARD), BF),
            DMA((NW,)),
            DMA((NW,)),
            DMA((NW,)),
            DMA((NW,)),
            DMA((NG,)),
            DMA((NG,)),
            DMA((4,)),
            DMA((4,)),
            DMA((RING_SENDS + 4,)),
            DMA((4, 4, 5)),
            DMA((2,)),
            DMA((6,)),
        ],
        compiler_params=params(1, 60),
        cost_estimate=pl.CostEstimate(flops=2 * 10**9, bytes_accessed=3 * 10**7, transcendentals=0),
    )(*args)


ORDER = tuple((i // 8) * 8 + (i % 2) * 4 + (i // 2) % 4 for i in range(NW))


def spread_rows(used, stride, at, repeat=1):
    picks = np.zeros((NW * stride, NW * used), np.float32)
    for i, w in enumerate(ORDER):
        for j in range(repeat):
            for r in range(used):
                picks[i * stride + at + j * used + r, w * used + r] = 1.0
    return picks


def rope():
    half = HD // 2
    freqs = np.float32(rope_base) ** (-(np.arange(half, dtype=np.float32) * np.float32(2.0)) / np.float32(HD))
    angles = freqs.astype(np.float32)[:, None] * np.arange(T, dtype=np.float32)[None, :]
    return np.concatenate([np.cos(angles), np.sin(angles)], 0).astype(np.float32)


def turned(values):
    return values.T


def gain_columns(gains):
    return jnp.concatenate([gains[:, 0, :], jnp.zeros((125, D), F32)], 0).T


def rms(values, gain):
    scale = lax.rsqrt(jnp.mean(values * values, 0, keepdims=True) + norm_eps)
    return values * scale * gain


def rms_back(values, gain, grad):
    scale = lax.rsqrt(jnp.mean(values * values, 0, keepdims=True) + norm_eps)
    pulled = grad * gain
    middle = jnp.mean(values * pulled, 0, keepdims=True)
    back = scale * pulled - values * (scale * scale * scale) * middle
    return back, jnp.sum(grad * values * scale, 1, keepdims=True)


def mask_of(tok):
    row = tok[0:1, :]
    column = jnp.broadcast_to(row.astype(F32), (128, T)).T[:, 0:1].astype(jnp.int32)
    down = lax.broadcasted_iota(jnp.int32, (T, T), 0)
    across = lax.broadcasted_iota(jnp.int32, (T, T), 1)
    return (down <= across) & (row == column)


def mm(a, b):
    return jnp.dot(a, b, preferred_element_type=F32)


def mm_nt(a, b):
    return lax.dot_general(a, b, (((1,), (1,)), ((), ())), preferred_element_type=F32)


def mm_tn(a, b):
    return lax.dot_general(a, b, (((0,), (0,)), ((), ())), preferred_element_type=F32)


def rotated(x, rot):
    cosine, sine = rot[0:32, :], rot[32:64, :]
    one, two = x[0:32, :], x[32:64, :]
    return jnp.concatenate([one * cosine - two * sine, two * cosine + one * sine], 0)


def unrotated(x, rot):
    cosine, sine = rot[0:32, :], rot[32:64, :]
    one, two = x[0:32, :], x[32:64, :]
    return jnp.concatenate([one * cosine + two * sine, two * cosine - one * sine], 0)


def load_trunk(packed, ffn, down, attn, sem):
    loads = [
        pltpu.make_async_copy(packed.at[:, :, :, ATTN_AT:PACKED], attn, sem.at[0]),
        pltpu.make_async_copy(packed.at[:, :, :, FFN_AT:DOWN_AT], ffn, sem.at[1]),
        pltpu.make_async_copy(packed.at[:, :, :, DOWN_AT:ATTN_AT, 0:512], down, sem.at[2]),
    ]
    for load in loads:
        load.start()
    return loads


TRUNK_SCRATCH = [
    pltpu.VMEM((4, 4, 2, 96, D), BF),
    pltpu.VMEM((4, 4, 2, 64, 512), BF),
    pltpu.VMEM((4, 4, 2, 48, D), BF),
    DMA((3,)),
]


def forward_kernel(
    more, emb, picks, packed, gains, rot, tok,
    final, h0, n1, q, k, v, lse, att, h1, n2, gate_up_out, inner, h2,
    ffn, down, attn, sem, mixed, gate_up, save_sem,
):
    loads = load_trunk(packed, ffn, down, attn, sem)
    columns = gain_columns(gains)
    allowed = mask_of(tok)
    start = turned(mm(picks[...], emb[...]) + more[...])
    h0[...] = start
    normed = rms(start, columns[:, 0:1]).astype(BF)
    n1[...] = normed
    loads[0].wait()
    rows48 = attn[...].reshape(NW * 48, D)
    product = mm(rows48, normed)
    for i, w in enumerate(ORDER):
        mixed[w * 30 : w * 30 + 30, :] = product[i * 48 : i * 48 + 30, :]
    for kv in range(KVH):
        k[kv * HD : (kv + 1) * HD, :] = rotated(
            mixed[D + kv * HD : D + (kv + 1) * HD, :], rot[...]
        ).astype(BF)
        at = D + (KVH + kv) * HD
        v[kv * HD : (kv + 1) * HD, :] = mixed[at : at + HD, :].astype(BF)
    logs = []
    for h in range(H):
        kv = h // (H // KVH)
        query = rotated(mixed[h * HD : (h + 1) * HD, :], rot[...]).astype(BF)
        q[h * HD : (h + 1) * HD, :] = query
        scores = mm_tn(k[kv * HD : (kv + 1) * HD, :], query) * HD ** (-0.5)
        scores = jnp.where(allowed, scores, masked_score)
        top = jnp.max(scores, 0, keepdims=True)
        power = jnp.exp(scores - top)
        total = jnp.sum(power, 0, keepdims=True)
        probs = (power / total).astype(BF)
        att[h * HD : (h + 1) * HD, :] = mm(v[kv * HD : (kv + 1) * HD, :], probs).astype(BF)
        logs.append(top + jnp.log(total))
    lse[...] = jnp.concatenate(logs + [jnp.zeros((16 - H, T), F32)], 0)
    product = mm(rows48, att[...])
    for i, w in enumerate(ORDER):
        mixed[w * 18 : w * 18 + 18, :] = product[i * 48 + 30 : i * 48 + 48, :]
    middle = start + mixed[0:D, :]
    h1[...] = middle
    normed = rms(middle, columns[:, 1:2]).astype(BF)
    n2[...] = normed
    loads[1].wait()
    gate_up[...] = mm(ffn[...].reshape(NW * 96, D), normed)
    save = pltpu.make_async_copy(gate_up, gate_up_out, save_sem.at[0])
    save.start()
    for i in range(NW // 2):
        gate = gate_up[i * 96 : (i + 1) * 96, :]
        up = gate_up[FF + i * 96 : FF + (i + 1) * 96, :]
        w = ORDER[i]
        inner[w * 96 : (w + 1) * 96, :] = (gate / (1.0 + jnp.exp(-gate)) * up).astype(BF)
    loads[2].wait()
    rows64 = down[...].reshape(NW * 64, 512)
    for j in range(3):
        product = mm(rows64, inner[j * 512 : (j + 1) * 512, :])
        for i, w in enumerate(ORDER):
            piece = product[i * 64 + j * 18 : i * 64 + j * 18 + 18, :]
            if j:
                mixed[w * 18 : w * 18 + 18, :] += piece
            else:
                mixed[w * 18 : w * 18 + 18, :] = piece
    last = middle + mixed[0:D, :]
    h2[...] = last
    final[...] = rms(last, columns[:, 2:3]).astype(BF)
    save.wait()


def forward(more, emb, picks, packed, gains, rot, tok):
    def out(rows, kind):
        return jax.ShapeDtypeStruct((rows, T), kind)

    return pl.pallas_call(
        forward_kernel,
        name="forward",
        out_shape=(
            out(D, BF), out(D, F32), out(D, BF), out(D, BF), out(KVH * HD, BF), out(KVH * HD, BF), out(16, F32),
            out(D, BF), out(D, F32), out(D, BF), out(2 * FF, F32), out(FF, BF), out(D, F32),
        ),
        in_specs=[VMEM, VMEM, VMEM, ANY, VMEM, VMEM, VMEM],
        out_specs=(VMEM,) * 10 + (ANY, VMEM, VMEM),
        scratch_shapes=TRUNK_SCRATCH
        + [pltpu.VMEM((QKV, T), F32), pltpu.VMEM((2 * FF, T), F32), DMA((1,))],
        compiler_params=pltpu.CompilerParams(vmem_limit_bytes=60 * MIB),
        cost_estimate=pl.CostEstimate(flops=4 * 10**9, bytes_accessed=2 * 10**7, transcendentals=10**6),
    )(more, emb, picks, packed, gains, rot, tok)


def more_rows_kernel(msg, table, got, emb, hot, rows, msg_s, msg_r, emb_s, emb_r):
    me = lax.axis_index("wide")
    greet_wide(me)
    ask = Scatter(lambda p: msg.at[p], lambda p: got.at[p], msg_s, msg_r, me)
    ask.start()
    got[me] = msg[me]
    ask.wait_recv()
    look_up(got, table, hot, rows, 0)
    reply = Scatter(lambda p: rows.at[slots(p)], lambda p: emb.at[slots(p)], emb_s, emb_r, me)
    reply.start()
    emb[slots(me), :] = rows[slots(me), :]
    reply.wait_recv()
    ask.wait_send()
    reply.wait_send()


def more_rows(msg, table):
    return pl.pallas_call(
        more_rows_kernel,
        name="more_rows",
        out_shape=(
            jax.ShapeDtypeStruct((NW, 8, 128), jnp.int32),
            jax.ShapeDtypeStruct((NW * CAP, D), BF),
        ),
        in_specs=[VMEM, VMEM],
        out_specs=(VMEM, VMEM),
        scratch_shapes=[pltpu.VMEM((8 * CAP, SHARD), BF), pltpu.VMEM((NW * CAP, D), BF)]
        + [DMA((NW,))] * 4,
        compiler_params=params(2, 40),
    )(msg, table)[1]


def more_grads_kernel(msg, rows, got, out, msg_s, msg_r, row_s, row_r):
    me = lax.axis_index("wide")
    greet_wide(me)
    ask = Scatter(lambda p: msg.at[p], lambda p: got.at[p], msg_s, msg_r, me)
    ask.start()
    give = Scatter(lambda p: rows.at[slots(p)], lambda p: out.at[slots(p)], row_s, row_r, me)
    give.start()
    got[me] = msg[me]
    out[slots(me), :] = rows[slots(me), :]
    ask.wait_recv()
    give.wait_recv()
    ask.wait_send()
    give.wait_send()


def more_grads(msg, rows):
    return pl.pallas_call(
        more_grads_kernel,
        name="more_grads",
        out_shape=(
            jax.ShapeDtypeStruct((NW, 8, 128), jnp.int32),
            jax.ShapeDtypeStruct((NW * CAP, D), BF),
        ),
        in_specs=[VMEM, VMEM],
        out_specs=(VMEM, VMEM),
        scratch_shapes=[DMA((NW,))] * 4,
        compiler_params=params(3, 20),
    )(msg, rows)


VOC = 2 * SHARD
TOK = 16 * T
CH = 512
NCH = VOC // CH
QUART = D // 4


def cols(j):
    return pl.ds(pl.multiple_of(j * T, T), T)


def head_kernel(
    final, rows_t, table_in, table_other_in, goal, weights,
    grad_final, head_out, head_other, loss,
    table, table_other, head_own, big, fall, expo, tops, stat, stat_in, coef, coef_in, parts,
    part_a, part_b, whole_a, whole_b, sum_a, sum_b, part_a2, part_b2, whole_a2, whole_b2,
    g_s, g_r, st_s, st_r, co_s, co_r, a_s, b_s, pa_r, pb_r, wa_r, wb_r, a2_s, b2_s, a2_r, b2_r,
):
    me, y, xh, z = place()
    mine = y * 4 + z
    tables = [
        pltpu.make_async_copy(table_in, table, big.at[0]),
        pltpu.make_async_copy(table_other_in, table_other, big.at[1]),
    ]
    for load in tables:
        load.start()

    def dev(j):
        return flat(j // 4, xh, lax.rem(j, 4))

    barrier = pltpu.get_barrier_semaphore()

    def greet(k, carry):
        pl.semaphore_signal(
            barrier, inc=1, device_id={"wide": dev(lax.rem(mine + k, 16))}, device_id_type=MESH
        )
        return carry

    lax.fori_loop(1, 16, greet, 0)
    pl.semaphore_wait(barrier, 15)

    sent = []

    def send(src, dst, ssem, rsem, to):
        copy = remote(src, dst, ssem, rsem, wide=to)
        copy.start()
        sent.append(copy)

    def arrived(dst, rsem):
        remote(dst, dst, g_s.at[0], rsem, wide=dev(mine)).wait_recv()

    ring = Ring(
        lambda Y, Z, first, count: fall.at[pl.ds(first, count), cols(Y * 4 + Z)],
        lambda Y, Z, index: g_r.at[Y * 4 + Z, index],
        tuple(QUART * k for k in range(5)),
        g_s,
    )
    ring.own(final, fall.at[:, cols(mine)], 0)
    fall[:, cols(mine)] = final[...]

    def logits(j):
        seen = fall[:, cols(j)]
        goals = goal[j]
        group, hit = goals >> 3, jnp.zeros((8, T), F32)
        tip, weight = [], []
        for c in range(NCH):
            part = jnp.dot(rows_t[c * CH : (c + 1) * CH, :], seen, preferred_element_type=F32)
            top = jnp.max(part, 0, keepdims=True)
            power = jnp.exp(part - top)
            for r in range(CH // 8):
                hit = jnp.where(group == c * (CH // 8) + r, part[8 * r : 8 * r + 8, :], hit)
            expo[c * CH : (c + 1) * CH, cols(j)] = power.astype(BF)
            tip.append(top)
            weight.append(jnp.sum(power, 0, keepdims=True))
        spot = lax.broadcasted_iota(jnp.int32, (8, T), 0)
        hit = jnp.sum(jnp.where(spot == (goals & 7), hit, 0.0), 0, keepdims=True)
        top = functools.reduce(jnp.maximum, tip)
        total = sum(w * jnp.exp(t - top) for w, t in zip(weight, tip))
        zero = jnp.zeros((1, T), F32)
        tops[j] = jnp.concatenate(tip + [zero] * (8 - NCH), 0)
        stat[j] = jnp.concatenate([top, total, hit] + [zero] * 5, 0)

    def tell(j):
        return remote(stat.at[j], stat_in.at[mine], st_s.at[j], st_r.at[mine], wide=dev(j))

    def block(dy, dz):
        return turn4(y, dy) * 4 + turn4(z, dz)

    def forward(offsets):
        def one(k, carry):
            j = block(*offsets(k))
            logits(j)
            tell(j).start()
            return carry

        return one

    def odd(k):
        return 1 + 2 * lax.rem(k, 2)

    logits(mine)
    stat_in[mine] = stat[mine]
    ring.near()
    lax.fori_loop(0, 4, forward(lambda k: ((1 - k // 2) * odd(k), (k // 2) * odd(k))), 0)
    ring.far()
    lax.fori_loop(0, 2, forward(lambda k: (2 * (1 - k), 2 * k)), 0)
    ring.cross()
    lax.fori_loop(0, 4, forward(lambda k: (odd(k // 2), odd(k))), 0)
    ring.last()
    lax.fori_loop(
        0,
        4,
        forward(lambda k: (2 * (1 - k // 2) + odd(k) * (k // 2), odd(k) * (1 - k // 2) + 2 * (k // 2))),
        0,
    )
    forward(lambda k: (2, 2))(0, 0)

    def hear(k, carry):
        j = lax.rem(mine + k, 16)
        arrived(stat_in.at[j], st_r.at[j])
        return carry

    lax.fori_loop(1, 16, hear, 0)
    tip, weight, hit = stat_in[:, 0, :], stat_in[:, 1, :], stat_in[:, 2, :]
    top = jnp.max(tip, 0, keepdims=True)
    lse = top + jnp.log(jnp.sum(weight * jnp.exp(tip - top), 0, keepdims=True))
    picked = jnp.sum(hit, 0, keepdims=True)
    share, plain = weights[0:1, :], weights[1:2, :]
    zero = jnp.zeros((1, T), F32)
    coef[...] = jnp.concatenate(
        [lse, share * (1.0 + 2.0 * penalty_weight * lse), share] + [zero] * 5, 0
    )
    loss[...] = jnp.concatenate(
        [plain * (lse - picked + penalty_weight * lse * lse)] + [zero] * 7, 0
    )
    coef_in[mine] = coef[...]

    def spread(k):
        j = lax.rem(mine + k, 16)
        return remote(coef, coef_in.at[mine], co_s.at[k], co_r.at[mine], wide=dev(j))

    def spread_start(k, carry):
        spread(k).start()
        return carry

    lax.fori_loop(1, 16, spread_start, 0)

    up, down = 1, 3
    z_to = {step: flat(y, xh, turn4(z, step)) for step in (up, down)}
    y_to = {step: flat(turn4(y, step), xh, z) for step in (up, down)}

    def piece_a(j, index):
        row = j // 4
        return remote(
            parts.at[j, pl.ds(index * QUART, QUART)], part_a.at[index, row],
            a_s.at[j, index], pa_r.at[index, row], wide=z_to[(up, down)[index]],
        )

    def piece_b(j, index):
        column = lax.rem(j, 4)
        return remote(
            parts.at[j, pl.ds((2 + index) * QUART, QUART)], part_b.at[index, column],
            b_s.at[j, index], pb_r.at[index, column], wide=y_to[(up, down)[index]],
        )

    def half_a(j, index):
        row = j // 4
        return remote(
            parts.at[j, pl.ds(0, 2 * QUART)], whole_a.at[index, row],
            a_s.at[j, 0], wa_r.at[index, row], wide=z_to[(up, down)[index]],
        )

    def half_b(j, index):
        column = lax.rem(j, 4)
        return remote(
            parts.at[j, pl.ds(2 * QUART, 2 * QUART)], whole_b.at[index, column],
            b_s.at[j, 0], wb_r.at[index, column], wide=y_to[(up, down)[index]],
        )

    def offsets(k):
        return lax.rem(2 + k // 4, 4), lax.rem(2 + k, 4)

    def post(k):
        dy, dz = offsets(k)
        j = block(dy, dz)

        @pl.when(dz == 2)
        def _():
            piece_a(j, 0).start()
            piece_a(j, 1).start()

        @pl.when(dy == 2)
        def _():
            piece_b(j, 0).start()
            piece_b(j, 1).start()

        for index, step in enumerate((up, down)):

            @pl.when(dz == step)
            def _():
                row = j // 4
                arrived(part_a.at[index, row], pa_r.at[index, row])
                rows = pl.ds(index * QUART, QUART)
                total = parts[j, rows, :].astype(F32) + part_a[index, row].astype(F32)
                parts[j, rows, :] = total.astype(BF)
                half_a(j, index).start()

            @pl.when(dy == step)
            def _():
                column = lax.rem(j, 4)
                arrived(part_b.at[index, column], pb_r.at[index, column])
                rows = pl.ds((2 + index) * QUART, QUART)
                total = parts[j, rows, :].astype(F32) + part_b[index, column].astype(F32)
                parts[j, rows, :] = total.astype(BF)
                half_b(j, index).start()

    def backward(k, carry):
        j = block(*offsets(k))

        @pl.when(k != 10)
        def _():
            arrived(coef_in.at[j], co_r.at[j])

        lse, soft, pick = coef_in[j, 0:1, :], coef_in[j, 1:2, :], coef_in[j, 2:3, :]
        goals = goal[j]
        group = goals >> 3
        pick = jnp.where(lax.broadcasted_iota(jnp.int32, (8, T), 0) == (goals & 7), pick, 0.0)
        for c in range(NCH):
            scale = soft * jnp.exp(tops[j, c : c + 1, :] - lse)
            power = expo[c * CH : (c + 1) * CH, cols(j)].astype(F32)
            spot = lax.broadcasted_iota(jnp.int32, (CH // 8, 8, T), 0) + c * (CH // 8)
            drop = jnp.where(spot == group[None], pick[None], 0.0).reshape(CH, T)
            expo[c * CH : (c + 1) * CH, cols(j)] = (power * scale - drop).astype(BF)
        product = jnp.dot(table[...], expo[0:SHARD, cols(j)], preferred_element_type=F32)
        product += jnp.dot(table_other[...], expo[SHARD:VOC, cols(j)], preferred_element_type=F32)
        parts[j] = product.astype(BF)

        @pl.when(k > 0)
        def _():
            post(k - 1)

        return carry

    for load in tables:
        load.wait()
    lax.fori_loop(0, 16, backward, 0)
    post(15)

    def head_chunk(c):
        return lax.dot_general(
            fall[...],
            expo[pl.ds(pl.multiple_of(c * 256, 256), 256), :],
            (((1,), (1,)), ((), ())),
            preferred_element_type=F32,
        )

    def other_chunk(c, carry):
        head_other[:, cols(c)] = head_chunk(c + SHARD // 256).astype(BF)
        return carry

    def own_chunk(c, carry):
        head_own[:, cols(c)] = head_chunk(c)
        return carry

    lax.fori_loop(0, SHARD // 256, other_chunk, 0)

    kinds = (
        (whole_a, wa_r, sum_a, part_a2, whole_a2, a2_s, a2_r, y_to, 0),
        (whole_b, wb_r, sum_b, part_b2, whole_b2, b2_s, b2_r, z_to, 2 * QUART),
    )
    for d in (2, 1, 3, 0):
        for kind, (whole, w_r, total, part2, whole2, s2, r2, to, base) in enumerate(kinds):
            at = turn4(y if kind == 0 else z, d)
            j = at * 4 + z if kind == 0 else y * 4 + at
            acc = parts[j, base : base + 2 * QUART, :].astype(F32)
            for index in range(2):
                arrived(whole.at[index, at], w_r.at[index, at])
                acc = acc + whole[index, at].astype(F32)
            if d == 0:
                grad_final[base : base + 2 * QUART, :] = acc
            else:
                total[d - 1] = acc.astype(BF)
            if d == 2:
                for index, step in enumerate((up, down)):
                    piece = total.at[1, pl.ds(index * QUART, QUART)]
                    send(piece, part2.at[index], s2.at[index], r2.at[index], to[step])
    lax.fori_loop(0, SHARD // 512, own_chunk, 0)
    for kind, (whole, w_r, total, part2, whole2, s2, r2, to, base) in enumerate(kinds):
        for index, step in enumerate((up, down)):
            arrived(part2.at[index], r2.at[index])
            rows = pl.ds(index * QUART, QUART)
            added = total[step - 1, rows, :].astype(F32) + part2[index].astype(F32)
            total[step - 1, rows, :] = added.astype(BF)
            send(total.at[step - 1], whole2.at[index], s2.at[2 + index], r2.at[2 + index], to[step])
    lax.fori_loop(SHARD // 512, SHARD // 256, own_chunk, 0)
    store = pltpu.make_async_copy(head_own, head_out, big.at[0])
    store.start()
    for kind, (whole, w_r, total, part2, whole2, s2, r2, to, base) in enumerate(kinds):
        for index in range(2):
            arrived(whole2.at[index], r2.at[2 + index])
        grad_final[base : base + 2 * QUART, :] += whole2[0].astype(F32) + whole2[1].astype(F32)

    def finish(k, carry):
        j = lax.rem(mine + k, 16)
        tell(j).wait_send()
        spread(k).wait_send()
        return carry

    lax.fori_loop(1, 16, finish, 0)
    for copy in sent:
        copy.wait_send()
    ring.finish()

    def finish_pieces(k, carry):
        row, column = block(k, 2), block(2, k)
        piece_a(row, 0).wait_send()
        piece_a(row, 1).wait_send()
        piece_b(column, 0).wait_send()
        piece_b(column, 1).wait_send()
        for index, step in enumerate((up, down)):
            half_a(block(k, step), index).wait_send()
            half_b(block(step, k), index).wait_send()
        return carry

    lax.fori_loop(0, 4, finish_pieces, 0)
    store.wait()


def head(final, rows_t, table, table_other, goal, weights):
    return pl.pallas_call(
        head_kernel,
        name="head",
        out_shape=(
            jax.ShapeDtypeStruct((D, T), F32),
            jax.ShapeDtypeStruct((D, SHARD), F32),
            jax.ShapeDtypeStruct((D, SHARD), BF),
            jax.ShapeDtypeStruct((8, T), F32),
        ),
        in_specs=[VMEM, VMEM, ANY, ANY, VMEM, VMEM],
        out_specs=(VMEM, ANY, VMEM, VMEM),
        scratch_shapes=[
            pltpu.VMEM((D, SHARD), BF),
            pltpu.VMEM((D, SHARD), BF),
            pltpu.VMEM((D, SHARD), F32),
            DMA((2,)),
            pltpu.VMEM((D, TOK), BF),
            pltpu.VMEM((VOC, TOK), BF),
            pltpu.VMEM((16, 8, T), F32),
            pltpu.VMEM((16, 8, T), F32),
            pltpu.VMEM((16, 8, T), F32),
            pltpu.VMEM((8, T), F32),
            pltpu.VMEM((16, 8, T), F32),
            pltpu.VMEM((16, D, T), BF),
            pltpu.VMEM((2, 4, QUART, T), BF),
            pltpu.VMEM((2, 4, QUART, T), BF),
            pltpu.VMEM((2, 4, 2 * QUART, T), BF),
            pltpu.VMEM((2, 4, 2 * QUART, T), BF),
            pltpu.VMEM((3, 2 * QUART, T), BF),
            pltpu.VMEM((3, 2 * QUART, T), BF),
            pltpu.VMEM((2, QUART, T), BF),
            pltpu.VMEM((2, QUART, T), BF),
            pltpu.VMEM((2, 2 * QUART, T), BF),
            pltpu.VMEM((2, 2 * QUART, T), BF),
            DMA((RING_SENDS,)),
            DMA((16, 4)),
            DMA((16,)),
            DMA((16,)),
            DMA((16,)),
            DMA((16,)),
            DMA((16, 2)),
            DMA((16, 2)),
            DMA((2, 4)),
            DMA((2, 4)),
            DMA((2, 4)),
            DMA((2, 4)),
            DMA((4,)),
            DMA((4,)),
            DMA((4,)),
            DMA((4,)),
        ],
        compiler_params=params(4, 61),
        cost_estimate=pl.CostEstimate(
            flops=6 * VOC * TOK * D, bytes_accessed=2 * 10**7, transcendentals=VOC * TOK
        ),
    )(final, rows_t, table, table_other, goal, weights)


class Reduce:
    def __init__(self, parts, base, sizes, along_z, refs):
        (
            self.first, part_a, part_b, self.whole1, self.second, next_a, next_b, self.whole2,
            self.third, self.stop, self.third_in, self.s, self.r,
        ) = refs
        self.part1, self.part2 = (part_a, part_b), (next_a, next_b)
        self.parts, self.base, self.sizes, self.along_z = parts, base, sizes, along_z
        self.rows = (pl.ds(0, sizes[0]), pl.ds(sizes[0], sizes[1]), pl.ds(0, sum(sizes)))
        self.me, self.y, self.xh, self.z = place()
        self.sent = []

    def send(self, src, dst, at, **to):
        copy = remote(src, dst, self.s.at[at], self.r.at[at], **to)
        copy.start()
        self.sent.append(copy)

    def wait(self, dst, at):
        remote(dst, dst, self.s.at[at], self.r.at[at], wide=self.me).wait_recv()

    def item1(self, step, which):
        rows = pl.ds(self.base + self.rows[which].start, self.rows[which].size)
        if self.along_z:
            return (slice(None), turn4(self.z, step), slice(None), rows)
        return (turn4(self.y, step), slice(None), slice(None), rows)

    def item2(self, step, which):
        return (turn4(self.y if self.along_z else self.z, step), slice(None), self.rows[which])

    def to(self, stage, step):
        if self.along_z == (stage == 1):
            return flat(self.y, self.xh, turn4(self.z, step))
        return flat(turn4(self.y, step), self.xh, self.z)

    def split(self, stage, ref, item, part, base):
        for index, step in enumerate((1, 3)):
            self.send(ref.at[item(2, index)], part[index], base + index, wide=self.to(stage, step))

    def join(self, stage, ref, item, part, whole, base):
        for index, step in enumerate((1, 3)):
            self.wait(part[index], base + index)
            at = item(step, index)
            ref[at] = (ref[at].astype(F32) + part[index][...].astype(F32)).astype(BF)
            self.send(ref.at[item(step, 2)], whole.at[index], base + 2 + index, wide=self.to(stage, step))

    def add(self, ref, item, whole, base):
        acc = ref[item(0, 2)].astype(F32)
        for index in range(2):
            self.wait(whole.at[index], base + 2 + index)
            acc = acc + whole[index].astype(F32)
        return acc

    def one(self):
        self.split(1, self.parts, self.item1, self.part1, 0)

    def two(self):
        self.join(1, self.parts, self.item1, self.part1, self.whole1, 0)

    def three(self):
        self.first[...] = self.add(self.parts, self.item1, self.whole1, 0).astype(BF)
        self.split(2, self.first, self.item2, self.part2, 4)

    def four(self):
        self.join(2, self.first, self.item2, self.part2, self.whole2, 4)

    def five(self):
        self.second[...] = self.add(self.first, self.item2, self.whole2, 4)
        self.third[...] = self.second[1 - self.xh].astype(BF)
        self.send(self.third, self.stop, 8, **beside(1 if self.along_z else 3))

    def six(self):
        self.wait(self.stop, 8)
        self.send(self.stop, self.third_in, 9, **beside(1 if self.along_z else 3))

    def total(self):
        self.wait(self.third_in, 9)
        return self.second[self.xh] + self.third_in[...].astype(F32)

    def finish(self):
        for copy in self.sent:
            copy.wait_send()


STREAMS = ((0, (48, 32), True), (80, (48, 32), False), (160, (16, 16), True), (192, (16, 16), False))


def reduce_scratch():
    shapes = []
    for _, sizes, _ in STREAMS:
        half = sum(sizes)
        shapes += [
            pltpu.VMEM((4, 2, half, D), BF),
            pltpu.VMEM((4, 2, sizes[0], D), BF),
            pltpu.VMEM((4, 2, sizes[1], D), BF),
            pltpu.VMEM((2, 4, 2, half, D), BF),
            pltpu.VMEM((2, half, D), F32),
            pltpu.VMEM((2, sizes[0], D), BF),
            pltpu.VMEM((2, sizes[1], D), BF),
            pltpu.VMEM((2, 2, half, D), BF),
            pltpu.VMEM((half, D), BF),
            pltpu.VMEM((half, D), BF),
            pltpu.VMEM((half, D), BF),
            DMA((10,)),
            DMA((10,)),
        ]
    return shapes


def back_kernel(
    grad_final, h0, n1, q, k, v, lse, att, h1, n2, gate_up, inner, h2,
    packed, gains, rot, tok, slot_row, loss, head_other, lay_attn_in, lay_out_in, lay_down_in,
    summed, rows_in, head_in, extra_sum, grad_embedded,
    ffn, down, attn, sem, lay_attn, lay_out, lay_down, lay_sem, parts, rows, grad_up, grad_mixed, spread, stops,
    row_s, row_r, swap_s, swap_r, hold, land_z, land_y, land_x, tree_s, tree_r, *reducers,
):
    me, y, xh, z = place()
    lays = [
        pltpu.make_async_copy(src, dst, lay_sem.at[i])
        for i, (src, dst) in enumerate(
            ((lay_down_in, lay_down), (lay_out_in, lay_out), (lay_attn_in, lay_attn))
        )
    ]
    lays[0].start()
    loads = load_trunk(packed, ffn, down, attn, sem)
    lays[1].start()
    lays[2].start()
    greet_wide(me, sides=True)
    halves = (pl.ds(0, D // 2), pl.ds(D // 2, D // 2))
    trade = Relay(
        [head_other.at[half] for half in halves],
        [stops.at[i] for i in range(2)],
        [head_in.at[half] for half in halves],
        swap_s,
        swap_r,
    )
    trade.start()
    streams = [
        Reduce(parts, base, sizes, along, reducers[13 * i : 13 * i + 13])
        for i, (base, sizes, along) in enumerate(STREAMS)
    ]
    early, late = streams[:2], streams[2:]
    columns = gain_columns(gains)

    grad_h2, gain3 = rms_back(h2[...], columns[:, 2:3], grad_final[...])
    lays[0].wait()
    spread[...] = mm(lay_down[...], grad_h2.astype(BF)).astype(BF)
    chunk = lax.broadcasted_iota(jnp.int32, (NW * 64, T), 0) & 63
    zero = jnp.zeros((NW * 64, T), BF)
    wide = jnp.concatenate(
        [
            jnp.where((chunk >= 18 * j) & (chunk < 18 * (j + 1)), spread[...].astype(F32), 0.0).astype(BF)
            for j in range(3)
        ],
        1,
    )
    inners = jnp.concatenate([inner[j * 512 : (j + 1) * 512, :] for j in range(3)], 1)
    grad_down = mm_nt(wide, inners).astype(BF).reshape(4, 4, 2, 64, 512)
    parts[:, :, :, DOWN_AT:ATTN_AT, 0:512] = grad_down
    parts[:, :, :, DOWN_AT:ATTN_AT, 512:D] = jnp.zeros((4, 4, 2, 64, D - 512), BF)
    loads[2].wait()
    grad_inner = mm_tn(down[...].reshape(NW * 64, 512), wide)
    for i in range(NW // 2):
        w = ORDER[i]
        gate = gate_up[i * 96 : (i + 1) * 96, :]
        up = gate_up[FF + i * 96 : FF + (i + 1) * 96, :]
        pieces = []
        for at in range(w * 96, w * 96 + 96, 32):
            j, r = at // 512, at % 512
            pieces.append(grad_inner[r : r + 32, j * T : (j + 1) * T])
        grad = jnp.concatenate(pieces, 0)
        sigmoid = 1.0 / (1.0 + jnp.exp(-gate))
        slope = sigmoid * (1.0 + gate * (1.0 - sigmoid))
        grad_up[i * 96 : (i + 1) * 96, :] = (grad * up * slope).astype(BF)
        grad_up[FF + i * 96 : FF + (i + 1) * 96, :] = (grad * (gate * sigmoid)).astype(BF)
    parts[:, :, :, FFN_AT:DOWN_AT, :] = mm_nt(grad_up[...], n2[...]).astype(BF).reshape(4, 4, 2, 96, D)
    for stream in early:
        stream.one()
    loads[1].wait()
    grad_normed = turned(mm_tn(grad_up[...], ffn[...].reshape(NW * 96, D)))
    part, gain2 = rms_back(h1[...], columns[:, 1:2], grad_normed)
    grad_h1 = grad_h2 + part
    lays[1].wait()
    out_rows = mm(lay_out[...], grad_h1.astype(BF)).astype(BF)
    loads[0].wait()
    rows48 = attn[...].reshape(NW * 48, D)
    grad_att = turned(mm_tn(out_rows, rows48)).astype(BF)
    for stream in early:
        stream.two()

    allowed = mask_of(tok)
    group = H // KVH
    for kv in range(KVH):
        keys = k[kv * HD : (kv + 1) * HD, :]
        values = v[kv * HD : (kv + 1) * HD, :]
        grad_k, grad_v = jnp.zeros((HD, T), F32), jnp.zeros((HD, T), F32)
        for h in range(kv * group, (kv + 1) * group):
            query = q[h * HD : (h + 1) * HD, :]
            grad_out = grad_att[h * HD : (h + 1) * HD, :]
            scores = mm_tn(keys, query) * HD ** (-0.5)
            scores = jnp.where(allowed, scores, masked_score)
            soft = jnp.exp(scores - lse[h : h + 1, :])
            grad_probs = mm_tn(values, grad_out)
            mean = jnp.sum(soft * grad_probs, 0, keepdims=True)
            grad_scores = (soft * (grad_probs - mean)).astype(BF)
            grad_q = mm(keys, grad_scores) * HD ** (-0.5)
            grad_mixed[h * HD : (h + 1) * HD, :] = unrotated(grad_q, rot[...]).astype(BF)
            grad_k = grad_k + mm_nt(query, grad_scores) * HD ** (-0.5)
            grad_v = grad_v + mm_nt(grad_out, soft.astype(BF))
        at = D + kv * HD
        grad_mixed[at : at + HD, :] = unrotated(grad_k, rot[...]).astype(BF)
        at = D + (KVH + kv) * HD
        grad_mixed[at : at + HD, :] = grad_v.astype(BF)
    for stream in early:
        stream.three()
    lays[2].wait()
    attn_rows = mm(lay_attn[...], grad_mixed[...]).astype(BF)
    both = jnp.concatenate([attn_rows, out_rows], 1)
    seen = jnp.concatenate([n1[...], att[...]], 1)
    parts[:, :, :, ATTN_AT:PACKED, :] = mm_nt(both, seen).astype(BF).reshape(4, 4, 2, 48, D)
    parts[:, :, :, PACKED:SUMMED, :] = jnp.zeros((4, 4, 2, SUMMED - PACKED, D), BF)
    for stream in late:
        stream.one()
    grad_normed = turned(mm_tn(attn_rows, rows48))
    part, gain1 = rms_back(h0[...], columns[:, 0:1], grad_normed)
    grad_h0 = (grad_h1 + part).astype(BF)
    grad_embedded[...] = grad_h0
    slot = lax.broadcasted_iota(jnp.int32, (NW * CAP, T), 0)
    picks = jnp.where(slot == slot_row[0:1, :], 1.0, 0.0).astype(BF)
    rows[...] = mm_nt(picks, grad_h0).astype(BF)
    give = Scatter(lambda p: rows.at[slots(p)], lambda p: rows_in.at[slots(p)], row_s, row_r, me)
    give.start()
    for stream in early:
        stream.four()
    trade.forward()
    lane = lax.broadcasted_iota(jnp.int32, (D, 128), 1)
    table = jnp.where(lane == 0, gain1, jnp.where(lane == 1, gain2, jnp.where(lane == 2, gain3, 0.0)))
    lost = jnp.sum(loss[0:1, :], 1, keepdims=True)
    table = table.T[0:8, :]
    tree = Tree(hold, land_z, land_y, land_x, tree_s, tree_r)
    tree.start(jnp.where(lax.broadcasted_iota(jnp.int32, (8, D), 0) == 3, lost, table))
    rows_in[slots(me), :] = rows[slots(me), :]
    for stream in late:
        stream.two()
    for stream in early:
        stream.five()
    tree.next(0)
    for stream in late:
        stream.three()
    for stream in late:
        stream.four()
    tree.next(1)
    for stream in early:
        stream.six()
    for stream in late:
        stream.five()
    extra_sum[...] = tree.collect(2)
    for stream in late:
        stream.six()
    for stream in streams:
        summed[stream.base : stream.base + sum(stream.sizes), :] = stream.total()
    give.wait_recv()
    trade.wait()
    for stream in streams:
        stream.finish()
    give.wait_send()
    tree.finish()
    trade.finish()


def back(grad_final, kept, packed, gains, rot, tok, slot_row, loss, head_other):
    lays = [
        jnp.asarray(spread_rows(30, 48, 0), BF),
        jnp.asarray(spread_rows(18, 48, 30), BF),
        jnp.asarray(spread_rows(18, 64, 0, 3), BF),
    ]
    return pl.pallas_call(
        back_kernel,
        name="back",
        out_shape=(
            jax.ShapeDtypeStruct((SUMMED, D), F32),
            jax.ShapeDtypeStruct((NW * CAP, D), BF),
            jax.ShapeDtypeStruct((D, SHARD), BF),
            jax.ShapeDtypeStruct((8, D), F32),
            jax.ShapeDtypeStruct((D, T), BF),
        ),
        in_specs=[VMEM] * 13 + [ANY] + [VMEM] * 5 + [ANY] * 4,
        out_specs=(VMEM, VMEM, ANY, VMEM, VMEM),
        scratch_shapes=TRUNK_SCRATCH
        + [
            pltpu.VMEM((NW * 48, QKV), BF),
            pltpu.VMEM((NW * 48, D), BF),
            pltpu.VMEM((NW * 64, D), BF),
            DMA((3,)),
            pltpu.VMEM((4, 4, 2, SUMMED, D), BF),
            pltpu.VMEM((NW * CAP, D), BF),
            pltpu.VMEM((2 * FF, T), BF),
            pltpu.VMEM((QKV, T), BF),
            pltpu.VMEM((NW * 64, T), BF),
            pltpu.VMEM((2, D // 2, SHARD), BF),
        ]
        + [DMA((NW,)), DMA((NW,)), DMA((4,)), DMA((4,))]
        + tree_scratch(D)
        + reduce_scratch(),
        compiler_params=params(5, 60),
        cost_estimate=pl.CostEstimate(flops=10**10, bytes_accessed=3 * 10**7, transcendentals=10**6),
    )(grad_final, *kept, packed, gains, rot, tok, slot_row, loss, head_other, *lays)


def adam_update(weight, grad, first, second, rate, decay):
    first = beta_one * first + (1.0 - beta_one) * grad
    second = beta_two * second + (1.0 - beta_two) * grad * grad
    ratio = first / (1.0 - beta_one**STEP) / (jnp.sqrt(second / (1.0 - beta_two**STEP)) + adam_eps)
    return (weight - rate * (ratio + decay * weight), first, second)


def adam_diff(weight, grad, first, second, anchor, rate, decay):
    return anchor - adam_update(weight, grad, first, second, rate, decay)[0]


PIECES = ((0, 0, 96), (0, 96, 96), (0, 192, 96), (1, 0, 112))


def update_kernel(
    rows, hot, head, head_in, summed, extra, tm, tf, ts, ta, *refs
):
    trunk, gains = [refs[3 * i : 3 * i + 3] for i in range(4)], refs[12:16]
    update_body(rows, hot, head, head_in, summed, extra, tm, tf, ts, ta, trunk, gains, *refs[16:])


def update_body(
    rows, hot, head, head_in, summed, extra, tm, tf, ts, ta, trunk_in, gains,
    table_grad, total_t, total_k, total_g, norms,
    v_rows, v_hot, v_head, v_head_in, vm, vf, vs, va, flipped,
    one_t, one_t_in, two_t, two_t_in, one_k, one_k_in, two_k, two_k_in, gains_out, gains_in,
    load_sem, one_s, one_r, two_s, two_r, three_s, three_r, gains_s, gains_r,
    hold, land_z, land_y, land_x, tree_s, tree_r, km, kf, ks, ka,
):
    me, y, xh, z = place()
    grp = lax.axis_index("grp")
    core, x = lax.rem(grp, 2), grp // 2
    near, far = x * 2 + 1 - core, (1 - x) * 2 + core
    loads = [
        pltpu.make_async_copy(src, dst, load_sem.at[i])
        for i, (src, dst) in enumerate(
            zip((rows, hot, head, head_in, tm, tf, ts, ta), (v_rows, v_hot, v_head, v_head_in, vm, vf, vs, va))
        )
    ]
    for load in loads:
        load.start()
    barrier = pltpu.get_barrier_semaphore()
    for peer in near_peers(me, y, xh, z):
        pl.semaphore_signal(barrier, inc=1, device_id={"wide": peer}, device_id_type=MESH)
    for k in range(1, NG):
        pl.semaphore_signal(
            barrier, inc=1, device_id={"grp": lax.rem(grp + k, NG)}, device_id_type=MESH
        )
    pl.semaphore_wait(barrier, 7 + NG - 1)
    for load in loads[:4]:
        load.wait()
    for c in range(0, NW * CAP, 256):
        flipped[:, c : c + 256] = v_rows[c : c + 256, :].T
    squares = jnp.zeros((1, 512), F32)
    for c in range(0, SHARD, 512):
        part = v_head[:, c : c + 512] + v_head_in[:, c : c + 512].astype(F32)
        part = part + mm(flipped[...], v_hot[:, c : c + 512])
        table_grad[:, c : c + 512] = part
        squares = squares + jnp.sum(part * part, 0, keepdims=True)
    squares = jnp.sum(squares, 1, keepdims=True)
    trunk = jnp.sum(summed[...] * summed[...], 0, keepdims=True)
    squares = squares + jnp.sum(trunk, 1, keepdims=True)
    tree = Tree(hold, land_z, land_y, land_x, tree_s, tree_r)
    tree.start(jnp.broadcast_to(squares, (8, 128)))
    for out, (attn, ffn, proj) in zip((km, kf, ks, ka), trunk_in):
        if out is ka:
            pack_rows(out, attn[...], ffn[...], proj[...])
        else:
            pack_rows(out, attn[:, 0, :], ffn[...], proj[:, 0, :])
        out[PACKED:SUMMED, :] = jnp.zeros((SUMMED - PACKED, D), F32)
    gain_grads = extra[0:3, :]
    gain_squares = jnp.sum(jnp.sum(gain_grads * gain_grads, 0, keepdims=True), 1, keepdims=True)
    tree.next(0)
    for load in loads[4:]:
        load.wait()
    tree.next(1)
    norm = jnp.sqrt(tree.collect(2)[0:1, 0:1] + gain_squares)
    factor = jnp.minimum(1.0, clip_norm / norm)
    down = lax.broadcasted_iota(jnp.int32, (8, 128), 0)
    norms[...] = jnp.where(down == 0, norm, factor)

    parts = (
        (vm, table_grad, vf, vs, va, total_t, D // 2, one_t, one_t_in, two_t, two_t_in),
        (km, summed, kf, ks, ka, total_k, SUMMED // 2, one_k, one_k_in, two_k, two_k_in),
    )
    sent = []

    def span(which, at, count, side):
        half = parts[which][6]
        return pl.ds(pl.multiple_of(side * half + at, 16), count)

    def diff(which, at, count, side):
        m, g, f, s2, a = parts[which][:5]
        rows = span(which, at, count, side)
        return adam_diff(
            m[rows, :], g[rows, :] * factor, f[rows, :], s2[rows, :], a[rows, :], inner_rate, weight_decay
        )

    for i, (which, at, count) in enumerate(PIECES):
        one, one_in = parts[which][7:9]
        rows = pl.ds(at, count)
        one[rows, :] = diff(which, at, count, 1 - core).astype(BF)
        copy = remote(one.at[rows], one_in.at[rows], one_s.at[i], one_r.at[i], grp=near)
        copy.start()
        sent.append(copy)
    for i, (which, at, count) in enumerate(PIECES):
        one, one_in, two, two_in = parts[which][7:11]
        rows = pl.ds(at, count)
        own = diff(which, at, count, core)
        sent[i].wait_recv()
        two[rows, :] = (own + one_in[rows, :].astype(F32)).astype(BF)
        copy = remote(two.at[rows], two_in.at[rows], two_s.at[i], two_r.at[i], grp=far)
        copy.start()
        sent.append(copy)
    gains_out[0:3, :] = adam_diff(
        gains[0][:, 0, :], gain_grads * factor, gains[1][:, 0, :], gains[2][:, 0, :], gains[3][...], gain_rate, 0.0
    )
    gains_out[3:8, :] = jnp.zeros((5, D), F32)
    told = []
    for k in range(1, NG):
        to = lax.rem(grp + k, NG)
        told.append(remote(gains_out, gains_in.at[grp], gains_s.at[k], gains_r.at[grp], grp=to))
        told[-1].start()
    gains_in[grp] = gains_out[...]
    for i, (which, at, count) in enumerate(PIECES):
        total, two, two_in = parts[which][5], parts[which][9], parts[which][10]
        rows = pl.ds(at, count)
        sent[len(PIECES) + i].wait_recv()
        kept = span(which, at, count, core)
        total[kept, :] = two[rows, :].astype(F32) + two_in[rows, :].astype(F32)
        copy = remote(total.at[kept], total.at[kept], three_s.at[i], three_r.at[i], grp=near)
        copy.start()
        sent.append(copy)
    for k in range(1, NG):
        other = lax.rem(grp + k, NG)
        remote(
            gains_out, gains_in.at[other], gains_s.at[k], gains_r.at[other], grp=other
        ).wait_recv()
    total_g[...] = (gains_in[0] + gains_in[1]) + (gains_in[2] + gains_in[3])
    for i, (which, at, count) in enumerate(PIECES):
        away = parts[which][5].at[span(which, at, count, 1 - core)]
        remote(away, away, three_s.at[i], three_r.at[i], grp=near).wait_recv()
    for copy in sent + told:
        copy.wait_send()
    tree.finish()


def update(rows, hot, head, head_in, summed, extra, table, trunk, gains):
    def exchange(size, lanes):
        return [pltpu.VMEM((size // 2, lanes), BF)] * 4

    table_f32 = pltpu.VMEM((D, SHARD), F32)
    pieces = DMA((len(PIECES),))
    return pl.pallas_call(
        update_kernel,
        name="update",
        out_shape=(
            jax.ShapeDtypeStruct((D, SHARD), F32),
            jax.ShapeDtypeStruct((D, SHARD), F32),
            jax.ShapeDtypeStruct((SUMMED, D), F32),
            jax.ShapeDtypeStruct((8, D), F32),
            jax.ShapeDtypeStruct((8, 128), F32),
        ),
        in_specs=[ANY] * 4 + [VMEM] * 2 + [ANY] * 4 + [VMEM] * 16,
        out_specs=(VMEM,) * 5,
        scratch_shapes=[
            pltpu.VMEM((NW * CAP, D), BF),
            pltpu.VMEM((NW * CAP, SHARD), BF),
            table_f32,
            pltpu.VMEM((D, SHARD), BF),
            table_f32,
            table_f32,
            table_f32,
            table_f32,
            pltpu.VMEM((D, NW * CAP), BF),
        ]
        + exchange(D, SHARD)
        + exchange(SUMMED, D)
        + [pltpu.VMEM((8, D), F32), pltpu.VMEM((NG, 8, D), F32), DMA((8,))]
        + [pieces] * 6
        + [DMA((NG,)), DMA((NG,))]
        + tree_scratch(128)
        + [pltpu.VMEM((SUMMED, D), F32)] * 4,
        compiler_params=params(6, 50),
        cost_estimate=pl.CostEstimate(flops=2 * 10**9, bytes_accessed=3 * 10**7, transcendentals=10**6),
    )(rows, hot, head, head_in, summed, extra, *table, *trunk, *gains)


def settle(total, momentum, anchor, grad, first, second):
    average = total * (1.0 / NG)
    outer = outer_momentum * momentum + average
    weight = anchor - outer_rate * (average + outer_momentum * outer)
    first = beta_one * first + (1.0 - beta_one) * grad
    second = beta_two * second + (1.0 - beta_two) * grad * grad
    return average, outer, weight, first, second


def rows_of(packed):
    down = [packed[DOWN_AT + 18 * j : DOWN_AT + 18 * j + 18, 0:512] for j in range(3)]
    proj = jnp.concatenate([packed[ATTN_AT + 30 : PACKED, :]] + down, 1)
    return packed[ATTN_AT : ATTN_AT + 30, :], packed[FFN_AT:DOWN_AT, :], proj


def finish_kernel(norms, *refs):
    table, summed, total_k, extra, total_g = refs[:6], refs[6], refs[7], refs[8], refs[9]
    small = [refs[10 + 4 * i : 14 + 4 * i] for i in range(4)]
    outs = [refs[26 + 5 * i : 31 + 5 * i] for i in range(5)]
    factor = norms[1:2, 0:1]
    total, momentum, anchor, grad, first, second = table
    values = settle(
        total[...], momentum[...], anchor[...], grad[...] * factor, first[...], second[...]
    )
    for out, value in zip(outs[0], values):
        out[...] = value

    @pl.when(pl.program_id(0) == 0)
    def _():
        grads = rows_of(summed) + (extra[0:3, :],)
        totals = rows_of(total_k) + (total_g[0:3, :],)
        for i in range(4):
            momentum, anchor, first, second = small[i]
            flat_moments = i == 1
            if flat_moments:
                moments = first[...], second[...]
            else:
                moments = first[:, 0, :], second[:, 0, :]
            values = settle(totals[i], momentum[...], anchor[...], grads[i] * factor, *moments)
            for n, (out, value) in enumerate(zip(outs[i + 1], values)):
                if n < 3 or flat_moments:
                    out[...] = value
                else:
                    out[:, 0, :] = value


def finish(norms, table, summed, total_k, extra, total_g, small):
    block = pl.BlockSpec((96, SHARD), lambda i: (i, 0))

    def whole(value):
        return pl.BlockSpec(value.shape, lambda i, rank=len(value.shape): (0,) * rank)

    rest = [summed, total_k, extra, total_g] + [value for kind in small for value in kind]
    shapes = [jax.ShapeDtypeStruct((D, SHARD), F32)] * 5
    for momentum, anchor, first, second in small:
        shapes += [jax.ShapeDtypeStruct(momentum.shape, F32)] * 3
        shapes += [jax.ShapeDtypeStruct(first.shape, F32)] * 2
    return pl.pallas_call(
        finish_kernel,
        name="finish",
        grid=(D // 96,),
        out_shape=tuple(shapes),
        in_specs=[whole(norms)] + [block] * 6 + [whole(value) for value in rest],
        out_specs=tuple([block] * 5 + [whole(shape) for shape in shapes[5:]]),
        compiler_params=pltpu.CompilerParams(vmem_limit_bytes=40 * MIB),
        cost_estimate=pl.CostEstimate(flops=2 * 10**7, bytes_accessed=4 * 10**7, transcendentals=0),
    )(norms, *table, *rest)


def dot(spec, a, b):
    return jnp.einsum(spec, a, b, preferred_element_type=F32)


def on_device(
    token_ids,
    targets,
    segment_ids,
    row_counts,
    embed_table_master,
    embed_table_first,
    embed_table_second,
    embed_table_anchor,
    embed_table_momentum,
    attn_in_master,
    attn_in_first,
    attn_in_second,
    attn_in_anchor,
    attn_in_momentum,
    ffn_in_master,
    ffn_in_first,
    ffn_in_second,
    ffn_in_anchor,
    ffn_in_momentum,
    proj_out_master,
    proj_out_first,
    proj_out_second,
    proj_out_anchor,
    proj_out_momentum,
    norm_gains_master,
    norm_gains_first,
    norm_gains_second,
    norm_gains_anchor,
    norm_gains_momentum,
):
    ids = token_ids[0]

    def rows_apart(value):
        return value.transpose(2, 0, 1)

    ffn = [v.T for v in (ffn_in_master[0], ffn_in_first[0], ffn_in_second[0], ffn_in_anchor, ffn_in_momentum)]
    attn = [rows_apart(v) for v in (attn_in_master, attn_in_first, attn_in_second)]
    attn += [attn_in_anchor.T, attn_in_momentum.T]
    proj = [rows_apart(v) for v in (proj_out_master, proj_out_first, proj_out_second)]
    proj += [proj_out_anchor.T, proj_out_momentum.T]
    gains = [v.transpose(1, 0, 2) for v in (norm_gains_master, norm_gains_first, norm_gains_second)]
    gains += [norm_gains_anchor, norm_gains_momentum]
    tables = [v.T for v in (embed_table_master[0], embed_table_first[0], embed_table_second[0])]
    tables += [embed_table_anchor.T, embed_table_momentum.T]
    (
        got, rows, most, table, table_other, rows_t, packed_all, picks, slot_row, hot, goals, weights,
    ) = front(
        token_ids, targets, row_counts[0], tables[0], attn[0], ffn[0], proj[0]
    )
    turns = (most[0, 0] + CAP - 1) // CAP

    def asked_in(turn):
        ids_now = jnp.where(turn > 0, ids, 0)
        owner = ids_now // SHARD
        same = ids_now[:, None] == ids_now[None, :]
        before = jnp.arange(T)[None, :] < jnp.arange(T)[:, None]
        first_seen = ~jnp.any(same & before, 1)
        smaller = (owner[None, :] == owner[:, None]) & (ids_now[None, :] < ids_now[:, None])
        rank = jnp.sum(first_seen[None, :] & smaller, 1, dtype=jnp.int32) - turn * CAP
        slot = jnp.where((rank >= 0) & (rank < CAP), owner * CAP + rank, -1)
        chosen = jnp.arange(NW * CAP)[:, None] == slot[None, :]
        asked = jnp.max(jnp.where(chosen, (ids_now - owner * SHARD)[None, :], -1), 1).reshape(NW, 1, CAP)
        asked = jnp.pad(asked, ((0, 0), (0, 0), (0, 128 - CAP)), constant_values=-1)
        return jnp.pad(asked, ((0, 0), (0, 7), (0, 0))), chosen.astype(BF)

    def more_tokens(carry):
        turn, hidden = carry
        message, chosen = asked_in(turn)
        return turn + 1, hidden + dot("sd,st->td", more_rows(message, table), chosen)

    more = lax.while_loop(
        lambda carry: carry[0] < turns, more_tokens, (jnp.int32(1), jnp.zeros((T, D), F32))
    )[1]

    rot = jnp.asarray(rope())
    final, *kept = forward(more, rows, picks, packed_all, gains[0], rot, segment_ids)
    total = weights[2, 0]
    grad_final, head_own, head_other, loss = head(final, rows_t, table, table_other, goals, weights)
    summed, rows_in, head_in, extra_sum, grad_embedded = back(
        grad_final, kept, packed_all, gains[0], rot, segment_ids, slot_row, loss, head_other
    )

    def more_table(carry):
        turn, grad = carry
        message, chosen = asked_in(turn)
        mine = dot("st,dt->sd", chosen, grad_embedded).astype(BF)
        got_now, rows_now = more_grads(message, mine)
        asked = got_now[:, 0, :CAP].reshape(NW * CAP)
        hot_now = (asked[:, None] == jnp.arange(SHARD)[None, :]).astype(BF)
        return turn + 1, grad + dot("sd,sv->dv", rows_now, hot_now)

    head_grad = lax.while_loop(lambda carry: carry[0] < turns, more_table, (jnp.int32(1), head_own))[1]
    table_grad, total_t, total_k, total_g, norms = update(
        rows_in,
        hot,
        head_grad,
        head_in,
        summed,
        extra_sum,
        tables[:4],
        [kind[i] for i in range(4) for kind in (attn, ffn, proj)],
        gains[:4],
    )
    outs = finish(
        norms,
        (total_t, tables[4], tables[3], table_grad, tables[1], tables[2]),
        summed,
        total_k,
        extra_sum,
        total_g,
        [(kind[4], kind[3], kind[1], kind[2]) for kind in (attn, ffn, proj, gains)],
    )
    results = [extra_sum[3, 0:1], total.reshape(1), norms[0, 0:1]]
    for index in range(5):
        average, outer, weight, first, second = outs[5 * index : 5 * index + 5]
        if index < 4:
            average, outer, weight = average.T, outer.T, weight.T
        if index in (0, 2):
            first, second = first.T[None], second.T[None]
        elif index == 4:
            first, second = first.transpose(1, 0, 2), second.transpose(1, 0, 2)
        else:
            first, second = first.transpose(1, 2, 0), second.transpose(1, 2, 0)
        results += [average, outer, weight, first, second]
    return tuple(results)


def solution(mesh):
    in_specs = (
        P("grp", "wide"),
        P("grp", "wide"),
        P("grp", "wide"),
        P("grp", "wide", None),
        P("grp", "wide", None),
        P("grp", "wide", None),
        P("grp", "wide", None),
        P("wide", None),
        P("wide", None),
        P("grp", None, "wide"),
        P("grp", None, "wide"),
        P("grp", None, "wide"),
        P(None, "wide"),
        P(None, "wide"),
        P("grp", None, "wide"),
        P("grp", None, "wide"),
        P("grp", None, "wide"),
        P(None, "wide"),
        P(None, "wide"),
        P("grp", None, "wide"),
        P("grp", None, "wide"),
        P("grp", None, "wide"),
        P(None, "wide"),
        P(None, "wide"),
        P("grp", None, None),
        P("grp", None, None),
        P("grp", None, None),
        P(),
        P(),
    )
    out_specs = (
        P("grp"),
        P("grp"),
        P("grp"),
        P("wide", None),
        P("wide", None),
        P("wide", None),
        P("grp", "wide", None),
        P("grp", "wide", None),
        P(None, "wide"),
        P(None, "wide"),
        P(None, "wide"),
        P("grp", None, "wide"),
        P("grp", None, "wide"),
        P(None, "wide"),
        P(None, "wide"),
        P(None, "wide"),
        P("grp", None, "wide"),
        P("grp", None, "wide"),
        P(None, "wide"),
        P(None, "wide"),
        P(None, "wide"),
        P("grp", None, "wide"),
        P("grp", None, "wide"),
        P(),
        P(),
        P(),
        P("grp", None, None),
        P("grp", None, None),
    )
    return jax.shard_map(
        on_device, mesh=mesh, in_specs=in_specs, out_specs=out_specs, check_vma=False
    )
```

```python
import functools

import jax
import jax.numpy as jnp
import numpy as np
from jax import lax
from jax.experimental import pallas as pl
from jax.experimental.pallas import tpu as pltpu
from jax.sharding import PartitionSpec as P

D = 576
H = 9
KVH = 3
HD = 64
FF = 1536
QKV = 960
STEP = 8
T = 256
SHARD = 1536
NW = 32
NG = 4
CAP = 32
FFN_AT, DOWN_AT, ATTN_AT, PACKED = 0, 96, 160, 208
SUMMED = 224

beta_one = 0.9
beta_two = 0.999
adam_eps = 1e-08
weight_decay = 0.1
inner_rate = 0.02
gain_rate = 0.2
clip_norm = 0.01
penalty_weight = 0.005
outer_rate = 0.7
outer_momentum = 0.9
rope_base = 100000.0
norm_eps = 1e-05
masked_score = -1e30

BF = jnp.bfloat16
F32 = jnp.float32
MESH = pl.DeviceIdType.MESH
VMEM = pl.BlockSpec(memory_space=pltpu.VMEM)
ANY = pl.BlockSpec(memory_space=pl.ANY)
DMA = pltpu.SemaphoreType.DMA
MIB = 1 << 20


def params(collective, mib):
    return pltpu.CompilerParams(
        collective_id=collective, has_side_effects=True, vmem_limit_bytes=mib * MIB
    )


def place():
    me = lax.axis_index("wide")
    return me, me // 8, lax.rem(me // 4, 2), lax.rem(me, 4)


def flat(y, xh, z):
    return y * 8 + xh * 4 + z


def turn4(at, by):
    return lax.rem(at + by, 4)


def remote(src, dst, ssem, rsem, **device):
    return pltpu.make_async_remote_copy(
        src_ref=src,
        dst_ref=dst,
        send_sem=ssem,
        recv_sem=rsem,
        device_id=device,
        device_id_type=MESH,
    )


def greet_wide(me, grp=None, sides=False, meanwhile=None):
    barrier = pltpu.get_barrier_semaphore()

    def one(k, carry):
        pl.semaphore_signal(
            barrier, inc=1, device_id={"wide": lax.rem(me + k, NW)}, device_id_type=MESH
        )
        return carry

    lax.fori_loop(1, NW, one, 0)
    count = NW - 1
    if grp is not None:
        for k in range(1, NG):
            pl.semaphore_signal(
                barrier, inc=1, device_id={"grp": lax.rem(grp + k, NG)}, device_id_type=MESH
            )
        count += NG - 1
    if sides:
        for step in (1, 3):
            pl.semaphore_signal(barrier, inc=1, device_id=beside(step), device_id_type=MESH)
        count += 2
    if meanwhile is not None:
        meanwhile()
    pl.semaphore_wait(barrier, count)


def near_peers(me, y, xh, z):
    peers = [flat(y, xh, turn4(z, k)) for k in (1, 2, 3)] + [flat(turn4(y, k), xh, z) for k in (1, 2, 3)]
    return peers + [flat(y, 1 - xh, z)]


class Tree:
    def __init__(self, hold, land_z, land_y, land_x, ssem, rsem):
        self.hold, self.lands = hold, (land_z, land_y, land_x)
        self.ssem, self.rsem = ssem, rsem
        me, self.y, self.xh, self.z = place()
        self.sent = []

    def send(self, stage):
        y, xh, z = self.y, self.xh, self.z
        at = (z, y, xh)[stage]
        land, src = self.lands[stage], self.hold.at[stage]
        for k in range(1, 2 if stage == 2 else 4):
            if stage == 0:
                to = flat(y, xh, turn4(z, k))
            elif stage == 1:
                to = flat(turn4(y, k), xh, z)
            else:
                to = flat(y, 1 - xh, z)
            copy = remote(src, land.at[at], self.ssem.at[stage, k], self.rsem.at[stage, at], wide=to)
            copy.start()
            self.sent.append(copy)
        land[at] = self.hold[stage]

    def start(self, value):
        self.hold[0] = value
        self.send(0)

    def collect(self, stage):
        at = (self.z, self.y, self.xh)[stage]
        land = self.lands[stage]
        size = 2 if stage == 2 else 4
        for k in range(1, size):
            other = lax.rem(at + k, size)
            remote(
                land.at[other], land.at[other], self.ssem.at[stage, k], self.rsem.at[stage, other],
                wide=flat(self.y, self.xh, self.z),
            ).wait_recv()
        total = land[0]
        for k in range(1, size):
            total = total + land[k]
        return total

    def next(self, stage):
        self.hold[stage + 1] = self.collect(stage)
        self.send(stage + 1)

    def finish(self):
        for copy in self.sent:
            copy.wait_send()


def tree_scratch(lanes):
    return [
        pltpu.VMEM((3, 8, lanes), F32),
        pltpu.VMEM((4, 8, lanes), F32),
        pltpu.VMEM((4, 8, lanes), F32),
        pltpu.VMEM((2, 8, lanes), F32),
        DMA((3, 4)),
        DMA((3, 4)),
    ]


class Scatter:
    def __init__(self, src_at, dst_at, ssem, rsem, me):
        self.src_at, self.dst_at, self.ssem, self.rsem, self.me = src_at, dst_at, ssem, rsem, me

    def copy(self, k):
        peer = lax.rem(self.me + k, NW)
        return remote(
            self.src_at(peer), self.dst_at(self.me), self.ssem.at[k], self.rsem.at[self.me], wide=peer
        )

    def start(self):
        def one(k, carry):
            self.copy(k).start()
            return carry

        lax.fori_loop(1, NW, one, 0)

    def wait_recv(self):
        def one(k, carry):
            peer = lax.rem(self.me + k, NW)
            remote(
                self.src_at(peer), self.dst_at(peer), self.ssem.at[k], self.rsem.at[peer], wide=peer
            ).wait_recv()
            return carry

        lax.fori_loop(1, NW, one, 0)

    def wait_send(self):
        def one(k, carry):
            self.copy(k).wait_send()
            return carry

        lax.fori_loop(1, NW, one, 0)


class Ring:
    def __init__(self, view, sem, bounds, ssem):
        self.view, self.sem, self.bounds = view, sem, bounds
        self.ssem, self.used, self.sent = ssem, 0, []
        self.me, self.y, self.xh, self.z = place()

    def send(self, src, dst, rsem, to):
        copy = remote(src, dst, self.ssem.at[self.used], rsem, wide=flat(to[0], self.xh, to[1]))
        self.used += 1
        copy.start()
        self.sent.append(copy)

    def piece(self, y, z, first, count):
        return self.view(y, z, self.bounds[first], self.bounds[first + count] - self.bounds[first])

    def pass_on(self, y, z, first, count, index, *to):
        piece = self.piece(y, z, first, count)
        for one in to:
            self.send(piece, piece, self.sem(y, z, index), one)

    def landed(self, piece, sem):
        remote(piece, piece, self.ssem.at[0], sem, wide=self.me).wait_recv()

    def wait(self, y, z, first, count, index):
        self.landed(self.piece(y, z, first, count), self.sem(y, z, index))

    def around(self):
        y, z = self.y, self.z
        return y, z, (turn4(y, 1), z), (turn4(y, 3), z), (y, turn4(z, 1)), (y, turn4(z, 3))

    def own(self, src, dst, index):
        y, z, y_up, y_down, z_up, z_down = self.around()
        for to in (y_up, y_down, z_up, z_down):
            self.send(src, dst, self.sem(y, z, index), to)

    def near(self, parts=None):
        y, z, y_up, y_down, z_up, z_down = self.around()
        for at, far, turn, half, sides in (
            (y_down, y_up, 0, 0, (z_up, z_down)),
            (y_up, y_down, 1, 0, (z_up, z_down)),
            (z_down, z_up, 0, 2, (y_up, y_down)),
            (z_up, z_down, 1, 2, (y_up, y_down)),
        ):
            if parts is None:
                self.wait(*at, 0, 4, 0)
            else:
                for part, index in parts:
                    self.landed(part(*at), self.sem(*at, index))
            self.pass_on(*at, turn, 1, turn, far)
            self.pass_on(*at, 2 + turn, 1, 2 + turn, far)
            self.pass_on(*at, half, 2, half, *sides)

    def far(self):
        y, z, y_up, y_down, z_up, z_down = self.around()
        for at, half, sides in (
            ((turn4(y, 2), z), 0, (z_up, z_down)),
            ((y, turn4(z, 2)), 2, (y_up, y_down)),
        ):
            for index in range(4):
                self.wait(*at, index, 1, index)
            self.pass_on(*at, half, 2, half, *sides)

    def cross(self):
        y, z, y_up, y_down, z_up, z_down = self.around()
        for k in (1, 3, 2):
            row, column = turn4(y, k), turn4(z, k)
            self.wait(row, z_down[1], 0, 2, 0)
            self.pass_on(row, z_down[1], 0, 1, 0, z_up)
            self.wait(row, z_up[1], 0, 2, 0)
            self.pass_on(row, z_up[1], 1, 1, 1, z_down)
            self.wait(y_down[0], column, 2, 2, 2)
            self.pass_on(y_down[0], column, 2, 1, 2, y_up)
            self.wait(y_up[0], column, 2, 2, 2)
            self.pass_on(y_up[0], column, 3, 1, 3, y_down)

    def last(self):
        y, z = self.y, self.z
        for k in (1, 3, 2):
            row, column = turn4(y, k), turn4(z, k)
            for index in range(2):
                self.wait(row, turn4(z, 2), index, 1, index)
                self.wait(turn4(y, 2), column, 2 + index, 1, 2 + index)

    def finish(self):
        for copy in self.sent:
            copy.wait_send()


RING_SENDS = 36


def beside(step):
    me, y, xh, z = place()
    grp = lax.axis_index("grp")
    low = grp // 2
    side = lax.rem(xh + low + (0 if step == 1 else 1), 2)
    return {"grp": (1 - low) * 2 + lax.rem(grp, 2), "wide": flat(y, side, z)}


class Relay:
    def __init__(self, sources, stops, ends, ssem, rsem):
        self.sources, self.stops, self.ends, self.ssem, self.rsem = sources, stops, ends, ssem, rsem

    def copy(self, src, dst, at, step):
        return remote(src, dst, self.ssem.at[at], self.rsem.at[at], **beside(step))

    def legs(self, hop):
        for i, step in enumerate((1, 3)):
            src = self.sources[i] if hop == 0 else self.stops[i]
            dst = self.stops[i] if hop == 0 else self.ends[i]
            yield self.copy(src, dst, 2 * hop + i, step)

    def start(self):
        for copy in self.legs(0):
            copy.start()

    def forward(self):
        for first, second in zip(self.legs(0), self.legs(1)):
            first.wait_recv()
            second.start()

    def wait(self):
        for copy in self.legs(1):
            copy.wait_recv()

    def finish(self):
        for hop in (0, 1):
            for copy in self.legs(hop):
                copy.wait_send()


def look_up(got, table, hot, rows, slot_row):
    asked = got[:, slot_row, :].astype(F32)
    asked = jnp.concatenate([asked, jnp.zeros((128 - NW, 128), F32)], 0).T
    step = 8 * CAP
    for first in range(0, NW, 8):
        for d in range(8):
            column = asked[0:CAP, first + d : first + d + 1]
            lanes = lax.broadcasted_iota(jnp.int32, (CAP, SHARD), 1).astype(F32)
            hot[d * CAP : (d + 1) * CAP, :] = jnp.where(lanes == column, 1.0, 0.0).astype(BF)
        picked = lax.dot_general(
            hot[...], table[...], (((1,), (1,)), ((), ())), preferred_element_type=F32
        )
        rows[first * CAP : first * CAP + step, :] = picked.astype(BF)


def slots(at):
    return pl.ds(pl.multiple_of(at * CAP, CAP), CAP)


def turn_over(table, rows, first):
    for c in range(0, SHARD, 256):
        rows[first + c : first + c + 256, :] = table[:, c : c + 256].T


def owner_of(ids):
    return (((ids >> 9) * 171) >> 9).astype(jnp.int32)


def pack_rows(out, attn, ffn, proj):
    out[FFN_AT:DOWN_AT, :] = ffn
    out[DOWN_AT:ATTN_AT, :] = jnp.zeros((ATTN_AT - DOWN_AT, D), F32)
    for j in range(3):
        at = DOWN_AT + 18 * j
        out[at : at + 18, 0:512] = proj[:, D + 512 * j : D + 512 * (j + 1)]
    out[ATTN_AT : ATTN_AT + 30, :] = attn
    out[ATTN_AT + 30 : PACKED, :] = proj[:, 0:D]


def ask_rows(ids, targets, weight, msg, picks, slot_out):
    row = ids[0:1, :]
    column = jnp.broadcast_to(row.astype(F32), (128, T)).T[:, 0:1].astype(jnp.int32)
    row_owner, column_owner = owner_of(row), owner_of(column)
    down = lax.broadcasted_iota(jnp.int32, (T, T), 0)
    across = lax.broadcasted_iota(jnp.int32, (T, T), 1)
    same = row == column

    def count(which, axis):
        return jnp.sum(jnp.where(which, 1.0, 0.0), axis, keepdims=True)

    first_row = count(same & (down < across), 0) == 0.0
    first_column = count(same & (across < down), 1) == 0.0
    near = row_owner == column_owner
    rank_row = count(near & (column < row) & first_column, 0)
    rank_column = count(near & (row < column) & first_row, 1)
    slot_row = jnp.where(rank_row < CAP, row_owner.astype(F32) * CAP + rank_row, -1.0)
    slot_column = jnp.where(rank_column < CAP, column_owner.astype(F32) * CAP + rank_column, -1.0)
    lanes = lax.broadcasted_iota(jnp.int32, (T, NW * CAP), 1).astype(F32)
    hit = lanes == slot_column
    picks[...] = jnp.where(hit, 1.0, 0.0).astype(BF)
    slot_out[...] = jnp.broadcast_to(slot_row, (8, T)).astype(jnp.int32)
    local = (column - column_owner * SHARD).astype(F32)
    asked = jnp.max(jnp.where(hit, local, -1.0), 0, keepdims=True).astype(jnp.int32)
    most = (jnp.max(rank_row, 1, keepdims=True) + 1.0).astype(jnp.int32)
    rest = [
        targets[0:1, 0:128], targets[0:1, 128:256], weight[:, 0:128], jnp.broadcast_to(most, (1, 128)),
    ] + [jnp.zeros((1, 128), jnp.int32)] * 3
    for g in range(8):
        msg[g] = jnp.concatenate([asked[:, g * 128 : (g + 1) * 128]] + rest, 0)


def find_rows(got, table, asked_t, hot, rows, part):
    asked = got[:, 0, :].astype(F32)
    asked_t[...] = jnp.concatenate([asked, jnp.full((128 - NW, 128), -1.0, F32)], 0).T
    mine = asked_t[pl.ds(pl.multiple_of(part * CAP, CAP), CAP), :]
    lanes = lax.broadcasted_iota(jnp.int32, (CAP, SHARD), 1).astype(F32)
    for d in range(NW):
        hot[d * CAP : (d + 1) * CAP, :] = jnp.where(lanes == mine[:, d : d + 1], 1.0, 0.0).astype(BF)
    step = 16 * CAP
    for first in range(0, NW * CAP, step):
        picked = lax.dot_general(
            hot[first : first + step, :], table[...], (((1,), (1,)), ((), ())), preferred_element_type=F32
        )
        rows[first : first + step, :] = picked.astype(BF)


def turn_over(table, rows, first):
    for c in range(0, SHARD, 256):
        rows[first + c : first + c + 256, :] = table[:, c : c + 256].T


def front_kernel(
    ids, targets, counts, master, attn, ffn, proj,
    got, emb, most_out, table_out, other_out, rows_t_out, packed_all, picks, slot_out, hot_out, goal, weights,
    wide, table, table_other, rows_t, hot, long, packed, most, msg, asked_t, rows, own_most, stops, msg_s, msg_r, emb_s, emb_r, most_s, most_r, swap_s, swap_r,
    ring_s, ring_r, x_sem, local,
):
    me, y, xh, z = place()
    grp = lax.axis_index("grp")
    other = flat(y, 1 - xh, z)
    load = pltpu.make_async_copy(master, wide, local.at[1])
    load.start()
    by_source = lax.broadcasted_iota(jnp.int32, (1, 3), 1) + 1
    weight = jnp.sum((counts[...] * by_source).astype(F32), 1, keepdims=True)
    weight = jnp.broadcast_to(weight, (1, T)).astype(jnp.int32)

    def prepare():
        pack_rows(long, attn[:, 0, :], ffn[...], proj[:, 0, :])
        packed[...] = long[...].astype(BF)
        ask_rows(ids, targets, weight, msg, picks, slot_out)

    greet_wide(me, grp, sides=True, meanwhile=prepare)
    over = remote(packed, packed_all.at[y, z, xh], x_sem.at[0], x_sem.at[1], wide=other)
    over.start()
    ask = Scatter(lambda p: msg.at[p // 4], lambda p: got.at[p], msg_s, msg_r, me)
    ask.start()
    got[me] = msg[me // 4]
    ring = Ring(
        lambda Y, Z, first, count: packed_all.at[Y, Z, :, pl.ds(first, count)],
        lambda Y, Z, index: ring_r.at[Y, Z, index],
        (0, 48, 96, 144, 208),
        ring_s,
    )
    ring.own(packed, packed_all.at[y, z, xh], 0)
    keep = pltpu.make_async_copy(packed, packed_all.at[y, z, xh], local.at[0])
    keep.start()
    load.wait()
    table[...] = wide[...].astype(BF)
    saves = [pltpu.make_async_copy(table, table_out, local.at[1])]
    saves[0].start()
    halves = (pl.ds(0, D // 2), pl.ds(D // 2, D // 2))
    trade = Relay(
        [table.at[half] for half in halves],
        [stops.at[i] for i in range(2)],
        [table_other.at[half] for half in halves],
        swap_s,
        swap_r,
    )
    trade.start()
    over.wait_recv()
    ring.own(packed_all.at[y, z, 1 - xh], packed_all.at[y, z, 1 - xh], 4)
    ask.wait_recv()
    find_rows(got, table, asked_t, hot, rows, lax.rem(me, 4))
    saves.append(pltpu.make_async_copy(hot, hot_out, local.at[2]))
    saves[-1].start()
    ring.near(
        [
            (lambda Y, Z: packed_all.at[Y, Z, xh], 0),
            (lambda Y, Z: packed_all.at[Y, Z, 1 - xh], 4),
        ]
    )
    reply = Scatter(lambda p: rows.at[slots(p)], lambda p: emb.at[slots(p)], emb_s, emb_r, me)
    reply.start()
    emb[slots(me), :] = rows[slots(me), :]
    turn_over(table, rows_t, 0)
    saves.append(pltpu.make_async_copy(rows_t.at[0:SHARD], rows_t_out.at[0:SHARD], local.at[3]))
    saves[-1].start()
    largest = jnp.max(got[:, 4, :], 0, keepdims=True)
    own_most[...] = jnp.broadcast_to(largest, (8, 128))
    most[grp] = own_most[...]
    told = []
    for k in range(1, NG):
        to = lax.rem(grp + k, NG)
        told.append(remote(own_most, most.at[grp], most_s.at[k], most_r.at[grp], grp=to))
        told[-1].start()
    total = jnp.sum(got[:, 3, :].astype(F32), 0, keepdims=True)
    total = jnp.concatenate([total, total], 1) * T
    plain = weight.astype(F32)
    weights[...] = jnp.concatenate([plain / total, plain, total] + [jnp.zeros((1, T), F32)] * 5, 0)

    def place_goal(j, carry):
        from_dev = flat(j // 4, xh, lax.rem(j, 4))
        goals = jnp.concatenate([got[from_dev, 1:2, :], got[from_dev, 2:3, :]], 1)
        near, far = goals - me * SHARD, goals - other * SHARD
        at = jnp.where((far >= 0) & (far < SHARD), far + SHARD, -1)
        at = jnp.where((near >= 0) & (near < SHARD), near, at)
        goal[j] = jnp.broadcast_to(at, (8, T))
        return carry

    lax.fori_loop(0, 16, place_goal, 0)
    trade.forward()
    ring.far()
    ring.cross()
    reply.wait_recv()
    for k in range(1, NG):
        to = lax.rem(grp + k, NG)
        remote(own_most, most.at[to], most_s.at[k], most_r.at[to], grp=to).wait_recv()
    most_out[...] = jnp.maximum(jnp.maximum(most[0], most[1]), jnp.maximum(most[2], most[3]))
    trade.wait()
    saves.append(pltpu.make_async_copy(table_other, other_out, local.at[4]))
    saves[-1].start()
    turn_over(table_other, rows_t, SHARD)
    rest = pl.ds(SHARD, SHARD)
    saves.append(pltpu.make_async_copy(rows_t.at[rest], rows_t_out.at[rest], local.at[5]))
    saves[-1].start()
    ring.last()
    keep.wait()
    for save in saves:
        save.wait()
    over.wait_send()
    ask.wait_send()
    reply.wait_send()
    trade.finish()
    for copy in told:
        copy.wait_send()
    ring.finish()


def front(*args):
    return pl.pallas_call(
        front_kernel,
        name="front",
        out_shape=(
            jax.ShapeDtypeStruct((NW, 8, 128), jnp.int32),
            jax.ShapeDtypeStruct((NW * CAP, D), BF),
            jax.ShapeDtypeStruct((8, 128), jnp.int32),
            jax.ShapeDtypeStruct((D, SHARD), BF),
            jax.ShapeDtypeStruct((D, SHARD), BF),
            jax.ShapeDtypeStruct((2 * SHARD, D), BF),
            jax.ShapeDtypeStruct((4, 4, 2, PACKED, D), BF),
            jax.ShapeDtypeStruct((T, NW * CAP), BF),
            jax.ShapeDtypeStruct((8, T), jnp.int32),
            jax.ShapeDtypeStruct((NW * CAP, SHARD), BF),
            jax.ShapeDtypeStruct((16, 8, T), jnp.int32),
            jax.ShapeDtypeStruct((8, T), F32),
        ),
        in_specs=[VMEM, VMEM, VMEM, ANY, VMEM, VMEM, VMEM],
        out_specs=(VMEM, VMEM, VMEM, ANY, ANY, ANY, ANY, VMEM, VMEM, ANY, VMEM, VMEM),
        scratch_shapes=[
            pltpu.VMEM((D, SHARD), F32),
            pltpu.VMEM((D, SHARD), BF),
            pltpu.VMEM((D, SHARD), BF),
            pltpu.VMEM((2 * SHARD, D), BF),
            pltpu.VMEM((NW * CAP, SHARD), BF),
            pltpu.VMEM((PACKED, D), F32),
            pltpu.VMEM((PACKED, D), BF),
            pltpu.VMEM((NG, 8, 128), jnp.int32),
            pltpu.VMEM((8, 8, 128), jnp.int32),
            pltpu.VMEM((128, 128), F32),
            pltpu.VMEM((NW * CAP, D), BF),
            pltpu.VMEM((8, 128), jnp.int32),
            pltpu.VMEM((2, D // 2, SHARD), BF),
            DMA((NW,)),
            DMA((NW,)),
            DMA((NW,)),
            DMA((NW,)),
            DMA((NG,)),
            DMA((NG,)),
            DMA((4,)),
            DMA((4,)),
            DMA((RING_SENDS + 4,)),
            DMA((4, 4, 5)),
            DMA((2,)),
            DMA((6,)),
        ],
        compiler_params=params(1, 60),
        cost_estimate=pl.CostEstimate(flops=2 * 10**9, bytes_accessed=3 * 10**7, transcendentals=0),
    )(*args)


ORDER = tuple((i // 8) * 8 + (i % 2) * 4 + (i // 2) % 4 for i in range(NW))


def spread_rows(used, stride, at, repeat=1):
    picks = np.zeros((NW * stride, NW * used), np.float32)
    for i, w in enumerate(ORDER):
        for j in range(repeat):
            for r in range(used):
                picks[i * stride + at + j * used + r, w * used + r] = 1.0
    return picks


def rope():
    half = HD // 2
    freqs = np.float32(rope_base) ** (-(np.arange(half, dtype=np.float32) * np.float32(2.0)) / np.float32(HD))
    angles = freqs.astype(np.float32)[:, None] * np.arange(T, dtype=np.float32)[None, :]
    return np.concatenate([np.cos(angles), np.sin(angles)], 0).astype(np.float32)


def turned(values):
    return values.T


def gain_columns(gains):
    return jnp.concatenate([gains[:, 0, :], jnp.zeros((125, D), F32)], 0).T


def rms(values, gain):
    scale = lax.rsqrt(jnp.mean(values * values, 0, keepdims=True) + norm_eps)
    return values * scale * gain


def rms_back(values, gain, grad):
    scale = lax.rsqrt(jnp.mean(values * values, 0, keepdims=True) + norm_eps)
    pulled = grad * gain
    middle = jnp.mean(values * pulled, 0, keepdims=True)
    back = scale * pulled - values * (scale * scale * scale) * middle
    return back, jnp.sum(grad * values * scale, 1, keepdims=True)


def mask_of(tok):
    row = tok[0:1, :]
    column = jnp.broadcast_to(row.astype(F32), (128, T)).T[:, 0:1].astype(jnp.int32)
    down = lax.broadcasted_iota(jnp.int32, (T, T), 0)
    across = lax.broadcasted_iota(jnp.int32, (T, T), 1)
    return (down <= across) & (row == column)


def mm(a, b):
    return jnp.dot(a, b, preferred_element_type=F32)


def mm_nt(a, b):
    return lax.dot_general(a, b, (((1,), (1,)), ((), ())), preferred_element_type=F32)


def mm_tn(a, b):
    return lax.dot_general(a, b, (((0,), (0,)), ((), ())), preferred_element_type=F32)


def rotated(x, rot):
    cosine, sine = rot[0:32, :], rot[32:64, :]
    one, two = x[0:32, :], x[32:64, :]
    return jnp.concatenate([one * cosine - two * sine, two * cosine + one * sine], 0)


def unrotated(x, rot):
    cosine, sine = rot[0:32, :], rot[32:64, :]
    one, two = x[0:32, :], x[32:64, :]
    return jnp.concatenate([one * cosine + two * sine, two * cosine - one * sine], 0)


def load_trunk(packed, ffn, down, attn, sem):
    loads = [
        pltpu.make_async_copy(packed.at[:, :, :, ATTN_AT:PACKED], attn, sem.at[0]),
        pltpu.make_async_copy(packed.at[:, :, :, FFN_AT:DOWN_AT], ffn, sem.at[1]),
        pltpu.make_async_copy(packed.at[:, :, :, DOWN_AT:ATTN_AT, 0:512], down, sem.at[2]),
    ]
    for load in loads:
        load.start()
    return loads


TRUNK_SCRATCH = [
    pltpu.VMEM((4, 4, 2, 96, D), BF),
    pltpu.VMEM((4, 4, 2, 64, 512), BF),
    pltpu.VMEM((4, 4, 2, 48, D), BF),
    DMA((3,)),
]


def forward_kernel(
    more, emb, picks, packed, gains, rot, tok,
    final, h0, n1, q, k, v, lse, att, h1, n2, gate_up_out, inner, h2,
    ffn, down, attn, sem, mixed, gate_up, save_sem,
):
    loads = load_trunk(packed, ffn, down, attn, sem)
    columns = gain_columns(gains)
    allowed = mask_of(tok)
    start = turned(mm(picks[...], emb[...])) + more[...]
    h0[...] = start
    normed = rms(start, columns[:, 0:1]).astype(BF)
    n1[...] = normed
    loads[0].wait()
    rows48 = attn[...].reshape(NW * 48, D)
    product = mm(rows48, normed)
    for i, w in enumerate(ORDER):
        mixed[w * 30 : w * 30 + 30, :] = product[i * 48 : i * 48 + 30, :]
    for kv in range(KVH):
        k[kv * HD : (kv + 1) * HD, :] = rotated(
            mixed[D + kv * HD : D + (kv + 1) * HD, :], rot[...]
        ).astype(BF)
        at = D + (KVH + kv) * HD
        v[kv * HD : (kv + 1) * HD, :] = mixed[at : at + HD, :].astype(BF)
    logs = []
    for h in range(H):
        kv = h // (H // KVH)
        query = rotated(mixed[h * HD : (h + 1) * HD, :], rot[...]).astype(BF)
        q[h * HD : (h + 1) * HD, :] = query
        scores = mm_tn(k[kv * HD : (kv + 1) * HD, :], query) * HD ** (-0.5)
        scores = jnp.where(allowed, scores, masked_score)
        top = jnp.max(scores, 0, keepdims=True)
        power = jnp.exp(scores - top)
        total = jnp.sum(power, 0, keepdims=True)
        probs = (power / total).astype(BF)
        att[h * HD : (h + 1) * HD, :] = mm(v[kv * HD : (kv + 1) * HD, :], probs).astype(BF)
        logs.append(top + jnp.log(total))
    lse[...] = jnp.concatenate(logs + [jnp.zeros((16 - H, T), F32)], 0)
    product = mm(rows48, att[...])
    for i, w in enumerate(ORDER):
        mixed[w * 18 : w * 18 + 18, :] = product[i * 48 + 30 : i * 48 + 48, :]
    middle = start + mixed[0:D, :]
    h1[...] = middle
    normed = rms(middle, columns[:, 1:2]).astype(BF)
    n2[...] = normed
    loads[1].wait()
    gate_up[...] = mm(ffn[...].reshape(NW * 96, D), normed)
    save = pltpu.make_async_copy(gate_up, gate_up_out, save_sem.at[0])
    save.start()
    for i in range(NW // 2):
        gate = gate_up[i * 96 : (i + 1) * 96, :]
        up = gate_up[FF + i * 96 : FF + (i + 1) * 96, :]
        w = ORDER[i]
        inner[w * 96 : (w + 1) * 96, :] = (gate / (1.0 + jnp.exp(-gate)) * up).astype(BF)
    loads[2].wait()
    rows64 = down[...].reshape(NW * 64, 512)
    for j in range(3):
        product = mm(rows64, inner[j * 512 : (j + 1) * 512, :])
        for i, w in enumerate(ORDER):
            piece = product[i * 64 + j * 18 : i * 64 + j * 18 + 18, :]
            if j:
                mixed[w * 18 : w * 18 + 18, :] += piece
            else:
                mixed[w * 18 : w * 18 + 18, :] = piece
    last = middle + mixed[0:D, :]
    h2[...] = last
    final[...] = rms(last, columns[:, 2:3]).astype(BF)
    save.wait()


def forward(more, emb, picks, packed, gains, rot, tok):
    def out(rows, kind):
        return jax.ShapeDtypeStruct((rows, T), kind)

    return pl.pallas_call(
        forward_kernel,
        name="forward",
        out_shape=(
            out(D, BF), out(D, F32), out(D, BF), out(D, BF), out(KVH * HD, BF), out(KVH * HD, BF), out(16, F32),
            out(D, BF), out(D, F32), out(D, BF), out(2 * FF, F32), out(FF, BF), out(D, F32),
        ),
        in_specs=[VMEM, VMEM, VMEM, ANY, VMEM, VMEM, VMEM],
        out_specs=(VMEM,) * 10 + (ANY, VMEM, VMEM),
        scratch_shapes=TRUNK_SCRATCH
        + [pltpu.VMEM((QKV, T), F32), pltpu.VMEM((2 * FF, T), F32), DMA((1,))],
        compiler_params=pltpu.CompilerParams(vmem_limit_bytes=60 * MIB),
        cost_estimate=pl.CostEstimate(flops=4 * 10**9, bytes_accessed=2 * 10**7, transcendentals=10**6),
    )(more, emb, picks, packed, gains, rot, tok)


def more_rows_kernel(msg, table, got, emb, hot, rows, msg_s, msg_r, emb_s, emb_r):
    me = lax.axis_index("wide")
    greet_wide(me)
    ask = Scatter(lambda p: msg.at[p], lambda p: got.at[p], msg_s, msg_r, me)
    ask.start()
    got[me] = msg[me]
    ask.wait_recv()
    look_up(got, table, hot, rows, 0)
    reply = Scatter(lambda p: rows.at[slots(p)], lambda p: emb.at[slots(p)], emb_s, emb_r, me)
    reply.start()
    emb[slots(me), :] = rows[slots(me), :]
    reply.wait_recv()
    ask.wait_send()
    reply.wait_send()


def more_rows(msg, table):
    return pl.pallas_call(
        more_rows_kernel,
        name="more_rows",
        out_shape=(
            jax.ShapeDtypeStruct((NW, 8, 128), jnp.int32),
            jax.ShapeDtypeStruct((NW * CAP, D), BF),
        ),
        in_specs=[VMEM, VMEM],
        out_specs=(VMEM, VMEM),
        scratch_shapes=[pltpu.VMEM((8 * CAP, SHARD), BF), pltpu.VMEM((NW * CAP, D), BF)]
        + [DMA((NW,))] * 4,
        compiler_params=params(2, 40),
    )(msg, table)[1]


def more_grads_kernel(msg, rows, got, out, msg_s, msg_r, row_s, row_r):
    me = lax.axis_index("wide")
    greet_wide(me)
    ask = Scatter(lambda p: msg.at[p], lambda p: got.at[p], msg_s, msg_r, me)
    ask.start()
    give = Scatter(lambda p: rows.at[slots(p)], lambda p: out.at[slots(p)], row_s, row_r, me)
    give.start()
    got[me] = msg[me]
    out[slots(me), :] = rows[slots(me), :]
    ask.wait_recv()
    give.wait_recv()
    ask.wait_send()
    give.wait_send()


def more_grads(msg, rows):
    return pl.pallas_call(
        more_grads_kernel,
        name="more_grads",
        out_shape=(
            jax.ShapeDtypeStruct((NW, 8, 128), jnp.int32),
            jax.ShapeDtypeStruct((NW * CAP, D), BF),
        ),
        in_specs=[VMEM, VMEM],
        out_specs=(VMEM, VMEM),
        scratch_shapes=[DMA((NW,))] * 4,
        compiler_params=params(3, 20),
    )(msg, rows)


VOC = 2 * SHARD
TOK = 16 * T
CH = 512
NCH = VOC // CH
QUART = D // 4


def cols(j):
    return pl.ds(pl.multiple_of(j * T, T), T)


def head_kernel(
    final, rows_t, table_in, table_other_in, goal, weights,
    grad_final, head_out, head_other, loss,
    table, table_other, head_own, big, fall, expo, tops, stat, stat_in, coef, coef_in, parts,
    part_a, part_b, whole_a, whole_b, sum_a, sum_b, part_a2, part_b2, whole_a2, whole_b2,
    g_s, g_r, st_s, st_r, co_s, co_r, a_s, b_s, pa_r, pb_r, wa_r, wb_r, a2_s, b2_s, a2_r, b2_r,
):
    me, y, xh, z = place()
    mine = y * 4 + z
    tables = [
        pltpu.make_async_copy(table_in, table, big.at[0]),
        pltpu.make_async_copy(table_other_in, table_other, big.at[1]),
    ]
    for load in tables:
        load.start()

    def dev(j):
        return flat(j // 4, xh, lax.rem(j, 4))

    barrier = pltpu.get_barrier_semaphore()

    def greet(k, carry):
        pl.semaphore_signal(
            barrier, inc=1, device_id={"wide": dev(lax.rem(mine + k, 16))}, device_id_type=MESH
        )
        return carry

    lax.fori_loop(1, 16, greet, 0)
    pl.semaphore_wait(barrier, 15)

    sent = []

    def send(src, dst, ssem, rsem, to):
        copy = remote(src, dst, ssem, rsem, wide=to)
        copy.start()
        sent.append(copy)

    def arrived(dst, rsem):
        remote(dst, dst, g_s.at[0], rsem, wide=dev(mine)).wait_recv()

    ring = Ring(
        lambda Y, Z, first, count: fall.at[pl.ds(first, count), cols(Y * 4 + Z)],
        lambda Y, Z, index: g_r.at[Y * 4 + Z, index],
        tuple(QUART * k for k in range(5)),
        g_s,
    )
    ring.own(final, fall.at[:, cols(mine)], 0)
    fall[:, cols(mine)] = final[...]

    def logits(j):
        seen = fall[:, cols(j)]
        goals = goal[j]
        group, hit = goals >> 3, jnp.zeros((8, T), F32)
        tip, weight = [], []
        for c in range(NCH):
            part = jnp.dot(rows_t[c * CH : (c + 1) * CH, :], seen, preferred_element_type=F32)
            top = jnp.max(part, 0, keepdims=True)
            power = jnp.exp(part - top)
            for r in range(CH // 8):
                hit = jnp.where(group == c * (CH // 8) + r, part[8 * r : 8 * r + 8, :], hit)
            expo[c * CH : (c + 1) * CH, cols(j)] = power.astype(BF)
            tip.append(top)
            weight.append(jnp.sum(power, 0, keepdims=True))
        spot = lax.broadcasted_iota(jnp.int32, (8, T), 0)
        hit = jnp.sum(jnp.where(spot == (goals & 7), hit, 0.0), 0, keepdims=True)
        top = functools.reduce(jnp.maximum, tip)
        total = sum(w * jnp.exp(t - top) for w, t in zip(weight, tip))
        zero = jnp.zeros((1, T), F32)
        tops[j] = jnp.concatenate(tip + [zero] * (8 - NCH), 0)
        stat[j] = jnp.concatenate([top, total, hit] + [zero] * 5, 0)

    def tell(j):
        return remote(stat.at[j], stat_in.at[mine], st_s.at[j], st_r.at[mine], wide=dev(j))

    def block(dy, dz):
        return turn4(y, dy) * 4 + turn4(z, dz)

    def forward(offsets):
        def one(k, carry):
            j = block(*offsets(k))
            logits(j)
            tell(j).start()
            return carry

        return one

    def odd(k):
        return 1 + 2 * lax.rem(k, 2)

    logits(mine)
    stat_in[mine] = stat[mine]
    ring.near()
    lax.fori_loop(0, 4, forward(lambda k: ((1 - k // 2) * odd(k), (k // 2) * odd(k))), 0)
    ring.far()
    lax.fori_loop(0, 2, forward(lambda k: (2 * (1 - k), 2 * k)), 0)
    ring.cross()
    lax.fori_loop(0, 4, forward(lambda k: (odd(k // 2), odd(k))), 0)
    ring.last()
    lax.fori_loop(
        0,
        4,
        forward(lambda k: (2 * (1 - k // 2) + odd(k) * (k // 2), odd(k) * (1 - k // 2) + 2 * (k // 2))),
        0,
    )
    forward(lambda k: (2, 2))(0, 0)

    def hear(k, carry):
        j = lax.rem(mine + k, 16)
        arrived(stat_in.at[j], st_r.at[j])
        return carry

    lax.fori_loop(1, 16, hear, 0)
    tip, weight, hit = stat_in[:, 0, :], stat_in[:, 1, :], stat_in[:, 2, :]
    top = jnp.max(tip, 0, keepdims=True)
    lse = top + jnp.log(jnp.sum(weight * jnp.exp(tip - top), 0, keepdims=True))
    picked = jnp.sum(hit, 0, keepdims=True)
    share, plain = weights[0:1, :], weights[1:2, :]
    zero = jnp.zeros((1, T), F32)
    coef[...] = jnp.concatenate(
        [lse, share * (1.0 + 2.0 * penalty_weight * lse), share] + [zero] * 5, 0
    )
    loss[...] = jnp.concatenate(
        [plain * (lse - picked + penalty_weight * lse * lse)] + [zero] * 7, 0
    )
    coef_in[mine] = coef[...]

    def spread(k):
        j = lax.rem(mine + k, 16)
        return remote(coef, coef_in.at[mine], co_s.at[k], co_r.at[mine], wide=dev(j))

    def spread_start(k, carry):
        spread(k).start()
        return carry

    lax.fori_loop(1, 16, spread_start, 0)

    up, down = 1, 3
    z_to = {step: flat(y, xh, turn4(z, step)) for step in (up, down)}
    y_to = {step: flat(turn4(y, step), xh, z) for step in (up, down)}

    def piece_a(j, index):
        row = j // 4
        return remote(
            parts.at[j, pl.ds(index * QUART, QUART)], part_a.at[index, row],
            a_s.at[j, index], pa_r.at[index, row], wide=z_to[(up, down)[index]],
        )

    def piece_b(j, index):
        column = lax.rem(j, 4)
        return remote(
            parts.at[j, pl.ds((2 + index) * QUART, QUART)], part_b.at[index, column],
            b_s.at[j, index], pb_r.at[index, column], wide=y_to[(up, down)[index]],
        )

    def half_a(j, index):
        row = j // 4
        return remote(
            parts.at[j, pl.ds(0, 2 * QUART)], whole_a.at[index, row],
            a_s.at[j, 0], wa_r.at[index, row], wide=z_to[(up, down)[index]],
        )

    def half_b(j, index):
        column = lax.rem(j, 4)
        return remote(
            parts.at[j, pl.ds(2 * QUART, 2 * QUART)], whole_b.at[index, column],
            b_s.at[j, 0], wb_r.at[index, column], wide=y_to[(up, down)[index]],
        )

    def offsets(k):
        return lax.rem(2 + k // 4, 4), lax.rem(2 + k, 4)

    def post(k):
        dy, dz = offsets(k)
        j = block(dy, dz)

        @pl.when(dz == 2)
        def _():
            piece_a(j, 0).start()
            piece_a(j, 1).start()

        @pl.when(dy == 2)
        def _():
            piece_b(j, 0).start()
            piece_b(j, 1).start()

        for index, step in enumerate((up, down)):

            @pl.when(dz == step)
            def _():
                row = j // 4
                arrived(part_a.at[index, row], pa_r.at[index, row])
                rows = pl.ds(index * QUART, QUART)
                total = parts[j, rows, :].astype(F32) + part_a[index, row].astype(F32)
                parts[j, rows, :] = total.astype(BF)
                half_a(j, index).start()

            @pl.when(dy == step)
            def _():
                column = lax.rem(j, 4)
                arrived(part_b.at[index, column], pb_r.at[index, column])
                rows = pl.ds((2 + index) * QUART, QUART)
                total = parts[j, rows, :].astype(F32) + part_b[index, column].astype(F32)
                parts[j, rows, :] = total.astype(BF)
                half_b(j, index).start()

    def backward(k, carry):
        j = block(*offsets(k))

        @pl.when(k != 10)
        def _():
            arrived(coef_in.at[j], co_r.at[j])

        lse, soft, pick = coef_in[j, 0:1, :], coef_in[j, 1:2, :], coef_in[j, 2:3, :]
        goals = goal[j]
        group = goals >> 3
        pick = jnp.where(lax.broadcasted_iota(jnp.int32, (8, T), 0) == (goals & 7), pick, 0.0)
        for c in range(NCH):
            scale = soft * jnp.exp(tops[j, c : c + 1, :] - lse)
            power = expo[c * CH : (c + 1) * CH, cols(j)].astype(F32)
            spot = lax.broadcasted_iota(jnp.int32, (CH // 8, 8, T), 0) + c * (CH // 8)
            drop = jnp.where(spot == group[None], pick[None], 0.0).reshape(CH, T)
            expo[c * CH : (c + 1) * CH, cols(j)] = (power * scale - drop).astype(BF)
        product = jnp.dot(table[...], expo[0:SHARD, cols(j)], preferred_element_type=F32)
        product += jnp.dot(table_other[...], expo[SHARD:VOC, cols(j)], preferred_element_type=F32)
        parts[j] = product.astype(BF)

        @pl.when(k > 0)
        def _():
            post(k - 1)

        return carry

    for load in tables:
        load.wait()
    lax.fori_loop(0, 16, backward, 0)
    post(15)

    def head_chunk(c):
        return lax.dot_general(
            fall[...],
            expo[pl.ds(pl.multiple_of(c * 256, 256), 256), :],
            (((1,), (1,)), ((), ())),
            preferred_element_type=F32,
        )

    def other_chunk(c, carry):
        head_other[:, cols(c)] = head_chunk(c + SHARD // 256).astype(BF)
        return carry

    def own_chunk(c, carry):
        head_own[:, cols(c)] = head_chunk(c)
        return carry

    lax.fori_loop(0, SHARD // 256, other_chunk, 0)

    kinds = (
        (whole_a, wa_r, sum_a, part_a2, whole_a2, a2_s, a2_r, y_to, 0),
        (whole_b, wb_r, sum_b, part_b2, whole_b2, b2_s, b2_r, z_to, 2 * QUART),
    )
    for d in (2, 1, 3, 0):
        for kind, (whole, w_r, total, part2, whole2, s2, r2, to, base) in enumerate(kinds):
            at = turn4(y if kind == 0 else z, d)
            j = at * 4 + z if kind == 0 else y * 4 + at
            acc = parts[j, base : base + 2 * QUART, :].astype(F32)
            for index in range(2):
                arrived(whole.at[index, at], w_r.at[index, at])
                acc = acc + whole[index, at].astype(F32)
            if d == 0:
                grad_final[base : base + 2 * QUART, :] = acc
            else:
                total[d - 1] = acc.astype(BF)
            if d == 2:
                for index, step in enumerate((up, down)):
                    piece = total.at[1, pl.ds(index * QUART, QUART)]
                    send(piece, part2.at[index], s2.at[index], r2.at[index], to[step])
    lax.fori_loop(0, SHARD // 512, own_chunk, 0)
    for kind, (whole, w_r, total, part2, whole2, s2, r2, to, base) in enumerate(kinds):
        for index, step in enumerate((up, down)):
            arrived(part2.at[index], r2.at[index])
            rows = pl.ds(index * QUART, QUART)
            added = total[step - 1, rows, :].astype(F32) + part2[index].astype(F32)
            total[step - 1, rows, :] = added.astype(BF)
            send(total.at[step - 1], whole2.at[index], s2.at[2 + index], r2.at[2 + index], to[step])
    lax.fori_loop(SHARD // 512, SHARD // 256, own_chunk, 0)
    store = pltpu.make_async_copy(head_own, head_out, big.at[0])
    store.start()
    for kind, (whole, w_r, total, part2, whole2, s2, r2, to, base) in enumerate(kinds):
        for index in range(2):
            arrived(whole2.at[index], r2.at[2 + index])
        grad_final[base : base + 2 * QUART, :] += whole2[0].astype(F32) + whole2[1].astype(F32)

    def finish(k, carry):
        j = lax.rem(mine + k, 16)
        tell(j).wait_send()
        spread(k).wait_send()
        return carry

    lax.fori_loop(1, 16, finish, 0)
    for copy in sent:
        copy.wait_send()
    ring.finish()

    def finish_pieces(k, carry):
        row, column = block(k, 2), block(2, k)
        piece_a(row, 0).wait_send()
        piece_a(row, 1).wait_send()
        piece_b(column, 0).wait_send()
        piece_b(column, 1).wait_send()
        for index, step in enumerate((up, down)):
            half_a(block(k, step), index).wait_send()
            half_b(block(step, k), index).wait_send()
        return carry

    lax.fori_loop(0, 4, finish_pieces, 0)
    store.wait()


def head(final, rows_t, table, table_other, goal, weights):
    return pl.pallas_call(
        head_kernel,
        name="head",
        out_shape=(
            jax.ShapeDtypeStruct((D, T), F32),
            jax.ShapeDtypeStruct((D, SHARD), F32),
            jax.ShapeDtypeStruct((D, SHARD), BF),
            jax.ShapeDtypeStruct((8, T), F32),
        ),
        in_specs=[VMEM, VMEM, ANY, ANY, VMEM, VMEM],
        out_specs=(VMEM, ANY, VMEM, VMEM),
        scratch_shapes=[
            pltpu.VMEM((D, SHARD), BF),
            pltpu.VMEM((D, SHARD), BF),
            pltpu.VMEM((D, SHARD), F32),
            DMA((2,)),
            pltpu.VMEM((D, TOK), BF),
            pltpu.VMEM((VOC, TOK), BF),
            pltpu.VMEM((16, 8, T), F32),
            pltpu.VMEM((16, 8, T), F32),
            pltpu.VMEM((16, 8, T), F32),
            pltpu.VMEM((8, T), F32),
            pltpu.VMEM((16, 8, T), F32),
            pltpu.VMEM((16, D, T), BF),
            pltpu.VMEM((2, 4, QUART, T), BF),
            pltpu.VMEM((2, 4, QUART, T), BF),
            pltpu.VMEM((2, 4, 2 * QUART, T), BF),
            pltpu.VMEM((2, 4, 2 * QUART, T), BF),
            pltpu.VMEM((3, 2 * QUART, T), BF),
            pltpu.VMEM((3, 2 * QUART, T), BF),
            pltpu.VMEM((2, QUART, T), BF),
            pltpu.VMEM((2, QUART, T), BF),
            pltpu.VMEM((2, 2 * QUART, T), BF),
            pltpu.VMEM((2, 2 * QUART, T), BF),
            DMA((RING_SENDS,)),
            DMA((16, 4)),
            DMA((16,)),
            DMA((16,)),
            DMA((16,)),
            DMA((16,)),
            DMA((16, 2)),
            DMA((16, 2)),
            DMA((2, 4)),
            DMA((2, 4)),
            DMA((2, 4)),
            DMA((2, 4)),
            DMA((4,)),
            DMA((4,)),
            DMA((4,)),
            DMA((4,)),
        ],
        compiler_params=params(4, 61),
        cost_estimate=pl.CostEstimate(
            flops=6 * VOC * TOK * D, bytes_accessed=2 * 10**7, transcendentals=VOC * TOK
        ),
    )(final, rows_t, table, table_other, goal, weights)


class Reduce:
    def __init__(self, parts, base, sizes, along_z, refs):
        (
            self.first, part_a, part_b, self.whole1, self.second, next_a, next_b, self.whole2,
            self.third, self.stop, self.third_in, self.s, self.r,
        ) = refs
        self.part1, self.part2 = (part_a, part_b), (next_a, next_b)
        self.parts, self.base, self.sizes, self.along_z = parts, base, sizes, along_z
        self.rows = (pl.ds(0, sizes[0]), pl.ds(sizes[0], sizes[1]), pl.ds(0, sum(sizes)))
        self.me, self.y, self.xh, self.z = place()
        self.sent = []

    def send(self, src, dst, at, **to):
        copy = remote(src, dst, self.s.at[at], self.r.at[at], **to)
        copy.start()
        self.sent.append(copy)

    def wait(self, dst, at):
        remote(dst, dst, self.s.at[at], self.r.at[at], wide=self.me).wait_recv()

    def item1(self, step, which):
        rows = pl.ds(self.base + self.rows[which].start, self.rows[which].size)
        if self.along_z:
            return (slice(None), turn4(self.z, step), slice(None), rows)
        return (turn4(self.y, step), slice(None), slice(None), rows)

    def item2(self, step, which):
        return (turn4(self.y if self.along_z else self.z, step), slice(None), self.rows[which])

    def to(self, stage, step):
        if self.along_z == (stage == 1):
            return flat(self.y, self.xh, turn4(self.z, step))
        return flat(turn4(self.y, step), self.xh, self.z)

    def split(self, stage, ref, item, part, base):
        for index, step in enumerate((1, 3)):
            self.send(ref.at[item(2, index)], part[index], base + index, wide=self.to(stage, step))

    def join(self, stage, ref, item, part, whole, base):
        for index, step in enumerate((1, 3)):
            self.wait(part[index], base + index)
            at = item(step, index)
            ref[at] = (ref[at].astype(F32) + part[index][...].astype(F32)).astype(BF)
            self.send(ref.at[item(step, 2)], whole.at[index], base + 2 + index, wide=self.to(stage, step))

    def add(self, ref, item, whole, base):
        acc = ref[item(0, 2)].astype(F32)
        for index in range(2):
            self.wait(whole.at[index], base + 2 + index)
            acc = acc + whole[index].astype(F32)
        return acc

    def one(self):
        self.split(1, self.parts, self.item1, self.part1, 0)

    def two(self):
        self.join(1, self.parts, self.item1, self.part1, self.whole1, 0)

    def three(self):
        self.first[...] = self.add(self.parts, self.item1, self.whole1, 0).astype(BF)
        self.split(2, self.first, self.item2, self.part2, 4)

    def four(self):
        self.join(2, self.first, self.item2, self.part2, self.whole2, 4)

    def five(self):
        self.second[...] = self.add(self.first, self.item2, self.whole2, 4)
        self.third[...] = self.second[1 - self.xh].astype(BF)
        self.send(self.third, self.stop, 8, **beside(1 if self.along_z else 3))

    def six(self):
        self.wait(self.stop, 8)
        self.send(self.stop, self.third_in, 9, **beside(1 if self.along_z else 3))

    def total(self):
        self.wait(self.third_in, 9)
        return self.second[self.xh] + self.third_in[...].astype(F32)

    def finish(self):
        for copy in self.sent:
            copy.wait_send()


STREAMS = ((0, (48, 32), True), (80, (48, 32), False), (160, (16, 16), True), (192, (16, 16), False))


def reduce_scratch():
    shapes = []
    for _, sizes, _ in STREAMS:
        half = sum(sizes)
        shapes += [
            pltpu.VMEM((4, 2, half, D), BF),
            pltpu.VMEM((4, 2, sizes[0], D), BF),
            pltpu.VMEM((4, 2, sizes[1], D), BF),
            pltpu.VMEM((2, 4, 2, half, D), BF),
            pltpu.VMEM((2, half, D), F32),
            pltpu.VMEM((2, sizes[0], D), BF),
            pltpu.VMEM((2, sizes[1], D), BF),
            pltpu.VMEM((2, 2, half, D), BF),
            pltpu.VMEM((half, D), BF),
            pltpu.VMEM((half, D), BF),
            pltpu.VMEM((half, D), BF),
            DMA((10,)),
            DMA((10,)),
        ]
    return shapes


def back_kernel(
    grad_final, h0, n1, q, k, v, lse, att, h1, n2, gate_up_in, inner, h2,
    packed, gains, rot, tok, slot_row, loss, head_other, lay_attn_in, lay_out_in, lay_down_in,
    summed, rows_in, head_in, extra_sum, grad_embedded,
    ffn, down, attn, sem, lay_attn, lay_out, lay_down, lay_sem, gate_up, parts, rows, grad_up, grad_mixed, spread, stops,
    row_s, row_r, swap_s, swap_r, hold, land_z, land_y, land_x, tree_s, tree_r, *reducers,
):
    me, y, xh, z = place()
    lays = [
        pltpu.make_async_copy(src, dst, lay_sem.at[i])
        for i, (src, dst) in enumerate(
            ((lay_down_in, lay_down), (lay_out_in, lay_out), (lay_attn_in, lay_attn))
        )
    ]
    lays.append(pltpu.make_async_copy(gate_up_in, gate_up, lay_sem.at[3]))
    lays[0].start()
    lays[3].start()
    loads = load_trunk(packed, ffn, down, attn, sem)
    lays[1].start()
    lays[2].start()
    columns = gain_columns(gains)
    begun = []

    def begin():
        begun.extend(rms_back(h2[...], columns[:, 2:3], grad_final[...]))
        lays[0].wait()
        spread[...] = mm(lay_down[...], begun[0].astype(BF)).astype(BF)

    greet_wide(me, sides=True, meanwhile=begin)
    grad_h2, gain3 = begun
    halves = (pl.ds(0, D // 2), pl.ds(D // 2, D // 2))
    trade = Relay(
        [head_other.at[half] for half in halves],
        [stops.at[i] for i in range(2)],
        [head_in.at[half] for half in halves],
        swap_s,
        swap_r,
    )
    trade.start()
    streams = [
        Reduce(parts, base, sizes, along, reducers[13 * i : 13 * i + 13])
        for i, (base, sizes, along) in enumerate(STREAMS)
    ]
    early, late = streams[:2], streams[2:]
    chunk = lax.broadcasted_iota(jnp.int32, (NW * 64, T), 0) & 63
    zero = jnp.zeros((NW * 64, T), BF)
    wide = jnp.concatenate(
        [
            jnp.where((chunk >= 18 * j) & (chunk < 18 * (j + 1)), spread[...].astype(F32), 0.0).astype(BF)
            for j in range(3)
        ],
        1,
    )
    inners = jnp.concatenate([inner[j * 512 : (j + 1) * 512, :] for j in range(3)], 1)
    grad_down = mm_nt(wide, inners).astype(BF).reshape(4, 4, 2, 64, 512)
    parts[:, :, :, DOWN_AT:ATTN_AT, 0:512] = grad_down
    parts[:, :, :, DOWN_AT:ATTN_AT, 512:D] = jnp.zeros((4, 4, 2, 64, D - 512), BF)
    loads[2].wait()
    grad_inner = mm_tn(down[...].reshape(NW * 64, 512), wide)
    lays[3].wait()
    for i in range(NW // 2):
        w = ORDER[i]
        gate = gate_up[i * 96 : (i + 1) * 96, :]
        up = gate_up[FF + i * 96 : FF + (i + 1) * 96, :]
        pieces = []
        for at in range(w * 96, w * 96 + 96, 32):
            j, r = at // 512, at % 512
            pieces.append(grad_inner[r : r + 32, j * T : (j + 1) * T])
        grad = jnp.concatenate(pieces, 0)
        sigmoid = 1.0 / (1.0 + jnp.exp(-gate))
        slope = sigmoid * (1.0 + gate * (1.0 - sigmoid))
        grad_up[i * 96 : (i + 1) * 96, :] = (grad * up * slope).astype(BF)
        grad_up[FF + i * 96 : FF + (i + 1) * 96, :] = (grad * (gate * sigmoid)).astype(BF)
    parts[:, :, :, FFN_AT:DOWN_AT, :] = mm_nt(grad_up[...], n2[...]).astype(BF).reshape(4, 4, 2, 96, D)
    for stream in early:
        stream.one()
    loads[1].wait()
    grad_normed = turned(mm_tn(grad_up[...], ffn[...].reshape(NW * 96, D)))
    part, gain2 = rms_back(h1[...], columns[:, 1:2], grad_normed)
    grad_h1 = grad_h2 + part
    lays[1].wait()
    out_rows = mm(lay_out[...], grad_h1.astype(BF)).astype(BF)
    loads[0].wait()
    rows48 = attn[...].reshape(NW * 48, D)
    grad_att = turned(mm_tn(out_rows, rows48)).astype(BF)
    for stream in early:
        stream.two()
    trade.forward()

    allowed = mask_of(tok)
    group = H // KVH
    for kv in range(KVH):
        keys = k[kv * HD : (kv + 1) * HD, :]
        values = v[kv * HD : (kv + 1) * HD, :]
        grad_k, grad_v = jnp.zeros((HD, T), F32), jnp.zeros((HD, T), F32)
        for h in range(kv * group, (kv + 1) * group):
            query = q[h * HD : (h + 1) * HD, :]
            grad_out = grad_att[h * HD : (h + 1) * HD, :]
            scores = mm_tn(keys, query) * HD ** (-0.5)
            scores = jnp.where(allowed, scores, masked_score)
            soft = jnp.exp(scores - lse[h : h + 1, :])
            grad_probs = mm_tn(values, grad_out)
            mean = jnp.sum(soft * grad_probs, 0, keepdims=True)
            grad_scores = (soft * (grad_probs - mean)).astype(BF)
            grad_q = mm(keys, grad_scores) * HD ** (-0.5)
            grad_mixed[h * HD : (h + 1) * HD, :] = unrotated(grad_q, rot[...]).astype(BF)
            grad_k = grad_k + mm_nt(query, grad_scores) * HD ** (-0.5)
            grad_v = grad_v + mm_nt(grad_out, soft.astype(BF))
        at = D + kv * HD
        grad_mixed[at : at + HD, :] = unrotated(grad_k, rot[...]).astype(BF)
        at = D + (KVH + kv) * HD
        grad_mixed[at : at + HD, :] = grad_v.astype(BF)
    for stream in early:
        stream.three()
    lays[2].wait()
    attn_rows = mm(lay_attn[...], grad_mixed[...]).astype(BF)
    both = jnp.concatenate([attn_rows, out_rows], 1)
    seen = jnp.concatenate([n1[...], att[...]], 1)
    parts[:, :, :, ATTN_AT:PACKED, :] = mm_nt(both, seen).astype(BF).reshape(4, 4, 2, 48, D)
    parts[:, :, :, PACKED:SUMMED, :] = jnp.zeros((4, 4, 2, SUMMED - PACKED, D), BF)
    for stream in late:
        stream.one()
    grad_normed = turned(mm_tn(attn_rows, rows48))
    part, gain1 = rms_back(h0[...], columns[:, 0:1], grad_normed)
    grad_h0 = (grad_h1 + part).astype(BF)
    grad_embedded[...] = grad_h0
    slot = lax.broadcasted_iota(jnp.int32, (NW * CAP, T), 0)
    picks = jnp.where(slot == slot_row[0:1, :], 1.0, 0.0).astype(BF)
    rows[...] = mm_nt(picks, grad_h0).astype(BF)
    for stream in early:
        stream.four()
    lane = lax.broadcasted_iota(jnp.int32, (D, 128), 1)
    table = jnp.where(lane == 0, gain1, jnp.where(lane == 1, gain2, jnp.where(lane == 2, gain3, 0.0)))
    lost = jnp.sum(loss[0:1, :], 1, keepdims=True)
    table = table.T[0:8, :]
    tree = Tree(hold, land_z, land_y, land_x, tree_s, tree_r)
    tree.start(jnp.where(lax.broadcasted_iota(jnp.int32, (8, D), 0) == 3, lost, table))
    rows_in[slots(me), :] = rows[slots(me), :]
    for stream in late:
        stream.two()
    give = Scatter(lambda p: rows.at[slots(p)], lambda p: rows_in.at[slots(p)], row_s, row_r, me)
    give.start()
    for stream in early:
        stream.five()
    tree.next(0)
    for stream in late:
        stream.three()
    for stream in late:
        stream.four()
    tree.next(1)
    for stream in early:
        stream.six()
    for stream in late:
        stream.five()
    extra_sum[...] = tree.collect(2)
    for stream in late:
        stream.six()
    for stream in streams:
        summed[stream.base : stream.base + sum(stream.sizes), :] = stream.total()
    give.wait_recv()
    trade.wait()
    for stream in streams:
        stream.finish()
    give.wait_send()
    tree.finish()
    trade.finish()


def back(grad_final, kept, packed, gains, rot, tok, slot_row, loss, head_other):
    lays = [
        jnp.asarray(spread_rows(30, 48, 0), BF),
        jnp.asarray(spread_rows(18, 48, 30), BF),
        jnp.asarray(spread_rows(18, 64, 0, 3), BF),
    ]
    return pl.pallas_call(
        back_kernel,
        name="back",
        out_shape=(
            jax.ShapeDtypeStruct((SUMMED, D), F32),
            jax.ShapeDtypeStruct((NW * CAP, D), BF),
            jax.ShapeDtypeStruct((D, SHARD), BF),
            jax.ShapeDtypeStruct((8, D), F32),
            jax.ShapeDtypeStruct((D, T), BF),
        ),
        in_specs=[VMEM] * 10 + [ANY, VMEM, VMEM, ANY] + [VMEM] * 5 + [ANY] * 4,
        out_specs=(VMEM, VMEM, ANY, VMEM, VMEM),
        scratch_shapes=TRUNK_SCRATCH
        + [
            pltpu.VMEM((NW * 48, QKV), BF),
            pltpu.VMEM((NW * 48, D), BF),
            pltpu.VMEM((NW * 64, D), BF),
            DMA((4,)),
            pltpu.VMEM((2 * FF, T), F32),
            pltpu.VMEM((4, 4, 2, SUMMED, D), BF),
            pltpu.VMEM((NW * CAP, D), BF),
            pltpu.VMEM((2 * FF, T), BF),
            pltpu.VMEM((QKV, T), BF),
            pltpu.VMEM((NW * 64, T), BF),
            pltpu.VMEM((2, D // 2, SHARD), BF),
        ]
        + [DMA((NW,)), DMA((NW,)), DMA((4,)), DMA((4,))]
        + tree_scratch(D)
        + reduce_scratch(),
        compiler_params=params(5, 60),
        cost_estimate=pl.CostEstimate(flops=10**10, bytes_accessed=3 * 10**7, transcendentals=10**6),
    )(grad_final, *kept, packed, gains, rot, tok, slot_row, loss, head_other, *lays)


def adam_update(weight, grad, first, second, rate, decay):
    first = beta_one * first + (1.0 - beta_one) * grad
    second = beta_two * second + (1.0 - beta_two) * grad * grad
    ratio = first / (1.0 - beta_one**STEP) / (jnp.sqrt(second / (1.0 - beta_two**STEP)) + adam_eps)
    return (weight - rate * (ratio + decay * weight), first, second)


def adam_diff(weight, grad, first, second, anchor, rate, decay):
    return anchor - adam_update(weight, grad, first, second, rate, decay)[0]


PIECES = ((0, 0, 96), (0, 96, 96), (0, 192, 96), (1, 0, 112))


def update_kernel(
    rows, hot, head, head_in, summed, extra, tm, tf, ts, ta, *refs
):
    trunk, gains = [refs[3 * i : 3 * i + 3] for i in range(4)], refs[12:16]
    update_body(rows, hot, head, head_in, summed, extra, tm, tf, ts, ta, trunk, gains, *refs[16:])


def update_body(
    rows, hot, head, head_in, summed, extra, tm, tf, ts, ta, trunk_in, gains,
    table_grad_out, total_t, total_k, total_g, norms,
    table_grad, v_rows, v_hot, v_head, v_head_in, vm, vf, vs, va, flipped,
    one_t, one_t_in, two_t, two_t_in, one_k, one_k_in, two_k, two_k_in, gains_out, gains_in,
    load_sem, one_s, one_r, two_s, two_r, three_s, three_r, gains_s, gains_r,
    hold, land_z, land_y, land_x, tree_s, tree_r, km, kf, ks, ka,
):
    me, y, xh, z = place()
    grp = lax.axis_index("grp")
    core, x = lax.rem(grp, 2), grp // 2
    near, far = x * 2 + 1 - core, (1 - x) * 2 + core
    loads = [
        pltpu.make_async_copy(src, dst, load_sem.at[i])
        for i, (src, dst) in enumerate(
            zip((rows, hot, head, head_in, tm, tf, ts, ta), (v_rows, v_hot, v_head, v_head_in, vm, vf, vs, va))
        )
    ]
    for load in loads:
        load.start()
    barrier = pltpu.get_barrier_semaphore()
    for peer in near_peers(me, y, xh, z):
        pl.semaphore_signal(barrier, inc=1, device_id={"wide": peer}, device_id_type=MESH)
    for k in range(1, NG):
        pl.semaphore_signal(
            barrier, inc=1, device_id={"grp": lax.rem(grp + k, NG)}, device_id_type=MESH
        )
    pl.semaphore_wait(barrier, 7 + NG - 1)
    loads[0].wait()
    for c in range(0, NW * CAP, 256):
        flipped[:, c : c + 256] = v_rows[c : c + 256, :].T
    for load in loads[1:4]:
        load.wait()
    squares = jnp.zeros((1, 512), F32)
    for c in range(0, SHARD, 512):
        part = v_head[:, c : c + 512] + v_head_in[:, c : c + 512].astype(F32)
        part = part + mm(flipped[...], v_hot[:, c : c + 512])
        table_grad[:, c : c + 512] = part
        squares = squares + jnp.sum(part * part, 0, keepdims=True)
    save = pltpu.make_async_copy(table_grad, table_grad_out, load_sem.at[0])
    save.start()
    squares = jnp.sum(squares, 1, keepdims=True)
    trunk = jnp.sum(summed[...] * summed[...], 0, keepdims=True)
    squares = squares + jnp.sum(trunk, 1, keepdims=True)
    tree = Tree(hold, land_z, land_y, land_x, tree_s, tree_r)
    tree.start(jnp.broadcast_to(squares, (8, 128)))
    for out, (attn, ffn, proj) in zip((km, kf, ks, ka), trunk_in):
        if out is ka:
            pack_rows(out, attn[...], ffn[...], proj[...])
        else:
            pack_rows(out, attn[:, 0, :], ffn[...], proj[:, 0, :])
        out[PACKED:SUMMED, :] = jnp.zeros((SUMMED - PACKED, D), F32)
    gain_grads = extra[0:3, :]
    gain_squares = jnp.sum(jnp.sum(gain_grads * gain_grads, 0, keepdims=True), 1, keepdims=True)
    tree.next(0)
    for load in loads[4:]:
        load.wait()
    tree.next(1)
    norm = jnp.sqrt(tree.collect(2)[0:1, 0:1] + gain_squares)
    factor = jnp.minimum(1.0, clip_norm / norm)
    down = lax.broadcasted_iota(jnp.int32, (8, 128), 0)
    norms[...] = jnp.where(down == 0, norm, factor)

    parts = (
        (vm, table_grad, vf, vs, va, total_t, D // 2, one_t, one_t_in, two_t, two_t_in),
        (km, summed, kf, ks, ka, total_k, SUMMED // 2, one_k, one_k_in, two_k, two_k_in),
    )
    sent = []

    def span(which, at, count, side):
        half = parts[which][6]
        return pl.ds(pl.multiple_of(side * half + at, 16), count)

    def diff(which, at, count, side):
        m, g, f, s2, a = parts[which][:5]
        rows = span(which, at, count, side)
        return adam_diff(
            m[rows, :], g[rows, :] * factor, f[rows, :], s2[rows, :], a[rows, :], inner_rate, weight_decay
        )

    for i, (which, at, count) in enumerate(PIECES):
        one, one_in = parts[which][7:9]
        rows = pl.ds(at, count)
        one[rows, :] = diff(which, at, count, 1 - core).astype(BF)
        copy = remote(one.at[rows], one_in.at[rows], one_s.at[i], one_r.at[i], grp=near)
        copy.start()
        sent.append(copy)
    for i, (which, at, count) in enumerate(PIECES):
        one, one_in, two, two_in = parts[which][7:11]
        rows = pl.ds(at, count)
        own = diff(which, at, count, core)
        sent[i].wait_recv()
        two[rows, :] = (own + one_in[rows, :].astype(F32)).astype(BF)
        copy = remote(two.at[rows], two_in.at[rows], two_s.at[i], two_r.at[i], grp=far)
        copy.start()
        sent.append(copy)
    gains_out[0:3, :] = adam_diff(
        gains[0][:, 0, :], gain_grads * factor, gains[1][:, 0, :], gains[2][:, 0, :], gains[3][...], gain_rate, 0.0
    )
    gains_out[3:8, :] = jnp.zeros((5, D), F32)
    told = []
    for k in range(1, NG):
        to = lax.rem(grp + k, NG)
        told.append(remote(gains_out, gains_in.at[grp], gains_s.at[k], gains_r.at[grp], grp=to))
        told[-1].start()
    gains_in[grp] = gains_out[...]
    for i, (which, at, count) in enumerate(PIECES):
        total, two, two_in = parts[which][5], parts[which][9], parts[which][10]
        rows = pl.ds(at, count)
        sent[len(PIECES) + i].wait_recv()
        kept = span(which, at, count, core)
        total[kept, :] = two[rows, :].astype(F32) + two_in[rows, :].astype(F32)
        copy = remote(total.at[kept], total.at[kept], three_s.at[i], three_r.at[i], grp=near)
        copy.start()
        sent.append(copy)
    for k in range(1, NG):
        other = lax.rem(grp + k, NG)
        remote(
            gains_out, gains_in.at[other], gains_s.at[k], gains_r.at[other], grp=other
        ).wait_recv()
    total_g[...] = (gains_in[0] + gains_in[1]) + (gains_in[2] + gains_in[3])
    for i, (which, at, count) in enumerate(PIECES):
        away = parts[which][5].at[span(which, at, count, 1 - core)]
        remote(away, away, three_s.at[i], three_r.at[i], grp=near).wait_recv()
    for copy in sent + told:
        copy.wait_send()
    tree.finish()
    save.wait()


def update(rows, hot, head, head_in, summed, extra, table, trunk, gains):
    def exchange(size, lanes):
        return [pltpu.VMEM((size // 2, lanes), BF)] * 4

    table_f32 = pltpu.VMEM((D, SHARD), F32)
    pieces = DMA((len(PIECES),))
    return pl.pallas_call(
        update_kernel,
        name="update",
        out_shape=(
            jax.ShapeDtypeStruct((D, SHARD), F32),
            jax.ShapeDtypeStruct((D, SHARD), F32),
            jax.ShapeDtypeStruct((SUMMED, D), F32),
            jax.ShapeDtypeStruct((8, D), F32),
            jax.ShapeDtypeStruct((8, 128), F32),
        ),
        in_specs=[ANY] * 4 + [VMEM] * 2 + [ANY] * 4 + [VMEM] * 16,
        out_specs=(ANY,) + (VMEM,) * 4,
        scratch_shapes=[
            table_f32,
            pltpu.VMEM((NW * CAP, D), BF),
            pltpu.VMEM((NW * CAP, SHARD), BF),
            table_f32,
            pltpu.VMEM((D, SHARD), BF),
            table_f32,
            table_f32,
            table_f32,
            table_f32,
            pltpu.VMEM((D, NW * CAP), BF),
        ]
        + exchange(D, SHARD)
        + exchange(SUMMED, D)
        + [pltpu.VMEM((8, D), F32), pltpu.VMEM((NG, 8, D), F32), DMA((8,))]
        + [pieces] * 6
        + [DMA((NG,)), DMA((NG,))]
        + tree_scratch(128)
        + [pltpu.VMEM((SUMMED, D), F32)] * 4,
        compiler_params=params(6, 62),
        cost_estimate=pl.CostEstimate(flops=2 * 10**9, bytes_accessed=3 * 10**7, transcendentals=10**6),
    )(rows, hot, head, head_in, summed, extra, *table, *trunk, *gains)


def settle(total, momentum, anchor, grad, first, second):
    average = total * (1.0 / NG)
    outer = outer_momentum * momentum + average
    weight = anchor - outer_rate * (average + outer_momentum * outer)
    first = beta_one * first + (1.0 - beta_one) * grad
    second = beta_two * second + (1.0 - beta_two) * grad * grad
    return average, outer, weight, first, second


def rows_of(packed):
    down = [packed[DOWN_AT + 18 * j : DOWN_AT + 18 * j + 18, 0:512] for j in range(3)]
    proj = jnp.concatenate([packed[ATTN_AT + 30 : PACKED, :]] + down, 1)
    return packed[ATTN_AT : ATTN_AT + 30, :], packed[FFN_AT:DOWN_AT, :], proj


def finish_kernel(norms, *refs):
    table, summed, total_k, extra, total_g = refs[:6], refs[6], refs[7], refs[8], refs[9]
    small = [refs[10 + 4 * i : 14 + 4 * i] for i in range(4)]
    outs = [refs[26 + 5 * i : 31 + 5 * i] for i in range(5)]
    factor = norms[1:2, 0:1]
    total, momentum, anchor, grad, first, second = table
    values = settle(
        total[...], momentum[...], anchor[...], grad[...] * factor, first[...], second[...]
    )
    for out, value in zip(outs[0], values):
        out[...] = value

    @pl.when(pl.program_id(0) == 0)
    def _():
        grads = rows_of(summed) + (extra[0:3, :],)
        totals = rows_of(total_k) + (total_g[0:3, :],)
        for i in range(4):
            momentum, anchor, first, second = small[i]
            flat_moments = i == 1
            if flat_moments:
                moments = first[...], second[...]
            else:
                moments = first[:, 0, :], second[:, 0, :]
            values = settle(totals[i], momentum[...], anchor[...], grads[i] * factor, *moments)
            for n, (out, value) in enumerate(zip(outs[i + 1], values)):
                if n < 3 or flat_moments:
                    out[...] = value
                else:
                    out[:, 0, :] = value


def finish(norms, table, summed, total_k, extra, total_g, small):
    block = pl.BlockSpec((48, SHARD), lambda i: (i, 0))

    def whole(value):
        return pl.BlockSpec(value.shape, lambda i, rank=len(value.shape): (0,) * rank)

    rest = [summed, total_k, extra, total_g] + [value for kind in small for value in kind]
    shapes = [jax.ShapeDtypeStruct((D, SHARD), F32)] * 5
    for momentum, anchor, first, second in small:
        shapes += [jax.ShapeDtypeStruct(momentum.shape, F32)] * 3
        shapes += [jax.ShapeDtypeStruct(first.shape, F32)] * 2
    return pl.pallas_call(
        finish_kernel,
        name="finish",
        grid=(D // 48,),
        out_shape=tuple(shapes),
        in_specs=[whole(norms)] + [block] * 6 + [whole(value) for value in rest],
        out_specs=tuple([block] * 5 + [whole(shape) for shape in shapes[5:]]),
        compiler_params=pltpu.CompilerParams(vmem_limit_bytes=40 * MIB),
        cost_estimate=pl.CostEstimate(flops=2 * 10**7, bytes_accessed=4 * 10**7, transcendentals=0),
    )(norms, *table, *rest)


def dot(spec, a, b):
    return jnp.einsum(spec, a, b, preferred_element_type=F32)


def on_device(
    token_ids,
    targets,
    segment_ids,
    row_counts,
    embed_table_master,
    embed_table_first,
    embed_table_second,
    embed_table_anchor,
    embed_table_momentum,
    attn_in_master,
    attn_in_first,
    attn_in_second,
    attn_in_anchor,
    attn_in_momentum,
    ffn_in_master,
    ffn_in_first,
    ffn_in_second,
    ffn_in_anchor,
    ffn_in_momentum,
    proj_out_master,
    proj_out_first,
    proj_out_second,
    proj_out_anchor,
    proj_out_momentum,
    norm_gains_master,
    norm_gains_first,
    norm_gains_second,
    norm_gains_anchor,
    norm_gains_momentum,
):
    ids = token_ids[0]

    def rows_apart(value):
        return value.transpose(2, 0, 1)

    ffn = [v.T for v in (ffn_in_master[0], ffn_in_first[0], ffn_in_second[0], ffn_in_anchor, ffn_in_momentum)]
    attn = [rows_apart(v) for v in (attn_in_master, attn_in_first, attn_in_second)]
    attn += [attn_in_anchor.T, attn_in_momentum.T]
    proj = [rows_apart(v) for v in (proj_out_master, proj_out_first, proj_out_second)]
    proj += [proj_out_anchor.T, proj_out_momentum.T]
    gains = [v.transpose(1, 0, 2) for v in (norm_gains_master, norm_gains_first, norm_gains_second)]
    gains += [norm_gains_anchor, norm_gains_momentum]
    tables = [v.T for v in (embed_table_master[0], embed_table_first[0], embed_table_second[0])]
    tables += [embed_table_anchor.T, embed_table_momentum.T]
    (
        got, rows, most, table, table_other, rows_t, packed_all, picks, slot_row, hot, goals, weights,
    ) = front(
        token_ids, targets, row_counts[0], tables[0], attn[0], ffn[0], proj[0]
    )
    turns = (most[0, 0] + CAP - 1) // CAP

    def asked_in(turn):
        ids_now = jnp.where(turn > 0, ids, 0)
        owner = ids_now // SHARD
        same = ids_now[:, None] == ids_now[None, :]
        before = jnp.arange(T)[None, :] < jnp.arange(T)[:, None]
        first_seen = ~jnp.any(same & before, 1)
        smaller = (owner[None, :] == owner[:, None]) & (ids_now[None, :] < ids_now[:, None])
        rank = jnp.sum(first_seen[None, :] & smaller, 1, dtype=jnp.int32) - turn * CAP
        slot = jnp.where((rank >= 0) & (rank < CAP), owner * CAP + rank, -1)
        chosen = jnp.arange(NW * CAP)[:, None] == slot[None, :]
        asked = jnp.max(jnp.where(chosen, (ids_now - owner * SHARD)[None, :], -1), 1).reshape(NW, 1, CAP)
        asked = jnp.pad(asked, ((0, 0), (0, 0), (0, 128 - CAP)), constant_values=-1)
        return jnp.pad(asked, ((0, 0), (0, 7), (0, 0))), chosen.astype(BF)

    def more_tokens(carry):
        turn, hidden = carry
        message, chosen = asked_in(turn)
        return turn + 1, hidden + dot("sd,st->dt", more_rows(message, table), chosen)

    more = lax.while_loop(
        lambda carry: carry[0] < turns, more_tokens, (jnp.int32(1), jnp.zeros((D, T), F32))
    )[1]

    rot = jnp.asarray(rope())
    final, *kept = forward(more, rows, picks, packed_all, gains[0], rot, segment_ids)
    total = weights[2, 0]
    grad_final, head_own, head_other, loss = head(final, rows_t, table, table_other, goals, weights)
    summed, rows_in, head_in, extra_sum, grad_embedded = back(
        grad_final, kept, packed_all, gains[0], rot, segment_ids, slot_row, loss, head_other
    )

    def more_table(carry):
        turn, grad = carry
        message, chosen = asked_in(turn)
        mine = dot("st,dt->sd", chosen, grad_embedded).astype(BF)
        got_now, rows_now = more_grads(message, mine)
        asked = got_now[:, 0, :CAP].reshape(NW * CAP)
        hot_now = (asked[:, None] == jnp.arange(SHARD)[None, :]).astype(BF)
        return turn + 1, grad + dot("sd,sv->dv", rows_now, hot_now)

    head_grad = lax.while_loop(lambda carry: carry[0] < turns, more_table, (jnp.int32(1), head_own))[1]
    table_grad, total_t, total_k, total_g, norms = update(
        rows_in,
        hot,
        head_grad,
        head_in,
        summed,
        extra_sum,
        tables[:4],
        [kind[i] for i in range(4) for kind in (attn, ffn, proj)],
        gains[:4],
    )
    outs = finish(
        norms,
        (total_t, tables[4], tables[3], table_grad, tables[1], tables[2]),
        summed,
        total_k,
        extra_sum,
        total_g,
        [(kind[4], kind[3], kind[1], kind[2]) for kind in (attn, ffn, proj, gains)],
    )
    results = [extra_sum[3, 0:1], total.reshape(1), norms[0, 0:1]]
    for index in range(5):
        average, outer, weight, first, second = outs[5 * index : 5 * index + 5]
        if index < 4:
            average, outer, weight = average.T, outer.T, weight.T
        if index in (0, 2):
            first, second = first.T[None], second.T[None]
        elif index == 4:
            first, second = first.transpose(1, 0, 2), second.transpose(1, 0, 2)
        else:
            first, second = first.transpose(1, 2, 0), second.transpose(1, 2, 0)
        results += [average, outer, weight, first, second]
    return tuple(results)


def solution(mesh):
    in_specs = (
        P("grp", "wide"),
        P("grp", "wide"),
        P("grp", "wide"),
        P("grp", "wide", None),
        P("grp", "wide", None),
        P("grp", "wide", None),
        P("grp", "wide", None),
        P("wide", None),
        P("wide", None),
        P("grp", None, "wide"),
        P("grp", None, "wide"),
        P("grp", None, "wide"),
        P(None, "wide"),
        P(None, "wide"),
        P("grp", None, "wide"),
        P("grp", None, "wide"),
        P("grp", None, "wide"),
        P(None, "wide"),
        P(None, "wide"),
        P("grp", None, "wide"),
        P("grp", None, "wide"),
        P("grp", None, "wide"),
        P(None, "wide"),
        P(None, "wide"),
        P("grp", None, None),
        P("grp", None, None),
        P("grp", None, None),
        P(),
        P(),
    )
    out_specs = (
        P("grp"),
        P("grp"),
        P("grp"),
        P("wide", None),
        P("wide", None),
        P("wide", None),
        P("grp", "wide", None),
        P("grp", "wide", None),
        P(None, "wide"),
        P(None, "wide"),
        P(None, "wide"),
        P("grp", None, "wide"),
        P("grp", None, "wide"),
        P(None, "wide"),
        P(None, "wide"),
        P(None, "wide"),
        P("grp", None, "wide"),
        P("grp", None, "wide"),
        P(None, "wide"),
        P(None, "wide"),
        P(None, "wide"),
        P("grp", None, "wide"),
        P("grp", None, "wide"),
        P(),
        P(),
        P(),
        P("grp", None, None),
        P("grp", None, None),
    )
    return jax.shard_map(
        on_device, mesh=mesh, in_specs=in_specs, out_specs=out_specs, check_vma=False
    )
```

```python
import jax
import jax.numpy as jnp
import numpy as np
from jax import lax
from jax.experimental import pallas as pl
from jax.experimental.pallas import tpu as pltpu
from jax.sharding import PartitionSpec as P

D = 576
H = 9
KVH = 3
HD = 64
FF = 1536
QKV = 960
STEP = 8
T = 256
SHARD = 1536
NW = 32
NG = 4
CAP = 32
FFN_AT, DOWN_AT, ATTN_AT, PACKED = 0, 96, 160, 208
SUMMED = 224

beta_one = 0.9
beta_two = 0.999
adam_eps = 1e-08
weight_decay = 0.1
inner_rate = 0.02
gain_rate = 0.2
clip_norm = 0.01
penalty_weight = 0.005
outer_rate = 0.7
outer_momentum = 0.9
rope_base = 100000.0
norm_eps = 1e-05
masked_score = -1e30

BF = jnp.bfloat16
F32 = jnp.float32
MESH = pl.DeviceIdType.MESH
VMEM = pl.BlockSpec(memory_space=pltpu.VMEM)
ANY = pl.BlockSpec(memory_space=pl.ANY)
DMA = pltpu.SemaphoreType.DMA
MIB = 1 << 20


def params(collective, mib):
    return pltpu.CompilerParams(
        collective_id=collective, has_side_effects=True, vmem_limit_bytes=mib * MIB
    )


def place():
    me = lax.axis_index("wide")
    return me, me // 8, lax.rem(me // 4, 2), lax.rem(me, 4)


def flat(y, xh, z):
    return y * 8 + xh * 4 + z


def turn4(at, by):
    return lax.rem(at + by, 4)


def remote(src, dst, ssem, rsem, **device):
    return pltpu.make_async_remote_copy(
        src_ref=src,
        dst_ref=dst,
        send_sem=ssem,
        recv_sem=rsem,
        device_id=device,
        device_id_type=MESH,
    )


def greet_wide(me, grp=None, sides=False, meanwhile=None):
    barrier = pltpu.get_barrier_semaphore()

    def one(k, carry):
        pl.semaphore_signal(
            barrier, inc=1, device_id={"wide": lax.rem(me + k, NW)}, device_id_type=MESH
        )
        return carry

    lax.fori_loop(1, NW, one, 0)
    count = NW - 1
    if grp is not None:
        for k in range(1, NG):
            pl.semaphore_signal(
                barrier, inc=1, device_id={"grp": lax.rem(grp + k, NG)}, device_id_type=MESH
            )
        count += NG - 1
    if sides:
        for step in (1, 3):
            pl.semaphore_signal(barrier, inc=1, device_id=beside(step), device_id_type=MESH)
        count += 2
    if meanwhile is not None:
        meanwhile()
    pl.semaphore_wait(barrier, count)


def near_peers(me, y, xh, z):
    peers = [flat(y, xh, turn4(z, k)) for k in (1, 2, 3)] + [flat(turn4(y, k), xh, z) for k in (1, 2, 3)]
    return peers + [flat(y, 1 - xh, z)]


class Tree:
    def __init__(self, hold, land_z, land_y, land_x, ssem, rsem):
        self.hold, self.lands = hold, (land_z, land_y, land_x)
        self.ssem, self.rsem = ssem, rsem
        me, self.y, self.xh, self.z = place()
        self.sent = []

    def send(self, stage):
        y, xh, z = self.y, self.xh, self.z
        at = (z, y, xh)[stage]
        land, src = self.lands[stage], self.hold.at[stage]
        for k in range(1, 2 if stage == 2 else 4):
            if stage == 0:
                to = flat(y, xh, turn4(z, k))
            elif stage == 1:
                to = flat(turn4(y, k), xh, z)
            else:
                to = flat(y, 1 - xh, z)
            copy = remote(src, land.at[at], self.ssem.at[stage, k], self.rsem.at[stage, at], wide=to)
            copy.start()
            self.sent.append(copy)
        land[at] = self.hold[stage]

    def start(self, value):
        self.hold[0] = value
        self.send(0)

    def collect(self, stage):
        at = (self.z, self.y, self.xh)[stage]
        land = self.lands[stage]
        size = 2 if stage == 2 else 4
        for k in range(1, size):
            other = lax.rem(at + k, size)
            remote(
                land.at[other], land.at[other], self.ssem.at[stage, k], self.rsem.at[stage, other],
                wide=flat(self.y, self.xh, self.z),
            ).wait_recv()
        total = land[0]
        for k in range(1, size):
            total = total + land[k]
        return total

    def next(self, stage):
        self.hold[stage + 1] = self.collect(stage)
        self.send(stage + 1)

    def finish(self):
        for copy in self.sent:
            copy.wait_send()


def tree_scratch(lanes):
    return [
        pltpu.VMEM((3, 8, lanes), F32),
        pltpu.VMEM((4, 8, lanes), F32),
        pltpu.VMEM((4, 8, lanes), F32),
        pltpu.VMEM((2, 8, lanes), F32),
        DMA((3, 4)),
        DMA((3, 4)),
    ]


class Scatter:
    def __init__(self, src_at, dst_at, ssem, rsem, me):
        self.src_at, self.dst_at, self.ssem, self.rsem, self.me = src_at, dst_at, ssem, rsem, me

    def copy(self, k):
        peer = lax.rem(self.me + k, NW)
        return remote(
            self.src_at(peer), self.dst_at(self.me), self.ssem.at[k], self.rsem.at[self.me], wide=peer
        )

    def start(self):
        def one(k, carry):
            self.copy(k).start()
            return carry

        lax.fori_loop(1, NW, one, 0)

    def wait_recv(self):
        def one(k, carry):
            peer = lax.rem(self.me + k, NW)
            remote(
                self.src_at(peer), self.dst_at(peer), self.ssem.at[k], self.rsem.at[peer], wide=peer
            ).wait_recv()
            return carry

        lax.fori_loop(1, NW, one, 0)

    def wait_send(self):
        def one(k, carry):
            self.copy(k).wait_send()
            return carry

        lax.fori_loop(1, NW, one, 0)


class Ring:
    def __init__(self, view, sem, bounds, ssem):
        self.view, self.sem, self.bounds = view, sem, bounds
        self.ssem, self.used, self.sent = ssem, 0, []
        self.me, self.y, self.xh, self.z = place()

    def send(self, src, dst, rsem, to):
        copy = remote(src, dst, self.ssem.at[self.used], rsem, wide=flat(to[0], self.xh, to[1]))
        self.used += 1
        copy.start()
        self.sent.append(copy)

    def piece(self, y, z, first, count):
        return self.view(y, z, self.bounds[first], self.bounds[first + count] - self.bounds[first])

    def pass_on(self, y, z, first, count, index, *to):
        piece = self.piece(y, z, first, count)
        for one in to:
            self.send(piece, piece, self.sem(y, z, index), one)

    def landed(self, piece, sem):
        remote(piece, piece, self.ssem.at[0], sem, wide=self.me).wait_recv()

    def wait(self, y, z, first, count, index):
        self.landed(self.piece(y, z, first, count), self.sem(y, z, index))

    def around(self):
        y, z = self.y, self.z
        return y, z, (turn4(y, 1), z), (turn4(y, 3), z), (y, turn4(z, 1)), (y, turn4(z, 3))

    def own(self, src, dst, index):
        y, z, y_up, y_down, z_up, z_down = self.around()
        for to in (y_up, y_down, z_up, z_down):
            self.send(src, dst, self.sem(y, z, index), to)

    def near(self, parts=None):
        y, z, y_up, y_down, z_up, z_down = self.around()
        for at, far, turn, half, sides in (
            (y_down, y_up, 0, 0, (z_up, z_down)),
            (y_up, y_down, 1, 0, (z_up, z_down)),
            (z_down, z_up, 0, 2, (y_up, y_down)),
            (z_up, z_down, 1, 2, (y_up, y_down)),
        ):
            if parts is None:
                self.wait(*at, 0, 4, 0)
            else:
                for part, index in parts:
                    self.landed(part(*at), self.sem(*at, index))
            self.pass_on(*at, turn, 1, turn, far)
            self.pass_on(*at, 2 + turn, 1, 2 + turn, far)
            self.pass_on(*at, half, 2, half, *sides)

    def far(self):
        y, z, y_up, y_down, z_up, z_down = self.around()
        for at, half, sides in (
            ((turn4(y, 2), z), 0, (z_up, z_down)),
            ((y, turn4(z, 2)), 2, (y_up, y_down)),
        ):
            for index in range(4):
                self.wait(*at, index, 1, index)
            self.pass_on(*at, half, 2, half, *sides)

    def cross(self):
        y, z, y_up, y_down, z_up, z_down = self.around()
        for k in (1, 3, 2):
            row, column = turn4(y, k), turn4(z, k)
            self.wait(row, z_down[1], 0, 2, 0)
            self.pass_on(row, z_down[1], 0, 1, 0, z_up)
            self.wait(row, z_up[1], 0, 2, 0)
            self.pass_on(row, z_up[1], 1, 1, 1, z_down)
            self.wait(y_down[0], column, 2, 2, 2)
            self.pass_on(y_down[0], column, 2, 1, 2, y_up)
            self.wait(y_up[0], column, 2, 2, 2)
            self.pass_on(y_up[0], column, 3, 1, 3, y_down)

    def last(self):
        y, z = self.y, self.z
        for k in (1, 3, 2):
            row, column = turn4(y, k), turn4(z, k)
            for index in range(2):
                self.wait(row, turn4(z, 2), index, 1, index)
                self.wait(turn4(y, 2), column, 2 + index, 1, 2 + index)

    def finish(self):
        for copy in self.sent:
            copy.wait_send()


RING_SENDS = 36


def beside(step):
    me, y, xh, z = place()
    grp = lax.axis_index("grp")
    low = grp // 2
    side = lax.rem(xh + low + (0 if step == 1 else 1), 2)
    return {"grp": (1 - low) * 2 + lax.rem(grp, 2), "wide": flat(y, side, z)}


class Relay:
    def __init__(self, sources, stops, ends, ssem, rsem):
        self.sources, self.stops, self.ends, self.ssem, self.rsem = sources, stops, ends, ssem, rsem

    def copy(self, src, dst, at, step):
        return remote(src, dst, self.ssem.at[at], self.rsem.at[at], **beside(step))

    def legs(self, hop):
        for i, step in enumerate((1, 3)):
            src = self.sources[i] if hop == 0 else self.stops[i]
            dst = self.stops[i] if hop == 0 else self.ends[i]
            yield self.copy(src, dst, 2 * hop + i, step)

    def start(self):
        for copy in self.legs(0):
            copy.start()

    def forward(self):
        for first, second in zip(self.legs(0), self.legs(1)):
            first.wait_recv()
            second.start()

    def wait(self):
        for copy in self.legs(1):
            copy.wait_recv()

    def finish(self):
        for hop in (0, 1):
            for copy in self.legs(hop):
                copy.wait_send()


def look_up(got, table, hot, rows, slot_row):
    asked = got[:, slot_row, :].astype(F32)
    asked = jnp.concatenate([asked, jnp.zeros((128 - NW, 128), F32)], 0).T
    step = 8 * CAP
    for first in range(0, NW, 8):
        for d in range(8):
            column = asked[0:CAP, first + d : first + d + 1]
            lanes = lax.broadcasted_iota(jnp.int32, (CAP, SHARD), 1).astype(F32)
            hot[d * CAP : (d + 1) * CAP, :] = jnp.where(lanes == column, 1.0, 0.0).astype(BF)
        picked = lax.dot_general(
            hot[...], table[...], (((1,), (1,)), ((), ())), preferred_element_type=F32
        )
        rows[first * CAP : first * CAP + step, :] = picked.astype(BF)


def slots(at):
    return pl.ds(pl.multiple_of(at * CAP, CAP), CAP)


def turn_over(table, rows, first):
    for c in range(0, SHARD, 256):
        rows[first + c : first + c + 256, :] = table[:, c : c + 256].T


def owner_of(ids):
    return (((ids >> 9) * 171) >> 9).astype(jnp.int32)


def pack_rows(out, attn, ffn, proj):
    out[FFN_AT:DOWN_AT, :] = ffn
    out[DOWN_AT:ATTN_AT, :] = jnp.zeros((ATTN_AT - DOWN_AT, D), F32)
    for j in range(3):
        at = DOWN_AT + 18 * j
        out[at : at + 18, 0:512] = proj[:, D + 512 * j : D + 512 * (j + 1)]
    out[ATTN_AT : ATTN_AT + 30, :] = attn
    out[ATTN_AT + 30 : PACKED, :] = proj[:, 0:D]


def ask_rows(ids, targets, weight, msg, picks, slot_out):
    row = ids[0:1, :]
    column = jnp.broadcast_to(row.astype(F32), (128, T)).T[:, 0:1].astype(jnp.int32)
    row_owner, column_owner = owner_of(row), owner_of(column)
    down = lax.broadcasted_iota(jnp.int32, (T, T), 0)
    across = lax.broadcasted_iota(jnp.int32, (T, T), 1)
    same = row == column

    def count(which, axis):
        return jnp.sum(jnp.where(which, 1.0, 0.0), axis, keepdims=True)

    first_row = count(same & (down < across), 0) == 0.0
    first_column = count(same & (across < down), 1) == 0.0
    near = row_owner == column_owner
    rank_row = count(near & (column < row) & first_column, 0)
    rank_column = count(near & (row < column) & first_row, 1)
    slot_row = jnp.where(rank_row < CAP, row_owner.astype(F32) * CAP + rank_row, -1.0)
    slot_column = jnp.where(rank_column < CAP, column_owner.astype(F32) * CAP + rank_column, -1.0)
    lanes = lax.broadcasted_iota(jnp.int32, (T, NW * CAP), 1).astype(F32)
    hit = lanes == slot_column
    picks[...] = jnp.where(hit, 1.0, 0.0).astype(BF)
    slot_out[...] = jnp.broadcast_to(slot_row, (8, T)).astype(jnp.int32)
    local = (column - column_owner * SHARD).astype(F32)
    asked = jnp.max(jnp.where(hit, local, -1.0), 0, keepdims=True).astype(jnp.int32)
    most = (jnp.max(rank_row, 1, keepdims=True) + 1.0).astype(jnp.int32)
    rest = [
        targets[0:1, 0:128], targets[0:1, 128:256], weight[:, 0:128], jnp.broadcast_to(most, (1, 128)),
    ] + [jnp.zeros((1, 128), jnp.int32)] * 3
    for g in range(8):
        msg[g] = jnp.concatenate([asked[:, g * 128 : (g + 1) * 128]] + rest, 0)


def find_rows(got, table, asked_t, hot, rows, part):
    asked = got[:, 0, :].astype(F32)
    asked_t[...] = jnp.concatenate([asked, jnp.full((128 - NW, 128), -1.0, F32)], 0).T
    mine = asked_t[pl.ds(pl.multiple_of(part * CAP, CAP), CAP), :]
    lanes = lax.broadcasted_iota(jnp.int32, (CAP, SHARD), 1).astype(F32)
    for d in range(NW):
        hot[d * CAP : (d + 1) * CAP, :] = jnp.where(lanes == mine[:, d : d + 1], 1.0, 0.0).astype(BF)
    step = 16 * CAP
    for first in range(0, NW * CAP, step):
        picked = lax.dot_general(
            hot[first : first + step, :], table[...], (((1,), (1,)), ((), ())), preferred_element_type=F32
        )
        rows[first : first + step, :] = picked.astype(BF)


def turn_over(table, rows, first):
    for c in range(0, SHARD, 256):
        rows[first + c : first + c + 256, :] = table[:, c : c + 256].T


def front_kernel(
    ids, targets, counts, master, attn, ffn, proj,
    got, emb, most_out, table_out, other_out, rows_t_out, packed_all, picks, slot_out, hot_out, goal, weights,
    wide, table, table_other, rows_t, hot, long, packed, most, msg, asked_t, rows, own_most, stops, msg_s, msg_r, emb_s, emb_r, most_s, most_r, swap_s, swap_r,
    ring_s, ring_r, x_sem, local,
):
    me, y, xh, z = place()
    grp = lax.axis_index("grp")
    other = flat(y, 1 - xh, z)
    load = pltpu.make_async_copy(master, wide, local.at[1])
    load.start()
    by_source = lax.broadcasted_iota(jnp.int32, (1, 3), 1) + 1
    weight = jnp.sum((counts[...] * by_source).astype(F32), 1, keepdims=True)
    weight = jnp.broadcast_to(weight, (1, T)).astype(jnp.int32)

    def prepare():
        pack_rows(long, attn[:, 0, :], ffn[...], proj[:, 0, :])
        packed[...] = long[...].astype(BF)
        ask_rows(ids, targets, weight, msg, picks, slot_out)

    greet_wide(me, grp, sides=True, meanwhile=prepare)
    over = remote(packed, packed_all.at[y, z, xh], x_sem.at[0], x_sem.at[1], wide=other)
    over.start()
    ask = Scatter(lambda p: msg.at[p // 4], lambda p: got.at[p], msg_s, msg_r, me)
    ask.start()
    got[me] = msg[me // 4]
    ring = Ring(
        lambda Y, Z, first, count: packed_all.at[Y, Z, :, pl.ds(first, count)],
        lambda Y, Z, index: ring_r.at[Y, Z, index],
        (0, 48, 96, 144, 208),
        ring_s,
    )
    ring.own(packed, packed_all.at[y, z, xh], 0)
    keep = pltpu.make_async_copy(packed, packed_all.at[y, z, xh], local.at[0])
    keep.start()
    load.wait()
    table[...] = wide[...].astype(BF)
    saves = [pltpu.make_async_copy(table, table_out, local.at[1])]
    saves[0].start()
    halves = (pl.ds(0, D // 2), pl.ds(D // 2, D // 2))
    trade = Relay(
        [table.at[half] for half in halves],
        [stops.at[i] for i in range(2)],
        [table_other.at[half] for half in halves],
        swap_s,
        swap_r,
    )
    trade.start()
    over.wait_recv()
    ring.own(packed_all.at[y, z, 1 - xh], packed_all.at[y, z, 1 - xh], 4)
    ask.wait_recv()
    find_rows(got, table, asked_t, hot, rows, lax.rem(me, 4))
    saves.append(pltpu.make_async_copy(hot, hot_out, local.at[2]))
    saves[-1].start()
    ring.near(
        [
            (lambda Y, Z: packed_all.at[Y, Z, xh], 0),
            (lambda Y, Z: packed_all.at[Y, Z, 1 - xh], 4),
        ]
    )
    reply = Scatter(lambda p: rows.at[slots(p)], lambda p: emb.at[slots(p)], emb_s, emb_r, me)
    reply.start()
    emb[slots(me), :] = rows[slots(me), :]
    turn_over(table, rows_t, 0)
    saves.append(pltpu.make_async_copy(rows_t.at[0:SHARD], rows_t_out.at[0:SHARD], local.at[3]))
    saves[-1].start()
    largest = jnp.max(got[:, 4, :], 0, keepdims=True)
    own_most[...] = jnp.broadcast_to(largest, (8, 128))
    most[grp] = own_most[...]
    told = []
    for k in range(1, NG):
        to = lax.rem(grp + k, NG)
        told.append(remote(own_most, most.at[grp], most_s.at[k], most_r.at[grp], grp=to))
        told[-1].start()
    total = jnp.sum(got[:, 3, :].astype(F32), 0, keepdims=True)
    total = jnp.concatenate([total, total], 1) * T
    plain = weight.astype(F32)
    weights[...] = jnp.concatenate([plain / total, plain, total] + [jnp.zeros((1, T), F32)] * 5, 0)

    def place_goal(j, carry):
        from_dev = flat(j // 4, xh, lax.rem(j, 4))
        goals = jnp.concatenate([got[from_dev, 1:2, :], got[from_dev, 2:3, :]], 1)
        near, far = goals - me * SHARD, goals - other * SHARD
        at = jnp.where((far >= 0) & (far < SHARD), far + SHARD, -1)
        at = jnp.where((near >= 0) & (near < SHARD), near, at)
        goal[j] = jnp.broadcast_to(at, (8, T))
        return carry

    lax.fori_loop(0, 16, place_goal, 0)
    trade.forward()
    ring.far()
    ring.cross()
    reply.wait_recv()
    for k in range(1, NG):
        to = lax.rem(grp + k, NG)
        remote(own_most, most.at[to], most_s.at[k], most_r.at[to], grp=to).wait_recv()
    most_out[...] = jnp.maximum(jnp.maximum(most[0], most[1]), jnp.maximum(most[2], most[3]))
    trade.wait()
    saves.append(pltpu.make_async_copy(table_other, other_out, local.at[4]))
    saves[-1].start()
    turn_over(table_other, rows_t, SHARD)
    rest = pl.ds(SHARD, SHARD)
    saves.append(pltpu.make_async_copy(rows_t.at[rest], rows_t_out.at[rest], local.at[5]))
    saves[-1].start()
    ring.last()
    keep.wait()
    for save in saves:
        save.wait()
    over.wait_send()
    ask.wait_send()
    reply.wait_send()
    trade.finish()
    for copy in told:
        copy.wait_send()
    ring.finish()


def front(*args):
    return pl.pallas_call(
        front_kernel,
        name="front",
        out_shape=(
            jax.ShapeDtypeStruct((NW, 8, 128), jnp.int32),
            jax.ShapeDtypeStruct((NW * CAP, D), BF),
            jax.ShapeDtypeStruct((8, 128), jnp.int32),
            jax.ShapeDtypeStruct((D, SHARD), BF),
            jax.ShapeDtypeStruct((D, SHARD), BF),
            jax.ShapeDtypeStruct((2 * SHARD, D), BF),
            jax.ShapeDtypeStruct((4, 4, 2, PACKED, D), BF),
            jax.ShapeDtypeStruct((T, NW * CAP), BF),
            jax.ShapeDtypeStruct((8, T), jnp.int32),
            jax.ShapeDtypeStruct((NW * CAP, SHARD), BF),
            jax.ShapeDtypeStruct((16, 8, T), jnp.int32),
            jax.ShapeDtypeStruct((8, T), F32),
        ),
        in_specs=[VMEM, VMEM, VMEM, ANY, VMEM, VMEM, VMEM],
        out_specs=(VMEM, VMEM, VMEM, ANY, ANY, ANY, ANY, VMEM, VMEM, ANY, VMEM, VMEM),
        scratch_shapes=[
            pltpu.VMEM((D, SHARD), F32),
            pltpu.VMEM((D, SHARD), BF),
            pltpu.VMEM((D, SHARD), BF),
            pltpu.VMEM((2 * SHARD, D), BF),
            pltpu.VMEM((NW * CAP, SHARD), BF),
            pltpu.VMEM((PACKED, D), F32),
            pltpu.VMEM((PACKED, D), BF),
            pltpu.VMEM((NG, 8, 128), jnp.int32),
            pltpu.VMEM((8, 8, 128), jnp.int32),
            pltpu.VMEM((128, 128), F32),
            pltpu.VMEM((NW * CAP, D), BF),
            pltpu.VMEM((8, 128), jnp.int32),
            pltpu.VMEM((2, D // 2, SHARD), BF),
            DMA((NW,)),
            DMA((NW,)),
            DMA((NW,)),
            DMA((NW,)),
            DMA((NG,)),
            DMA((NG,)),
            DMA((4,)),
            DMA((4,)),
            DMA((RING_SENDS + 4,)),
            DMA((4, 4, 5)),
            DMA((2,)),
            DMA((6,)),
        ],
        compiler_params=params(1, 60),
        cost_estimate=pl.CostEstimate(flops=2 * 10**9, bytes_accessed=3 * 10**7, transcendentals=0),
    )(*args)


ORDER = tuple((i // 8) * 8 + (i % 2) * 4 + (i // 2) % 4 for i in range(NW))


def spread_rows(used, stride, at, repeat=1):
    picks = np.zeros((NW * stride, NW * used), np.float32)
    for i, w in enumerate(ORDER):
        for j in range(repeat):
            for r in range(used):
                picks[i * stride + at + j * used + r, w * used + r] = 1.0
    return picks


def rope():
    half = HD // 2
    freqs = np.float32(rope_base) ** (-(np.arange(half, dtype=np.float32) * np.float32(2.0)) / np.float32(HD))
    angles = freqs.astype(np.float32)[:, None] * np.arange(T, dtype=np.float32)[None, :]
    return np.concatenate([np.cos(angles), np.sin(angles)], 0).astype(np.float32)


def turned(values):
    return values.T


def gain_columns(gains):
    return jnp.concatenate([gains[:, 0, :], jnp.zeros((125, D), F32)], 0).T


def rms(values, gain):
    scale = lax.rsqrt(jnp.mean(values * values, 0, keepdims=True) + norm_eps)
    return values * scale * gain


def rms_back(values, gain, grad):
    scale = lax.rsqrt(jnp.mean(values * values, 0, keepdims=True) + norm_eps)
    pulled = grad * gain
    middle = jnp.mean(values * pulled, 0, keepdims=True)
    back = scale * pulled - values * (scale * scale * scale) * middle
    return back, jnp.sum(grad * values * scale, 1, keepdims=True)


def mask_of(tok):
    row = tok[0:1, :]
    column = jnp.broadcast_to(row.astype(F32), (128, T)).T[:, 0:1].astype(jnp.int32)
    down = lax.broadcasted_iota(jnp.int32, (T, T), 0)
    across = lax.broadcasted_iota(jnp.int32, (T, T), 1)
    return (down <= across) & (row == column)


def mm(a, b):
    return jnp.dot(a, b, preferred_element_type=F32)


def mm_nt(a, b):
    return lax.dot_general(a, b, (((1,), (1,)), ((), ())), preferred_element_type=F32)


def mm_tn(a, b):
    return lax.dot_general(a, b, (((0,), (0,)), ((), ())), preferred_element_type=F32)


def rotated(x, rot):
    cosine, sine = rot[0:32, :], rot[32:64, :]
    one, two = x[0:32, :], x[32:64, :]
    return jnp.concatenate([one * cosine - two * sine, two * cosine + one * sine], 0)


def unrotated(x, rot):
    cosine, sine = rot[0:32, :], rot[32:64, :]
    one, two = x[0:32, :], x[32:64, :]
    return jnp.concatenate([one * cosine + two * sine, two * cosine - one * sine], 0)


def load_trunk(packed, ffn, down, attn, sem):
    loads = [
        pltpu.make_async_copy(packed.at[:, :, :, ATTN_AT:PACKED], attn, sem.at[0]),
        pltpu.make_async_copy(packed.at[:, :, :, FFN_AT:DOWN_AT], ffn, sem.at[1]),
        pltpu.make_async_copy(packed.at[:, :, :, DOWN_AT:ATTN_AT, 0:512], down, sem.at[2]),
    ]
    for load in loads:
        load.start()
    return loads


TRUNK_SCRATCH = [
    pltpu.VMEM((4, 4, 2, 96, D), BF),
    pltpu.VMEM((4, 4, 2, 64, 512), BF),
    pltpu.VMEM((4, 4, 2, 48, D), BF),
    DMA((3,)),
]


def forward_kernel(
    more, emb, picks, packed, gains, rot, tok,
    final, h0, n1, q, k, v, lse, att, h1, n2, gate_up_out, inner, h2,
    ffn, down, attn, sem, mixed, gate_up, save_sem,
):
    loads = load_trunk(packed, ffn, down, attn, sem)
    columns = gain_columns(gains)
    allowed = mask_of(tok)
    start = turned(mm(picks[...], emb[...])) + more[...]
    h0[...] = start
    normed = rms(start, columns[:, 0:1]).astype(BF)
    n1[...] = normed
    loads[0].wait()
    rows48 = attn[...].reshape(NW * 48, D)
    product = mm(rows48, normed)
    for i, w in enumerate(ORDER):
        mixed[w * 30 : w * 30 + 30, :] = product[i * 48 : i * 48 + 30, :]
    for kv in range(KVH):
        k[kv * HD : (kv + 1) * HD, :] = rotated(
            mixed[D + kv * HD : D + (kv + 1) * HD, :], rot[...]
        ).astype(BF)
        at = D + (KVH + kv) * HD
        v[kv * HD : (kv + 1) * HD, :] = mixed[at : at + HD, :].astype(BF)
    logs = []
    for h in range(H):
        kv = h // (H // KVH)
        query = rotated(mixed[h * HD : (h + 1) * HD, :], rot[...]).astype(BF)
        q[h * HD : (h + 1) * HD, :] = query
        scores = mm_tn(k[kv * HD : (kv + 1) * HD, :], query) * HD ** (-0.5)
        scores = jnp.where(allowed, scores, masked_score)
        top = jnp.max(scores, 0, keepdims=True)
        power = jnp.exp(scores - top)
        total = jnp.sum(power, 0, keepdims=True)
        probs = (power / total).astype(BF)
        att[h * HD : (h + 1) * HD, :] = mm(v[kv * HD : (kv + 1) * HD, :], probs).astype(BF)
        logs.append(top + jnp.log(total))
    lse[...] = jnp.concatenate(logs + [jnp.zeros((16 - H, T), F32)], 0)
    product = mm(rows48, att[...])
    for i, w in enumerate(ORDER):
        mixed[w * 18 : w * 18 + 18, :] = product[i * 48 + 30 : i * 48 + 48, :]
    middle = start + mixed[0:D, :]
    h1[...] = middle
    normed = rms(middle, columns[:, 1:2]).astype(BF)
    n2[...] = normed
    loads[1].wait()
    gate_up[...] = mm(ffn[...].reshape(NW * 96, D), normed)
    save = pltpu.make_async_copy(gate_up, gate_up_out, save_sem.at[0])
    save.start()
    for i in range(NW // 2):
        gate = gate_up[i * 96 : (i + 1) * 96, :]
        up = gate_up[FF + i * 96 : FF + (i + 1) * 96, :]
        w = ORDER[i]
        inner[w * 96 : (w + 1) * 96, :] = (gate / (1.0 + jnp.exp(-gate)) * up).astype(BF)
    loads[2].wait()
    rows64 = down[...].reshape(NW * 64, 512)
    for j in range(3):
        product = mm(rows64, inner[j * 512 : (j + 1) * 512, :])
        for i, w in enumerate(ORDER):
            piece = product[i * 64 + j * 18 : i * 64 + j * 18 + 18, :]
            if j:
                mixed[w * 18 : w * 18 + 18, :] += piece
            else:
                mixed[w * 18 : w * 18 + 18, :] = piece
    last = middle + mixed[0:D, :]
    h2[...] = last
    final[...] = rms(last, columns[:, 2:3]).astype(BF)
    save.wait()


def forward(more, emb, picks, packed, gains, rot, tok):
    def out(rows, kind):
        return jax.ShapeDtypeStruct((rows, T), kind)

    return pl.pallas_call(
        forward_kernel,
        name="forward",
        out_shape=(
            out(D, BF), out(D, F32), out(D, BF), out(D, BF), out(KVH * HD, BF), out(KVH * HD, BF), out(16, F32),
            out(D, BF), out(D, F32), out(D, BF), out(2 * FF, F32), out(FF, BF), out(D, F32),
        ),
        in_specs=[VMEM, VMEM, VMEM, ANY, VMEM, VMEM, VMEM],
        out_specs=(VMEM,) * 10 + (ANY, VMEM, VMEM),
        scratch_shapes=TRUNK_SCRATCH
        + [pltpu.VMEM((QKV, T), F32), pltpu.VMEM((2 * FF, T), F32), DMA((1,))],
        compiler_params=pltpu.CompilerParams(vmem_limit_bytes=60 * MIB),
        cost_estimate=pl.CostEstimate(flops=4 * 10**9, bytes_accessed=2 * 10**7, transcendentals=10**6),
    )(more, emb, picks, packed, gains, rot, tok)


def more_rows_kernel(msg, table, got, emb, hot, rows, msg_s, msg_r, emb_s, emb_r):
    me = lax.axis_index("wide")
    greet_wide(me)
    ask = Scatter(lambda p: msg.at[p], lambda p: got.at[p], msg_s, msg_r, me)
    ask.start()
    got[me] = msg[me]
    ask.wait_recv()
    look_up(got, table, hot, rows, 0)
    reply = Scatter(lambda p: rows.at[slots(p)], lambda p: emb.at[slots(p)], emb_s, emb_r, me)
    reply.start()
    emb[slots(me), :] = rows[slots(me), :]
    reply.wait_recv()
    ask.wait_send()
    reply.wait_send()


def more_rows(msg, table):
    return pl.pallas_call(
        more_rows_kernel,
        name="more_rows",
        out_shape=(
            jax.ShapeDtypeStruct((NW, 8, 128), jnp.int32),
            jax.ShapeDtypeStruct((NW * CAP, D), BF),
        ),
        in_specs=[VMEM, VMEM],
        out_specs=(VMEM, VMEM),
        scratch_shapes=[pltpu.VMEM((8 * CAP, SHARD), BF), pltpu.VMEM((NW * CAP, D), BF)]
        + [DMA((NW,))] * 4,
        compiler_params=params(2, 40),
    )(msg, table)[1]


def more_grads_kernel(msg, rows, got, out, msg_s, msg_r, row_s, row_r):
    me = lax.axis_index("wide")
    greet_wide(me)
    ask = Scatter(lambda p: msg.at[p], lambda p: got.at[p], msg_s, msg_r, me)
    ask.start()
    give = Scatter(lambda p: rows.at[slots(p)], lambda p: out.at[slots(p)], row_s, row_r, me)
    give.start()
    got[me] = msg[me]
    out[slots(me), :] = rows[slots(me), :]
    ask.wait_recv()
    give.wait_recv()
    ask.wait_send()
    give.wait_send()


def more_grads(msg, rows):
    return pl.pallas_call(
        more_grads_kernel,
        name="more_grads",
        out_shape=(
            jax.ShapeDtypeStruct((NW, 8, 128), jnp.int32),
            jax.ShapeDtypeStruct((NW * CAP, D), BF),
        ),
        in_specs=[VMEM, VMEM],
        out_specs=(VMEM, VMEM),
        scratch_shapes=[DMA((NW,))] * 4,
        compiler_params=params(3, 20),
    )(msg, rows)


VOC = 2 * SHARD
TOK = 16 * T
CH = 128
GROUPS = CH // 8
NCH = VOC // CH
QUART = D // 4


def cols(j):
    return pl.ds(pl.multiple_of(j * T, T), T)


def head_kernel(
    final, rows_t, table_in, table_other_in, goal, weights,
    grad_final, head_out, head_other, loss,
    table, table_other, head_own, big, fall, expo, tops, stat, stat_in, coef, coef_in, parts,
    part_a, part_b, whole_a, whole_b, sum_a, sum_b, part_a2, part_b2, whole_a2, whole_b2,
    g_s, g_r, st_s, st_r, co_s, co_r, a_s, b_s, pa_r, pb_r, wa_r, wb_r, a2_s, b2_s, a2_r, b2_r,
):
    me, y, xh, z = place()
    mine = y * 4 + z
    tables = [
        pltpu.make_async_copy(table_in, table, big.at[0]),
        pltpu.make_async_copy(table_other_in, table_other, big.at[1]),
    ]
    for load in tables:
        load.start()

    def dev(j):
        return flat(j // 4, xh, lax.rem(j, 4))

    barrier = pltpu.get_barrier_semaphore()

    def greet(k, carry):
        pl.semaphore_signal(
            barrier, inc=1, device_id={"wide": dev(lax.rem(mine + k, 16))}, device_id_type=MESH
        )
        return carry

    lax.fori_loop(1, 16, greet, 0)
    pl.semaphore_wait(barrier, 15)

    sent = []

    def send(src, dst, ssem, rsem, to):
        copy = remote(src, dst, ssem, rsem, wide=to)
        copy.start()
        sent.append(copy)

    def arrived(dst, rsem):
        remote(dst, dst, g_s.at[0], rsem, wide=dev(mine)).wait_recv()

    ring = Ring(
        lambda Y, Z, first, count: fall.at[pl.ds(first, count), cols(Y * 4 + Z)],
        lambda Y, Z, index: g_r.at[Y * 4 + Z, index],
        tuple(QUART * k for k in range(5)),
        g_s,
    )
    ring.own(final, fall.at[:, cols(mine)], 0)
    fall[:, cols(mine)] = final[...]

    def logits(j):
        seen = fall[:, cols(j)]
        goals = goal[j]
        group, hit = goals >> 3, jnp.zeros((8, T), F32)
        best = total = None
        for c in range(NCH):
            part = mm(rows_t[c * CH : (c + 1) * CH, :], seen).reshape(GROUPS, 8, T)
            top = jnp.max(part, 0)
            power = jnp.exp(part - top[None])
            for r in range(GROUPS):
                hit = jnp.where(group == c * GROUPS + r, part[r], hit)
            expo[c * CH : (c + 1) * CH, cols(j)] = power.reshape(CH, T).astype(BF)
            tops[j, c] = top
            weight = jnp.sum(power, 0)
            if c:
                higher = jnp.maximum(best, top)
                total = total * jnp.exp(best - higher) + weight * jnp.exp(top - higher)
                best = higher
            else:
                best, total = top, weight
        spot = lax.broadcasted_iota(jnp.int32, (8, T), 0)
        hit = jnp.sum(jnp.where(spot == (goals & 7), hit, 0.0), 0, keepdims=True)
        top = jnp.max(best, 0, keepdims=True)
        total = jnp.sum(total * jnp.exp(best - top), 0, keepdims=True)
        zero = jnp.zeros((1, T), F32)
        stat[j] = jnp.concatenate([top, total, hit] + [zero] * 5, 0)

    def tell(j):
        return remote(stat.at[j], stat_in.at[mine], st_s.at[j], st_r.at[mine], wide=dev(j))

    def block(dy, dz):
        return turn4(y, dy) * 4 + turn4(z, dz)

    def forward(offsets):
        def one(k, carry):
            j = block(*offsets(k))
            logits(j)
            tell(j).start()
            return carry

        return one

    def odd(k):
        return 1 + 2 * lax.rem(k, 2)

    logits(mine)
    stat_in[mine] = stat[mine]
    ring.near()
    lax.fori_loop(0, 4, forward(lambda k: ((1 - k // 2) * odd(k), (k // 2) * odd(k))), 0)
    ring.far()
    lax.fori_loop(0, 2, forward(lambda k: (2 * (1 - k), 2 * k)), 0)
    ring.cross()
    lax.fori_loop(0, 4, forward(lambda k: (odd(k // 2), odd(k))), 0)
    ring.last()
    lax.fori_loop(
        0,
        4,
        forward(lambda k: (2 * (1 - k // 2) + odd(k) * (k // 2), odd(k) * (1 - k // 2) + 2 * (k // 2))),
        0,
    )
    forward(lambda k: (2, 2))(0, 0)

    def hear(k, carry):
        j = lax.rem(mine + k, 16)
        arrived(stat_in.at[j], st_r.at[j])
        return carry

    lax.fori_loop(1, 16, hear, 0)
    tip, weight, hit = stat_in[:, 0, :], stat_in[:, 1, :], stat_in[:, 2, :]
    top = jnp.max(tip, 0, keepdims=True)
    lse = top + jnp.log(jnp.sum(weight * jnp.exp(tip - top), 0, keepdims=True))
    picked = jnp.sum(hit, 0, keepdims=True)
    share, plain = weights[0:1, :], weights[1:2, :]
    zero = jnp.zeros((1, T), F32)
    coef[...] = jnp.concatenate(
        [lse, share * (1.0 + 2.0 * penalty_weight * lse), share] + [zero] * 5, 0
    )
    loss[...] = jnp.concatenate(
        [plain * (lse - picked + penalty_weight * lse * lse)] + [zero] * 7, 0
    )
    coef_in[mine] = coef[...]

    def spread(k):
        j = lax.rem(mine + k, 16)
        return remote(coef, coef_in.at[mine], co_s.at[k], co_r.at[mine], wide=dev(j))

    def spread_start(k, carry):
        spread(k).start()
        return carry

    lax.fori_loop(1, 16, spread_start, 0)

    up, down = 1, 3
    z_to = {step: flat(y, xh, turn4(z, step)) for step in (up, down)}
    y_to = {step: flat(turn4(y, step), xh, z) for step in (up, down)}

    def piece_a(j, index):
        row = j // 4
        return remote(
            parts.at[j, pl.ds(index * QUART, QUART)], part_a.at[index, row],
            a_s.at[j, index], pa_r.at[index, row], wide=z_to[(up, down)[index]],
        )

    def piece_b(j, index):
        column = lax.rem(j, 4)
        return remote(
            parts.at[j, pl.ds((2 + index) * QUART, QUART)], part_b.at[index, column],
            b_s.at[j, index], pb_r.at[index, column], wide=y_to[(up, down)[index]],
        )

    def half_a(j, index):
        row = j // 4
        return remote(
            parts.at[j, pl.ds(0, 2 * QUART)], whole_a.at[index, row],
            a_s.at[j, 0], wa_r.at[index, row], wide=z_to[(up, down)[index]],
        )

    def half_b(j, index):
        column = lax.rem(j, 4)
        return remote(
            parts.at[j, pl.ds(2 * QUART, 2 * QUART)], whole_b.at[index, column],
            b_s.at[j, 0], wb_r.at[index, column], wide=y_to[(up, down)[index]],
        )

    def offsets(k):
        return lax.rem(2 + k // 4, 4), lax.rem(2 + k, 4)

    def post(k):
        dy, dz = offsets(k)
        j = block(dy, dz)

        @pl.when(dz == 2)
        def _():
            piece_a(j, 0).start()
            piece_a(j, 1).start()

        @pl.when(dy == 2)
        def _():
            piece_b(j, 0).start()
            piece_b(j, 1).start()

        for index, step in enumerate((up, down)):

            @pl.when(dz == step)
            def _():
                row = j // 4
                arrived(part_a.at[index, row], pa_r.at[index, row])
                rows = pl.ds(index * QUART, QUART)
                total = parts[j, rows, :].astype(F32) + part_a[index, row].astype(F32)
                parts[j, rows, :] = total.astype(BF)
                half_a(j, index).start()

            @pl.when(dy == step)
            def _():
                column = lax.rem(j, 4)
                arrived(part_b.at[index, column], pb_r.at[index, column])
                rows = pl.ds((2 + index) * QUART, QUART)
                total = parts[j, rows, :].astype(F32) + part_b[index, column].astype(F32)
                parts[j, rows, :] = total.astype(BF)
                half_b(j, index).start()

    def backward(k, carry):
        j = block(*offsets(k))

        @pl.when(k != 10)
        def _():
            arrived(coef_in.at[j], co_r.at[j])

        lse, soft, pick = coef_in[j, 0:1, :], coef_in[j, 1:2, :], coef_in[j, 2:3, :]
        goals = goal[j]
        group = goals >> 3
        pick = jnp.where(lax.broadcasted_iota(jnp.int32, (8, T), 0) == (goals & 7), pick, 0.0)
        for c in range(NCH):
            scale = soft * jnp.exp(tops[j, c] - lse)
            power = expo[c * CH : (c + 1) * CH, cols(j)].astype(F32).reshape(GROUPS, 8, T)
            spot = lax.broadcasted_iota(jnp.int32, (GROUPS, 8, T), 0) + c * GROUPS
            drop = jnp.where(spot == group[None], pick[None], 0.0)
            grad = (power * scale[None] - drop).reshape(CH, T)
            expo[c * CH : (c + 1) * CH, cols(j)] = grad.astype(BF)
        product = jnp.dot(table[...], expo[0:SHARD, cols(j)], preferred_element_type=F32)
        product += jnp.dot(table_other[...], expo[SHARD:VOC, cols(j)], preferred_element_type=F32)
        parts[j] = product.astype(BF)

        @pl.when(k > 0)
        def _():
            post(k - 1)

        return carry

    for load in tables:
        load.wait()
    lax.fori_loop(0, 16, backward, 0)
    post(15)

    def head_chunk(c):
        return lax.dot_general(
            fall[...],
            expo[pl.ds(pl.multiple_of(c * 256, 256), 256), :],
            (((1,), (1,)), ((), ())),
            preferred_element_type=F32,
        )

    def other_chunk(c, carry):
        head_other[:, cols(c)] = head_chunk(c + SHARD // 256).astype(BF)
        return carry

    def own_chunk(c, carry):
        head_own[:, cols(c)] = head_chunk(c)
        return carry

    lax.fori_loop(0, SHARD // 256, other_chunk, 0)

    kinds = (
        (whole_a, wa_r, sum_a, part_a2, whole_a2, a2_s, a2_r, y_to, 0),
        (whole_b, wb_r, sum_b, part_b2, whole_b2, b2_s, b2_r, z_to, 2 * QUART),
    )
    for d in (2, 1, 3, 0):
        for kind, (whole, w_r, total, part2, whole2, s2, r2, to, base) in enumerate(kinds):
            at = turn4(y if kind == 0 else z, d)
            j = at * 4 + z if kind == 0 else y * 4 + at
            acc = parts[j, base : base + 2 * QUART, :].astype(F32)
            for index in range(2):
                arrived(whole.at[index, at], w_r.at[index, at])
                acc = acc + whole[index, at].astype(F32)
            if d == 0:
                grad_final[base : base + 2 * QUART, :] = acc
            else:
                total[d - 1] = acc.astype(BF)
            if d == 2:
                for index, step in enumerate((up, down)):
                    piece = total.at[1, pl.ds(index * QUART, QUART)]
                    send(piece, part2.at[index], s2.at[index], r2.at[index], to[step])
    lax.fori_loop(0, SHARD // 512, own_chunk, 0)
    for kind, (whole, w_r, total, part2, whole2, s2, r2, to, base) in enumerate(kinds):
        for index, step in enumerate((up, down)):
            arrived(part2.at[index], r2.at[index])
            rows = pl.ds(index * QUART, QUART)
            added = total[step - 1, rows, :].astype(F32) + part2[index].astype(F32)
            total[step - 1, rows, :] = added.astype(BF)
            send(total.at[step - 1], whole2.at[index], s2.at[2 + index], r2.at[2 + index], to[step])
    lax.fori_loop(SHARD // 512, SHARD // 256, own_chunk, 0)
    store = pltpu.make_async_copy(head_own, head_out, big.at[0])
    store.start()
    for kind, (whole, w_r, total, part2, whole2, s2, r2, to, base) in enumerate(kinds):
        for index in range(2):
            arrived(whole2.at[index], r2.at[2 + index])
        grad_final[base : base + 2 * QUART, :] += whole2[0].astype(F32) + whole2[1].astype(F32)

    def finish(k, carry):
        j = lax.rem(mine + k, 16)
        tell(j).wait_send()
        spread(k).wait_send()
        return carry

    lax.fori_loop(1, 16, finish, 0)
    for copy in sent:
        copy.wait_send()
    ring.finish()

    def finish_pieces(k, carry):
        row, column = block(k, 2), block(2, k)
        piece_a(row, 0).wait_send()
        piece_a(row, 1).wait_send()
        piece_b(column, 0).wait_send()
        piece_b(column, 1).wait_send()
        for index, step in enumerate((up, down)):
            half_a(block(k, step), index).wait_send()
            half_b(block(step, k), index).wait_send()
        return carry

    lax.fori_loop(0, 4, finish_pieces, 0)
    store.wait()


def head(final, rows_t, table, table_other, goal, weights):
    return pl.pallas_call(
        head_kernel,
        name="head",
        out_shape=(
            jax.ShapeDtypeStruct((D, T), F32),
            jax.ShapeDtypeStruct((D, SHARD), F32),
            jax.ShapeDtypeStruct((D, SHARD), BF),
            jax.ShapeDtypeStruct((8, T), F32),
        ),
        in_specs=[VMEM, VMEM, ANY, ANY, VMEM, VMEM],
        out_specs=(VMEM, ANY, VMEM, VMEM),
        scratch_shapes=[
            pltpu.VMEM((D, SHARD), BF),
            pltpu.VMEM((D, SHARD), BF),
            pltpu.VMEM((D, SHARD), F32),
            DMA((2,)),
            pltpu.VMEM((D, TOK), BF),
            pltpu.VMEM((VOC, TOK), BF),
            pltpu.VMEM((16, NCH, 8, T), F32),
            pltpu.VMEM((16, 8, T), F32),
            pltpu.VMEM((16, 8, T), F32),
            pltpu.VMEM((8, T), F32),
            pltpu.VMEM((16, 8, T), F32),
            pltpu.VMEM((16, D, T), BF),
            pltpu.VMEM((2, 4, QUART, T), BF),
            pltpu.VMEM((2, 4, QUART, T), BF),
            pltpu.VMEM((2, 4, 2 * QUART, T), BF),
            pltpu.VMEM((2, 4, 2 * QUART, T), BF),
            pltpu.VMEM((3, 2 * QUART, T), BF),
            pltpu.VMEM((3, 2 * QUART, T), BF),
            pltpu.VMEM((2, QUART, T), BF),
            pltpu.VMEM((2, QUART, T), BF),
            pltpu.VMEM((2, 2 * QUART, T), BF),
            pltpu.VMEM((2, 2 * QUART, T), BF),
            DMA((RING_SENDS,)),
            DMA((16, 4)),
            DMA((16,)),
            DMA((16,)),
            DMA((16,)),
            DMA((16,)),
            DMA((16, 2)),
            DMA((16, 2)),
            DMA((2, 4)),
            DMA((2, 4)),
            DMA((2, 4)),
            DMA((2, 4)),
            DMA((4,)),
            DMA((4,)),
            DMA((4,)),
            DMA((4,)),
        ],
        compiler_params=params(4, 61),
        cost_estimate=pl.CostEstimate(
            flops=6 * VOC * TOK * D, bytes_accessed=2 * 10**7, transcendentals=VOC * TOK
        ),
    )(final, rows_t, table, table_other, goal, weights)


class Reduce:
    def __init__(self, parts, base, sizes, along_z, refs):
        (
            self.first, part_a, part_b, self.whole1, self.second, next_a, next_b, self.whole2,
            self.third, self.stop, self.third_in, self.s, self.r,
        ) = refs
        self.part1, self.part2 = (part_a, part_b), (next_a, next_b)
        self.parts, self.base, self.sizes, self.along_z = parts, base, sizes, along_z
        self.rows = (pl.ds(0, sizes[0]), pl.ds(sizes[0], sizes[1]), pl.ds(0, sum(sizes)))
        self.me, self.y, self.xh, self.z = place()
        self.sent = []

    def send(self, src, dst, at, **to):
        copy = remote(src, dst, self.s.at[at], self.r.at[at], **to)
        copy.start()
        self.sent.append(copy)

    def wait(self, dst, at):
        remote(dst, dst, self.s.at[at], self.r.at[at], wide=self.me).wait_recv()

    def item1(self, step, which):
        rows = pl.ds(self.base + self.rows[which].start, self.rows[which].size)
        if self.along_z:
            return (slice(None), turn4(self.z, step), slice(None), rows)
        return (turn4(self.y, step), slice(None), slice(None), rows)

    def item2(self, step, which):
        return (turn4(self.y if self.along_z else self.z, step), slice(None), self.rows[which])

    def to(self, stage, step):
        if self.along_z == (stage == 1):
            return flat(self.y, self.xh, turn4(self.z, step))
        return flat(turn4(self.y, step), self.xh, self.z)

    def split(self, stage, ref, item, part, base):
        for index, step in enumerate((1, 3)):
            self.send(ref.at[item(2, index)], part[index], base + index, wide=self.to(stage, step))

    def join(self, stage, ref, item, part, whole, base):
        for index, step in enumerate((1, 3)):
            self.wait(part[index], base + index)
            at = item(step, index)
            ref[at] = (ref[at].astype(F32) + part[index][...].astype(F32)).astype(BF)
            self.send(ref.at[item(step, 2)], whole.at[index], base + 2 + index, wide=self.to(stage, step))

    def add(self, ref, item, whole, base):
        acc = ref[item(0, 2)].astype(F32)
        for index in range(2):
            self.wait(whole.at[index], base + 2 + index)
            acc = acc + whole[index].astype(F32)
        return acc

    def one(self):
        self.split(1, self.parts, self.item1, self.part1, 0)

    def two(self):
        self.join(1, self.parts, self.item1, self.part1, self.whole1, 0)

    def three(self):
        self.first[...] = self.add(self.parts, self.item1, self.whole1, 0).astype(BF)
        self.split(2, self.first, self.item2, self.part2, 4)

    def four(self):
        self.join(2, self.first, self.item2, self.part2, self.whole2, 4)

    def five(self):
        self.second[...] = self.add(self.first, self.item2, self.whole2, 4)
        self.third[...] = self.second[1 - self.xh].astype(BF)
        self.send(self.third, self.stop, 8, **beside(1 if self.along_z else 3))

    def six(self):
        self.wait(self.stop, 8)
        self.send(self.stop, self.third_in, 9, **beside(1 if self.along_z else 3))

    def total(self):
        self.wait(self.third_in, 9)
        return self.second[self.xh] + self.third_in[...].astype(F32)

    def finish(self):
        for copy in self.sent:
            copy.wait_send()


STREAMS = ((0, (48, 32), True), (80, (48, 32), False), (160, (16, 16), True), (192, (16, 16), False))


def reduce_scratch():
    shapes = []
    for _, sizes, _ in STREAMS:
        half = sum(sizes)
        shapes += [
            pltpu.VMEM((4, 2, half, D), BF),
            pltpu.VMEM((4, 2, sizes[0], D), BF),
            pltpu.VMEM((4, 2, sizes[1], D), BF),
            pltpu.VMEM((2, 4, 2, half, D), BF),
            pltpu.VMEM((2, half, D), F32),
            pltpu.VMEM((2, sizes[0], D), BF),
            pltpu.VMEM((2, sizes[1], D), BF),
            pltpu.VMEM((2, 2, half, D), BF),
            pltpu.VMEM((half, D), BF),
            pltpu.VMEM((half, D), BF),
            pltpu.VMEM((half, D), BF),
            DMA((10,)),
            DMA((10,)),
        ]
    return shapes


def back_kernel(
    grad_final, h0, n1, q, k, v, lse, att, h1, n2, gate_up_in, inner, h2,
    packed, gains, rot, tok, slot_row, loss, head_other, lay_attn_in, lay_out_in, lay_down_in,
    summed, rows_in, head_in, extra_sum, grad_embedded,
    ffn, down, attn, sem, lay_attn, lay_out, lay_down, lay_sem, gate_up, parts, rows, grad_up, grad_mixed, spread, stops,
    row_s, row_r, swap_s, swap_r, hold, land_z, land_y, land_x, tree_s, tree_r, *reducers,
):
    me, y, xh, z = place()
    lays = [
        pltpu.make_async_copy(src, dst, lay_sem.at[i])
        for i, (src, dst) in enumerate(
            ((lay_down_in, lay_down), (lay_out_in, lay_out), (lay_attn_in, lay_attn))
        )
    ]
    lays.append(pltpu.make_async_copy(gate_up_in, gate_up, lay_sem.at[3]))
    lays[0].start()
    lays[3].start()
    loads = load_trunk(packed, ffn, down, attn, sem)
    lays[1].start()
    lays[2].start()
    columns = gain_columns(gains)
    begun = []

    def begin():
        begun.extend(rms_back(h2[...], columns[:, 2:3], grad_final[...]))
        lays[0].wait()
        spread[...] = mm(lay_down[...], begun[0].astype(BF)).astype(BF)

    greet_wide(me, sides=True, meanwhile=begin)
    grad_h2, gain3 = begun
    halves = (pl.ds(0, D // 2), pl.ds(D // 2, D // 2))
    trade = Relay(
        [head_other.at[half] for half in halves],
        [stops.at[i] for i in range(2)],
        [head_in.at[half] for half in halves],
        swap_s,
        swap_r,
    )
    trade.start()
    streams = [
        Reduce(parts, base, sizes, along, reducers[13 * i : 13 * i + 13])
        for i, (base, sizes, along) in enumerate(STREAMS)
    ]
    early, late = streams[:2], streams[2:]
    chunk = lax.broadcasted_iota(jnp.int32, (NW * 64, T), 0) & 63
    zero = jnp.zeros((NW * 64, T), BF)
    wide = jnp.concatenate(
        [
            jnp.where((chunk >= 18 * j) & (chunk < 18 * (j + 1)), spread[...].astype(F32), 0.0).astype(BF)
            for j in range(3)
        ],
        1,
    )
    inners = jnp.concatenate([inner[j * 512 : (j + 1) * 512, :] for j in range(3)], 1)
    grad_down = mm_nt(wide, inners).astype(BF).reshape(4, 4, 2, 64, 512)
    parts[:, :, :, DOWN_AT:ATTN_AT, 0:512] = grad_down
    parts[:, :, :, DOWN_AT:ATTN_AT, 512:D] = jnp.zeros((4, 4, 2, 64, D - 512), BF)
    loads[2].wait()
    grad_inner = mm_tn(down[...].reshape(NW * 64, 512), wide)
    lays[3].wait()
    for i in range(NW // 2):
        w = ORDER[i]
        gate = gate_up[i * 96 : (i + 1) * 96, :]
        up = gate_up[FF + i * 96 : FF + (i + 1) * 96, :]
        pieces = []
        for at in range(w * 96, w * 96 + 96, 32):
            j, r = at // 512, at % 512
            pieces.append(grad_inner[r : r + 32, j * T : (j + 1) * T])
        grad = jnp.concatenate(pieces, 0)
        sigmoid = 1.0 / (1.0 + jnp.exp(-gate))
        slope = sigmoid * (1.0 + gate * (1.0 - sigmoid))
        grad_up[i * 96 : (i + 1) * 96, :] = (grad * up * slope).astype(BF)
        grad_up[FF + i * 96 : FF + (i + 1) * 96, :] = (grad * (gate * sigmoid)).astype(BF)
    parts[:, :, :, FFN_AT:DOWN_AT, :] = mm_nt(grad_up[...], n2[...]).astype(BF).reshape(4, 4, 2, 96, D)
    for stream in early:
        stream.one()
    loads[1].wait()
    grad_normed = turned(mm_tn(grad_up[...], ffn[...].reshape(NW * 96, D)))
    part, gain2 = rms_back(h1[...], columns[:, 1:2], grad_normed)
    grad_h1 = grad_h2 + part
    lays[1].wait()
    out_rows = mm(lay_out[...], grad_h1.astype(BF)).astype(BF)
    loads[0].wait()
    rows48 = attn[...].reshape(NW * 48, D)
    grad_att = turned(mm_tn(out_rows, rows48)).astype(BF)
    for stream in early:
        stream.two()
    trade.forward()

    allowed = mask_of(tok)
    group = H // KVH
    for kv in range(KVH):
        keys = k[kv * HD : (kv + 1) * HD, :]
        values = v[kv * HD : (kv + 1) * HD, :]
        grad_k, grad_v = jnp.zeros((HD, T), F32), jnp.zeros((HD, T), F32)
        for h in range(kv * group, (kv + 1) * group):
            query = q[h * HD : (h + 1) * HD, :]
            grad_out = grad_att[h * HD : (h + 1) * HD, :]
            scores = mm_tn(keys, query) * HD ** (-0.5)
            scores = jnp.where(allowed, scores, masked_score)
            soft = jnp.exp(scores - lse[h : h + 1, :])
            grad_probs = mm_tn(values, grad_out)
            mean = jnp.sum(soft * grad_probs, 0, keepdims=True)
            grad_scores = (soft * (grad_probs - mean)).astype(BF)
            grad_q = mm(keys, grad_scores) * HD ** (-0.5)
            grad_mixed[h * HD : (h + 1) * HD, :] = unrotated(grad_q, rot[...]).astype(BF)
            grad_k = grad_k + mm_nt(query, grad_scores) * HD ** (-0.5)
            grad_v = grad_v + mm_nt(grad_out, soft.astype(BF))
        at = D + kv * HD
        grad_mixed[at : at + HD, :] = unrotated(grad_k, rot[...]).astype(BF)
        at = D + (KVH + kv) * HD
        grad_mixed[at : at + HD, :] = grad_v.astype(BF)
    for stream in early:
        stream.three()
    lays[2].wait()
    attn_rows = mm(lay_attn[...], grad_mixed[...]).astype(BF)
    both = jnp.concatenate([attn_rows, out_rows], 1)
    seen = jnp.concatenate([n1[...], att[...]], 1)
    parts[:, :, :, ATTN_AT:PACKED, :] = mm_nt(both, seen).astype(BF).reshape(4, 4, 2, 48, D)
    parts[:, :, :, PACKED:SUMMED, :] = jnp.zeros((4, 4, 2, SUMMED - PACKED, D), BF)
    for stream in late:
        stream.one()
    grad_normed = turned(mm_tn(attn_rows, rows48))
    part, gain1 = rms_back(h0[...], columns[:, 0:1], grad_normed)
    grad_h0 = (grad_h1 + part).astype(BF)
    grad_embedded[...] = grad_h0
    slot = lax.broadcasted_iota(jnp.int32, (NW * CAP, T), 0)
    picks = jnp.where(slot == slot_row[0:1, :], 1.0, 0.0).astype(BF)
    rows[...] = mm_nt(picks, grad_h0).astype(BF)
    for stream in early:
        stream.four()
    lane = lax.broadcasted_iota(jnp.int32, (D, 128), 1)
    table = jnp.where(lane == 0, gain1, jnp.where(lane == 1, gain2, jnp.where(lane == 2, gain3, 0.0)))
    lost = jnp.sum(loss[0:1, :], 1, keepdims=True)
    table = table.T[0:8, :]
    tree = Tree(hold, land_z, land_y, land_x, tree_s, tree_r)
    tree.start(jnp.where(lax.broadcasted_iota(jnp.int32, (8, D), 0) == 3, lost, table))
    rows_in[slots(me), :] = rows[slots(me), :]
    for stream in late:
        stream.two()
    give = Scatter(lambda p: rows.at[slots(p)], lambda p: rows_in.at[slots(p)], row_s, row_r, me)
    give.start()
    for stream in early:
        stream.five()
    tree.next(0)
    for stream in late:
        stream.three()
    for stream in late:
        stream.four()
    tree.next(1)
    for stream in early:
        stream.six()
    for stream in late:
        stream.five()
    extra_sum[...] = tree.collect(2)
    for stream in late:
        stream.six()
    for stream in streams:
        summed[stream.base : stream.base + sum(stream.sizes), :] = stream.total()
    give.wait_recv()
    trade.wait()
    for stream in streams:
        stream.finish()
    give.wait_send()
    tree.finish()
    trade.finish()


def back(grad_final, kept, packed, gains, rot, tok, slot_row, loss, head_other):
    lays = [
        jnp.asarray(spread_rows(30, 48, 0), BF),
        jnp.asarray(spread_rows(18, 48, 30), BF),
        jnp.asarray(spread_rows(18, 64, 0, 3), BF),
    ]
    return pl.pallas_call(
        back_kernel,
        name="back",
        out_shape=(
            jax.ShapeDtypeStruct((SUMMED, D), F32),
            jax.ShapeDtypeStruct((NW * CAP, D), BF),
            jax.ShapeDtypeStruct((D, SHARD), BF),
            jax.ShapeDtypeStruct((8, D), F32),
            jax.ShapeDtypeStruct((D, T), BF),
        ),
        in_specs=[VMEM] * 10 + [ANY, VMEM, VMEM, ANY] + [VMEM] * 5 + [ANY] * 4,
        out_specs=(VMEM, VMEM, ANY, VMEM, VMEM),
        scratch_shapes=TRUNK_SCRATCH
        + [
            pltpu.VMEM((NW * 48, QKV), BF),
            pltpu.VMEM((NW * 48, D), BF),
            pltpu.VMEM((NW * 64, D), BF),
            DMA((4,)),
            pltpu.VMEM((2 * FF, T), F32),
            pltpu.VMEM((4, 4, 2, SUMMED, D), BF),
            pltpu.VMEM((NW * CAP, D), BF),
            pltpu.VMEM((2 * FF, T), BF),
            pltpu.VMEM((QKV, T), BF),
            pltpu.VMEM((NW * 64, T), BF),
            pltpu.VMEM((2, D // 2, SHARD), BF),
        ]
        + [DMA((NW,)), DMA((NW,)), DMA((4,)), DMA((4,))]
        + tree_scratch(D)
        + reduce_scratch(),
        compiler_params=params(5, 60),
        cost_estimate=pl.CostEstimate(flops=10**10, bytes_accessed=3 * 10**7, transcendentals=10**6),
    )(grad_final, *kept, packed, gains, rot, tok, slot_row, loss, head_other, *lays)


def adam_update(weight, grad, first, second, rate, decay):
    first = beta_one * first + (1.0 - beta_one) * grad
    second = beta_two * second + (1.0 - beta_two) * grad * grad
    ratio = first / (1.0 - beta_one**STEP) / (jnp.sqrt(second / (1.0 - beta_two**STEP)) + adam_eps)
    return (weight - rate * (ratio + decay * weight), first, second)


def adam_diff(weight, grad, first, second, anchor, rate, decay):
    return anchor - adam_update(weight, grad, first, second, rate, decay)[0]


PIECES = ((0, 0, 96), (0, 96, 96), (0, 192, 96), (1, 0, 112))


def update_kernel(
    rows, hot, head, head_in, summed, extra, tm, tf, ts, ta, *refs
):
    trunk, gains = [refs[3 * i : 3 * i + 3] for i in range(4)], refs[12:16]
    update_body(rows, hot, head, head_in, summed, extra, tm, tf, ts, ta, trunk, gains, *refs[16:])


def update_body(
    rows, hot, head, head_in, summed, extra, tm, tf, ts, ta, trunk_in, gains,
    table_grad_out, total_t, total_k, total_g, norms,
    table_grad, v_rows, v_hot, v_head, v_head_in, vm, vf, vs, va, flipped,
    one_t, one_t_in, two_t, two_t_in, one_k, one_k_in, two_k, two_k_in, gains_out, gains_in,
    load_sem, one_s, one_r, two_s, two_r, three_s, three_r, gains_s, gains_r,
    hold, land_z, land_y, land_x, tree_s, tree_r, km, kf, ks, ka,
):
    me, y, xh, z = place()
    grp = lax.axis_index("grp")
    core, x = lax.rem(grp, 2), grp // 2
    near, far = x * 2 + 1 - core, (1 - x) * 2 + core
    loads = [
        pltpu.make_async_copy(src, dst, load_sem.at[i])
        for i, (src, dst) in enumerate(
            zip((rows, hot, head, head_in, tm, tf, ts, ta), (v_rows, v_hot, v_head, v_head_in, vm, vf, vs, va))
        )
    ]
    for load in loads:
        load.start()
    barrier = pltpu.get_barrier_semaphore()
    for peer in near_peers(me, y, xh, z):
        pl.semaphore_signal(barrier, inc=1, device_id={"wide": peer}, device_id_type=MESH)
    for k in range(1, NG):
        pl.semaphore_signal(
            barrier, inc=1, device_id={"grp": lax.rem(grp + k, NG)}, device_id_type=MESH
        )
    pl.semaphore_wait(barrier, 7 + NG - 1)
    loads[0].wait()
    for c in range(0, NW * CAP, 256):
        flipped[:, c : c + 256] = v_rows[c : c + 256, :].T
    for load in loads[1:4]:
        load.wait()
    squares = jnp.zeros((1, 512), F32)
    for c in range(0, SHARD, 512):
        part = v_head[:, c : c + 512] + v_head_in[:, c : c + 512].astype(F32)
        part = part + mm(flipped[...], v_hot[:, c : c + 512])
        table_grad[:, c : c + 512] = part
        squares = squares + jnp.sum(part * part, 0, keepdims=True)
    save = pltpu.make_async_copy(table_grad, table_grad_out, load_sem.at[0])
    save.start()
    squares = jnp.sum(squares, 1, keepdims=True)
    trunk = jnp.sum(summed[...] * summed[...], 0, keepdims=True)
    squares = squares + jnp.sum(trunk, 1, keepdims=True)
    tree = Tree(hold, land_z, land_y, land_x, tree_s, tree_r)
    tree.start(jnp.broadcast_to(squares, (8, 128)))
    for out, (attn, ffn, proj) in zip((km, kf, ks, ka), trunk_in):
        if out is ka:
            pack_rows(out, attn[...], ffn[...], proj[...])
        else:
            pack_rows(out, attn[:, 0, :], ffn[...], proj[:, 0, :])
        out[PACKED:SUMMED, :] = jnp.zeros((SUMMED - PACKED, D), F32)
    gain_grads = extra[0:3, :]
    gain_squares = jnp.sum(jnp.sum(gain_grads * gain_grads, 0, keepdims=True), 1, keepdims=True)
    tree.next(0)
    for load in loads[4:]:
        load.wait()
    tree.next(1)
    norm = jnp.sqrt(tree.collect(2)[0:1, 0:1] + gain_squares)
    factor = jnp.minimum(1.0, clip_norm / norm)
    down = lax.broadcasted_iota(jnp.int32, (8, 128), 0)
    norms[...] = jnp.where(down == 0, norm, factor)

    parts = (
        (vm, table_grad, vf, vs, va, total_t, D // 2, one_t, one_t_in, two_t, two_t_in),
        (km, summed, kf, ks, ka, total_k, SUMMED // 2, one_k, one_k_in, two_k, two_k_in),
    )
    sent = []

    def span(which, at, count, side):
        half = parts[which][6]
        return pl.ds(pl.multiple_of(side * half + at, 16), count)

    def diff(which, at, count, side):
        m, g, f, s2, a = parts[which][:5]
        rows = span(which, at, count, side)
        return adam_diff(
            m[rows, :], g[rows, :] * factor, f[rows, :], s2[rows, :], a[rows, :], inner_rate, weight_decay
        )

    for i, (which, at, count) in enumerate(PIECES):
        one, one_in = parts[which][7:9]
        rows = pl.ds(at, count)
        one[rows, :] = diff(which, at, count, 1 - core).astype(BF)
        copy = remote(one.at[rows], one_in.at[rows], one_s.at[i], one_r.at[i], grp=near)
        copy.start()
        sent.append(copy)
    for i, (which, at, count) in enumerate(PIECES):
        one, one_in, two, two_in = parts[which][7:11]
        rows = pl.ds(at, count)
        own = diff(which, at, count, core)
        sent[i].wait_recv()
        two[rows, :] = (own + one_in[rows, :].astype(F32)).astype(BF)
        copy = remote(two.at[rows], two_in.at[rows], two_s.at[i], two_r.at[i], grp=far)
        copy.start()
        sent.append(copy)
    gains_out[0:3, :] = adam_diff(
        gains[0][:, 0, :], gain_grads * factor, gains[1][:, 0, :], gains[2][:, 0, :], gains[3][...], gain_rate, 0.0
    )
    gains_out[3:8, :] = jnp.zeros((5, D), F32)
    told = []
    for k in range(1, NG):
        to = lax.rem(grp + k, NG)
        told.append(remote(gains_out, gains_in.at[grp], gains_s.at[k], gains_r.at[grp], grp=to))
        told[-1].start()
    gains_in[grp] = gains_out[...]
    for i, (which, at, count) in enumerate(PIECES):
        total, two, two_in = parts[which][5], parts[which][9], parts[which][10]
        rows = pl.ds(at, count)
        sent[len(PIECES) + i].wait_recv()
        kept = span(which, at, count, core)
        total[kept, :] = two[rows, :].astype(F32) + two_in[rows, :].astype(F32)
        copy = remote(total.at[kept], total.at[kept], three_s.at[i], three_r.at[i], grp=near)
        copy.start()
        sent.append(copy)
    for k in range(1, NG):
        other = lax.rem(grp + k, NG)
        remote(
            gains_out, gains_in.at[other], gains_s.at[k], gains_r.at[other], grp=other
        ).wait_recv()
    total_g[...] = (gains_in[0] + gains_in[1]) + (gains_in[2] + gains_in[3])
    for i, (which, at, count) in enumerate(PIECES):
        away = parts[which][5].at[span(which, at, count, 1 - core)]
        remote(away, away, three_s.at[i], three_r.at[i], grp=near).wait_recv()
    for copy in sent + told:
        copy.wait_send()
    tree.finish()
    save.wait()


def update(rows, hot, head, head_in, summed, extra, table, trunk, gains):
    def exchange(size, lanes):
        return [pltpu.VMEM((size // 2, lanes), BF)] * 4

    table_f32 = pltpu.VMEM((D, SHARD), F32)
    pieces = DMA((len(PIECES),))
    return pl.pallas_call(
        update_kernel,
        name="update",
        out_shape=(
            jax.ShapeDtypeStruct((D, SHARD), F32),
            jax.ShapeDtypeStruct((D, SHARD), F32),
            jax.ShapeDtypeStruct((SUMMED, D), F32),
            jax.ShapeDtypeStruct((8, D), F32),
            jax.ShapeDtypeStruct((8, 128), F32),
        ),
        in_specs=[ANY] * 4 + [VMEM] * 2 + [ANY] * 4 + [VMEM] * 16,
        out_specs=(ANY,) + (VMEM,) * 4,
        scratch_shapes=[
            table_f32,
            pltpu.VMEM((NW * CAP, D), BF),
            pltpu.VMEM((NW * CAP, SHARD), BF),
            table_f32,
            pltpu.VMEM((D, SHARD), BF),
            table_f32,
            table_f32,
            table_f32,
            table_f32,
            pltpu.VMEM((D, NW * CAP), BF),
        ]
        + exchange(D, SHARD)
        + exchange(SUMMED, D)
        + [pltpu.VMEM((8, D), F32), pltpu.VMEM((NG, 8, D), F32), DMA((8,))]
        + [pieces] * 6
        + [DMA((NG,)), DMA((NG,))]
        + tree_scratch(128)
        + [pltpu.VMEM((SUMMED, D), F32)] * 4,
        compiler_params=params(6, 62),
        cost_estimate=pl.CostEstimate(flops=2 * 10**9, bytes_accessed=3 * 10**7, transcendentals=10**6),
    )(rows, hot, head, head_in, summed, extra, *table, *trunk, *gains)


def settle(total, momentum, anchor, grad, first, second):
    average = total * (1.0 / NG)
    outer = outer_momentum * momentum + average
    weight = anchor - outer_rate * (average + outer_momentum * outer)
    first = beta_one * first + (1.0 - beta_one) * grad
    second = beta_two * second + (1.0 - beta_two) * grad * grad
    return average, outer, weight, first, second


def rows_of(packed):
    down = [packed[DOWN_AT + 18 * j : DOWN_AT + 18 * j + 18, 0:512] for j in range(3)]
    proj = jnp.concatenate([packed[ATTN_AT + 30 : PACKED, :]] + down, 1)
    return packed[ATTN_AT : ATTN_AT + 30, :], packed[FFN_AT:DOWN_AT, :], proj


def finish_kernel(norms, *refs):
    table, summed, total_k, extra, total_g = refs[:6], refs[6], refs[7], refs[8], refs[9]
    small = [refs[10 + 4 * i : 14 + 4 * i] for i in range(4)]
    outs = [refs[26 + 5 * i : 31 + 5 * i] for i in range(5)]
    factor = norms[1:2, 0:1]
    total, momentum, anchor, grad, first, second = table
    values = settle(
        total[...], momentum[...], anchor[...], grad[...] * factor, first[...], second[...]
    )
    for out, value in zip(outs[0], values):
        out[...] = value

    @pl.when(pl.program_id(0) == 0)
    def _():
        grads = rows_of(summed) + (extra[0:3, :],)
        totals = rows_of(total_k) + (total_g[0:3, :],)
        for i in range(4):
            momentum, anchor, first, second = small[i]
            flat_moments = i == 1
            if flat_moments:
                moments = first[...], second[...]
            else:
                moments = first[:, 0, :], second[:, 0, :]
            values = settle(totals[i], momentum[...], anchor[...], grads[i] * factor, *moments)
            for n, (out, value) in enumerate(zip(outs[i + 1], values)):
                if n < 3 or flat_moments:
                    out[...] = value
                else:
                    out[:, 0, :] = value


def finish(norms, table, summed, total_k, extra, total_g, small):
    block = pl.BlockSpec((96, SHARD), lambda i: (i, 0))

    def whole(value):
        return pl.BlockSpec(value.shape, lambda i, rank=len(value.shape): (0,) * rank)

    rest = [summed, total_k, extra, total_g] + [value for kind in small for value in kind]
    shapes = [jax.ShapeDtypeStruct((D, SHARD), F32)] * 5
    for momentum, anchor, first, second in small:
        shapes += [jax.ShapeDtypeStruct(momentum.shape, F32)] * 3
        shapes += [jax.ShapeDtypeStruct(first.shape, F32)] * 2
    return pl.pallas_call(
        finish_kernel,
        name="finish",
        grid=(D // 96,),
        out_shape=tuple(shapes),
        in_specs=[whole(norms)] + [block] * 6 + [whole(value) for value in rest],
        out_specs=tuple([block] * 5 + [whole(shape) for shape in shapes[5:]]),
        compiler_params=pltpu.CompilerParams(vmem_limit_bytes=62 * MIB),
        cost_estimate=pl.CostEstimate(flops=2 * 10**7, bytes_accessed=4 * 10**7, transcendentals=0),
    )(norms, *table, *rest)


def dot(spec, a, b):
    return jnp.einsum(spec, a, b, preferred_element_type=F32)


def on_device(
    token_ids,
    targets,
    segment_ids,
    row_counts,
    embed_table_master,
    embed_table_first,
    embed_table_second,
    embed_table_anchor,
    embed_table_momentum,
    attn_in_master,
    attn_in_first,
    attn_in_second,
    attn_in_anchor,
    attn_in_momentum,
    ffn_in_master,
    ffn_in_first,
    ffn_in_second,
    ffn_in_anchor,
    ffn_in_momentum,
    proj_out_master,
    proj_out_first,
    proj_out_second,
    proj_out_anchor,
    proj_out_momentum,
    norm_gains_master,
    norm_gains_first,
    norm_gains_second,
    norm_gains_anchor,
    norm_gains_momentum,
):
    ids = token_ids[0]

    def rows_apart(value):
        return value.transpose(2, 0, 1)

    ffn = [v.T for v in (ffn_in_master[0], ffn_in_first[0], ffn_in_second[0], ffn_in_anchor, ffn_in_momentum)]
    attn = [rows_apart(v) for v in (attn_in_master, attn_in_first, attn_in_second)]
    attn += [attn_in_anchor.T, attn_in_momentum.T]
    proj = [rows_apart(v) for v in (proj_out_master, proj_out_first, proj_out_second)]
    proj += [proj_out_anchor.T, proj_out_momentum.T]
    gains = [v.transpose(1, 0, 2) for v in (norm_gains_master, norm_gains_first, norm_gains_second)]
    gains += [norm_gains_anchor, norm_gains_momentum]
    tables = [v.T for v in (embed_table_master[0], embed_table_first[0], embed_table_second[0])]
    tables += [embed_table_anchor.T, embed_table_momentum.T]
    (
        got, rows, most, table, table_other, rows_t, packed_all, picks, slot_row, hot, goals, weights,
    ) = front(
        token_ids, targets, row_counts[0], tables[0], attn[0], ffn[0], proj[0]
    )
    turns = (most[0, 0] + CAP - 1) // CAP

    def asked_in(turn):
        ids_now = jnp.where(turn > 0, ids, 0)
        owner = ids_now // SHARD
        same = ids_now[:, None] == ids_now[None, :]
        before = jnp.arange(T)[None, :] < jnp.arange(T)[:, None]
        first_seen = ~jnp.any(same & before, 1)
        smaller = (owner[None, :] == owner[:, None]) & (ids_now[None, :] < ids_now[:, None])
        rank = jnp.sum(first_seen[None, :] & smaller, 1, dtype=jnp.int32) - turn * CAP
        slot = jnp.where((rank >= 0) & (rank < CAP), owner * CAP + rank, -1)
        chosen = jnp.arange(NW * CAP)[:, None] == slot[None, :]
        asked = jnp.max(jnp.where(chosen, (ids_now - owner * SHARD)[None, :], -1), 1).reshape(NW, 1, CAP)
        asked = jnp.pad(asked, ((0, 0), (0, 0), (0, 128 - CAP)), constant_values=-1)
        return jnp.pad(asked, ((0, 0), (0, 7), (0, 0))), chosen.astype(BF)

    def more_tokens(carry):
        turn, hidden = carry
        message, chosen = asked_in(turn)
        return turn + 1, hidden + dot("sd,st->dt", more_rows(message, table), chosen)

    more = lax.while_loop(
        lambda carry: carry[0] < turns, more_tokens, (jnp.int32(1), jnp.zeros((D, T), F32))
    )[1]

    rot = jnp.asarray(rope())
    final, *kept = forward(more, rows, picks, packed_all, gains[0], rot, segment_ids)
    total = weights[2, 0]
    grad_final, head_own, head_other, loss = head(final, rows_t, table, table_other, goals, weights)
    summed, rows_in, head_in, extra_sum, grad_embedded = back(
        grad_final, kept, packed_all, gains[0], rot, segment_ids, slot_row, loss, head_other
    )

    def more_table(carry):
        turn, grad = carry
        message, chosen = asked_in(turn)
        mine = dot("st,dt->sd", chosen, grad_embedded).astype(BF)
        got_now, rows_now = more_grads(message, mine)
        asked = got_now[:, 0, :CAP].reshape(NW * CAP)
        hot_now = (asked[:, None] == jnp.arange(SHARD)[None, :]).astype(BF)
        return turn + 1, grad + dot("sd,sv->dv", rows_now, hot_now)

    head_grad = lax.while_loop(lambda carry: carry[0] < turns, more_table, (jnp.int32(1), head_own))[1]
    table_grad, total_t, total_k, total_g, norms = update(
        rows_in,
        hot,
        head_grad,
        head_in,
        summed,
        extra_sum,
        tables[:4],
        [kind[i] for i in range(4) for kind in (attn, ffn, proj)],
        gains[:4],
    )
    outs = finish(
        norms,
        (total_t, tables[4], tables[3], table_grad, tables[1], tables[2]),
        summed,
        total_k,
        extra_sum,
        total_g,
        [(kind[4], kind[3], kind[1], kind[2]) for kind in (attn, ffn, proj, gains)],
    )
    results = [extra_sum[3, 0:1], total.reshape(1), norms[0, 0:1]]
    for index in range(5):
        average, outer, weight, first, second = outs[5 * index : 5 * index + 5]
        if index < 4:
            average, outer, weight = average.T, outer.T, weight.T
        if index in (0, 2):
            first, second = first.T[None], second.T[None]
        elif index == 4:
            first, second = first.transpose(1, 0, 2), second.transpose(1, 0, 2)
        else:
            first, second = first.transpose(1, 2, 0), second.transpose(1, 2, 0)
        results += [average, outer, weight, first, second]
    return tuple(results)


def solution(mesh):
    in_specs = (
        P("grp", "wide"),
        P("grp", "wide"),
        P("grp", "wide"),
        P("grp", "wide", None),
        P("grp", "wide", None),
        P("grp", "wide", None),
        P("grp", "wide", None),
        P("wide", None),
        P("wide", None),
        P("grp", None, "wide"),
        P("grp", None, "wide"),
        P("grp", None, "wide"),
        P(None, "wide"),
        P(None, "wide"),
        P("grp", None, "wide"),
        P("grp", None, "wide"),
        P("grp", None, "wide"),
        P(None, "wide"),
        P(None, "wide"),
        P("grp", None, "wide"),
        P("grp", None, "wide"),
        P("grp", None, "wide"),
        P(None, "wide"),
        P(None, "wide"),
        P("grp", None, None),
        P("grp", None, None),
        P("grp", None, None),
        P(),
        P(),
    )
    out_specs = (
        P("grp"),
        P("grp"),
        P("grp"),
        P("wide", None),
        P("wide", None),
        P("wide", None),
        P("grp", "wide", None),
        P("grp", "wide", None),
        P(None, "wide"),
        P(None, "wide"),
        P(None, "wide"),
        P("grp", None, "wide"),
        P("grp", None, "wide"),
        P(None, "wide"),
        P(None, "wide"),
        P(None, "wide"),
        P("grp", None, "wide"),
        P("grp", None, "wide"),
        P(None, "wide"),
        P(None, "wide"),
        P(None, "wide"),
        P("grp", None, "wide"),
        P("grp", None, "wide"),
        P(),
        P(),
        P(),
        P("grp", None, None),
        P("grp", None, None),
    )
    return jax.shard_map(
        on_device, mesh=mesh, in_specs=in_specs, out_specs=out_specs, check_vma=False
    )
```

```python
import jax
import jax.numpy as jnp
import numpy as np
from jax import lax
from jax.experimental import pallas as pl
from jax.experimental.pallas import tpu as pltpu
from jax.sharding import PartitionSpec as P

D = 576
H = 9
KVH = 3
HD = 64
FF = 1536
QKV = 960
STEP = 8
T = 256
SHARD = 1536
NW = 32
NG = 4
CAP = 32
FFN_AT, DOWN_AT, ATTN_AT, PACKED = 0, 96, 160, 208
SUMMED = 224

beta_one = 0.9
beta_two = 0.999
adam_eps = 1e-08
weight_decay = 0.1
inner_rate = 0.02
gain_rate = 0.2
clip_norm = 0.01
penalty_weight = 0.005
outer_rate = 0.7
outer_momentum = 0.9
rope_base = 100000.0
norm_eps = 1e-05
masked_score = -1e30

BF = jnp.bfloat16
F32 = jnp.float32
MESH = pl.DeviceIdType.MESH
VMEM = pl.BlockSpec(memory_space=pltpu.VMEM)
ANY = pl.BlockSpec(memory_space=pl.ANY)
DMA = pltpu.SemaphoreType.DMA
MIB = 1 << 20


def params(collective, mib):
    return pltpu.CompilerParams(
        collective_id=collective, has_side_effects=True, vmem_limit_bytes=mib * MIB
    )


def place():
    me = lax.axis_index("wide")
    return me, me // 8, lax.rem(me // 4, 2), lax.rem(me, 4)


def flat(y, xh, z):
    return y * 8 + xh * 4 + z


def turn4(at, by):
    return lax.rem(at + by, 4)


def remote(src, dst, ssem, rsem, **device):
    return pltpu.make_async_remote_copy(
        src_ref=src,
        dst_ref=dst,
        send_sem=ssem,
        recv_sem=rsem,
        device_id=device,
        device_id_type=MESH,
    )


def greet_wide(me, grp=None, sides=False, meanwhile=None):
    barrier = pltpu.get_barrier_semaphore()

    def one(k, carry):
        pl.semaphore_signal(
            barrier, inc=1, device_id={"wide": lax.rem(me + k, NW)}, device_id_type=MESH
        )
        return carry

    lax.fori_loop(1, NW, one, 0)
    count = NW - 1
    if grp is not None:
        for k in range(1, NG):
            pl.semaphore_signal(
                barrier, inc=1, device_id={"grp": lax.rem(grp + k, NG)}, device_id_type=MESH
            )
        count += NG - 1
    if sides:
        for step in (1, 3):
            pl.semaphore_signal(barrier, inc=1, device_id=beside(step), device_id_type=MESH)
        count += 2
    if meanwhile is not None:
        meanwhile()
    pl.semaphore_wait(barrier, count)


def near_peers(me, y, xh, z):
    peers = [flat(y, xh, turn4(z, k)) for k in (1, 2, 3)] + [flat(turn4(y, k), xh, z) for k in (1, 2, 3)]
    return peers + [flat(y, 1 - xh, z)]


class Tree:
    def __init__(self, hold, land_z, land_y, land_x, ssem, rsem):
        self.hold, self.lands = hold, (land_z, land_y, land_x)
        self.ssem, self.rsem = ssem, rsem
        me, self.y, self.xh, self.z = place()
        self.sent = []

    def send(self, stage):
        y, xh, z = self.y, self.xh, self.z
        at = (z, y, xh)[stage]
        land, src = self.lands[stage], self.hold.at[stage]
        for k in range(1, 2 if stage == 2 else 4):
            if stage == 0:
                to = flat(y, xh, turn4(z, k))
            elif stage == 1:
                to = flat(turn4(y, k), xh, z)
            else:
                to = flat(y, 1 - xh, z)
            copy = remote(src, land.at[at], self.ssem.at[stage, k], self.rsem.at[stage, at], wide=to)
            copy.start()
            self.sent.append(copy)
        land[at] = self.hold[stage]

    def start(self, value):
        self.hold[0] = value
        self.send(0)

    def collect(self, stage):
        at = (self.z, self.y, self.xh)[stage]
        land = self.lands[stage]
        size = 2 if stage == 2 else 4
        for k in range(1, size):
            other = lax.rem(at + k, size)
            remote(
                land.at[other], land.at[other], self.ssem.at[stage, k], self.rsem.at[stage, other],
                wide=flat(self.y, self.xh, self.z),
            ).wait_recv()
        total = land[0]
        for k in range(1, size):
            total = total + land[k]
        return total

    def next(self, stage):
        self.hold[stage + 1] = self.collect(stage)
        self.send(stage + 1)

    def finish(self):
        for copy in self.sent:
            copy.wait_send()


def tree_scratch(lanes):
    return [
        pltpu.VMEM((3, 8, lanes), F32),
        pltpu.VMEM((4, 8, lanes), F32),
        pltpu.VMEM((4, 8, lanes), F32),
        pltpu.VMEM((2, 8, lanes), F32),
        DMA((3, 4)),
        DMA((3, 4)),
    ]


class Scatter:
    def __init__(self, src_at, dst_at, ssem, rsem, me):
        self.src_at, self.dst_at, self.ssem, self.rsem, self.me = src_at, dst_at, ssem, rsem, me

    def copy(self, k):
        peer = lax.rem(self.me + k, NW)
        return remote(
            self.src_at(peer), self.dst_at(self.me), self.ssem.at[k], self.rsem.at[self.me], wide=peer
        )

    def start(self):
        def one(k, carry):
            self.copy(k).start()
            return carry

        lax.fori_loop(1, NW, one, 0)

    def wait_recv(self):
        def one(k, carry):
            peer = lax.rem(self.me + k, NW)
            remote(
                self.src_at(peer), self.dst_at(peer), self.ssem.at[k], self.rsem.at[peer], wide=peer
            ).wait_recv()
            return carry

        lax.fori_loop(1, NW, one, 0)

    def wait_send(self):
        def one(k, carry):
            self.copy(k).wait_send()
            return carry

        lax.fori_loop(1, NW, one, 0)


class Ring:
    def __init__(self, view, sem, bounds, ssem):
        self.view, self.sem, self.bounds = view, sem, bounds
        self.ssem, self.used, self.sent = ssem, 0, []
        self.me, self.y, self.xh, self.z = place()

    def send(self, src, dst, rsem, to):
        copy = remote(src, dst, self.ssem.at[self.used], rsem, wide=flat(to[0], self.xh, to[1]))
        self.used += 1
        copy.start()
        self.sent.append(copy)

    def piece(self, y, z, first, count):
        return self.view(y, z, self.bounds[first], self.bounds[first + count] - self.bounds[first])

    def pass_on(self, y, z, first, count, index, *to):
        piece = self.piece(y, z, first, count)
        for one in to:
            self.send(piece, piece, self.sem(y, z, index), one)

    def landed(self, piece, sem):
        remote(piece, piece, self.ssem.at[0], sem, wide=self.me).wait_recv()

    def wait(self, y, z, first, count, index):
        self.landed(self.piece(y, z, first, count), self.sem(y, z, index))

    def around(self):
        y, z = self.y, self.z
        return y, z, (turn4(y, 1), z), (turn4(y, 3), z), (y, turn4(z, 1)), (y, turn4(z, 3))

    def own(self, src, dst, index):
        y, z, y_up, y_down, z_up, z_down = self.around()
        for to in (y_up, y_down, z_up, z_down):
            self.send(src, dst, self.sem(y, z, index), to)

    def near(self, parts=None):
        y, z, y_up, y_down, z_up, z_down = self.around()
        for at, far, turn, half, sides in (
            (y_down, y_up, 0, 0, (z_up, z_down)),
            (y_up, y_down, 1, 0, (z_up, z_down)),
            (z_down, z_up, 0, 2, (y_up, y_down)),
            (z_up, z_down, 1, 2, (y_up, y_down)),
        ):
            if parts is None:
                self.wait(*at, 0, 4, 0)
            else:
                for part, index in parts:
                    self.landed(part(*at), self.sem(*at, index))
            self.pass_on(*at, turn, 1, turn, far)
            self.pass_on(*at, 2 + turn, 1, 2 + turn, far)
            self.pass_on(*at, half, 2, half, *sides)

    def far(self):
        y, z, y_up, y_down, z_up, z_down = self.around()
        for at, half, sides in (
            ((turn4(y, 2), z), 0, (z_up, z_down)),
            ((y, turn4(z, 2)), 2, (y_up, y_down)),
        ):
            for index in range(4):
                self.wait(*at, index, 1, index)
            self.pass_on(*at, half, 2, half, *sides)

    def cross(self):
        y, z, y_up, y_down, z_up, z_down = self.around()
        for k in (1, 3, 2):
            row, column = turn4(y, k), turn4(z, k)
            self.wait(row, z_down[1], 0, 2, 0)
            self.pass_on(row, z_down[1], 0, 1, 0, z_up)
            self.wait(row, z_up[1], 0, 2, 0)
            self.pass_on(row, z_up[1], 1, 1, 1, z_down)
            self.wait(y_down[0], column, 2, 2, 2)
            self.pass_on(y_down[0], column, 2, 1, 2, y_up)
            self.wait(y_up[0], column, 2, 2, 2)
            self.pass_on(y_up[0], column, 3, 1, 3, y_down)

    def last(self):
        y, z = self.y, self.z
        for k in (1, 3, 2):
            row, column = turn4(y, k), turn4(z, k)
            for index in range(2):
                self.wait(row, turn4(z, 2), index, 1, index)
                self.wait(turn4(y, 2), column, 2 + index, 1, 2 + index)

    def finish(self):
        for copy in self.sent:
            copy.wait_send()


RING_SENDS = 36


def beside(step):
    me, y, xh, z = place()
    grp = lax.axis_index("grp")
    low = grp // 2
    side = lax.rem(xh + low + (0 if step == 1 else 1), 2)
    return {"grp": (1 - low) * 2 + lax.rem(grp, 2), "wide": flat(y, side, z)}


class Relay:
    def __init__(self, sources, stops, ends, ssem, rsem):
        self.sources, self.stops, self.ends, self.ssem, self.rsem = sources, stops, ends, ssem, rsem

    def copy(self, src, dst, at, step):
        return remote(src, dst, self.ssem.at[at], self.rsem.at[at], **beside(step))

    def legs(self, hop):
        for i, step in enumerate((1, 3)):
            src = self.sources[i] if hop == 0 else self.stops[i]
            dst = self.stops[i] if hop == 0 else self.ends[i]
            yield self.copy(src, dst, 2 * hop + i, step)

    def start(self):
        for copy in self.legs(0):
            copy.start()

    def forward(self):
        for first, second in zip(self.legs(0), self.legs(1)):
            first.wait_recv()
            second.start()

    def wait(self):
        for copy in self.legs(1):
            copy.wait_recv()

    def finish(self):
        for hop in (0, 1):
            for copy in self.legs(hop):
                copy.wait_send()


def look_up(got, table, hot, rows, slot_row):
    asked = got[:, slot_row, :].astype(F32)
    asked = jnp.concatenate([asked, jnp.zeros((128 - NW, 128), F32)], 0).T
    step = 8 * CAP
    for first in range(0, NW, 8):
        for d in range(8):
            column = asked[0:CAP, first + d : first + d + 1]
            lanes = lax.broadcasted_iota(jnp.int32, (CAP, SHARD), 1).astype(F32)
            hot[d * CAP : (d + 1) * CAP, :] = jnp.where(lanes == column, 1.0, 0.0).astype(BF)
        picked = lax.dot_general(
            hot[...], table[...], (((1,), (1,)), ((), ())), preferred_element_type=F32
        )
        rows[first * CAP : first * CAP + step, :] = picked.astype(BF)


def slots(at):
    return pl.ds(pl.multiple_of(at * CAP, CAP), CAP)


def turn_over(table, rows, first):
    for c in range(0, SHARD, 256):
        rows[first + c : first + c + 256, :] = table[:, c : c + 256].T


def owner_of(ids):
    return (((ids >> 9) * 171) >> 9).astype(jnp.int32)


def pack_rows(out, attn, ffn, proj):
    out[FFN_AT:DOWN_AT, :] = ffn
    out[DOWN_AT:ATTN_AT, :] = jnp.zeros((ATTN_AT - DOWN_AT, D), F32)
    for j in range(3):
        at = DOWN_AT + 18 * j
        out[at : at + 18, 0:512] = proj[:, D + 512 * j : D + 512 * (j + 1)]
    out[ATTN_AT : ATTN_AT + 30, :] = attn
    out[ATTN_AT + 30 : PACKED, :] = proj[:, 0:D]


def ask_rows(ids, targets, weight, msg, picks, slot_out):
    row = ids[0:1, :]
    column = jnp.broadcast_to(row.astype(F32), (128, T)).T[:, 0:1].astype(jnp.int32)
    row_owner, column_owner = owner_of(row), owner_of(column)
    down = lax.broadcasted_iota(jnp.int32, (T, T), 0)
    across = lax.broadcasted_iota(jnp.int32, (T, T), 1)
    same = row == column

    def count(which, axis):
        return jnp.sum(jnp.where(which, 1.0, 0.0), axis, keepdims=True)

    first_row = count(same & (down < across), 0) == 0.0
    first_column = count(same & (across < down), 1) == 0.0
    near = row_owner == column_owner
    rank_row = count(near & (column < row) & first_column, 0)
    rank_column = count(near & (row < column) & first_row, 1)
    slot_row = jnp.where(rank_row < CAP, row_owner.astype(F32) * CAP + rank_row, -1.0)
    slot_column = jnp.where(rank_column < CAP, column_owner.astype(F32) * CAP + rank_column, -1.0)
    lanes = lax.broadcasted_iota(jnp.int32, (T, NW * CAP), 1).astype(F32)
    hit = lanes == slot_column
    picks[...] = jnp.where(hit, 1.0, 0.0).astype(BF)
    slot_out[...] = jnp.broadcast_to(slot_row, (8, T)).astype(jnp.int32)
    local = (column - column_owner * SHARD).astype(F32)
    asked = jnp.max(jnp.where(hit, local, -1.0), 0, keepdims=True).astype(jnp.int32)
    most = (jnp.max(rank_row, 1, keepdims=True) + 1.0).astype(jnp.int32)
    rest = [
        targets[0:1, 0:128], targets[0:1, 128:256], weight[:, 0:128], jnp.broadcast_to(most, (1, 128)),
    ] + [jnp.zeros((1, 128), jnp.int32)] * 3
    for g in range(8):
        msg[g] = jnp.concatenate([asked[:, g * 128 : (g + 1) * 128]] + rest, 0)


def find_rows(got, table, asked_t, hot, rows, part):
    asked = got[:, 0, :].astype(F32)
    asked_t[...] = jnp.concatenate([asked, jnp.full((128 - NW, 128), -1.0, F32)], 0).T
    mine = asked_t[pl.ds(pl.multiple_of(part * CAP, CAP), CAP), :]
    lanes = lax.broadcasted_iota(jnp.int32, (CAP, SHARD), 1).astype(F32)
    for d in range(NW):
        hot[d * CAP : (d + 1) * CAP, :] = jnp.where(lanes == mine[:, d : d + 1], 1.0, 0.0).astype(BF)
    step = 16 * CAP
    for first in range(0, NW * CAP, step):
        picked = lax.dot_general(
            hot[first : first + step, :], table[...], (((1,), (1,)), ((), ())), preferred_element_type=F32
        )
        rows[first : first + step, :] = picked.astype(BF)


def turn_over(table, rows, first):
    for c in range(0, SHARD, 256):
        rows[first + c : first + c + 256, :] = table[:, c : c + 256].T


def front_kernel(
    ids, targets, counts, master, attn, ffn, proj,
    got, emb, most_out, table_out, other_out, rows_t_out, packed_all, picks, slot_out, hot_out, goal, weights,
    wide, table, table_other, rows_t, hot, long, packed, most, msg, asked_t, rows, own_most, stops, msg_s, msg_r, emb_s, emb_r, most_s, most_r, swap_s, swap_r,
    ring_s, ring_r, x_sem, local,
):
    me, y, xh, z = place()
    grp = lax.axis_index("grp")
    other = flat(y, 1 - xh, z)
    load = pltpu.make_async_copy(master, wide, local.at[1])
    load.start()
    by_source = lax.broadcasted_iota(jnp.int32, (1, 3), 1) + 1
    weight = jnp.sum((counts[...] * by_source).astype(F32), 1, keepdims=True)
    weight = jnp.broadcast_to(weight, (1, T)).astype(jnp.int32)

    def prepare():
        pack_rows(long, attn[:, 0, :], ffn[...], proj[:, 0, :])
        packed[...] = long[...].astype(BF)
        ask_rows(ids, targets, weight, msg, picks, slot_out)

    greet_wide(me, grp, sides=True, meanwhile=prepare)
    over = remote(packed, packed_all.at[y, z, xh], x_sem.at[0], x_sem.at[1], wide=other)
    over.start()
    ask = Scatter(lambda p: msg.at[p // 4], lambda p: got.at[p], msg_s, msg_r, me)
    ask.start()
    got[me] = msg[me // 4]
    ring = Ring(
        lambda Y, Z, first, count: packed_all.at[Y, Z, :, pl.ds(first, count)],
        lambda Y, Z, index: ring_r.at[Y, Z, index],
        (0, 48, 96, 144, 208),
        ring_s,
    )
    ring.own(packed, packed_all.at[y, z, xh], 0)
    keep = pltpu.make_async_copy(packed, packed_all.at[y, z, xh], local.at[0])
    keep.start()
    load.wait()
    table[...] = wide[...].astype(BF)
    saves = [pltpu.make_async_copy(table, table_out, local.at[1])]
    saves[0].start()
    halves = (pl.ds(0, D // 2), pl.ds(D // 2, D // 2))
    trade = Relay(
        [table.at[half] for half in halves],
        [stops.at[i] for i in range(2)],
        [table_other.at[half] for half in halves],
        swap_s,
        swap_r,
    )
    trade.start()
    over.wait_recv()
    ring.own(packed_all.at[y, z, 1 - xh], packed_all.at[y, z, 1 - xh], 4)
    ask.wait_recv()
    find_rows(got, table, asked_t, hot, rows, lax.rem(me, 4))
    saves.append(pltpu.make_async_copy(hot, hot_out, local.at[2]))
    saves[-1].start()
    ring.near(
        [
            (lambda Y, Z: packed_all.at[Y, Z, xh], 0),
            (lambda Y, Z: packed_all.at[Y, Z, 1 - xh], 4),
        ]
    )
    reply = Scatter(lambda p: rows.at[slots(p)], lambda p: emb.at[slots(p)], emb_s, emb_r, me)
    reply.start()
    emb[slots(me), :] = rows[slots(me), :]
    turn_over(table, rows_t, 0)
    saves.append(pltpu.make_async_copy(rows_t.at[0:SHARD], rows_t_out.at[0:SHARD], local.at[3]))
    saves[-1].start()
    largest = jnp.max(got[:, 4, :], 0, keepdims=True)
    own_most[...] = jnp.broadcast_to(largest, (8, 128))
    most[grp] = own_most[...]
    told = []
    for k in range(1, NG):
        to = lax.rem(grp + k, NG)
        told.append(remote(own_most, most.at[grp], most_s.at[k], most_r.at[grp], grp=to))
        told[-1].start()
    total = jnp.sum(got[:, 3, :].astype(F32), 0, keepdims=True)
    total = jnp.concatenate([total, total], 1) * T
    plain = weight.astype(F32)
    weights[...] = jnp.concatenate([plain / total, plain, total] + [jnp.zeros((1, T), F32)] * 5, 0)

    def place_goal(j, carry):
        from_dev = flat(j // 4, xh, lax.rem(j, 4))
        goals = jnp.concatenate([got[from_dev, 1:2, :], got[from_dev, 2:3, :]], 1)
        near, far = goals - me * SHARD, goals - other * SHARD
        at = jnp.where((far >= 0) & (far < SHARD), far + SHARD, -1)
        at = jnp.where((near >= 0) & (near < SHARD), near, at)
        goal[j] = jnp.broadcast_to(at, (8, T))
        return carry

    lax.fori_loop(0, 16, place_goal, 0)
    trade.forward()
    ring.far()
    ring.cross()
    reply.wait_recv()
    for k in range(1, NG):
        to = lax.rem(grp + k, NG)
        remote(own_most, most.at[to], most_s.at[k], most_r.at[to], grp=to).wait_recv()
    most_out[...] = jnp.maximum(jnp.maximum(most[0], most[1]), jnp.maximum(most[2], most[3]))
    trade.wait()
    saves.append(pltpu.make_async_copy(table_other, other_out, local.at[4]))
    saves[-1].start()
    turn_over(table_other, rows_t, SHARD)
    rest = pl.ds(SHARD, SHARD)
    saves.append(pltpu.make_async_copy(rows_t.at[rest], rows_t_out.at[rest], local.at[5]))
    saves[-1].start()
    ring.last()
    keep.wait()
    for save in saves:
        save.wait()
    over.wait_send()
    ask.wait_send()
    reply.wait_send()
    trade.finish()
    for copy in told:
        copy.wait_send()
    ring.finish()


def front(*args):
    return pl.pallas_call(
        front_kernel,
        name="front",
        out_shape=(
            jax.ShapeDtypeStruct((NW, 8, 128), jnp.int32),
            jax.ShapeDtypeStruct((NW * CAP, D), BF),
            jax.ShapeDtypeStruct((8, 128), jnp.int32),
            jax.ShapeDtypeStruct((D, SHARD), BF),
            jax.ShapeDtypeStruct((D, SHARD), BF),
            jax.ShapeDtypeStruct((2 * SHARD, D), BF),
            jax.ShapeDtypeStruct((4, 4, 2, PACKED, D), BF),
            jax.ShapeDtypeStruct((T, NW * CAP), BF),
            jax.ShapeDtypeStruct((8, T), jnp.int32),
            jax.ShapeDtypeStruct((NW * CAP, SHARD), BF),
            jax.ShapeDtypeStruct((16, 8, T), jnp.int32),
            jax.ShapeDtypeStruct((8, T), F32),
        ),
        in_specs=[VMEM, VMEM, VMEM, ANY, VMEM, VMEM, VMEM],
        out_specs=(VMEM, VMEM, VMEM, ANY, ANY, ANY, ANY, VMEM, VMEM, ANY, VMEM, VMEM),
        scratch_shapes=[
            pltpu.VMEM((D, SHARD), F32),
            pltpu.VMEM((D, SHARD), BF),
            pltpu.VMEM((D, SHARD), BF),
            pltpu.VMEM((2 * SHARD, D), BF),
            pltpu.VMEM((NW * CAP, SHARD), BF),
            pltpu.VMEM((PACKED, D), F32),
            pltpu.VMEM((PACKED, D), BF),
            pltpu.VMEM((NG, 8, 128), jnp.int32),
            pltpu.VMEM((8, 8, 128), jnp.int32),
            pltpu.VMEM((128, 128), F32),
            pltpu.VMEM((NW * CAP, D), BF),
            pltpu.VMEM((8, 128), jnp.int32),
            pltpu.VMEM((2, D // 2, SHARD), BF),
            DMA((NW,)),
            DMA((NW,)),
            DMA((NW,)),
            DMA((NW,)),
            DMA((NG,)),
            DMA((NG,)),
            DMA((4,)),
            DMA((4,)),
            DMA((RING_SENDS + 4,)),
            DMA((4, 4, 5)),
            DMA((2,)),
            DMA((6,)),
        ],
        compiler_params=params(1, 60),
        cost_estimate=pl.CostEstimate(flops=2 * 10**9, bytes_accessed=3 * 10**7, transcendentals=0),
    )(*args)


ORDER = tuple((i // 8) * 8 + (i % 2) * 4 + (i // 2) % 4 for i in range(NW))


def spread_rows(used, stride, at, repeat=1):
    picks = np.zeros((NW * stride, NW * used), np.float32)
    for i, w in enumerate(ORDER):
        for j in range(repeat):
            for r in range(used):
                picks[i * stride + at + j * used + r, w * used + r] = 1.0
    return picks


def rope():
    half = HD // 2
    freqs = np.float32(rope_base) ** (-(np.arange(half, dtype=np.float32) * np.float32(2.0)) / np.float32(HD))
    angles = freqs.astype(np.float32)[:, None] * np.arange(T, dtype=np.float32)[None, :]
    return np.concatenate([np.cos(angles), np.sin(angles)], 0).astype(np.float32)


def turned(values):
    return values.T


def gain_columns(gains):
    return jnp.concatenate([gains[:, 0, :], jnp.zeros((125, D), F32)], 0).T


def rms(values, gain):
    scale = lax.rsqrt(jnp.mean(values * values, 0, keepdims=True) + norm_eps)
    return values * scale * gain


def rms_back(values, gain, grad):
    scale = lax.rsqrt(jnp.mean(values * values, 0, keepdims=True) + norm_eps)
    pulled = grad * gain
    middle = jnp.mean(values * pulled, 0, keepdims=True)
    back = scale * pulled - values * (scale * scale * scale) * middle
    return back, jnp.sum(grad * values * scale, 1, keepdims=True)


def mask_of(tok):
    row = tok[0:1, :]
    column = jnp.broadcast_to(row.astype(F32), (128, T)).T[:, 0:1].astype(jnp.int32)
    down = lax.broadcasted_iota(jnp.int32, (T, T), 0)
    across = lax.broadcasted_iota(jnp.int32, (T, T), 1)
    return (down <= across) & (row == column)


def mm(a, b):
    return jnp.dot(a, b, preferred_element_type=F32)


def mm_nt(a, b):
    return lax.dot_general(a, b, (((1,), (1,)), ((), ())), preferred_element_type=F32)


def mm_tn(a, b):
    return lax.dot_general(a, b, (((0,), (0,)), ((), ())), preferred_element_type=F32)


def rotated(x, rot):
    cosine, sine = rot[0:32, :], rot[32:64, :]
    one, two = x[0:32, :], x[32:64, :]
    return jnp.concatenate([one * cosine - two * sine, two * cosine + one * sine], 0)


def unrotated(x, rot):
    cosine, sine = rot[0:32, :], rot[32:64, :]
    one, two = x[0:32, :], x[32:64, :]
    return jnp.concatenate([one * cosine + two * sine, two * cosine - one * sine], 0)


def load_trunk(packed, ffn, down, attn, sem):
    loads = [
        pltpu.make_async_copy(packed.at[:, :, :, ATTN_AT:PACKED], attn, sem.at[0]),
        pltpu.make_async_copy(packed.at[:, :, :, FFN_AT:DOWN_AT], ffn, sem.at[1]),
        pltpu.make_async_copy(packed.at[:, :, :, DOWN_AT:ATTN_AT, 0:512], down, sem.at[2]),
    ]
    for load in loads:
        load.start()
    return loads


TRUNK_SCRATCH = [
    pltpu.VMEM((4, 4, 2, 96, D), BF),
    pltpu.VMEM((4, 4, 2, 64, 512), BF),
    pltpu.VMEM((4, 4, 2, 48, D), BF),
    DMA((3,)),
]


def forward_kernel(
    more, emb, picks, packed, gains, rot, tok,
    final, h0, n1, q, k, v, lse, att, h1, n2, gate_up_out, inner, h2,
    ffn, down, attn, sem, mixed, gate_up, save_sem,
):
    loads = load_trunk(packed, ffn, down, attn, sem)
    columns = gain_columns(gains)
    allowed = mask_of(tok)
    start = turned(mm(picks[...], emb[...])) + more[...]
    h0[...] = start
    normed = rms(start, columns[:, 0:1]).astype(BF)
    n1[...] = normed
    loads[0].wait()
    rows48 = attn[...].reshape(NW * 48, D)
    product = mm(rows48, normed)
    for i, w in enumerate(ORDER):
        mixed[w * 30 : w * 30 + 30, :] = product[i * 48 : i * 48 + 30, :]
    for kv in range(KVH):
        k[kv * HD : (kv + 1) * HD, :] = rotated(
            mixed[D + kv * HD : D + (kv + 1) * HD, :], rot[...]
        ).astype(BF)
        at = D + (KVH + kv) * HD
        v[kv * HD : (kv + 1) * HD, :] = mixed[at : at + HD, :].astype(BF)
    logs = []
    for h in range(H):
        kv = h // (H // KVH)
        query = rotated(mixed[h * HD : (h + 1) * HD, :], rot[...]).astype(BF)
        q[h * HD : (h + 1) * HD, :] = query
        scores = mm_tn(k[kv * HD : (kv + 1) * HD, :], query) * HD ** (-0.5)
        scores = jnp.where(allowed, scores, masked_score)
        top = jnp.max(scores, 0, keepdims=True)
        power = jnp.exp(scores - top)
        total = jnp.sum(power, 0, keepdims=True)
        probs = (power / total).astype(BF)
        att[h * HD : (h + 1) * HD, :] = mm(v[kv * HD : (kv + 1) * HD, :], probs).astype(BF)
        logs.append(top + jnp.log(total))
    lse[...] = jnp.concatenate(logs + [jnp.zeros((16 - H, T), F32)], 0)
    product = mm(rows48, att[...])
    for i, w in enumerate(ORDER):
        mixed[w * 18 : w * 18 + 18, :] = product[i * 48 + 30 : i * 48 + 48, :]
    middle = start + mixed[0:D, :]
    h1[...] = middle
    normed = rms(middle, columns[:, 1:2]).astype(BF)
    n2[...] = normed
    loads[1].wait()
    gate_up[...] = mm(ffn[...].reshape(NW * 96, D), normed)
    save = pltpu.make_async_copy(gate_up, gate_up_out, save_sem.at[0])
    save.start()
    for i in range(NW // 2):
        gate = gate_up[i * 96 : (i + 1) * 96, :]
        up = gate_up[FF + i * 96 : FF + (i + 1) * 96, :]
        w = ORDER[i]
        inner[w * 96 : (w + 1) * 96, :] = (gate / (1.0 + jnp.exp(-gate)) * up).astype(BF)
    loads[2].wait()
    rows64 = down[...].reshape(NW * 64, 512)
    for j in range(3):
        product = mm(rows64, inner[j * 512 : (j + 1) * 512, :])
        for i, w in enumerate(ORDER):
            piece = product[i * 64 + j * 18 : i * 64 + j * 18 + 18, :]
            if j:
                mixed[w * 18 : w * 18 + 18, :] += piece
            else:
                mixed[w * 18 : w * 18 + 18, :] = piece
    last = middle + mixed[0:D, :]
    h2[...] = last
    final[...] = rms(last, columns[:, 2:3]).astype(BF)
    save.wait()


def forward(more, emb, picks, packed, gains, rot, tok):
    def out(rows, kind):
        return jax.ShapeDtypeStruct((rows, T), kind)

    return pl.pallas_call(
        forward_kernel,
        name="forward",
        out_shape=(
            out(D, BF), out(D, F32), out(D, BF), out(D, BF), out(KVH * HD, BF), out(KVH * HD, BF), out(16, F32),
            out(D, BF), out(D, F32), out(D, BF), out(2 * FF, F32), out(FF, BF), out(D, F32),
        ),
        in_specs=[VMEM, VMEM, VMEM, ANY, VMEM, VMEM, VMEM],
        out_specs=(VMEM,) * 10 + (ANY, VMEM, VMEM),
        scratch_shapes=TRUNK_SCRATCH
        + [pltpu.VMEM((QKV, T), F32), pltpu.VMEM((2 * FF, T), F32), DMA((1,))],
        compiler_params=pltpu.CompilerParams(vmem_limit_bytes=60 * MIB),
        cost_estimate=pl.CostEstimate(flops=4 * 10**9, bytes_accessed=2 * 10**7, transcendentals=10**6),
    )(more, emb, picks, packed, gains, rot, tok)


def more_rows_kernel(msg, table, got, emb, hot, rows, msg_s, msg_r, emb_s, emb_r):
    me = lax.axis_index("wide")
    greet_wide(me)
    ask = Scatter(lambda p: msg.at[p], lambda p: got.at[p], msg_s, msg_r, me)
    ask.start()
    got[me] = msg[me]
    ask.wait_recv()
    look_up(got, table, hot, rows, 0)
    reply = Scatter(lambda p: rows.at[slots(p)], lambda p: emb.at[slots(p)], emb_s, emb_r, me)
    reply.start()
    emb[slots(me), :] = rows[slots(me), :]
    reply.wait_recv()
    ask.wait_send()
    reply.wait_send()


def more_rows(msg, table):
    return pl.pallas_call(
        more_rows_kernel,
        name="more_rows",
        out_shape=(
            jax.ShapeDtypeStruct((NW, 8, 128), jnp.int32),
            jax.ShapeDtypeStruct((NW * CAP, D), BF),
        ),
        in_specs=[VMEM, VMEM],
        out_specs=(VMEM, VMEM),
        scratch_shapes=[pltpu.VMEM((8 * CAP, SHARD), BF), pltpu.VMEM((NW * CAP, D), BF)]
        + [DMA((NW,))] * 4,
        compiler_params=params(2, 40),
    )(msg, table)[1]


def more_grads_kernel(msg, rows, got, out, msg_s, msg_r, row_s, row_r):
    me = lax.axis_index("wide")
    greet_wide(me)
    ask = Scatter(lambda p: msg.at[p], lambda p: got.at[p], msg_s, msg_r, me)
    ask.start()
    give = Scatter(lambda p: rows.at[slots(p)], lambda p: out.at[slots(p)], row_s, row_r, me)
    give.start()
    got[me] = msg[me]
    out[slots(me), :] = rows[slots(me), :]
    ask.wait_recv()
    give.wait_recv()
    ask.wait_send()
    give.wait_send()


def more_grads(msg, rows):
    return pl.pallas_call(
        more_grads_kernel,
        name="more_grads",
        out_shape=(
            jax.ShapeDtypeStruct((NW, 8, 128), jnp.int32),
            jax.ShapeDtypeStruct((NW * CAP, D), BF),
        ),
        in_specs=[VMEM, VMEM],
        out_specs=(VMEM, VMEM),
        scratch_shapes=[DMA((NW,))] * 4,
        compiler_params=params(3, 20),
    )(msg, rows)


VOC = 2 * SHARD
TOK = 16 * T
CH = 128
GROUPS = CH // 8
NCH = VOC // CH
QUART = D // 4


def cols(j):
    return pl.ds(pl.multiple_of(j * T, T), T)


def head_kernel(
    final, rows_t, table_in, table_other_in, goal, weights,
    grad_final, head_out, head_other, loss,
    table, table_other, head_own, big, fall, expo, tops, stat, stat_in, coef, coef_in, parts,
    part_a, part_b, whole_a, whole_b, sum_a, sum_b, part_a2, part_b2, whole_a2, whole_b2,
    g_s, g_r, st_s, st_r, co_s, co_r, a_s, b_s, pa_r, pb_r, wa_r, wb_r, a2_s, b2_s, a2_r, b2_r,
):
    me, y, xh, z = place()
    mine = y * 4 + z
    tables = [
        pltpu.make_async_copy(table_in, table, big.at[0]),
        pltpu.make_async_copy(table_other_in, table_other, big.at[1]),
    ]
    for load in tables:
        load.start()

    def dev(j):
        return flat(j // 4, xh, lax.rem(j, 4))

    barrier = pltpu.get_barrier_semaphore()

    def greet(k, carry):
        pl.semaphore_signal(
            barrier, inc=1, device_id={"wide": dev(lax.rem(mine + k, 16))}, device_id_type=MESH
        )
        return carry

    lax.fori_loop(1, 16, greet, 0)
    pl.semaphore_wait(barrier, 15)

    sent = []

    def send(src, dst, ssem, rsem, to):
        copy = remote(src, dst, ssem, rsem, wide=to)
        copy.start()
        sent.append(copy)

    def arrived(dst, rsem):
        remote(dst, dst, g_s.at[0], rsem, wide=dev(mine)).wait_recv()

    ring = Ring(
        lambda Y, Z, first, count: fall.at[pl.ds(first, count), cols(Y * 4 + Z)],
        lambda Y, Z, index: g_r.at[Y * 4 + Z, index],
        tuple(QUART * k for k in range(5)),
        g_s,
    )
    ring.own(final, fall.at[:, cols(mine)], 0)
    fall[:, cols(mine)] = final[...]

    def logits(j):
        seen = fall[:, cols(j)]
        goals = goal[j]
        group, hit = goals >> 3, jnp.zeros((8, T), F32)
        best = total = None
        for c in range(NCH):
            part = mm(rows_t[c * CH : (c + 1) * CH, :], seen).reshape(GROUPS, 8, T)
            top = jnp.max(part, 0)
            power = jnp.exp(part - top[None])
            for r in range(GROUPS):
                hit = jnp.where(group == c * GROUPS + r, part[r], hit)
            expo[c * CH : (c + 1) * CH, cols(j)] = power.reshape(CH, T).astype(BF)
            tops[j, c] = top
            weight = jnp.sum(power, 0)
            if c:
                higher = jnp.maximum(best, top)
                total = total * jnp.exp(best - higher) + weight * jnp.exp(top - higher)
                best = higher
            else:
                best, total = top, weight
        spot = lax.broadcasted_iota(jnp.int32, (8, T), 0)
        hit = jnp.sum(jnp.where(spot == (goals & 7), hit, 0.0), 0, keepdims=True)
        top = jnp.max(best, 0, keepdims=True)
        total = jnp.sum(total * jnp.exp(best - top), 0, keepdims=True)
        zero = jnp.zeros((1, T), F32)
        stat[j] = jnp.concatenate([top, total, hit] + [zero] * 5, 0)

    def tell(j):
        return remote(stat.at[j], stat_in.at[mine], st_s.at[j], st_r.at[mine], wide=dev(j))

    def block(dy, dz):
        return turn4(y, dy) * 4 + turn4(z, dz)

    def forward(offsets):
        def one(k, carry):
            j = block(*offsets(k))
            logits(j)
            tell(j).start()
            return carry

        return one

    def odd(k):
        return 1 + 2 * lax.rem(k, 2)

    logits(mine)
    stat_in[mine] = stat[mine]
    ring.near()
    lax.fori_loop(0, 4, forward(lambda k: ((1 - k // 2) * odd(k), (k // 2) * odd(k))), 0)
    ring.far()
    lax.fori_loop(0, 2, forward(lambda k: (2 * (1 - k), 2 * k)), 0)
    ring.cross()
    lax.fori_loop(0, 4, forward(lambda k: (odd(k // 2), odd(k))), 0)
    ring.last()
    lax.fori_loop(
        0,
        4,
        forward(lambda k: (2 * (1 - k // 2) + odd(k) * (k // 2), odd(k) * (1 - k // 2) + 2 * (k // 2))),
        0,
    )
    forward(lambda k: (2, 2))(0, 0)

    def hear(k, carry):
        j = lax.rem(mine + k, 16)
        arrived(stat_in.at[j], st_r.at[j])
        return carry

    lax.fori_loop(1, 16, hear, 0)
    tip, weight, hit = stat_in[:, 0, :], stat_in[:, 1, :], stat_in[:, 2, :]
    top = jnp.max(tip, 0, keepdims=True)
    lse = top + jnp.log(jnp.sum(weight * jnp.exp(tip - top), 0, keepdims=True))
    picked = jnp.sum(hit, 0, keepdims=True)
    share, plain = weights[0:1, :], weights[1:2, :]
    zero = jnp.zeros((1, T), F32)
    coef[...] = jnp.concatenate(
        [lse, share * (1.0 + 2.0 * penalty_weight * lse), share] + [zero] * 5, 0
    )
    loss[...] = jnp.concatenate(
        [plain * (lse - picked + penalty_weight * lse * lse)] + [zero] * 7, 0
    )
    coef_in[mine] = coef[...]

    def spread(k):
        j = lax.rem(mine + k, 16)
        return remote(coef, coef_in.at[mine], co_s.at[k], co_r.at[mine], wide=dev(j))

    def spread_start(k, carry):
        spread(k).start()
        return carry

    lax.fori_loop(1, 16, spread_start, 0)

    up, down = 1, 3
    z_to = {step: flat(y, xh, turn4(z, step)) for step in (up, down)}
    y_to = {step: flat(turn4(y, step), xh, z) for step in (up, down)}

    def piece_a(j, index):
        row = j // 4
        return remote(
            parts.at[j, pl.ds(index * QUART, QUART)], part_a.at[index, row],
            a_s.at[j, index], pa_r.at[index, row], wide=z_to[(up, down)[index]],
        )

    def piece_b(j, index):
        column = lax.rem(j, 4)
        return remote(
            parts.at[j, pl.ds((2 + index) * QUART, QUART)], part_b.at[index, column],
            b_s.at[j, index], pb_r.at[index, column], wide=y_to[(up, down)[index]],
        )

    def half_a(j, index):
        row = j // 4
        return remote(
            parts.at[j, pl.ds(0, 2 * QUART)], whole_a.at[index, row],
            a_s.at[j, 0], wa_r.at[index, row], wide=z_to[(up, down)[index]],
        )

    def half_b(j, index):
        column = lax.rem(j, 4)
        return remote(
            parts.at[j, pl.ds(2 * QUART, 2 * QUART)], whole_b.at[index, column],
            b_s.at[j, 0], wb_r.at[index, column], wide=y_to[(up, down)[index]],
        )

    def offsets(k):
        return lax.rem(2 + k // 4, 4), lax.rem(2 + k, 4)

    def post(k):
        dy, dz = offsets(k)
        j = block(dy, dz)

        @pl.when(dz == 2)
        def _():
            piece_a(j, 0).start()
            piece_a(j, 1).start()

        @pl.when(dy == 2)
        def _():
            piece_b(j, 0).start()
            piece_b(j, 1).start()

        for index, step in enumerate((up, down)):

            @pl.when(dz == step)
            def _():
                row = j // 4
                arrived(part_a.at[index, row], pa_r.at[index, row])
                rows = pl.ds(index * QUART, QUART)
                total = parts[j, rows, :].astype(F32) + part_a[index, row].astype(F32)
                parts[j, rows, :] = total.astype(BF)
                half_a(j, index).start()

            @pl.when(dy == step)
            def _():
                column = lax.rem(j, 4)
                arrived(part_b.at[index, column], pb_r.at[index, column])
                rows = pl.ds((2 + index) * QUART, QUART)
                total = parts[j, rows, :].astype(F32) + part_b[index, column].astype(F32)
                parts[j, rows, :] = total.astype(BF)
                half_b(j, index).start()

    def backward(k, carry):
        j = block(*offsets(k))

        @pl.when(k != 10)
        def _():
            arrived(coef_in.at[j], co_r.at[j])

        lse, soft, pick = coef_in[j, 0:1, :], coef_in[j, 1:2, :], coef_in[j, 2:3, :]
        goals = goal[j]
        group = goals >> 3
        pick = jnp.where(lax.broadcasted_iota(jnp.int32, (8, T), 0) == (goals & 7), pick, 0.0)
        for c in range(NCH):
            scale = soft * jnp.exp(tops[j, c] - lse)
            power = expo[c * CH : (c + 1) * CH, cols(j)].astype(F32).reshape(GROUPS, 8, T)
            spot = lax.broadcasted_iota(jnp.int32, (GROUPS, 8, T), 0) + c * GROUPS
            drop = jnp.where(spot == group[None], pick[None], 0.0)
            grad = (power * scale[None] - drop).reshape(CH, T)
            expo[c * CH : (c + 1) * CH, cols(j)] = grad.astype(BF)
        for at in range(0, D, QUART):
            product = mm(table[at : at + QUART, :], expo[0:SHARD, cols(j)])
            product += mm(table_other[at : at + QUART, :], expo[SHARD:VOC, cols(j)])
            parts[j, at : at + QUART, :] = product.astype(BF)

        @pl.when(k > 0)
        def _():
            post(k - 1)

        return carry

    for load in tables:
        load.wait()
    lax.fori_loop(0, 16, backward, 0)
    post(15)

    def head_chunk(c):
        return lax.dot_general(
            fall[...],
            expo[pl.ds(pl.multiple_of(c * 256, 256), 256), :],
            (((1,), (1,)), ((), ())),
            preferred_element_type=F32,
        )

    def other_chunk(c, carry):
        head_other[:, cols(c)] = head_chunk(c + SHARD // 256).astype(BF)
        return carry

    def own_chunk(c, carry):
        head_own[:, cols(c)] = head_chunk(c)
        return carry

    lax.fori_loop(0, SHARD // 256, other_chunk, 0)

    kinds = (
        (whole_a, wa_r, sum_a, part_a2, whole_a2, a2_s, a2_r, y_to, 0),
        (whole_b, wb_r, sum_b, part_b2, whole_b2, b2_s, b2_r, z_to, 2 * QUART),
    )
    for d in (2, 1, 3, 0):
        for kind, (whole, w_r, total, part2, whole2, s2, r2, to, base) in enumerate(kinds):
            at = turn4(y if kind == 0 else z, d)
            j = at * 4 + z if kind == 0 else y * 4 + at
            acc = parts[j, base : base + 2 * QUART, :].astype(F32)
            for index in range(2):
                arrived(whole.at[index, at], w_r.at[index, at])
                acc = acc + whole[index, at].astype(F32)
            if d == 0:
                grad_final[base : base + 2 * QUART, :] = acc
            else:
                total[d - 1] = acc.astype(BF)
            if d == 2:
                for index, step in enumerate((up, down)):
                    piece = total.at[1, pl.ds(index * QUART, QUART)]
                    send(piece, part2.at[index], s2.at[index], r2.at[index], to[step])
    lax.fori_loop(0, SHARD // 512, own_chunk, 0)
    for kind, (whole, w_r, total, part2, whole2, s2, r2, to, base) in enumerate(kinds):
        for index, step in enumerate((up, down)):
            arrived(part2.at[index], r2.at[index])
            rows = pl.ds(index * QUART, QUART)
            added = total[step - 1, rows, :].astype(F32) + part2[index].astype(F32)
            total[step - 1, rows, :] = added.astype(BF)
            send(total.at[step - 1], whole2.at[index], s2.at[2 + index], r2.at[2 + index], to[step])
    lax.fori_loop(SHARD // 512, SHARD // 256, own_chunk, 0)
    store = pltpu.make_async_copy(head_own, head_out, big.at[0])
    store.start()
    for kind, (whole, w_r, total, part2, whole2, s2, r2, to, base) in enumerate(kinds):
        for index in range(2):
            arrived(whole2.at[index], r2.at[2 + index])
        grad_final[base : base + 2 * QUART, :] += whole2[0].astype(F32) + whole2[1].astype(F32)

    def finish(k, carry):
        j = lax.rem(mine + k, 16)
        tell(j).wait_send()
        spread(k).wait_send()
        return carry

    lax.fori_loop(1, 16, finish, 0)
    for copy in sent:
        copy.wait_send()
    ring.finish()

    def finish_pieces(k, carry):
        row, column = block(k, 2), block(2, k)
        piece_a(row, 0).wait_send()
        piece_a(row, 1).wait_send()
        piece_b(column, 0).wait_send()
        piece_b(column, 1).wait_send()
        for index, step in enumerate((up, down)):
            half_a(block(k, step), index).wait_send()
            half_b(block(step, k), index).wait_send()
        return carry

    lax.fori_loop(0, 4, finish_pieces, 0)
    store.wait()


def head(final, rows_t, table, table_other, goal, weights):
    return pl.pallas_call(
        head_kernel,
        name="head",
        out_shape=(
            jax.ShapeDtypeStruct((D, T), F32),
            jax.ShapeDtypeStruct((D, SHARD), F32),
            jax.ShapeDtypeStruct((D, SHARD), BF),
            jax.ShapeDtypeStruct((8, T), F32),
        ),
        in_specs=[VMEM, VMEM, ANY, ANY, VMEM, VMEM],
        out_specs=(VMEM, ANY, VMEM, VMEM),
        scratch_shapes=[
            pltpu.VMEM((D, SHARD), BF),
            pltpu.VMEM((D, SHARD), BF),
            pltpu.VMEM((D, SHARD), F32),
            DMA((2,)),
            pltpu.VMEM((D, TOK), BF),
            pltpu.VMEM((VOC, TOK), BF),
            pltpu.VMEM((16, NCH, 8, T), F32),
            pltpu.VMEM((16, 8, T), F32),
            pltpu.VMEM((16, 8, T), F32),
            pltpu.VMEM((8, T), F32),
            pltpu.VMEM((16, 8, T), F32),
            pltpu.VMEM((16, D, T), BF),
            pltpu.VMEM((2, 4, QUART, T), BF),
            pltpu.VMEM((2, 4, QUART, T), BF),
            pltpu.VMEM((2, 4, 2 * QUART, T), BF),
            pltpu.VMEM((2, 4, 2 * QUART, T), BF),
            pltpu.VMEM((3, 2 * QUART, T), BF),
            pltpu.VMEM((3, 2 * QUART, T), BF),
            pltpu.VMEM((2, QUART, T), BF),
            pltpu.VMEM((2, QUART, T), BF),
            pltpu.VMEM((2, 2 * QUART, T), BF),
            pltpu.VMEM((2, 2 * QUART, T), BF),
            DMA((RING_SENDS,)),
            DMA((16, 4)),
            DMA((16,)),
            DMA((16,)),
            DMA((16,)),
            DMA((16,)),
            DMA((16, 2)),
            DMA((16, 2)),
            DMA((2, 4)),
            DMA((2, 4)),
            DMA((2, 4)),
            DMA((2, 4)),
            DMA((4,)),
            DMA((4,)),
            DMA((4,)),
            DMA((4,)),
        ],
        compiler_params=params(4, 61),
        cost_estimate=pl.CostEstimate(
            flops=6 * VOC * TOK * D, bytes_accessed=2 * 10**7, transcendentals=VOC * TOK
        ),
    )(final, rows_t, table, table_other, goal, weights)


class Reduce:
    def __init__(self, parts, base, sizes, along_z, refs):
        (
            self.first, part_a, part_b, self.whole1, self.second, next_a, next_b, self.whole2,
            self.third, self.stop, self.third_in, self.s, self.r,
        ) = refs
        self.part1, self.part2 = (part_a, part_b), (next_a, next_b)
        self.parts, self.base, self.sizes, self.along_z = parts, base, sizes, along_z
        self.rows = (pl.ds(0, sizes[0]), pl.ds(sizes[0], sizes[1]), pl.ds(0, sum(sizes)))
        self.me, self.y, self.xh, self.z = place()
        self.sent = []

    def send(self, src, dst, at, **to):
        copy = remote(src, dst, self.s.at[at], self.r.at[at], **to)
        copy.start()
        self.sent.append(copy)

    def wait(self, dst, at):
        remote(dst, dst, self.s.at[at], self.r.at[at], wide=self.me).wait_recv()

    def item1(self, step, which):
        rows = pl.ds(self.base + self.rows[which].start, self.rows[which].size)
        if self.along_z:
            return (slice(None), turn4(self.z, step), slice(None), rows)
        return (turn4(self.y, step), slice(None), slice(None), rows)

    def item2(self, step, which):
        return (turn4(self.y if self.along_z else self.z, step), slice(None), self.rows[which])

    def to(self, stage, step):
        if self.along_z == (stage == 1):
            return flat(self.y, self.xh, turn4(self.z, step))
        return flat(turn4(self.y, step), self.xh, self.z)

    def split(self, stage, ref, item, part, base):
        for index, step in enumerate((1, 3)):
            self.send(ref.at[item(2, index)], part[index], base + index, wide=self.to(stage, step))

    def join(self, stage, ref, item, part, whole, base):
        for index, step in enumerate((1, 3)):
            self.wait(part[index], base + index)
            at = item(step, index)
            ref[at] = (ref[at].astype(F32) + part[index][...].astype(F32)).astype(BF)
            self.send(ref.at[item(step, 2)], whole.at[index], base + 2 + index, wide=self.to(stage, step))

    def add(self, ref, item, whole, base):
        acc = ref[item(0, 2)].astype(F32)
        for index in range(2):
            self.wait(whole.at[index], base + 2 + index)
            acc = acc + whole[index].astype(F32)
        return acc

    def one(self):
        self.split(1, self.parts, self.item1, self.part1, 0)

    def two(self):
        self.join(1, self.parts, self.item1, self.part1, self.whole1, 0)

    def three(self):
        self.first[...] = self.add(self.parts, self.item1, self.whole1, 0).astype(BF)
        self.split(2, self.first, self.item2, self.part2, 4)

    def four(self):
        self.join(2, self.first, self.item2, self.part2, self.whole2, 4)

    def five(self):
        self.second[...] = self.add(self.first, self.item2, self.whole2, 4)
        self.third[...] = self.second[1 - self.xh].astype(BF)
        self.send(self.third, self.stop, 8, **beside(1 if self.along_z else 3))

    def six(self):
        self.wait(self.stop, 8)
        self.send(self.stop, self.third_in, 9, **beside(1 if self.along_z else 3))

    def total(self):
        self.wait(self.third_in, 9)
        return self.second[self.xh] + self.third_in[...].astype(F32)

    def finish(self):
        for copy in self.sent:
            copy.wait_send()


STREAMS = ((0, (48, 32), True), (80, (48, 32), False), (160, (16, 16), True), (192, (16, 16), False))


def reduce_scratch():
    shapes = []
    for _, sizes, _ in STREAMS:
        half = sum(sizes)
        shapes += [
            pltpu.VMEM((4, 2, half, D), BF),
            pltpu.VMEM((4, 2, sizes[0], D), BF),
            pltpu.VMEM((4, 2, sizes[1], D), BF),
            pltpu.VMEM((2, 4, 2, half, D), BF),
            pltpu.VMEM((2, half, D), F32),
            pltpu.VMEM((2, sizes[0], D), BF),
            pltpu.VMEM((2, sizes[1], D), BF),
            pltpu.VMEM((2, 2, half, D), BF),
            pltpu.VMEM((half, D), BF),
            pltpu.VMEM((half, D), BF),
            pltpu.VMEM((half, D), BF),
            DMA((10,)),
            DMA((10,)),
        ]
    return shapes


def back_kernel(
    grad_final, h0, n1, q, k, v, lse, att, h1, n2, gate_up_in, inner, h2,
    packed, gains, rot, tok, slot_row, loss, head_other, lay_attn_in, lay_out_in, lay_down_in,
    summed, rows_in, head_in, extra_sum, grad_embedded,
    ffn, down, attn, sem, lay_attn, lay_out, lay_down, lay_sem, gate_up, parts, rows, grad_up, grad_mixed, spread, stops,
    row_s, row_r, swap_s, swap_r, hold, land_z, land_y, land_x, tree_s, tree_r, *reducers,
):
    me, y, xh, z = place()
    lays = [
        pltpu.make_async_copy(src, dst, lay_sem.at[i])
        for i, (src, dst) in enumerate(
            ((lay_down_in, lay_down), (lay_out_in, lay_out), (lay_attn_in, lay_attn))
        )
    ]
    lays.append(pltpu.make_async_copy(gate_up_in, gate_up, lay_sem.at[3]))
    lays[0].start()
    lays[3].start()
    loads = load_trunk(packed, ffn, down, attn, sem)
    lays[1].start()
    lays[2].start()
    columns = gain_columns(gains)
    begun = []

    def begin():
        begun.extend(rms_back(h2[...], columns[:, 2:3], grad_final[...]))
        lays[0].wait()
        spread[...] = mm(lay_down[...], begun[0].astype(BF)).astype(BF)

    greet_wide(me, sides=True, meanwhile=begin)
    grad_h2, gain3 = begun
    halves = (pl.ds(0, D // 2), pl.ds(D // 2, D // 2))
    trade = Relay(
        [head_other.at[half] for half in halves],
        [stops.at[i] for i in range(2)],
        [head_in.at[half] for half in halves],
        swap_s,
        swap_r,
    )
    trade.start()
    streams = [
        Reduce(parts, base, sizes, along, reducers[13 * i : 13 * i + 13])
        for i, (base, sizes, along) in enumerate(STREAMS)
    ]
    early, late = streams[:2], streams[2:]
    chunk = lax.broadcasted_iota(jnp.int32, (NW * 64, T), 0) & 63
    zero = jnp.zeros((NW * 64, T), BF)
    wide = jnp.concatenate(
        [
            jnp.where((chunk >= 18 * j) & (chunk < 18 * (j + 1)), spread[...].astype(F32), 0.0).astype(BF)
            for j in range(3)
        ],
        1,
    )
    inners = jnp.concatenate([inner[j * 512 : (j + 1) * 512, :] for j in range(3)], 1)
    grad_down = mm_nt(wide, inners).astype(BF).reshape(4, 4, 2, 64, 512)
    parts[:, :, :, DOWN_AT:ATTN_AT, 0:512] = grad_down
    parts[:, :, :, DOWN_AT:ATTN_AT, 512:D] = jnp.zeros((4, 4, 2, 64, D - 512), BF)
    loads[2].wait()
    grad_inner = mm_tn(down[...].reshape(NW * 64, 512), wide)
    lays[3].wait()
    for i in range(NW // 2):
        w = ORDER[i]
        gate = gate_up[i * 96 : (i + 1) * 96, :]
        up = gate_up[FF + i * 96 : FF + (i + 1) * 96, :]
        pieces = []
        for at in range(w * 96, w * 96 + 96, 32):
            j, r = at // 512, at % 512
            pieces.append(grad_inner[r : r + 32, j * T : (j + 1) * T])
        grad = jnp.concatenate(pieces, 0)
        sigmoid = 1.0 / (1.0 + jnp.exp(-gate))
        slope = sigmoid * (1.0 + gate * (1.0 - sigmoid))
        grad_up[i * 96 : (i + 1) * 96, :] = (grad * up * slope).astype(BF)
        grad_up[FF + i * 96 : FF + (i + 1) * 96, :] = (grad * (gate * sigmoid)).astype(BF)
    parts[:, :, :, FFN_AT:DOWN_AT, :] = mm_nt(grad_up[...], n2[...]).astype(BF).reshape(4, 4, 2, 96, D)
    for stream in early:
        stream.one()
    loads[1].wait()
    grad_normed = turned(mm_tn(grad_up[...], ffn[...].reshape(NW * 96, D)))
    part, gain2 = rms_back(h1[...], columns[:, 1:2], grad_normed)
    grad_h1 = grad_h2 + part
    lays[1].wait()
    out_rows = mm(lay_out[...], grad_h1.astype(BF)).astype(BF)
    loads[0].wait()
    rows48 = attn[...].reshape(NW * 48, D)
    grad_att = turned(mm_tn(out_rows, rows48)).astype(BF)
    for stream in early:
        stream.two()
    trade.forward()

    allowed = mask_of(tok)
    group = H // KVH
    for kv in range(KVH):
        keys = k[kv * HD : (kv + 1) * HD, :]
        values = v[kv * HD : (kv + 1) * HD, :]
        grad_k, grad_v = jnp.zeros((HD, T), F32), jnp.zeros((HD, T), F32)
        for h in range(kv * group, (kv + 1) * group):
            query = q[h * HD : (h + 1) * HD, :]
            grad_out = grad_att[h * HD : (h + 1) * HD, :]
            scores = mm_tn(keys, query) * HD ** (-0.5)
            scores = jnp.where(allowed, scores, masked_score)
            soft = jnp.exp(scores - lse[h : h + 1, :])
            grad_probs = mm_tn(values, grad_out)
            mean = jnp.sum(soft * grad_probs, 0, keepdims=True)
            grad_scores = (soft * (grad_probs - mean)).astype(BF)
            grad_q = mm(keys, grad_scores) * HD ** (-0.5)
            grad_mixed[h * HD : (h + 1) * HD, :] = unrotated(grad_q, rot[...]).astype(BF)
            grad_k = grad_k + mm_nt(query, grad_scores) * HD ** (-0.5)
            grad_v = grad_v + mm_nt(grad_out, soft.astype(BF))
        at = D + kv * HD
        grad_mixed[at : at + HD, :] = unrotated(grad_k, rot[...]).astype(BF)
        at = D + (KVH + kv) * HD
        grad_mixed[at : at + HD, :] = grad_v.astype(BF)
    for stream in early:
        stream.three()
    lays[2].wait()
    attn_rows = mm(lay_attn[...], grad_mixed[...]).astype(BF)
    both = jnp.concatenate([attn_rows, out_rows], 1)
    seen = jnp.concatenate([n1[...], att[...]], 1)
    parts[:, :, :, ATTN_AT:PACKED, :] = mm_nt(both, seen).astype(BF).reshape(4, 4, 2, 48, D)
    parts[:, :, :, PACKED:SUMMED, :] = jnp.zeros((4, 4, 2, SUMMED - PACKED, D), BF)
    for stream in late:
        stream.one()
    grad_normed = turned(mm_tn(attn_rows, rows48))
    part, gain1 = rms_back(h0[...], columns[:, 0:1], grad_normed)
    grad_h0 = (grad_h1 + part).astype(BF)
    grad_embedded[...] = grad_h0
    slot = lax.broadcasted_iota(jnp.int32, (NW * CAP, T), 0)
    picks = jnp.where(slot == slot_row[0:1, :], 1.0, 0.0).astype(BF)
    rows[...] = mm_nt(picks, grad_h0).astype(BF)
    for stream in early:
        stream.four()
    lane = lax.broadcasted_iota(jnp.int32, (D, 128), 1)
    table = jnp.where(lane == 0, gain1, jnp.where(lane == 1, gain2, jnp.where(lane == 2, gain3, 0.0)))
    lost = jnp.sum(loss[0:1, :], 1, keepdims=True)
    table = table.T[0:8, :]
    tree = Tree(hold, land_z, land_y, land_x, tree_s, tree_r)
    tree.start(jnp.where(lax.broadcasted_iota(jnp.int32, (8, D), 0) == 3, lost, table))
    rows_in[slots(me), :] = rows[slots(me), :]
    for stream in late:
        stream.two()
    give = Scatter(lambda p: rows.at[slots(p)], lambda p: rows_in.at[slots(p)], row_s, row_r, me)
    give.start()
    for stream in early:
        stream.five()
    tree.next(0)
    for stream in late:
        stream.three()
    for stream in late:
        stream.four()
    tree.next(1)
    for stream in early:
        stream.six()
    for stream in late:
        stream.five()
    extra_sum[...] = tree.collect(2)
    for stream in late:
        stream.six()
    for stream in streams:
        summed[stream.base : stream.base + sum(stream.sizes), :] = stream.total()
    give.wait_recv()
    trade.wait()
    for stream in streams:
        stream.finish()
    give.wait_send()
    tree.finish()
    trade.finish()


def back(grad_final, kept, packed, gains, rot, tok, slot_row, loss, head_other):
    lays = [
        jnp.asarray(spread_rows(30, 48, 0), BF),
        jnp.asarray(spread_rows(18, 48, 30), BF),
        jnp.asarray(spread_rows(18, 64, 0, 3), BF),
    ]
    return pl.pallas_call(
        back_kernel,
        name="back",
        out_shape=(
            jax.ShapeDtypeStruct((SUMMED, D), F32),
            jax.ShapeDtypeStruct((NW * CAP, D), BF),
            jax.ShapeDtypeStruct((D, SHARD), BF),
            jax.ShapeDtypeStruct((8, D), F32),
            jax.ShapeDtypeStruct((D, T), BF),
        ),
        in_specs=[VMEM] * 10 + [ANY, VMEM, VMEM, ANY] + [VMEM] * 5 + [ANY] * 4,
        out_specs=(VMEM, VMEM, ANY, VMEM, VMEM),
        scratch_shapes=TRUNK_SCRATCH
        + [
            pltpu.VMEM((NW * 48, QKV), BF),
            pltpu.VMEM((NW * 48, D), BF),
            pltpu.VMEM((NW * 64, D), BF),
            DMA((4,)),
            pltpu.VMEM((2 * FF, T), F32),
            pltpu.VMEM((4, 4, 2, SUMMED, D), BF),
            pltpu.VMEM((NW * CAP, D), BF),
            pltpu.VMEM((2 * FF, T), BF),
            pltpu.VMEM((QKV, T), BF),
            pltpu.VMEM((NW * 64, T), BF),
            pltpu.VMEM((2, D // 2, SHARD), BF),
        ]
        + [DMA((NW,)), DMA((NW,)), DMA((4,)), DMA((4,))]
        + tree_scratch(D)
        + reduce_scratch(),
        compiler_params=params(5, 60),
        cost_estimate=pl.CostEstimate(flops=10**10, bytes_accessed=3 * 10**7, transcendentals=10**6),
    )(grad_final, *kept, packed, gains, rot, tok, slot_row, loss, head_other, *lays)


def adam_update(weight, grad, first, second, rate, decay):
    first = beta_one * first + (1.0 - beta_one) * grad
    second = beta_two * second + (1.0 - beta_two) * grad * grad
    ratio = first / (1.0 - beta_one**STEP) / (jnp.sqrt(second / (1.0 - beta_two**STEP)) + adam_eps)
    return (weight - rate * (ratio + decay * weight), first, second)


def adam_diff(weight, grad, first, second, anchor, rate, decay):
    return anchor - adam_update(weight, grad, first, second, rate, decay)[0]


PIECES = ((0, 0, 96), (0, 96, 96), (0, 192, 96), (1, 0, 112))


def update_kernel(
    rows, hot, head, head_in, summed, extra, tm, tf, ts, ta, *refs
):
    trunk, gains = [refs[3 * i : 3 * i + 3] for i in range(4)], refs[12:16]
    update_body(rows, hot, head, head_in, summed, extra, tm, tf, ts, ta, trunk, gains, *refs[16:])


def update_body(
    rows, hot, head, head_in, summed, extra, tm, tf, ts, ta, trunk_in, gains,
    table_grad_out, total_t, total_k, total_g, norms,
    table_grad, v_rows, v_hot, v_head, v_head_in, vm, vf, vs, va, flipped,
    one_t, one_t_in, two_t, two_t_in, one_k, one_k_in, two_k, two_k_in, gains_out, gains_in,
    load_sem, one_s, one_r, two_s, two_r, three_s, three_r, gains_s, gains_r,
    hold, land_z, land_y, land_x, tree_s, tree_r, km, kf, ks, ka,
):
    me, y, xh, z = place()
    grp = lax.axis_index("grp")
    core, x = lax.rem(grp, 2), grp // 2
    near, far = x * 2 + 1 - core, (1 - x) * 2 + core
    loads = [
        pltpu.make_async_copy(src, dst, load_sem.at[i])
        for i, (src, dst) in enumerate(
            zip((rows, hot, head, head_in, tm, tf, ts, ta), (v_rows, v_hot, v_head, v_head_in, vm, vf, vs, va))
        )
    ]
    for load in loads:
        load.start()
    barrier = pltpu.get_barrier_semaphore()
    for peer in near_peers(me, y, xh, z):
        pl.semaphore_signal(barrier, inc=1, device_id={"wide": peer}, device_id_type=MESH)
    for k in range(1, NG):
        pl.semaphore_signal(
            barrier, inc=1, device_id={"grp": lax.rem(grp + k, NG)}, device_id_type=MESH
        )
    pl.semaphore_wait(barrier, 7 + NG - 1)
    loads[0].wait()
    for c in range(0, NW * CAP, 256):
        flipped[:, c : c + 256] = v_rows[c : c + 256, :].T
    for load in loads[1:4]:
        load.wait()
    squares = jnp.zeros((1, 512), F32)
    for c in range(0, SHARD, 512):
        part = v_head[:, c : c + 512] + v_head_in[:, c : c + 512].astype(F32)
        part = part + mm(flipped[...], v_hot[:, c : c + 512])
        table_grad[:, c : c + 512] = part
        squares = squares + jnp.sum(part * part, 0, keepdims=True)
    save = pltpu.make_async_copy(table_grad, table_grad_out, load_sem.at[0])
    save.start()
    squares = jnp.sum(squares, 1, keepdims=True)
    trunk = jnp.sum(summed[...] * summed[...], 0, keepdims=True)
    squares = squares + jnp.sum(trunk, 1, keepdims=True)
    tree = Tree(hold, land_z, land_y, land_x, tree_s, tree_r)
    tree.start(jnp.broadcast_to(squares, (8, 128)))
    for out, (attn, ffn, proj) in zip((km, kf, ks, ka), trunk_in):
        if out is ka:
            pack_rows(out, attn[...], ffn[...], proj[...])
        else:
            pack_rows(out, attn[:, 0, :], ffn[...], proj[:, 0, :])
        out[PACKED:SUMMED, :] = jnp.zeros((SUMMED - PACKED, D), F32)
    gain_grads = extra[0:3, :]
    gain_squares = jnp.sum(jnp.sum(gain_grads * gain_grads, 0, keepdims=True), 1, keepdims=True)
    tree.next(0)
    for load in loads[4:]:
        load.wait()
    tree.next(1)
    norm = jnp.sqrt(tree.collect(2)[0:1, 0:1] + gain_squares)
    factor = jnp.minimum(1.0, clip_norm / norm)
    down = lax.broadcasted_iota(jnp.int32, (8, 128), 0)
    norms[...] = jnp.where(down == 0, norm, factor)

    parts = (
        (vm, table_grad, vf, vs, va, total_t, D // 2, one_t, one_t_in, two_t, two_t_in),
        (km, summed, kf, ks, ka, total_k, SUMMED // 2, one_k, one_k_in, two_k, two_k_in),
    )
    sent = []

    def span(which, at, count, side):
        half = parts[which][6]
        return pl.ds(pl.multiple_of(side * half + at, 16), count)

    def diff(which, at, count, side):
        m, g, f, s2, a = parts[which][:5]
        rows = span(which, at, count, side)
        return adam_diff(
            m[rows, :], g[rows, :] * factor, f[rows, :], s2[rows, :], a[rows, :], inner_rate, weight_decay
        )

    for i, (which, at, count) in enumerate(PIECES):
        one, one_in = parts[which][7:9]
        rows = pl.ds(at, count)
        one[rows, :] = diff(which, at, count, 1 - core).astype(BF)
        copy = remote(one.at[rows], one_in.at[rows], one_s.at[i], one_r.at[i], grp=near)
        copy.start()
        sent.append(copy)
    for i, (which, at, count) in enumerate(PIECES):
        one, one_in, two, two_in = parts[which][7:11]
        rows = pl.ds(at, count)
        own = diff(which, at, count, core)
        sent[i].wait_recv()
        two[rows, :] = (own + one_in[rows, :].astype(F32)).astype(BF)
        copy = remote(two.at[rows], two_in.at[rows], two_s.at[i], two_r.at[i], grp=far)
        copy.start()
        sent.append(copy)
    gains_out[0:3, :] = adam_diff(
        gains[0][:, 0, :], gain_grads * factor, gains[1][:, 0, :], gains[2][:, 0, :], gains[3][...], gain_rate, 0.0
    )
    gains_out[3:8, :] = jnp.zeros((5, D), F32)
    told = []
    for k in range(1, NG):
        to = lax.rem(grp + k, NG)
        told.append(remote(gains_out, gains_in.at[grp], gains_s.at[k], gains_r.at[grp], grp=to))
        told[-1].start()
    gains_in[grp] = gains_out[...]
    for i, (which, at, count) in enumerate(PIECES):
        total, two, two_in = parts[which][5], parts[which][9], parts[which][10]
        rows = pl.ds(at, count)
        sent[len(PIECES) + i].wait_recv()
        kept = span(which, at, count, core)
        total[kept, :] = two[rows, :].astype(F32) + two_in[rows, :].astype(F32)
        copy = remote(total.at[kept], total.at[kept], three_s.at[i], three_r.at[i], grp=near)
        copy.start()
        sent.append(copy)
    for k in range(1, NG):
        other = lax.rem(grp + k, NG)
        remote(
            gains_out, gains_in.at[other], gains_s.at[k], gains_r.at[other], grp=other
        ).wait_recv()
    total_g[...] = (gains_in[0] + gains_in[1]) + (gains_in[2] + gains_in[3])
    for i, (which, at, count) in enumerate(PIECES):
        away = parts[which][5].at[span(which, at, count, 1 - core)]
        remote(away, away, three_s.at[i], three_r.at[i], grp=near).wait_recv()
    for copy in sent + told:
        copy.wait_send()
    tree.finish()
    save.wait()


def update(rows, hot, head, head_in, summed, extra, table, trunk, gains):
    def exchange(size, lanes):
        return [pltpu.VMEM((size // 2, lanes), BF)] * 4

    table_f32 = pltpu.VMEM((D, SHARD), F32)
    pieces = DMA((len(PIECES),))
    return pl.pallas_call(
        update_kernel,
        name="update",
        out_shape=(
            jax.ShapeDtypeStruct((D, SHARD), F32),
            jax.ShapeDtypeStruct((D, SHARD), F32),
            jax.ShapeDtypeStruct((SUMMED, D), F32),
            jax.ShapeDtypeStruct((8, D), F32),
            jax.ShapeDtypeStruct((8, 128), F32),
        ),
        in_specs=[ANY] * 4 + [VMEM] * 2 + [ANY] * 4 + [VMEM] * 16,
        out_specs=(ANY,) + (VMEM,) * 4,
        scratch_shapes=[
            table_f32,
            pltpu.VMEM((NW * CAP, D), BF),
            pltpu.VMEM((NW * CAP, SHARD), BF),
            table_f32,
            pltpu.VMEM((D, SHARD), BF),
            table_f32,
            table_f32,
            table_f32,
            table_f32,
            pltpu.VMEM((D, NW * CAP), BF),
        ]
        + exchange(D, SHARD)
        + exchange(SUMMED, D)
        + [pltpu.VMEM((8, D), F32), pltpu.VMEM((NG, 8, D), F32), DMA((8,))]
        + [pieces] * 6
        + [DMA((NG,)), DMA((NG,))]
        + tree_scratch(128)
        + [pltpu.VMEM((SUMMED, D), F32)] * 4,
        compiler_params=params(6, 62),
        cost_estimate=pl.CostEstimate(flops=2 * 10**9, bytes_accessed=3 * 10**7, transcendentals=10**6),
    )(rows, hot, head, head_in, summed, extra, *table, *trunk, *gains)


def settle(total, momentum, anchor, grad, first, second):
    average = total * (1.0 / NG)
    outer = outer_momentum * momentum + average
    weight = anchor - outer_rate * (average + outer_momentum * outer)
    first = beta_one * first + (1.0 - beta_one) * grad
    second = beta_two * second + (1.0 - beta_two) * grad * grad
    return average, outer, weight, first, second


def rows_of(packed):
    down = [packed[DOWN_AT + 18 * j : DOWN_AT + 18 * j + 18, 0:512] for j in range(3)]
    proj = jnp.concatenate([packed[ATTN_AT + 30 : PACKED, :]] + down, 1)
    return packed[ATTN_AT : ATTN_AT + 30, :], packed[FFN_AT:DOWN_AT, :], proj


def finish_kernel(norms, weights, *refs):
    table, summed, total_k, extra, total_g = refs[:6], refs[6], refs[7], refs[8], refs[9]
    small = [refs[10 + 4 * i : 14 + 4 * i] for i in range(4)]
    outs = [refs[26 + 5 * i : 31 + 5 * i] for i in range(5)]
    scalars = refs[51:54]
    factor = norms[1:2, 0:1]
    total, momentum, anchor, grad, first, second = table
    values = settle(
        total[...], momentum[...], anchor[...], grad[...] * factor, first[...], second[...]
    )
    for out, value in zip(outs[0], values):
        out[...] = value

    @pl.when(pl.program_id(0) == 0)
    def _():
        scalars[0][0] = jnp.sum(extra[3:4, 0:1])
        scalars[1][0] = jnp.sum(weights[2:3, 0:1])
        scalars[2][0] = jnp.sum(norms[0:1, 0:1])
        grads = rows_of(summed) + (extra[0:3, :],)
        totals = rows_of(total_k) + (total_g[0:3, :],)
        for i in range(4):
            momentum, anchor, first, second = small[i]
            flat_moments = i == 1
            if flat_moments:
                moments = first[...], second[...]
            else:
                moments = first[:, 0, :], second[:, 0, :]
            values = settle(totals[i], momentum[...], anchor[...], grads[i] * factor, *moments)
            for n, (out, value) in enumerate(zip(outs[i + 1], values)):
                if n < 3 or flat_moments:
                    out[...] = value
                else:
                    out[:, 0, :] = value


def finish(norms, weights, table, summed, total_k, extra, total_g, small):
    block = pl.BlockSpec((96, SHARD), lambda i: (i, 0))

    def whole(value):
        return pl.BlockSpec(value.shape, lambda i, rank=len(value.shape): (0,) * rank)

    rest = [summed, total_k, extra, total_g] + [value for kind in small for value in kind]
    shapes = [jax.ShapeDtypeStruct((D, SHARD), F32)] * 5
    for momentum, anchor, first, second in small:
        shapes += [jax.ShapeDtypeStruct(momentum.shape, F32)] * 3
        shapes += [jax.ShapeDtypeStruct(first.shape, F32)] * 2
    return pl.pallas_call(
        finish_kernel,
        name="finish",
        grid=(D // 96,),
        out_shape=tuple(shapes) + (jax.ShapeDtypeStruct((1,), F32),) * 3,
        in_specs=[whole(norms), whole(weights)] + [block] * 6 + [whole(value) for value in rest],
        out_specs=tuple([block] * 5 + [whole(shape) for shape in shapes[5:]])
        + (pl.BlockSpec(memory_space=pltpu.SMEM),) * 3,
        compiler_params=pltpu.CompilerParams(vmem_limit_bytes=62 * MIB),
        cost_estimate=pl.CostEstimate(flops=2 * 10**7, bytes_accessed=4 * 10**7, transcendentals=0),
    )(norms, weights, *table, *rest)


def dot(spec, a, b):
    return jnp.einsum(spec, a, b, preferred_element_type=F32)


def on_device(
    token_ids,
    targets,
    segment_ids,
    row_counts,
    embed_table_master,
    embed_table_first,
    embed_table_second,
    embed_table_anchor,
    embed_table_momentum,
    attn_in_master,
    attn_in_first,
    attn_in_second,
    attn_in_anchor,
    attn_in_momentum,
    ffn_in_master,
    ffn_in_first,
    ffn_in_second,
    ffn_in_anchor,
    ffn_in_momentum,
    proj_out_master,
    proj_out_first,
    proj_out_second,
    proj_out_anchor,
    proj_out_momentum,
    norm_gains_master,
    norm_gains_first,
    norm_gains_second,
    norm_gains_anchor,
    norm_gains_momentum,
):
    ids = token_ids[0]

    def rows_apart(value):
        return value.transpose(2, 0, 1)

    ffn = [v.T for v in (ffn_in_master[0], ffn_in_first[0], ffn_in_second[0], ffn_in_anchor, ffn_in_momentum)]
    attn = [rows_apart(v) for v in (attn_in_master, attn_in_first, attn_in_second)]
    attn += [attn_in_anchor.T, attn_in_momentum.T]
    proj = [rows_apart(v) for v in (proj_out_master, proj_out_first, proj_out_second)]
    proj += [proj_out_anchor.T, proj_out_momentum.T]
    gains = [v.transpose(1, 0, 2) for v in (norm_gains_master, norm_gains_first, norm_gains_second)]
    gains += [norm_gains_anchor, norm_gains_momentum]
    tables = [v.T for v in (embed_table_master[0], embed_table_first[0], embed_table_second[0])]
    tables += [embed_table_anchor.T, embed_table_momentum.T]
    (
        got, rows, most, table, table_other, rows_t, packed_all, picks, slot_row, hot, goals, weights,
    ) = front(
        token_ids, targets, row_counts[0], tables[0], attn[0], ffn[0], proj[0]
    )
    turns = (most[0, 0] + CAP - 1) // CAP

    def asked_in(turn):
        ids_now = jnp.where(turn > 0, ids, 0)
        owner = ids_now // SHARD
        same = ids_now[:, None] == ids_now[None, :]
        before = jnp.arange(T)[None, :] < jnp.arange(T)[:, None]
        first_seen = ~jnp.any(same & before, 1)
        smaller = (owner[None, :] == owner[:, None]) & (ids_now[None, :] < ids_now[:, None])
        rank = jnp.sum(first_seen[None, :] & smaller, 1, dtype=jnp.int32) - turn * CAP
        slot = jnp.where((rank >= 0) & (rank < CAP), owner * CAP + rank, -1)
        chosen = jnp.arange(NW * CAP)[:, None] == slot[None, :]
        asked = jnp.max(jnp.where(chosen, (ids_now - owner * SHARD)[None, :], -1), 1).reshape(NW, 1, CAP)
        asked = jnp.pad(asked, ((0, 0), (0, 0), (0, 128 - CAP)), constant_values=-1)
        return jnp.pad(asked, ((0, 0), (0, 7), (0, 0))), chosen.astype(BF)

    def more_tokens(carry):
        turn, hidden = carry
        message, chosen = asked_in(turn)
        return turn + 1, hidden + dot("sd,st->dt", more_rows(message, table), chosen)

    more = lax.while_loop(
        lambda carry: carry[0] < turns, more_tokens, (jnp.int32(1), jnp.zeros((D, T), F32))
    )[1]

    rot = jnp.asarray(rope())
    final, *kept = forward(more, rows, picks, packed_all, gains[0], rot, segment_ids)
    grad_final, head_own, head_other, loss = head(final, rows_t, table, table_other, goals, weights)
    summed, rows_in, head_in, extra_sum, grad_embedded = back(
        grad_final, kept, packed_all, gains[0], rot, segment_ids, slot_row, loss, head_other
    )

    def more_table(carry):
        turn, grad = carry
        message, chosen = asked_in(turn)
        mine = dot("st,dt->sd", chosen, grad_embedded).astype(BF)
        got_now, rows_now = more_grads(message, mine)
        asked = got_now[:, 0, :CAP].reshape(NW * CAP)
        hot_now = (asked[:, None] == jnp.arange(SHARD)[None, :]).astype(BF)
        return turn + 1, grad + dot("sd,sv->dv", rows_now, hot_now)

    head_grad = lax.while_loop(lambda carry: carry[0] < turns, more_table, (jnp.int32(1), head_own))[1]
    table_grad, total_t, total_k, total_g, norms = update(
        rows_in,
        hot,
        head_grad,
        head_in,
        summed,
        extra_sum,
        tables[:4],
        [kind[i] for i in range(4) for kind in (attn, ffn, proj)],
        gains[:4],
    )
    outs = finish(
        norms,
        weights,
        (total_t, tables[4], tables[3], table_grad, tables[1], tables[2]),
        summed,
        total_k,
        extra_sum,
        total_g,
        [(kind[4], kind[3], kind[1], kind[2]) for kind in (attn, ffn, proj, gains)],
    )
    results = list(outs[25:])
    for index in range(5):
        average, outer, weight, first, second = outs[5 * index : 5 * index + 5]
        if index < 4:
            average, outer, weight = average.T, outer.T, weight.T
        if index in (0, 2):
            first, second = first.T[None], second.T[None]
        elif index == 4:
            first, second = first.transpose(1, 0, 2), second.transpose(1, 0, 2)
        else:
            first, second = first.transpose(1, 2, 0), second.transpose(1, 2, 0)
        results += [average, outer, weight, first, second]
    return tuple(results)


def solution(mesh):
    in_specs = (
        P("grp", "wide"),
        P("grp", "wide"),
        P("grp", "wide"),
        P("grp", "wide", None),
        P("grp", "wide", None),
        P("grp", "wide", None),
        P("grp", "wide", None),
        P("wide", None),
        P("wide", None),
        P("grp", None, "wide"),
        P("grp", None, "wide"),
        P("grp", None, "wide"),
        P(None, "wide"),
        P(None, "wide"),
        P("grp", None, "wide"),
        P("grp", None, "wide"),
        P("grp", None, "wide"),
        P(None, "wide"),
        P(None, "wide"),
        P("grp", None, "wide"),
        P("grp", None, "wide"),
        P("grp", None, "wide"),
        P(None, "wide"),
        P(None, "wide"),
        P("grp", None, None),
        P("grp", None, None),
        P("grp", None, None),
        P(),
        P(),
    )
    out_specs = (
        P("grp"),
        P("grp"),
        P("grp"),
        P("wide", None),
        P("wide", None),
        P("wide", None),
        P("grp", "wide", None),
        P("grp", "wide", None),
        P(None, "wide"),
        P(None, "wide"),
        P(None, "wide"),
        P("grp", None, "wide"),
        P("grp", None, "wide"),
        P(None, "wide"),
        P(None, "wide"),
        P(None, "wide"),
        P("grp", None, "wide"),
        P("grp", None, "wide"),
        P(None, "wide"),
        P(None, "wide"),
        P(None, "wide"),
        P("grp", None, "wide"),
        P("grp", None, "wide"),
        P(),
        P(),
        P(),
        P("grp", None, None),
        P("grp", None, None),
    )
    return jax.shard_map(
        on_device, mesh=mesh, in_specs=in_specs, out_specs=out_specs, check_vma=False
    )
```
